32 devices in a mesh: gx: 8 (over z, y), gy: 4 (over x, core).
Axes of the slice: x: 2, y: 2, z: 4, core: 2. Of those that a mesh axis runs over, the one named last changes fastest.
Arguments:
- density0: float32 [96, 48, 128], P('gx', 'gy'), may hold values from 0.5 to 2
- energy0: float32 [96, 48, 128], P('gx', 'gy'), may hold values from 0.5 to 4.5
- x_velocity: float32 [96, 48, 128], P('gx', 'gy'), may hold values from -1 to 1.5
- y_velocity: float32 [96, 48, 128], P('gx', 'gy'), may hold values from -1 to 1.5
- z_velocity: float32 [96, 48, 128], P('gx', 'gy'), may hold values from -1 to 1.5
- time_increment: float32 [], replicated, may hold values from 0.02 to 0.05
Outputs:
- density_out: float32 [96, 48, 128], P('gx', 'gy')
- energy_out: float32 [96, 48, 128], P('gx', 'gy')
- x_flow: float32 [96, 48, 128], P('gx', 'gy')
- y_flow: float32 [96, 48, 128], P('gx', 'gy')
- z_flow: float32 [96, 48, 128], P('gx', 'gy')
- next_step: float32 [], replicated
The draws below stay inside these ranges and needn't reach their ends.
All inputs are finite; a program needn't handle non-finite values.
Results may differ from the reference program's by a relative error of at most 0.0003.
Values sent between devices are 32-bit elements; how exact they have to be, the bound alone decides.
No kernel may reach another device: no remote copies, remote signals or barrier semaphores. Data moves between devices by JAX's collectives and lax.ppermute only.
A program may use at most 64 MiB of HBM per device.

```python
import jax
import jax.numpy as jnp

NZ = 128
NX = 96
NY = 48


def block_cells(key, offset_x, offset_y):
    spot_key = jax.random.fold_in(key, 97)
    keys = jax.random.split(spot_key, 3)
    corner_x = (jax.random.randint(keys[0], (), 0, NX) + offset_x) % NX
    corner_y = (jax.random.randint(keys[1], (), 0, NY) + offset_y) % NY
    corner_z = jax.random.randint(keys[2], (), 0, NZ)
    inside_x = jnp.remainder(jnp.arange(NX, dtype=jnp.int32) - corner_x, NX) < 3
    inside_y = jnp.remainder(jnp.arange(NY, dtype=jnp.int32) - corner_y, NY) < 3
    inside_z = jnp.remainder(jnp.arange(NZ, dtype=jnp.int32) - corner_z, NZ) < 3
    return inside_x[:, None, None] & inside_y[None, :, None] & inside_z[None, None, :]


def velocity_field(key, offset_x, offset_y, base_field):
    inside = block_cells(key, offset_x, offset_y)
    return jnp.where(inside, jnp.float32(1.5), base_field)


def draw_energy0(key, part):
    inner_key = jax.random.fold_in(key, 11)
    positions = jnp.arange(NX, dtype=jnp.float32)
    profile = 1.0 + positions / (NX - 1)
    texture = jax.random.uniform(inner_key, (NX, NY, NZ), jnp.float32, 0.5, 1.5)
    inside = block_cells(key, 0, 0)
    return jnp.where(inside, jnp.float32(4.5), texture * profile[:, None, None])


def draw_x_velocity(key, part):
    inner_key = jax.random.fold_in(key, 21)
    base_field = jnp.clip(0.5 * jax.random.normal(inner_key, (NX, NY, NZ), jnp.float32), -1.0, 1.0)
    return velocity_field(key, 0, 0, base_field)


def draw_y_velocity(key, part):
    inner_key = jax.random.fold_in(key, 22)
    base_field = jnp.clip(0.5 * jax.random.normal(inner_key, (NX, NY, NZ), jnp.float32), -1.0, 1.0)
    return velocity_field(key, 0, 0, base_field)


def draw_z_velocity(key, part):
    inner_key = jax.random.fold_in(key, 23)
    base_field = jnp.clip(0.5 * jax.random.normal(inner_key, (NX, NY, NZ), jnp.float32), -1.0, 1.0)
    return velocity_field(key, 0, 0, base_field)


def level_of(own_key, dims, pieces, low, top_value):
    factor_of, own = 1.0, jax.random.fold_in(own_key, 6)
    for position, parts in pieces:
        heights = jnp.exp(jax.random.uniform(jax.random.fold_in(own, position), (parts,), jnp.float32, low / len(pieces), top_value / len(pieces)))
        factor_of = factor_of * jnp.repeat(heights, dims[position] // parts).reshape([-1 if axis == position else 1 for axis in range(len(dims))])
    return factor_of


def setup_inputs(seed: int = 0) -> dict:
    streams_of = jax.random.split(jax.random.key(seed), 7)
    return {
        "density0": jnp.clip(0.5 + 1.5 * jax.random.uniform(streams_of[0], (NX, NY, NZ), jnp.float32) ** level_of(streams_of[0], (NX, NY, NZ), ((0, 8), (1, 4)), -0.2, 0.2), 0.5, 2.0),
        "energy0": draw_energy0(jax.random.fold_in(streams_of[6], 71), 0),
        "x_velocity": draw_x_velocity(jax.random.fold_in(streams_of[6], 71), 0),
        "y_velocity": draw_y_velocity(jax.random.fold_in(streams_of[6], 71), 0),
        "z_velocity": draw_z_velocity(jax.random.fold_in(streams_of[6], 71), 0),
        "time_increment": jnp.clip(jax.random.uniform(streams_of[5], (), jnp.float32, 0.02, 0.05), 0.02, 0.05),
    }


def adjacent_cell(field, sweep_direction, shift):
    return jnp.roll(field, -shift, sweep_direction)

def minmod(first, second):
    return 0.5 * (jnp.sign(first) + jnp.sign(second)) * jnp.minimum(jnp.abs(first), jnp.abs(second))

def face_flux(minus_two, minus_one, centre, plus_one, courant_number):
    from_below = minus_one + 0.5 * (1.0 - courant_number) * minmod(centre - minus_one, minus_one - minus_two)
    from_above = centre - 0.5 * (1.0 + courant_number) * minmod(plus_one - centre, centre - minus_one)
    return courant_number * jnp.where(courant_number > 0.0, from_below, from_above)

def lagrange(density0, energy0, x_velocity, y_velocity, z_velocity, time_increment):
    divergence = 0.5 * (adjacent_cell(x_velocity, 0, 1) - adjacent_cell(x_velocity, 0, -1) + (adjacent_cell(y_velocity, 1, 1) - adjacent_cell(y_velocity, 1, -1)) + (adjacent_cell(z_velocity, 2, 1) - adjacent_cell(z_velocity, 2, -1)))
    pressure = 0.4 * density0 * energy0
    viscosity = 0.5 * density0 * jnp.square(jnp.minimum(divergence, 0.0))
    stress = pressure + viscosity
    density1 = density0 / (1.0 + time_increment * divergence)
    energy1 = energy0 - time_increment * stress * divergence / density0
    x_one = x_velocity - time_increment * (0.5 * (adjacent_cell(stress, 0, 1) - adjacent_cell(stress, 0, -1))) / density0
    y_one = y_velocity - time_increment * (0.5 * (adjacent_cell(stress, 1, 1) - adjacent_cell(stress, 1, -1))) / density0
    z_one = z_velocity - time_increment * (0.5 * (adjacent_cell(stress, 2, 1) - adjacent_cell(stress, 2, -1))) / density0
    return ([density1, density1 * energy1, x_one, y_one, z_one], energy1)

def sweep(field_stack, sweep_direction, time_increment):
    transport_field = field_stack[2 + sweep_direction]
    courant_number = time_increment * (0.5 * (adjacent_cell(transport_field, sweep_direction, -1) + transport_field))
    results = []
    for field in field_stack:
        fluxes = face_flux(adjacent_cell(field, sweep_direction, -2), adjacent_cell(field, sweep_direction, -1), field, adjacent_cell(field, sweep_direction, 1), courant_number)
        results.append(field - (adjacent_cell(fluxes, sweep_direction, 1) - fluxes))
    return results

def reference(density0, energy0, x_velocity, y_velocity, z_velocity, time_increment):
    field_stack, energy1 = lagrange(density0, energy0, x_velocity, y_velocity, z_velocity, time_increment)
    for sweep_direction in range(3):
        field_stack = sweep(field_stack, sweep_direction, time_increment)
    signal = jnp.sqrt(0.56 * energy1) + jnp.abs(field_stack[2]) + jnp.abs(field_stack[3]) + jnp.abs(field_stack[4])
    next_step = jnp.min(0.3 / signal)
    return (field_stack[0], field_stack[1], field_stack[2], field_stack[3], field_stack[4], next_step)
```

```python
import jax
import jax.numpy as jnp
from jax import lax
from jax.sharding import PartitionSpec as P


def extended(cells, sides, width):
    for axis, dim in sides:
        count = lax.axis_size(axis)
        head = lax.slice_in_dim(cells, 0, width, axis=dim)
        tail = lax.slice_in_dim(cells, cells.shape[dim] - width, cells.shape[dim], axis=dim)
        cells = jnp.concatenate(
            [
                lax.ppermute(tail, axis, [(i, (i + 1) % count) for i in range(count)]),
                cells,
                lax.ppermute(head, axis, [((i + 1) % count, i) for i in range(count)]),
            ],
            axis=dim,
        )
    return cells


def minmod(first, second):
    return 0.5 * (jnp.sign(first) + jnp.sign(second)) * jnp.minimum(jnp.abs(first), jnp.abs(second))


def face_flux(minus_two, minus_one, centre, plus_one, courant_number):
    from_below = minus_one + 0.5 * (1.0 - courant_number) * minmod(
        centre - minus_one, minus_one - minus_two
    )
    from_above = centre - 0.5 * (1.0 + courant_number) * minmod(
        plus_one - centre, centre - minus_one
    )
    return courant_number * jnp.where(courant_number > 0.0, from_below, from_above)


def window(field, along_x, along_y, margin_cut):
    extent_x = field.shape[0]
    extent_y = field.shape[1]
    return field[
        margin_cut + along_x : extent_x - margin_cut + along_x,
        margin_cut + along_y : extent_y - margin_cut + along_y,
    ]


def roll_z(field, shift):
    return jnp.roll(field, -shift, 2)


def lagrange(padded, time_increment):
    density0 = padded[0]
    energy0 = padded[1]
    x_velocity = padded[2]
    y_velocity = padded[3]
    z_velocity = padded[4]
    z_inner = window(z_velocity, 0, 0, 1)
    divergence = 0.5 * (
        window(x_velocity, 1, 0, 1)
        - window(x_velocity, -1, 0, 1)
        + (window(y_velocity, 0, 1, 1) - window(y_velocity, 0, -1, 1))
        + (roll_z(z_inner, 1) - roll_z(z_inner, -1))
    )
    density_a = window(density0, 0, 0, 1)
    energy_a = window(energy0, 0, 0, 1)
    pressure = 0.4 * density_a * energy_a
    viscosity = 0.5 * density_a * jnp.square(jnp.minimum(divergence, 0.0))
    stress = pressure + viscosity
    density_b = window(density0, 0, 0, 2)
    energy_b = window(energy0, 0, 0, 2)
    divergence_b = window(divergence, 0, 0, 1)
    stress_b = window(stress, 0, 0, 1)
    density1 = density_b / (1.0 + time_increment * divergence_b)
    energy1 = energy_b - time_increment * stress_b * divergence_b / density_b
    x_one = (
        window(x_velocity, 0, 0, 2)
        - time_increment * (0.5 * (window(stress, 1, 0, 1) - window(stress, -1, 0, 1))) / density_b
    )
    y_one = (
        window(y_velocity, 0, 0, 2)
        - time_increment * (0.5 * (window(stress, 0, 1, 1) - window(stress, 0, -1, 1))) / density_b
    )
    z_one = (
        window(z_velocity, 0, 0, 2)
        - time_increment * (0.5 * (roll_z(stress_b, 1) - roll_z(stress_b, -1))) / density_b
    )
    return (jnp.stack([density1, density1 * energy1, x_one, y_one, z_one]), energy1)


def edge_sweep(field_stack, stacking_axis, time_increment):
    length = field_stack.shape[stacking_axis]

    def cell_shift(array, shift):
        return lax.slice_in_dim(array, shift, shift + length - 3, axis=stacking_axis)

    transport_field = field_stack[stacking_axis + 1 : stacking_axis + 2]
    courant_number = time_increment * (
        0.5 * (cell_shift(transport_field, 1) + cell_shift(transport_field, 2))
    )
    fluxes = face_flux(
        cell_shift(field_stack, 0),
        cell_shift(field_stack, 1),
        cell_shift(field_stack, 2),
        cell_shift(field_stack, 3),
        courant_number,
    )
    inner = lax.slice_in_dim(field_stack, 2, length - 2, axis=stacking_axis)
    upper = lax.slice_in_dim(fluxes, 1, length - 3, axis=stacking_axis)
    lower = lax.slice_in_dim(fluxes, 0, length - 4, axis=stacking_axis)
    return inner - (upper - lower)


def roll_sweep(field_stack, time_increment):
    transport_field = field_stack[4:5]
    courant_number = time_increment * (0.5 * (jnp.roll(transport_field, 1, 3) + transport_field))
    fluxes = face_flux(
        jnp.roll(field_stack, 2, 3),
        jnp.roll(field_stack, 1, 3),
        field_stack,
        jnp.roll(field_stack, -1, 3),
        courant_number,
    )
    return field_stack - (jnp.roll(fluxes, -1, 3) - fluxes)


def global_min(local_min, axes):
    count = lax.axis_size(axes[0]) * lax.axis_size(axes[1])
    copies = jnp.broadcast_to(local_min, (count, 1, 128))
    gathered = lax.all_to_all(copies, axes, 0, 0, tiled=True)
    return jnp.min(gathered)


def body(density0, energy0, x_velocity, y_velocity, z_velocity, time_increment):
    field_stack = jnp.stack([density0, energy0, x_velocity, y_velocity, z_velocity])
    padded = extended(field_stack, (("gx", 1), ("gy", 2)), 2)
    field_stack, energy1 = lagrange(padded, time_increment)
    field_stack = extended(field_stack, (("gx", 1),), 2)
    field_stack = edge_sweep(field_stack, 1, time_increment)
    field_stack = extended(field_stack, (("gy", 2),), 2)
    field_stack = edge_sweep(field_stack, 2, time_increment)
    field_stack = roll_sweep(field_stack, time_increment)
    signal = (
        jnp.sqrt(0.56 * energy1)
        + jnp.abs(field_stack[2])
        + jnp.abs(field_stack[3])
        + jnp.abs(field_stack[4])
    )
    local_min = jnp.min(0.3 / signal)
    next_step = global_min(local_min, ("gx", "gy"))
    return (
        field_stack[0],
        field_stack[1],
        field_stack[2],
        field_stack[3],
        field_stack[4],
        next_step,
    )


def solution(mesh):
    return jax.shard_map(
        body,
        mesh=mesh,
        in_specs=(
            P("gx", "gy", None),
            P("gx", "gy", None),
            P("gx", "gy", None),
            P("gx", "gy", None),
            P("gx", "gy", None),
            P(),
        ),
        out_specs=(
            P("gx", "gy", None),
            P("gx", "gy", None),
            P("gx", "gy", None),
            P("gx", "gy", None),
            P("gx", "gy", None),
            P(),
        ),
        check_vma=False,
    )
```

```python
import functools

import jax
import jax.numpy as jnp
from jax import lax
from jax.experimental import pallas as pl
from jax.experimental.pallas import tpu as pltpu
from jax.sharding import PartitionSpec as P

DENSITY, ENERGY, XV, YV, ZV = range(5)
REACH = 4
SIDES = ((-1, 0), (1, 0), (0, -1), (0, 1), (-1, -1), (-1, 1), (1, -1), (1, 1))
TOP = 8
VMEM = pl.BlockSpec(memory_space=pltpu.VMEM)
SMEM = pl.BlockSpec(memory_space=pltpu.SMEM)


def rows_needed(field, a, nx, ny):
    past = max(-a, a - nx + 1, 0)
    if field == XV:
        reach = {0: 3, 1: 3, 2: 3, 3: 3, 4: 2}.get(past, -1)
    elif field == YV:
        reach = {0: 4, 1: 4, 2: 4, 3: 3}.get(past, -1)
    else:
        reach = {0: 3, 1: 3, 2: 3, 3: 2}.get(past, -1)
    return (-reach, ny + reach) if reach >= 0 else (0, 0)


def segments(side, nx, ny):
    columns = {-1: range(-REACH, 0), 0: range(nx), 1: range(nx, nx + REACH)}[side[0]]
    low, high = {-1: (-REACH, 0), 0: (0, ny), 1: (ny, ny + REACH)}[side[1]]
    found, offset = [], 0
    for a in columns:
        for field in range(5):
            first, last = rows_needed(field, a, nx, ny)
            first, last = max(first, low), min(last, high)
            if last > first:
                found.append((field, a, first, last - first, offset))
                offset += last - first
    return found, -(-offset // 8) * 8


def pack_kernel(nx, ny, zero_ref, *refs):
    fields, halos = refs[:5], refs[5:]
    zero = zero_ref[0]
    for side, halo in zip(SIDES, halos):
        for field, a, b, count, offset in segments(side, nx, ny)[0]:
            halo[pl.ds(zero + offset, count), :] = fields[field][
                a - side[0] * nx, pl.ds(zero + (b - side[1] * ny), count), :
            ]


def limited(above, below):
    return jnp.minimum(jnp.maximum(above, jnp.minimum(below, 0.0)), jnp.maximum(below, 0.0))


def face_factors(v_minus, v, half_increment):
    courant = half_increment * (v_minus + v)
    size = jnp.abs(courant)
    return courant, 0.5 * size * (1.0 - size), courant > 0.0


def face_flux(factors, f_minus, f, s_minus, s):
    courant, slope_factor, upward = factors
    return courant * jnp.where(upward, f_minus, f) + slope_factor * jnp.where(upward, s_minus, s)


def step_kernel(nx, ny, zero_ref, dt_ref, *refs):
    fields, halos, outs, peak_ref = refs[:5], refs[5:13], refs[13:18], refs[18]
    cells, stress, growth, heat, state, energy_one, swept, work = refs[19:]
    zero = zero_ref[0]
    dt = dt_ref[0]
    half = 0.5 * dt
    wide = ny + 4
    tall = ny + 12

    for field in range(5):
        for a in range(nx):
            cells[field, a + REACH, pl.ds(TOP, ny), :] = fields[field][a]
    for side, halo in zip(SIDES, halos):
        for field, a, b, count, offset in segments(side, nx, ny)[0]:
            cells[field, a + REACH, pl.ds(zero + (b + TOP), count), :] = halo[pl.ds(zero + offset, count), :]

    def at(ref, *index, start, count):
        return ref[(*index, pl.ds(zero + start, count), slice(None))]

    def up(value):
        return pltpu.roll(value, value.shape[-1] - 1, value.ndim - 1)

    def down(value):
        return pltpu.roll(value, 1, value.ndim - 1)

    for a in range(-3, nx + 3):
        get = functools.partial(at, cells, start=TOP - 4, count=tall)
        z = get(ZV, a + REACH)
        divergence = 0.5 * (
            get(XV, a + REACH + 1)
            - get(XV, a + REACH - 1)
            + (at(cells, YV, a + REACH, start=TOP - 3, count=tall) - at(cells, YV, a + REACH, start=TOP - 5, count=tall))
            + (up(z) - down(z))
        )
        per_mass = 0.4 * get(ENERGY, a + REACH) + 0.5 * jnp.square(jnp.minimum(divergence, 0.0))
        stress[a + 3] = get(DENSITY, a + REACH) * per_mass
        if -2 <= a < nx + 2:
            growth[a + 2] = dt * divergence
            heat[a + 2] = per_mass

    for a in range(-2, nx + 2):
        get = functools.partial(at, cells, start=TOP - 2, count=wide)
        density = get(DENSITY, a + REACH)
        grown = at(growth, a + 2, start=2, count=wide)
        centre = at(stress, a + 3, start=2, count=wide)
        scale = half / density
        density_one = density / (1.0 + grown)
        energy = get(ENERGY, a + REACH) - at(heat, a + 2, start=2, count=wide) * grown
        state[DENSITY, a + 2] = density_one
        state[ENERGY, a + 2] = density_one * energy
        state[XV, a + 2] = get(XV, a + REACH) - scale * (
            at(stress, a + 4, start=2, count=wide) - at(stress, a + 2, start=2, count=wide)
        )
        state[YV, a + 2] = get(YV, a + REACH) - scale * (
            at(stress, a + 3, start=3, count=wide) - at(stress, a + 3, start=1, count=wide)
        )
        state[ZV, a + 2] = get(ZV, a + REACH) - scale * (up(centre) - down(centre))
        if 0 <= a < nx:
            energy_one[a, 0:wide] = energy

    for part in range(0, wide, 8):
        rows = pl.ds(part, 8)
        before = [state[field, 1, rows] for field in range(5)]
        here = [state[field, 2, rows] for field in range(5)]
        steps = [h - b for h, b in zip(here, before)]
        slopes = [limited(st, b - state[field, 0, rows]) for field, (st, b) in enumerate(zip(steps, before))]
        lower = None
        for a in range(nx + 1):
            factors = face_factors(before[XV], here[XV], half)
            fluxes = []
            for field in range(5):
                after = state[field, a + 3, rows]
                step = after - here[field]
                slope = limited(step, steps[field])
                fluxes.append(face_flux(factors, before[field], here[field], slopes[field], slope))
                if lower is not None:
                    swept[field, a - 1, rows] = before[field] - (fluxes[field] - lower[field])
                before[field], here[field], steps[field], slopes[field] = here[field], after, step, slope
            lower = fluxes

    peak = jnp.zeros((wide, swept.shape[-1]), jnp.float32)
    for a in range(nx):
        below = [at(swept, field, a, start=1, count=wide) for field in range(5)]
        here = [at(swept, field, a, start=2, count=wide) for field in range(5)]
        factors = face_factors(below[YV], here[YV], half)
        moved = []
        for field in range(5):
            step = below[field] - swept[field, a, 0:wide]
            slope = limited(here[field] - below[field], step)
            work[field, a, 0:wide] = slope
            flux = face_flux(factors, below[field], here[field], slope, at(work, field, a, start=1, count=wide))
            work[5 + field, a, 0:wide] = flux
            moved.append(here[field] - (at(work, 5 + field, a, start=1, count=wide) - flux))
        below = [down(value) for value in moved]
        factors = face_factors(below[ZV], moved[ZV], half)
        final = []
        for field in range(5):
            step = moved[field] - below[field]
            slope = limited(up(step), step)
            flux = face_flux(factors, below[field], moved[field], down(slope), slope)
            final.append(moved[field] - (up(flux) - flux))
            outs[field][a] = final[field][:ny]
        peak = jnp.maximum(
            peak,
            jnp.sqrt(0.56 * at(energy_one, a, start=2, count=wide))
            + jnp.abs(final[XV])
            + jnp.abs(final[YV])
            + jnp.abs(final[ZV]),
        )
    row = lax.broadcasted_iota(jnp.int32, peak.shape, 0)
    peak = jnp.where(row < ny, peak, 0.0)
    peak_ref[...] = functools.reduce(jnp.maximum, [peak[part : part + 8] for part in range(0, wide, 8)])


def over(value, axis, offset):
    count = lax.axis_size(axis)
    return lax.ppermute(value, axis, [(i, (i + offset) % count) for i in range(count)])


def shifted(value, side):
    gx, gy = lax.axis_size("gx"), lax.axis_size("gy")
    pairs = [
        (((i + side[0]) % gx) * gy + (j + side[1]) % gy, i * gy + j) for i in range(gx) for j in range(gy)
    ]
    return lax.ppermute(value, ("gx", "gy"), pairs)


def all_max(value, axis, radix):
    count, stride = lax.axis_size(axis), 1
    while stride < count:
        offsets = [k * stride for k in range(1, radix) if k * stride < count]
        value = functools.reduce(jnp.maximum, [over(value, axis, offset) for offset in offsets], value)
        stride *= radix
    return value


def body(density0, energy0, x_velocity, y_velocity, z_velocity, time_increment):
    nx, ny, nz = density0.shape
    fields = (density0, energy0, x_velocity, y_velocity, z_velocity)
    zero = jnp.zeros((1,), jnp.int32)
    sizes = [segments(side, nx, ny)[1] for side in SIDES]
    halos = pl.pallas_call(
        functools.partial(pack_kernel, nx, ny),
        out_shape=[jax.ShapeDtypeStruct((size, nz), jnp.float32) for size in sizes],
        in_specs=[SMEM] + [VMEM] * 5,
        out_specs=[VMEM] * len(SIDES),
        name="pack",
    )(zero, *fields)
    halos = [shifted(halo, side) for halo, side in zip(halos, SIDES)]
    wide, tall = ny + 4, ny + 12

    def scratch(*shape):
        return pltpu.VMEM((*shape, nz), jnp.float32)

    *outs, peak = pl.pallas_call(
        functools.partial(step_kernel, nx, ny),
        out_shape=[jax.ShapeDtypeStruct((nx, ny, nz), jnp.float32)] * 5 + [jax.ShapeDtypeStruct((8, nz), jnp.float32)],
        in_specs=[SMEM, SMEM] + [VMEM] * 13,
        out_specs=[VMEM] * 6,
        scratch_shapes=[
            scratch(5, nx + 8, ny + 20),
            scratch(nx + 6, tall),
            scratch(nx + 4, tall),
            scratch(nx + 4, tall),
            scratch(5, nx + 4, wide),
            scratch(nx, wide + 8),
            scratch(5, nx, wide + 8),
            scratch(10, nx, wide + 8),
        ],
        compiler_params=pltpu.CompilerParams(vmem_limit_bytes=32 * 1024 * 1024),
        name="step",
    )(zero, time_increment.reshape(1), *fields, *halos)
    peak = all_max(all_max(peak, "gy", 4), "gx", 8)
    return (*outs, 0.3 / jnp.max(peak))


def solution(mesh):
    cells = P("gx", "gy", None)
    return jax.shard_map(
        body,
        mesh=mesh,
        in_specs=(cells,) * 5 + (P(),),
        out_specs=(cells,) * 5 + (P(),),
        check_vma=False,
    )
```

```python
import functools

import jax
import jax.numpy as jnp
from jax import lax
from jax.experimental import pallas as pl
from jax.experimental.pallas import tpu as pltpu
from jax.sharding import PartitionSpec as P

DENSITY, ENERGY, XV, YV, ZV = range(5)
REACH = 4
SIDES = ((-1, 0), (1, 0), (0, -1), (0, 1))
TOP = 8
VMEM = pl.BlockSpec(memory_space=pltpu.VMEM)
SMEM = pl.BlockSpec(memory_space=pltpu.SMEM)


def rows_needed(field, a, nx, ny):
    past = max(-a, a - nx + 1, 0)
    if field == XV:
        reach = {0: 3, 1: 3, 2: 3, 3: 3, 4: 2}.get(past, -1)
    elif field == YV:
        reach = {0: 4, 1: 4, 2: 4, 3: 3}.get(past, -1)
    else:
        reach = {0: 3, 1: 3, 2: 3, 3: 2}.get(past, -1)
    return (-reach, ny + reach) if reach >= 0 else (0, 0)


def segments(side, nx, ny):
    columns = {-1: range(-REACH, 0), 0: range(nx), 1: range(nx, nx + REACH)}[side[0]]
    low, high = {-1: (-REACH, 0), 0: (0, ny), 1: (ny, ny + REACH)}[side[1]]
    found, offset = [], 0
    for a in columns:
        for field in range(5):
            first, last = rows_needed(field, a, nx, ny)
            first, last = max(first, low), min(last, high)
            if last > first:
                found.append((field, a, first, last - first, offset))
                offset += last - first
    return found, -(-offset // 8) * 8


def corner_segments(side_y, nx, ny):
    found, offset = [], 0
    for side_x in (-1, 1):
        for field, a, first, count, _ in segments((side_x, side_y), nx, ny)[0]:
            found.append((side_x, field, a, first, count, offset))
            offset += count
    return found, -(-offset // 8) * 8


def pack_kernel(nx, ny, zero_ref, *refs):
    fields, halos = refs[:5], refs[5:]
    zero = zero_ref[0]
    for side, halo in zip(SIDES, halos):
        for field, a, b, count, offset in segments(side, nx, ny)[0]:
            halo[pl.ds(zero + offset, count), :] = fields[field][
                a - side[0] * nx, pl.ds(zero + (b - side[1] * ny), count), :
            ]


def corner_kernel(nx, ny, zero_ref, below_ref, above_ref, low_ref, high_ref):
    zero = zero_ref[0]
    held = {
        (side_x, field, a): (ref, offset)
        for side_x, ref in ((-1, below_ref), (1, above_ref))
        for field, a, _, _, offset in segments((side_x, 0), nx, ny)[0]
    }
    for side_y, out in ((-1, low_ref), (1, high_ref)):
        for side_x, field, a, b, count, offset in corner_segments(side_y, nx, ny)[0]:
            ref, start = held[side_x, field, a]
            out[pl.ds(zero + offset, count), :] = ref[pl.ds(zero + (start + b - side_y * ny), count), :]


def limited(above, below):
    return jnp.minimum(jnp.maximum(above, jnp.minimum(below, 0.0)), jnp.maximum(below, 0.0))


def face_factors(v_minus, v, half_increment):
    courant = half_increment * (v_minus + v)
    size = jnp.abs(courant)
    return courant, 0.5 * size * (1.0 - size), courant > 0.0


def face_flux(factors, f_minus, f, s_minus, s):
    courant, slope_factor, upward = factors
    return courant * jnp.where(upward, f_minus, f) + slope_factor * jnp.where(upward, s_minus, s)


def step_kernel(nx, ny, zero_ref, dt_ref, *refs):
    fields, halos, outs, peak_ref = refs[:5], refs[5:11], refs[11:16], refs[16]
    cells, stress, growth, heat, state, energy_one, swept, work = refs[17:]
    zero = zero_ref[0]
    dt = dt_ref[0]
    half = 0.5 * dt
    wide = ny + 4
    tall = ny + 12

    for field in range(5):
        for a in range(nx):
            cells[field, a + REACH, pl.ds(TOP, ny), :] = fields[field][a]
    for side, halo in zip(SIDES, halos):
        for field, a, b, count, offset in segments(side, nx, ny)[0]:
            cells[field, a + REACH, pl.ds(zero + (b + TOP), count), :] = halo[pl.ds(zero + offset, count), :]
    for side_y, halo in zip((-1, 1), halos[len(SIDES) :]):
        for _, field, a, b, count, offset in corner_segments(side_y, nx, ny)[0]:
            cells[field, a + REACH, pl.ds(zero + (b + TOP), count), :] = halo[pl.ds(zero + offset, count), :]

    def at(ref, *index, start, count):
        return ref[(*index, pl.ds(zero + start, count), slice(None))]

    def up(value):
        return pltpu.roll(value, value.shape[-1] - 1, value.ndim - 1)

    def down(value):
        return pltpu.roll(value, 1, value.ndim - 1)

    for a in range(-3, nx + 3):
        get = functools.partial(at, cells, start=TOP - 4, count=tall)
        z = get(ZV, a + REACH)
        divergence = 0.5 * (
            get(XV, a + REACH + 1)
            - get(XV, a + REACH - 1)
            + (at(cells, YV, a + REACH, start=TOP - 3, count=tall) - at(cells, YV, a + REACH, start=TOP - 5, count=tall))
            + (up(z) - down(z))
        )
        per_mass = 0.4 * get(ENERGY, a + REACH) + 0.5 * jnp.square(jnp.minimum(divergence, 0.0))
        stress[a + 3] = get(DENSITY, a + REACH) * per_mass
        if -2 <= a < nx + 2:
            growth[a + 2] = dt * divergence
            heat[a + 2] = per_mass

    for a in range(-2, nx + 2):
        get = functools.partial(at, cells, start=TOP - 2, count=wide)
        density = get(DENSITY, a + REACH)
        grown = at(growth, a + 2, start=2, count=wide)
        centre = at(stress, a + 3, start=2, count=wide)
        scale = half / density
        density_one = density / (1.0 + grown)
        energy = get(ENERGY, a + REACH) - at(heat, a + 2, start=2, count=wide) * grown
        state[DENSITY, a + 2] = density_one
        state[ENERGY, a + 2] = density_one * energy
        state[XV, a + 2] = get(XV, a + REACH) - scale * (
            at(stress, a + 4, start=2, count=wide) - at(stress, a + 2, start=2, count=wide)
        )
        state[YV, a + 2] = get(YV, a + REACH) - scale * (
            at(stress, a + 3, start=3, count=wide) - at(stress, a + 3, start=1, count=wide)
        )
        state[ZV, a + 2] = get(ZV, a + REACH) - scale * (up(centre) - down(centre))
        if 0 <= a < nx:
            energy_one[a, 0:wide] = energy

    for part in range(0, wide, 8):
        rows = pl.ds(part, 8)
        before = [state[field, 1, rows] for field in range(5)]
        here = [state[field, 2, rows] for field in range(5)]
        steps = [h - b for h, b in zip(here, before)]
        slopes = [limited(st, b - state[field, 0, rows]) for field, (st, b) in enumerate(zip(steps, before))]
        lower = None
        for a in range(nx + 1):
            factors = face_factors(before[XV], here[XV], half)
            fluxes = []
            for field in range(5):
                after = state[field, a + 3, rows]
                step = after - here[field]
                slope = limited(step, steps[field])
                fluxes.append(face_flux(factors, before[field], here[field], slopes[field], slope))
                if lower is not None:
                    swept[field, a - 1, rows] = before[field] - (fluxes[field] - lower[field])
                before[field], here[field], steps[field], slopes[field] = here[field], after, step, slope
            lower = fluxes

    peak = jnp.zeros((wide, swept.shape[-1]), jnp.float32)
    for a in range(nx):
        below = [at(swept, field, a, start=1, count=wide) for field in range(5)]
        here = [at(swept, field, a, start=2, count=wide) for field in range(5)]
        factors = face_factors(below[YV], here[YV], half)
        moved = []
        for field in range(5):
            step = below[field] - swept[field, a, 0:wide]
            slope = limited(here[field] - below[field], step)
            work[field, a, 0:wide] = slope
            flux = face_flux(factors, below[field], here[field], slope, at(work, field, a, start=1, count=wide))
            work[5 + field, a, 0:wide] = flux
            moved.append(here[field] - (at(work, 5 + field, a, start=1, count=wide) - flux))
        below = [down(value) for value in moved]
        factors = face_factors(below[ZV], moved[ZV], half)
        final = []
        for field in range(5):
            step = moved[field] - below[field]
            slope = limited(up(step), step)
            flux = face_flux(factors, below[field], moved[field], down(slope), slope)
            final.append(moved[field] - (up(flux) - flux))
            outs[field][a] = final[field][:ny]
        peak = jnp.maximum(
            peak,
            jnp.sqrt(0.56 * at(energy_one, a, start=2, count=wide))
            + jnp.abs(final[XV])
            + jnp.abs(final[YV])
            + jnp.abs(final[ZV]),
        )
    row = lax.broadcasted_iota(jnp.int32, peak.shape, 0)
    peak = jnp.where(row < ny, peak, 0.0)
    peak_ref[...] = jnp.max(peak, axis=0, keepdims=True)


def shifted(value, side):
    axis, step = ("gx", side[0]) if side[0] else ("gy", side[1])
    count = lax.axis_size(axis)
    return lax.ppermute(value, axis, [((i + step) % count, i) for i in range(count)])


def body(density0, energy0, x_velocity, y_velocity, z_velocity, time_increment):
    nx, ny, nz = density0.shape
    fields = (density0, energy0, x_velocity, y_velocity, z_velocity)
    zero = jnp.zeros((1,), jnp.int32)
    sizes = [segments(side, nx, ny)[1] for side in SIDES]
    halos = pl.pallas_call(
        functools.partial(pack_kernel, nx, ny),
        out_shape=[jax.ShapeDtypeStruct((size, nz), jnp.float32) for size in sizes],
        in_specs=[SMEM] + [VMEM] * 5,
        out_specs=[VMEM] * len(SIDES),
        name="pack",
    )(zero, *fields)
    halos = [shifted(halo, side) for halo, side in zip(halos, SIDES)]
    corner_rows = corner_segments(1, nx, ny)[1]
    corners = pl.pallas_call(
        functools.partial(corner_kernel, nx, ny),
        out_shape=[jax.ShapeDtypeStruct((corner_rows, nz), jnp.float32)] * 2,
        in_specs=[SMEM] + [VMEM] * 2,
        out_specs=[VMEM] * 2,
        name="corners",
    )(zero, halos[0], halos[1])
    halos += [shifted(corner, (0, side_y)) for corner, side_y in zip(corners, (-1, 1))]
    wide, tall = ny + 4, ny + 12

    def scratch(*shape):
        return pltpu.VMEM((*shape, nz), jnp.float32)

    *outs, peak = pl.pallas_call(
        functools.partial(step_kernel, nx, ny),
        out_shape=[jax.ShapeDtypeStruct((nx, ny, nz), jnp.float32)] * 5 + [jax.ShapeDtypeStruct((1, nz), jnp.float32)],
        in_specs=[SMEM, SMEM] + [VMEM] * 11,
        out_specs=[VMEM] * 6,
        scratch_shapes=[
            scratch(5, nx + 8, ny + 20),
            scratch(nx + 6, tall),
            scratch(nx + 4, tall),
            scratch(nx + 4, tall),
            scratch(5, nx + 4, wide),
            scratch(nx, wide + 8),
            scratch(5, nx, wide + 8),
            scratch(10, nx, wide + 8),
        ],
        compiler_params=pltpu.CompilerParams(vmem_limit_bytes=32 * 1024 * 1024),
        name="step",
    )(zero, time_increment.reshape(1), *fields, *halos)
    peak = lax.all_gather(peak, ("gx", "gy"), tiled=True)
    return (*outs, 0.3 / jnp.max(peak))


def solution(mesh):
    cells = P("gx", "gy", None)
    return jax.shard_map(
        body,
        mesh=mesh,
        in_specs=(cells,) * 5 + (P(),),
        out_specs=(cells,) * 5 + (P(),),
        check_vma=False,
    )
```

```python
import functools

import jax
import jax.numpy as jnp
from jax import lax
from jax.experimental import pallas as pl
from jax.experimental.pallas import tpu as pltpu
from jax.sharding import PartitionSpec as P

DENSITY, ENERGY, XV, YV, ZV = range(5)
REACH = 4
SIDES = ((-1, 0), (1, 0), (0, -1), (0, 1))
TOP = 8
VMEM = pl.BlockSpec(memory_space=pltpu.VMEM)
HBM = pl.BlockSpec(memory_space=pltpu.HBM)
SMEM = pl.BlockSpec(memory_space=pltpu.SMEM)


def rows_needed(field, a, nx, ny):
    past = max(-a, a - nx + 1, 0)
    if field == XV:
        reach = {0: 3, 1: 3, 2: 3, 3: 3, 4: 2}.get(past, -1)
    elif field == YV:
        reach = {0: 4, 1: 4, 2: 4, 3: 3}.get(past, -1)
    else:
        reach = {0: 3, 1: 3, 2: 3, 3: 2}.get(past, -1)
    return (-reach, ny + reach) if reach >= 0 else (0, 0)


def segments(side, nx, ny):
    columns = {-1: range(-REACH, 0), 0: range(nx), 1: range(nx, nx + REACH)}[side[0]]
    low, high = {-1: (-REACH, 0), 0: (0, ny), 1: (ny, ny + REACH)}[side[1]]
    found, offset = [], 0
    for a in columns:
        for field in range(5):
            first, last = rows_needed(field, a, nx, ny)
            first, last = max(first, low), min(last, high)
            if last > first:
                found.append((field, a, first, last - first, offset))
                offset += last - first
    return found, -(-offset // 8) * 8


def corner_segments(side_y, nx, ny):
    found, offset = [], 0
    for side_x in (-1, 1):
        for field, a, first, count, _ in segments((side_x, side_y), nx, ny)[0]:
            found.append((side_x, field, a, first, count, offset))
            offset += count
    return found, -(-offset // 8) * 8


def pack_kernel(nx, ny, zero_ref, *refs):
    fields, own, edges, arrived = refs[:5], refs[5], refs[6 : 6 + len(SIDES)], refs[-1]
    zero = zero_ref[0]
    copies = [pltpu.make_async_copy(fields[field], own.at[field], arrived.at[field]) for field in range(5)]
    for copy in copies:
        copy.start()
    for current, copy in enumerate(copies):
        copy.wait()
        for side, edge in zip(SIDES, edges):
            for field, a, b, count, offset in segments(side, nx, ny)[0]:
                if field == current:
                    edge[pl.ds(zero + offset, count), :] = own[
                        field, a - side[0] * nx, pl.ds(zero + (b - side[1] * ny), count), :
                    ]


def corner_kernel(nx, ny, zero_ref, below_ref, above_ref, low_ref, high_ref):
    zero = zero_ref[0]
    held = {
        (side_x, field, a): (ref, offset)
        for side_x, ref in ((-1, below_ref), (1, above_ref))
        for field, a, _, _, offset in segments((side_x, 0), nx, ny)[0]
    }
    for side_y, out in ((-1, low_ref), (1, high_ref)):
        for side_x, field, a, b, count, offset in corner_segments(side_y, nx, ny)[0]:
            ref, start = held[side_x, field, a]
            out[pl.ds(zero + offset, count), :] = ref[pl.ds(zero + (start + b - side_y * ny), count), :]


def limited(above, below):
    return jnp.minimum(jnp.maximum(above, jnp.minimum(below, 0.0)), jnp.maximum(below, 0.0))


def face_factors(v_minus, v, half_increment):
    courant = half_increment * (v_minus + v)
    size = jnp.abs(courant)
    return courant, 0.5 * size * (1.0 - size), courant > 0.0


def face_flux(factors, f_minus, f, s_minus, s):
    courant, slope_factor, upward = factors
    return courant * jnp.where(upward, f_minus, f) + slope_factor * jnp.where(upward, s_minus, s)


def step_kernel(nx, ny, zero_ref, dt_ref, *refs):
    own, halos, outs, peak_ref = refs[0], refs[1:7], refs[7:12], refs[12]
    cells, stress, growth, heat, state, energy_one, swept, work = refs[13:]
    zero = zero_ref[0]
    dt = dt_ref[0]
    half = 0.5 * dt
    wide = ny + 4
    tall = ny + 12

    for field in range(5):
        for a in range(nx):
            cells[field, a + REACH, pl.ds(TOP, ny), :] = own[field, a]
    for side, halo in zip(SIDES, halos):
        for field, a, b, count, offset in segments(side, nx, ny)[0]:
            cells[field, a + REACH, pl.ds(zero + (b + TOP), count), :] = halo[pl.ds(zero + offset, count), :]
    for side_y, halo in zip((-1, 1), halos[len(SIDES) :]):
        for _, field, a, b, count, offset in corner_segments(side_y, nx, ny)[0]:
            cells[field, a + REACH, pl.ds(zero + (b + TOP), count), :] = halo[pl.ds(zero + offset, count), :]

    def at(ref, *index, start, count):
        return ref[(*index, pl.ds(zero + start, count), slice(None))]

    def up(value):
        return pltpu.roll(value, value.shape[-1] - 1, value.ndim - 1)

    def down(value):
        return pltpu.roll(value, 1, value.ndim - 1)

    for a in range(-3, nx + 3):
        get = functools.partial(at, cells, start=TOP - 4, count=tall)
        z = get(ZV, a + REACH)
        divergence = 0.5 * (
            get(XV, a + REACH + 1)
            - get(XV, a + REACH - 1)
            + (at(cells, YV, a + REACH, start=TOP - 3, count=tall) - at(cells, YV, a + REACH, start=TOP - 5, count=tall))
            + (up(z) - down(z))
        )
        per_mass = 0.4 * get(ENERGY, a + REACH) + 0.5 * jnp.square(jnp.minimum(divergence, 0.0))
        stress[a + 3] = get(DENSITY, a + REACH) * per_mass
        if -2 <= a < nx + 2:
            growth[a + 2] = dt * divergence
            heat[a + 2] = per_mass

    for a in range(-2, nx + 2):
        get = functools.partial(at, cells, start=TOP - 2, count=wide)
        density = get(DENSITY, a + REACH)
        grown = at(growth, a + 2, start=2, count=wide)
        centre = at(stress, a + 3, start=2, count=wide)
        scale = half / density
        density_one = density / (1.0 + grown)
        energy = get(ENERGY, a + REACH) - at(heat, a + 2, start=2, count=wide) * grown
        state[DENSITY, a + 2] = density_one
        state[ENERGY, a + 2] = density_one * energy
        state[XV, a + 2] = get(XV, a + REACH) - scale * (
            at(stress, a + 4, start=2, count=wide) - at(stress, a + 2, start=2, count=wide)
        )
        state[YV, a + 2] = get(YV, a + REACH) - scale * (
            at(stress, a + 3, start=3, count=wide) - at(stress, a + 3, start=1, count=wide)
        )
        state[ZV, a + 2] = get(ZV, a + REACH) - scale * (up(centre) - down(centre))
        if 0 <= a < nx:
            energy_one[a, 0:wide] = energy

    for part in range(0, wide, 8):
        rows = pl.ds(part, 8)
        before = [state[field, 1, rows] for field in range(5)]
        here = [state[field, 2, rows] for field in range(5)]
        steps = [h - b for h, b in zip(here, before)]
        slopes = [limited(st, b - state[field, 0, rows]) for field, (st, b) in enumerate(zip(steps, before))]
        lower = None
        for a in range(nx + 1):
            factors = face_factors(before[XV], here[XV], half)
            fluxes = []
            for field in range(5):
                after = state[field, a + 3, rows]
                step = after - here[field]
                slope = limited(step, steps[field])
                fluxes.append(face_flux(factors, before[field], here[field], slopes[field], slope))
                if lower is not None:
                    swept[field, a - 1, rows] = before[field] - (fluxes[field] - lower[field])
                before[field], here[field], steps[field], slopes[field] = here[field], after, step, slope
            lower = fluxes

    peak = jnp.zeros((wide, swept.shape[-1]), jnp.float32)
    for a in range(nx):
        below = [at(swept, field, a, start=1, count=wide) for field in range(5)]
        here = [at(swept, field, a, start=2, count=wide) for field in range(5)]
        factors = face_factors(below[YV], here[YV], half)
        moved = []
        for field in range(5):
            step = below[field] - swept[field, a, 0:wide]
            slope = limited(here[field] - below[field], step)
            work[field, a, 0:wide] = slope
            flux = face_flux(factors, below[field], here[field], slope, at(work, field, a, start=1, count=wide))
            work[5 + field, a, 0:wide] = flux
            moved.append(here[field] - (at(work, 5 + field, a, start=1, count=wide) - flux))
        below = [down(value) for value in moved]
        factors = face_factors(below[ZV], moved[ZV], half)
        final = []
        for field in range(5):
            step = moved[field] - below[field]
            slope = limited(up(step), step)
            flux = face_flux(factors, below[field], moved[field], down(slope), slope)
            final.append(moved[field] - (up(flux) - flux))
            outs[field][a] = final[field][:ny]
        peak = jnp.maximum(
            peak,
            jnp.sqrt(0.56 * at(energy_one, a, start=2, count=wide))
            + jnp.abs(final[XV])
            + jnp.abs(final[YV])
            + jnp.abs(final[ZV]),
        )
    row = lax.broadcasted_iota(jnp.int32, peak.shape, 0)
    peak = jnp.where(row < ny, peak, 0.0)
    peak = jnp.max(peak, axis=0, keepdims=True)
    for copy in range(peak_ref.shape[0]):
        peak_ref[copy] = peak


def shifted(value, side):
    axis, step = ("gx", side[0]) if side[0] else ("gy", side[1])
    count = lax.axis_size(axis)
    return lax.ppermute(value, axis, [((i + step) % count, i) for i in range(count)])


def all_max(copies, axis):
    return jnp.max(lax.all_to_all(copies, axis, 0, 0, tiled=True), axis=0)


def body(density0, energy0, x_velocity, y_velocity, z_velocity, time_increment):
    nx, ny, nz = density0.shape
    fields = (density0, energy0, x_velocity, y_velocity, z_velocity)
    zero = jnp.zeros((1,), jnp.int32)
    wide, tall = ny + 4, ny + 12

    def array(*shape):
        return jax.ShapeDtypeStruct((*shape, nz), jnp.float32)

    def scratch(*shape):
        return pltpu.VMEM((*shape, nz), jnp.float32)

    def limit(mebibytes):
        return pltpu.CompilerParams(vmem_limit_bytes=mebibytes * 1024 * 1024)

    own, *edges = pl.pallas_call(
        functools.partial(pack_kernel, nx, ny),
        out_shape=[array(5, nx, ny)] + [array(segments(side, nx, ny)[1]) for side in SIDES],
        in_specs=[SMEM] + [HBM] * 5,
        out_specs=[VMEM] * (1 + len(SIDES)),
        scratch_shapes=[pltpu.SemaphoreType.DMA((5,))],
        compiler_params=limit(4),
        name="pack",
    )(zero, *[pltpu.with_memory_space_constraint(field, pltpu.HBM) for field in fields])
    edges = [shifted(edge, side) for edge, side in zip(edges, SIDES)]
    corners = pl.pallas_call(
        functools.partial(corner_kernel, nx, ny),
        out_shape=[array(corner_segments(1, nx, ny)[1])] * 2,
        in_specs=[SMEM] + [VMEM] * 2,
        out_specs=[VMEM] * 2,
        compiler_params=limit(4),
        name="corners",
    )(zero, edges[0], edges[1])
    corners = [shifted(corner, (0, side_y)) for corner, side_y in zip(corners, (-1, 1))]
    *outs, peak = pl.pallas_call(
        functools.partial(step_kernel, nx, ny),
        out_shape=[array(nx, ny)] * 5 + [array(lax.axis_size("gy"), 1)],
        in_specs=[SMEM, SMEM] + [VMEM] * 7,
        out_specs=[VMEM] * 6,
        scratch_shapes=[
            scratch(5, nx + 8, ny + 20),
            scratch(nx + 6, tall),
            scratch(nx + 4, tall),
            scratch(nx + 4, tall),
            scratch(5, nx + 4, wide),
            scratch(nx, wide + 8),
            scratch(5, nx, wide + 8),
            scratch(10, nx, wide + 8),
        ],
        compiler_params=limit(12),
        name="step",
    )(zero, time_increment.reshape(1), own, *edges, *corners)
    peak = all_max(peak, "gy")
    peak = all_max(jnp.broadcast_to(peak, (lax.axis_size("gx"), 1, nz)), "gx")
    return (*outs, 0.3 / jnp.max(peak))


def solution(mesh):
    cells = P("gx", "gy", None)
    return jax.shard_map(
        body,
        mesh=mesh,
        in_specs=(cells,) * 5 + (P(),),
        out_specs=(cells,) * 5 + (P(),),
        check_vma=False,
    )
```

```python
import functools

import jax
import jax.numpy as jnp
from jax import lax
from jax.experimental import pallas as pl
from jax.experimental.pallas import tpu as pltpu
from jax.sharding import PartitionSpec as P

DENSITY, ENERGY, XV, YV, ZV = range(5)
REACH = 4
SIDES = ((-1, 0), (1, 0), (0, -1), (0, 1))
TOP = 8
VMEM = pl.BlockSpec(memory_space=pltpu.VMEM)
HBM = pl.BlockSpec(memory_space=pltpu.HBM)
SMEM = pl.BlockSpec(memory_space=pltpu.SMEM)


def rows_needed(field, a, nx, ny):
    past = max(-a, a - nx + 1, 0)
    if field == XV:
        reach = {0: 3, 1: 3, 2: 3, 3: 3, 4: 2}.get(past, -1)
    elif field == YV:
        reach = {0: 4, 1: 4, 2: 4, 3: 3}.get(past, -1)
    else:
        reach = {0: 3, 1: 3, 2: 3, 3: 2}.get(past, -1)
    return (-reach, ny + reach) if reach >= 0 else (0, 0)


def segments(side, nx, ny):
    columns = {-1: range(-REACH, 0), 0: range(nx), 1: range(nx, nx + REACH)}[side[0]]
    low, high = {-1: (-REACH, 0), 0: (0, ny), 1: (ny, ny + REACH)}[side[1]]
    found, offset = [], 0
    for a in columns:
        for field in range(5):
            first, last = rows_needed(field, a, nx, ny)
            first, last = max(first, low), min(last, high)
            if last > first:
                found.append((field, a, first, last - first, offset))
                offset += last - first
    return found, -(-offset // 8) * 8


def corner_segments(side_y, nx, ny):
    found, offset = [], 0
    for side_x in (-1, 1):
        for field, a, first, count, _ in segments((side_x, side_y), nx, ny)[0]:
            found.append((side_x, field, a, first, count, offset))
            offset += count
    return found, -(-offset // 8) * 8


def pack_kernel(nx, ny, zero_ref, *refs):
    fields, own, edges, arrived = refs[:5], refs[5], refs[6 : 6 + len(SIDES)], refs[-1]
    zero = zero_ref[0]
    copies = [pltpu.make_async_copy(fields[field], own.at[field], arrived.at[field]) for field in range(5)]
    for copy in copies:
        copy.start()
    for current, copy in enumerate(copies):
        copy.wait()
        for side, edge in zip(SIDES, edges):
            for field, a, b, count, offset in segments(side, nx, ny)[0]:
                if field == current:
                    edge[pl.ds(zero + offset, count), :] = own[
                        field, a - side[0] * nx, pl.ds(zero + (b - side[1] * ny), count), :
                    ]


def corner_kernel(nx, ny, zero_ref, below_ref, above_ref, low_ref, high_ref):
    zero = zero_ref[0]
    held = {
        (side_x, field, a): (ref, offset)
        for side_x, ref in ((-1, below_ref), (1, above_ref))
        for field, a, _, _, offset in segments((side_x, 0), nx, ny)[0]
    }
    for side_y, out in ((-1, low_ref), (1, high_ref)):
        for side_x, field, a, b, count, offset in corner_segments(side_y, nx, ny)[0]:
            ref, start = held[side_x, field, a]
            out[pl.ds(zero + offset, count), :] = ref[pl.ds(zero + (start + b - side_y * ny), count), :]


def limited(above, below):
    return jnp.minimum(jnp.maximum(above, jnp.minimum(below, 0.0)), jnp.maximum(below, 0.0))


def face_factors(v_minus, v, half_increment):
    courant = half_increment * (v_minus + v)
    size = jnp.abs(courant)
    return courant, 0.5 * size * (1.0 - size), courant > 0.0


def face_flux(factors, f_minus, f, s_minus, s):
    courant, slope_factor, upward = factors
    return courant * jnp.where(upward, f_minus, f) + slope_factor * jnp.where(upward, s_minus, s)


def step_kernel(nx, ny, zero_ref, dt_ref, *refs):
    own, halos, outs, peak_ref = refs[0], refs[1:7], refs[7:12], refs[12]
    cells, stress, growth, heat, state, energy_one, swept, work = refs[13:]
    zero = zero_ref[0]
    dt = dt_ref[0]
    half = 0.5 * dt
    wide = ny + 4
    tall = ny + 12

    for field in range(5):
        for a in range(nx):
            cells[field, a + REACH, pl.ds(TOP, ny), :] = own[field, a]
    for side, halo in zip(SIDES, halos):
        for field, a, b, count, offset in segments(side, nx, ny)[0]:
            cells[field, a + REACH, pl.ds(zero + (b + TOP), count), :] = halo[pl.ds(zero + offset, count), :]
    for side_y, halo in zip((-1, 1), halos[len(SIDES) :]):
        for _, field, a, b, count, offset in corner_segments(side_y, nx, ny)[0]:
            cells[field, a + REACH, pl.ds(zero + (b + TOP), count), :] = halo[pl.ds(zero + offset, count), :]

    def at(ref, *index, start, count):
        return ref[(*index, pl.ds(zero + start, count), slice(None))]

    def up(value):
        return pltpu.roll(value, value.shape[-1] - 1, value.ndim - 1)

    def down(value):
        return pltpu.roll(value, 1, value.ndim - 1)

    for a in range(-3, nx + 3):
        get = functools.partial(at, cells, start=TOP - 4, count=tall)
        z = get(ZV, a + REACH)
        divergence = 0.5 * (
            get(XV, a + REACH + 1)
            - get(XV, a + REACH - 1)
            + (at(cells, YV, a + REACH, start=TOP - 3, count=tall) - at(cells, YV, a + REACH, start=TOP - 5, count=tall))
            + (up(z) - down(z))
        )
        per_mass = 0.4 * get(ENERGY, a + REACH) + 0.5 * jnp.square(jnp.minimum(divergence, 0.0))
        stress[a + 3] = get(DENSITY, a + REACH) * per_mass
        if -2 <= a < nx + 2:
            growth[a + 2] = dt * divergence
            heat[a + 2] = per_mass

    for a in range(-2, nx + 2):
        get = functools.partial(at, cells, start=TOP - 2, count=wide)
        density = get(DENSITY, a + REACH)
        grown = at(growth, a + 2, start=2, count=wide)
        centre = at(stress, a + 3, start=2, count=wide)
        scale = half / density
        density_one = density / (1.0 + grown)
        energy = get(ENERGY, a + REACH) - at(heat, a + 2, start=2, count=wide) * grown
        state[DENSITY, a + 2] = density_one
        state[ENERGY, a + 2] = density_one * energy
        state[XV, a + 2] = get(XV, a + REACH) - scale * (
            at(stress, a + 4, start=2, count=wide) - at(stress, a + 2, start=2, count=wide)
        )
        state[YV, a + 2] = get(YV, a + REACH) - scale * (
            at(stress, a + 3, start=3, count=wide) - at(stress, a + 3, start=1, count=wide)
        )
        state[ZV, a + 2] = get(ZV, a + REACH) - scale * (up(centre) - down(centre))
        if 0 <= a < nx:
            energy_one[a, 0:wide] = energy

    for part in range(0, wide, 8):
        rows = pl.ds(part, 8)
        before = [state[field, 1, rows] for field in range(5)]
        here = [state[field, 2, rows] for field in range(5)]
        steps = [h - b for h, b in zip(here, before)]
        slopes = [limited(st, b - state[field, 0, rows]) for field, (st, b) in enumerate(zip(steps, before))]
        lower = None
        for a in range(nx + 1):
            factors = face_factors(before[XV], here[XV], half)
            fluxes = []
            for field in range(5):
                after = state[field, a + 3, rows]
                step = after - here[field]
                slope = limited(step, steps[field])
                fluxes.append(face_flux(factors, before[field], here[field], slopes[field], slope))
                if lower is not None:
                    swept[field, a - 1, rows] = before[field] - (fluxes[field] - lower[field])
                before[field], here[field], steps[field], slopes[field] = here[field], after, step, slope
            lower = fluxes

    peak = jnp.zeros((wide, swept.shape[-1]), jnp.float32)
    for a in range(nx):
        below = [at(swept, field, a, start=1, count=wide) for field in range(5)]
        here = [at(swept, field, a, start=2, count=wide) for field in range(5)]
        factors = face_factors(below[YV], here[YV], half)
        moved = []
        for field in range(5):
            step = below[field] - swept[field, a, 0:wide]
            slope = limited(here[field] - below[field], step)
            work[field, a, 0:wide] = slope
            flux = face_flux(factors, below[field], here[field], slope, at(work, field, a, start=1, count=wide))
            work[5 + field, a, 0:wide] = flux
            moved.append(here[field] - (at(work, 5 + field, a, start=1, count=wide) - flux))
        below = [down(value) for value in moved]
        factors = face_factors(below[ZV], moved[ZV], half)
        final = []
        for field in range(5):
            step = moved[field] - below[field]
            slope = limited(up(step), step)
            flux = face_flux(factors, below[field], moved[field], down(slope), slope)
            final.append(moved[field] - (up(flux) - flux))
            outs[field][a] = final[field][:ny]
        peak = jnp.maximum(
            peak,
            jnp.sqrt(0.56 * at(energy_one, a, start=2, count=wide))
            + jnp.abs(final[XV])
            + jnp.abs(final[YV])
            + jnp.abs(final[ZV]),
        )
    row = lax.broadcasted_iota(jnp.int32, peak.shape, 0)
    peak = jnp.where(row < ny, peak, 0.0)
    peak_ref[...] = jnp.max(peak, axis=0, keepdims=True)


def shifted(value, side):
    axis, step = ("gx", side[0]) if side[0] else ("gy", side[1])
    count = lax.axis_size(axis)
    return lax.ppermute(value, axis, [((i + step) % count, i) for i in range(count)])


def tree(count, fan):
    nodes, levels = list(range(count)), []
    while len(nodes) > 1:
        groups = [nodes[i : i + fan] for i in range(0, len(nodes), fan)]
        nodes = [group[min(2, len(group) - 1)] for group in groups]
        members = [[node for node in group if node != hub] for group, hub in zip(groups, nodes)]
        levels.append(
            [
                [(group[k], hub) for group, hub in zip(members, nodes) if k < len(group)]
                for k in range(max(map(len, members)))
            ]
        )
    return levels


def all_max(row):
    axes = ("gx", "gy")
    levels = tree(lax.axis_size(axes), 6)
    for level in levels:
        row = functools.reduce(jnp.maximum, [lax.ppermute(row, axes, pairs) for pairs in level], row)
    for level in reversed(levels):
        arrived = [lax.ppermute(row, axes, [(hub, member) for member, hub in pairs]) for pairs in level]
        row = functools.reduce(jnp.maximum, arrived, row)
    return row


def body(density0, energy0, x_velocity, y_velocity, z_velocity, time_increment):
    nx, ny, nz = density0.shape
    fields = (density0, energy0, x_velocity, y_velocity, z_velocity)
    zero = jnp.zeros((1,), jnp.int32)
    wide, tall = ny + 4, ny + 12

    def array(*shape):
        return jax.ShapeDtypeStruct((*shape, nz), jnp.float32)

    def scratch(*shape):
        return pltpu.VMEM((*shape, nz), jnp.float32)

    def limit(mebibytes):
        return pltpu.CompilerParams(vmem_limit_bytes=mebibytes * 1024 * 1024)

    own, *edges = pl.pallas_call(
        functools.partial(pack_kernel, nx, ny),
        out_shape=[array(5, nx, ny)] + [array(segments(side, nx, ny)[1]) for side in SIDES],
        in_specs=[SMEM] + [HBM] * 5,
        out_specs=[VMEM] * (1 + len(SIDES)),
        scratch_shapes=[pltpu.SemaphoreType.DMA((5,))],
        compiler_params=limit(4),
        name="pack",
    )(zero, *[pltpu.with_memory_space_constraint(field, pltpu.HBM) for field in fields])
    edges = [shifted(edge, side) for edge, side in zip(edges, SIDES)]
    corners = pl.pallas_call(
        functools.partial(corner_kernel, nx, ny),
        out_shape=[array(corner_segments(1, nx, ny)[1])] * 2,
        in_specs=[SMEM] + [VMEM] * 2,
        out_specs=[VMEM] * 2,
        compiler_params=limit(4),
        name="corners",
    )(zero, edges[0], edges[1])
    corners = [shifted(corner, (0, side_y)) for corner, side_y in zip(corners, (-1, 1))]
    *outs, peak = pl.pallas_call(
        functools.partial(step_kernel, nx, ny),
        out_shape=[array(nx, ny)] * 5 + [array(1)],
        in_specs=[SMEM, SMEM] + [VMEM] * 7,
        out_specs=[VMEM] * 6,
        scratch_shapes=[
            scratch(5, nx + 8, ny + 20),
            scratch(nx + 6, tall),
            scratch(nx + 4, tall),
            scratch(nx + 4, tall),
            scratch(5, nx + 4, wide),
            scratch(nx, wide + 8),
            scratch(5, nx, wide + 8),
            scratch(10, nx, wide + 8),
        ],
        compiler_params=limit(12),
        name="step",
    )(zero, time_increment.reshape(1), own, *edges, *corners)
    return (*outs, 0.3 / jnp.max(all_max(peak)))


def solution(mesh):
    cells = P("gx", "gy", None)
    return jax.shard_map(
        body,
        mesh=mesh,
        in_specs=(cells,) * 5 + (P(),),
        out_specs=(cells,) * 5 + (P(),),
        check_vma=False,
    )
```

```python
import functools

import jax
import jax.numpy as jnp
from jax import lax
from jax.experimental import pallas as pl
from jax.experimental.pallas import tpu as pltpu
from jax.sharding import PartitionSpec as P

DENSITY, ENERGY, XV, YV, ZV = range(5)
REACH = 4
SIDES = ((-1, 0), (1, 0), (0, -1), (0, 1))
TOP = 8
VMEM = pl.BlockSpec(memory_space=pltpu.VMEM)
HBM = pl.BlockSpec(memory_space=pltpu.HBM)
SMEM = pl.BlockSpec(memory_space=pltpu.SMEM)


def rows_needed(field, a, nx, ny):
    past = max(-a, a - nx + 1, 0)
    if field == XV:
        reach = {0: 3, 1: 3, 2: 3, 3: 3, 4: 2}.get(past, -1)
    elif field == YV:
        reach = {0: 4, 1: 4, 2: 4, 3: 3}.get(past, -1)
    else:
        reach = {0: 3, 1: 3, 2: 3, 3: 2}.get(past, -1)
    return (-reach, ny + reach) if reach >= 0 else (0, 0)


def segments(side, nx, ny):
    columns = {-1: range(-REACH, 0), 0: range(nx), 1: range(nx, nx + REACH)}[side[0]]
    low, high = {-1: (-REACH, 0), 0: (0, ny), 1: (ny, ny + REACH)}[side[1]]
    found, offset = [], 0
    for a in columns:
        for field in range(5):
            first, last = rows_needed(field, a, nx, ny)
            first, last = max(first, low), min(last, high)
            if last > first:
                found.append((field, a, first, last - first, offset))
                offset += last - first
    return found, -(-offset // 8) * 8


def corner_segments(side_y, nx, ny):
    found, offset = [], 0
    for side_x in (-1, 1):
        for field, a, first, count, _ in segments((side_x, side_y), nx, ny)[0]:
            found.append((side_x, field, a, first, count, offset))
            offset += count
    return found, -(-offset // 8) * 8


def pack_kernel(nx, ny, zero_ref, *refs):
    fields, own, edges, arrived = refs[:5], refs[5], refs[6 : 6 + len(SIDES)], refs[-1]
    zero = zero_ref[0]
    copies = [pltpu.make_async_copy(fields[field], own.at[field], arrived.at[field]) for field in range(5)]
    for copy in copies:
        copy.start()
    for current, copy in enumerate(copies):
        copy.wait()
        for side, edge in zip(SIDES, edges):
            for field, a, b, count, offset in segments(side, nx, ny)[0]:
                if field == current:
                    edge[pl.ds(zero + offset, count), :] = own[
                        field, a - side[0] * nx, pl.ds(zero + (b - side[1] * ny), count), :
                    ]


def corner_kernel(nx, ny, zero_ref, below_ref, above_ref, low_ref, high_ref):
    zero = zero_ref[0]
    held = {
        (side_x, field, a): (ref, offset)
        for side_x, ref in ((-1, below_ref), (1, above_ref))
        for field, a, _, _, offset in segments((side_x, 0), nx, ny)[0]
    }
    for side_y, out in ((-1, low_ref), (1, high_ref)):
        for side_x, field, a, b, count, offset in corner_segments(side_y, nx, ny)[0]:
            ref, start = held[side_x, field, a]
            out[pl.ds(zero + offset, count), :] = ref[pl.ds(zero + (start + b - side_y * ny), count), :]


def limited(above, below):
    return jnp.minimum(jnp.maximum(above, jnp.minimum(below, 0.0)), jnp.maximum(below, 0.0))


def face_factors(v_minus, v, half_increment):
    courant = half_increment * (v_minus + v)
    size = jnp.abs(courant)
    return courant, 0.5 * size * (1.0 - size), courant > 0.0


def face_flux(factors, f_minus, f, s_minus, s):
    courant, slope_factor, upward = factors
    return courant * jnp.where(upward, f_minus, f) + slope_factor * jnp.where(upward, s_minus, s)


def up(value):
    return pltpu.roll(value, value.shape[-1] - 1, value.ndim - 1)


def down(value):
    return pltpu.roll(value, 1, value.ndim - 1)


def sweep_x(state, speed, swept, fields, half):
    for part in range(0, state.shape[2], 8):
        rows = pl.ds(part, 8)
        before = [state[field, 1, rows] for field in fields]
        here = [state[field, 2, rows] for field in fields]
        steps = [h - b for h, b in zip(here, before)]
        slopes = [limited(st, b - state[field, 0, rows]) for field, st, b in zip(fields, steps, before)]
        lower = None
        for a in range(swept.shape[1] + 1):
            factors = face_factors(speed[a + 1, rows], speed[a + 2, rows], half)
            fluxes = []
            for k, field in enumerate(fields):
                after = state[field, a + 3, rows]
                step = after - here[k]
                slope = limited(step, steps[k])
                fluxes.append(face_flux(factors, before[k], here[k], slopes[k], slope))
                if lower is not None:
                    swept[field, a - 1, rows] = before[k] - (fluxes[k] - lower[k])
                before[k], here[k], steps[k], slopes[k] = here[k], after, step, slope
            lower = fluxes


def sweep_y(zero, swept, work, a, fields, factors, wide):
    moved = []
    for field in fields:
        below = swept[field, a, pl.ds(zero + 1, wide)]
        here = swept[field, a, pl.ds(zero + 2, wide)]
        slope = limited(here - below, below - swept[field, a, 0:wide])
        work[0, field, a, 0:wide] = slope
        flux = face_flux(factors, below, here, slope, work[0, field, a, pl.ds(zero + 1, wide)])
        work[1, field, a, 0:wide] = flux
        moved.append(here - (work[1, field, a, pl.ds(zero + 1, wide)] - flux))
    return moved


def sweep_z(moved, factors):
    final = []
    for value in moved:
        below = down(value)
        step = value - below
        slope = limited(up(step), step)
        flux = face_flux(factors, below, value, down(slope), slope)
        final.append(value - (up(flux) - flux))
    return final


def step_kernel(nx, ny, zero_ref, dt_ref, *refs):
    own, halos = refs[0], refs[1:7]
    passive, speed, speed_y, speed_z, flows, peak_ref = refs[7:13]
    cells, stress, growth, heat, state, energy_one, swept, work = refs[13:]
    nz = own.shape[-1]
    zero = zero_ref[0]
    dt = dt_ref[0]
    half = 0.5 * dt
    wide = ny + 4
    tall = ny + 12

    for field in range(5):
        for a in range(nx):
            cells[field, a + REACH, pl.ds(TOP, ny), :] = own[field, a]
    for side, halo in zip(SIDES, halos):
        for field, a, b, count, offset in segments(side, nx, ny)[0]:
            cells[field, a + REACH, pl.ds(zero + (b + TOP), count), :] = halo[pl.ds(zero + offset, count), :]
    for side_y, halo in zip((-1, 1), halos[len(SIDES) :]):
        for _, field, a, b, count, offset in corner_segments(side_y, nx, ny)[0]:
            cells[field, a + REACH, pl.ds(zero + (b + TOP), count), :] = halo[pl.ds(zero + offset, count), :]

    def at(ref, *index, start, count):
        return ref[(*index, pl.ds(zero + start, count), slice(None))]

    for a in range(-3, nx + 3):
        get = functools.partial(at, cells, start=TOP - 4, count=tall)
        z = get(ZV, a + REACH)
        divergence = 0.5 * (
            get(XV, a + REACH + 1)
            - get(XV, a + REACH - 1)
            + (at(cells, YV, a + REACH, start=TOP - 3, count=tall) - at(cells, YV, a + REACH, start=TOP - 5, count=tall))
            + (up(z) - down(z))
        )
        per_mass = 0.4 * get(ENERGY, a + REACH) + 0.5 * jnp.square(jnp.minimum(divergence, 0.0))
        stress[a + 3] = get(DENSITY, a + REACH) * per_mass
        if -2 <= a < nx + 2:
            growth[a + 2] = dt * divergence
            heat[a + 2] = per_mass

    for a in range(-2, nx + 2):
        get = functools.partial(at, cells, start=TOP - 2, count=wide)
        density = get(DENSITY, a + REACH)
        grown = at(growth, a + 2, start=2, count=wide)
        centre = at(stress, a + 3, start=2, count=wide)
        scale = half / density
        density_one = density / (1.0 + grown)
        energy = get(ENERGY, a + REACH) - at(heat, a + 2, start=2, count=wide) * grown
        passive[0, a + 2] = density_one
        passive[1, a + 2] = density_one * energy
        x_one = get(XV, a + REACH) - scale * (
            at(stress, a + 4, start=2, count=wide) - at(stress, a + 2, start=2, count=wide)
        )
        state[0, a + 2] = x_one
        speed[a + 2] = x_one
        state[1, a + 2] = get(YV, a + REACH) - scale * (
            at(stress, a + 3, start=3, count=wide) - at(stress, a + 3, start=1, count=wide)
        )
        state[2, a + 2] = get(ZV, a + REACH) - scale * (up(centre) - down(centre))
        if 0 <= a < nx:
            energy_one[a, 0:wide] = energy

    sweep_x(state, speed, swept, (0, 1, 2), half)
    for a in range(nx):
        speed_y[a, 0:wide] = swept[1, a, 0:wide]

    peak = jnp.zeros((wide, nz), jnp.float32)
    for a in range(nx):
        below, here = at(swept, 1, a, start=1, count=wide), at(swept, 1, a, start=2, count=wide)
        moved = sweep_y(zero, swept, work, a, (0, 1, 2), face_factors(below, here, half), wide)
        speed_z[a] = moved[2]
        final = sweep_z(moved, face_factors(down(moved[2]), moved[2], half))
        for field in range(3):
            flows[field, a] = final[field][:ny]
        peak = jnp.maximum(
            peak,
            jnp.sqrt(0.56 * at(energy_one, a, start=2, count=wide))
            + jnp.abs(final[0])
            + jnp.abs(final[1])
            + jnp.abs(final[2]),
        )
    row = lax.broadcasted_iota(jnp.int32, peak.shape, 0)
    peak = jnp.max(jnp.where(row < ny, peak, 0.0), axis=0, keepdims=True)
    peak_ref[...] = jnp.broadcast_to(peak, peak_ref.shape)


def carry_kernel(nx, ny, zero_ref, dt_ref, *refs):
    state, speed, speed_y, speed_z, flows, density_out, energy_out = refs[:7]
    flow_outs, swept, work, written = refs[7:10], refs[10], refs[11], refs[12]
    zero = zero_ref[0]
    half = 0.5 * dt_ref[0]
    wide = ny + 4
    copies = [pltpu.make_async_copy(flows.at[k], flow_outs[k], written.at[k]) for k in range(3)]
    for copy in copies:
        copy.start()
    sweep_x(state, speed, swept, (0, 1), half)
    for a in range(nx):
        below, here = speed_y[a, pl.ds(zero + 1, wide)], speed_y[a, pl.ds(zero + 2, wide)]
        moved = sweep_y(zero, swept, work, a, (0, 1), face_factors(below, here, half), wide)
        final = sweep_z(moved, face_factors(down(speed_z[a]), speed_z[a], half))
        density_out[a] = final[0][:ny]
        energy_out[a] = final[1][:ny]
    for copy in copies:
        copy.wait()


def shifted(value, side):
    axis, step = ("gx", side[0]) if side[0] else ("gy", side[1])
    count = lax.axis_size(axis)
    return lax.ppermute(value, axis, [((i + step) % count, i) for i in range(count)])


def body(density0, energy0, x_velocity, y_velocity, z_velocity, time_increment):
    nx, ny, nz = density0.shape
    fields = (density0, energy0, x_velocity, y_velocity, z_velocity)
    zero = jnp.zeros((1,), jnp.int32)
    wide, tall = ny + 4, ny + 12

    def array(*shape):
        return jax.ShapeDtypeStruct((*shape, nz), jnp.float32)

    def scratch(*shape):
        return pltpu.VMEM((*shape, nz), jnp.float32)

    def limit(mebibytes):
        return pltpu.CompilerParams(vmem_limit_bytes=mebibytes * 1024 * 1024)

    own, *edges = pl.pallas_call(
        functools.partial(pack_kernel, nx, ny),
        out_shape=[array(5, nx, ny)] + [array(segments(side, nx, ny)[1]) for side in SIDES],
        in_specs=[SMEM] + [HBM] * 5,
        out_specs=[VMEM] * (1 + len(SIDES)),
        scratch_shapes=[pltpu.SemaphoreType.DMA((5,))],
        compiler_params=limit(4),
        name="pack",
    )(zero, *[pltpu.with_memory_space_constraint(field, pltpu.HBM) for field in fields])
    edges = [shifted(edge, side) for edge, side in zip(edges, SIDES)]
    corners = pl.pallas_call(
        functools.partial(corner_kernel, nx, ny),
        out_shape=[array(corner_segments(1, nx, ny)[1])] * 2,
        in_specs=[SMEM] + [VMEM] * 2,
        out_specs=[VMEM] * 2,
        compiler_params=limit(4),
        name="corners",
    )(zero, edges[0], edges[1])
    corners = [shifted(corner, (0, side_y)) for corner, side_y in zip(corners, (-1, 1))]
    count = lax.axis_size(("gx", "gy"))
    increment = time_increment.reshape(1)
    passed = [array(2, nx + 4, wide), array(nx + 4, wide), array(nx, wide + 8), array(nx, wide), array(3, nx, ny)]
    *passed, peak = pl.pallas_call(
        functools.partial(step_kernel, nx, ny),
        out_shape=passed + [array(count)],
        in_specs=[SMEM, SMEM] + [VMEM] * 7,
        out_specs=[VMEM] * 6,
        scratch_shapes=[
            scratch(5, nx + 8, ny + 20),
            scratch(nx + 6, tall),
            scratch(nx + 4, tall),
            scratch(nx + 4, tall),
            scratch(3, nx + 4, wide),
            scratch(nx, wide + 8),
            scratch(3, nx, wide + 8),
            scratch(2, 3, nx, wide + 8),
        ],
        compiler_params=limit(12),
        name="step",
    )(zero, increment, own, *edges, *corners)
    outs = pl.pallas_call(
        functools.partial(carry_kernel, nx, ny),
        out_shape=[array(nx, ny)] * 5,
        in_specs=[SMEM, SMEM] + [VMEM] * 5,
        out_specs=[VMEM] * 2 + [HBM] * 3,
        scratch_shapes=[
            scratch(2, nx, wide + 8),
            scratch(2, 2, nx, wide + 8),
            pltpu.SemaphoreType.DMA((3,)),
        ],
        compiler_params=limit(8),
        cost_estimate=pl.CostEstimate(flops=10**7, bytes_accessed=4 * 10**6, transcendentals=0),
        name="carry",
    )(zero, increment, *passed)
    peak = lax.all_to_all(peak, ("gx", "gy"), 0, 0, tiled=True)
    return (*outs, 0.3 / jnp.max(peak))


def solution(mesh):
    cells = P("gx", "gy", None)
    return jax.shard_map(
        body,
        mesh=mesh,
        in_specs=(cells,) * 5 + (P(),),
        out_specs=(cells,) * 5 + (P(),),
        check_vma=False,
    )
```

```python
import functools
import itertools

import jax
import jax.numpy as jnp
from jax import lax
from jax.experimental import pallas as pl
from jax.experimental.pallas import tpu as pltpu
from jax.sharding import PartitionSpec as P

DENSITY, ENERGY, XV, YV, ZV = range(5)
REACH = 4
NEAR, FAR = "near", "far"
LINKS = (FAR, NEAR)
TOP = 8
VMEM = pl.BlockSpec(memory_space=pltpu.VMEM)
HBM = pl.BlockSpec(memory_space=pltpu.HBM)
SMEM = pl.BlockSpec(memory_space=pltpu.SMEM)


def ghost_rows(field, past):
    if field == YV:
        return (4, 4, 4, 3, 0)[past]
    return (3, 3, 3, 3, 2)[past] if field == XV else (3, 3, 3, 2, 0)[past]


def x_layers():
    return [(field, past) for field in range(5) for past in range(1, REACH + 1) if ghost_rows(field, past)]


def y_layers(nx):
    found, offset = [], 0
    for a in range(nx):
        for field in range(5):
            found.append((field, a, ghost_rows(field, 0), offset))
            offset += ghost_rows(field, 0)
    return found, -(-offset // 8) * 8


def corner_layers():
    found, offset = [], 0
    for link in LINKS:
        for number, (field, past) in enumerate(x_layers()):
            rows = ghost_rows(field, past)
            found.append((link, number, field, past, rows, offset))
            offset += rows
    return found, -(-offset // 8) * 8


def is_low(axis, link):
    odd = lax.rem(lax.axis_index(axis), 2)
    return odd if link == NEAR else 1 - odd


def exchanged(value, axis, link):
    count = lax.axis_size(axis)
    partner = [i ^ 1 if link == NEAR else ((i - 1) ^ 1) + 1 for i in range(count)]
    return lax.ppermute(value, axis, [(i, j % count) for i, j in enumerate(partner)])


def pick(flag, one, other):
    return flag * one + (1 - flag) * other


def pack_kernel(nx, ny, zero_ref, *refs):
    fields, own, x_edges, y_edges, arrived = refs[:5], refs[5], refs[6:8], refs[8:10], refs[-1]
    zero = zero_ref[0]
    copies = [pltpu.make_async_copy(fields[field], own.at[field], arrived.at[field]) for field in range(5)]
    for copy in copies:
        copy.start()
    for current, copy in enumerate(copies):
        copy.wait()
        for link, edge in zip(LINKS, x_edges):
            low = is_low("gx", link)
            for number, (field, past) in enumerate(x_layers()):
                if field == current:
                    edge[pl.ds(zero + number * ny, ny), :] = own[field, pick(low, past - 1, nx - past)]
        for link, edge in zip(LINKS, y_edges):
            low = is_low("gy", link)
            for field, a, rows, offset in y_layers(nx)[0]:
                if field == current:
                    edge[pl.ds(zero + offset, rows), :] = own[field, a, pl.ds(pick(low, 0, ny - rows), rows), :]


def corner_kernel(ny, zero_ref, *refs):
    zero = zero_ref[0]
    for link_y, out in zip(LINKS, refs[2:]):
        low = is_low("gy", link_y)
        for link, number, _, _, rows, offset in corner_layers()[0]:
            edge = refs[LINKS.index(link)]
            out[pl.ds(zero + offset, rows), :] = edge[pl.ds(number * ny + pick(low, 0, ny - rows), rows), :]


def limited(above, below):
    return jnp.minimum(jnp.maximum(above, jnp.minimum(below, 0.0)), jnp.maximum(below, 0.0))


def face_factors(v_minus, v, half_increment):
    courant = half_increment * (v_minus + v)
    size = jnp.abs(courant)
    return courant, 0.5 * size * (1.0 - size), courant > 0.0


def face_flux(factors, f_minus, f, s_minus, s):
    courant, slope_factor, upward = factors
    return courant * jnp.where(upward, f_minus, f) + slope_factor * jnp.where(upward, s_minus, s)


def up(value):
    return pltpu.roll(value, value.shape[-1] - 1, value.ndim - 1)


def down(value):
    return pltpu.roll(value, 1, value.ndim - 1)


def sweep_x(state, speed, swept, fields, half):
    for part in range(0, state.shape[2], 8):
        rows = pl.ds(part, 8)
        before = [state[field, 1, rows] for field in fields]
        here = [state[field, 2, rows] for field in fields]
        steps = [h - b for h, b in zip(here, before)]
        slopes = [limited(st, b - state[field, 0, rows]) for field, st, b in zip(fields, steps, before)]
        lower = None
        for a in range(swept.shape[1] + 1):
            factors = face_factors(speed[a + 1, rows], speed[a + 2, rows], half)
            fluxes = []
            for k, field in enumerate(fields):
                after = state[field, a + 3, rows]
                step = after - here[k]
                slope = limited(step, steps[k])
                fluxes.append(face_flux(factors, before[k], here[k], slopes[k], slope))
                if lower is not None:
                    swept[field, a - 1, rows] = before[k] - (fluxes[k] - lower[k])
                before[k], here[k], steps[k], slopes[k] = here[k], after, step, slope
            lower = fluxes


def sweep_y(zero, swept, work, a, fields, factors, wide):
    moved = []
    for field in fields:
        below = swept[field, a, pl.ds(zero + 1, wide)]
        here = swept[field, a, pl.ds(zero + 2, wide)]
        slope = limited(here - below, below - swept[field, a, 0:wide])
        work[0, field, a, 0:wide] = slope
        flux = face_flux(factors, below, here, slope, work[0, field, a, pl.ds(zero + 1, wide)])
        work[1, field, a, 0:wide] = flux
        moved.append(here - (work[1, field, a, pl.ds(zero + 1, wide)] - flux))
    return moved


def sweep_z(moved, factors):
    final = []
    for value in moved:
        below = down(value)
        step = value - below
        slope = limited(up(step), step)
        flux = face_flux(factors, below, value, down(slope), slope)
        final.append(value - (up(flux) - flux))
    return final


def step_kernel(nx, ny, zero_ref, dt_ref, *refs):
    own, x_edges, y_edges, corners = refs[0], refs[1:3], refs[3:5], refs[5:7]
    passive, speed, speed_y, speed_z, flows, peak_ref = refs[7:13]
    cells, stress, growth, heat, state, energy_one, swept, work = refs[13:]
    nz = own.shape[-1]
    zero = zero_ref[0]
    dt = dt_ref[0]
    half = 0.5 * dt
    wide = ny + 4
    tall = ny + 12

    for field in range(5):
        for a in range(nx):
            cells[field, a + REACH, pl.ds(TOP, ny), :] = own[field, a]
    for link, edge in zip(LINKS, x_edges):
        low = is_low("gx", link)
        for number, (field, past) in enumerate(x_layers()):
            column = REACH + pick(low, -past, nx - 1 + past)
            cells[field, column, pl.ds(TOP, ny), :] = edge[pl.ds(zero + number * ny, ny), :]
    for link_y, edge, corner in zip(LINKS, y_edges, corners):
        low_y = is_low("gy", link_y)
        for field, a, rows, offset in y_layers(nx)[0]:
            to = pl.ds(TOP + pick(low_y, -rows, ny), rows)
            cells[field, a + REACH, to, :] = edge[pl.ds(zero + offset, rows), :]
        for link, _, field, past, rows, offset in corner_layers()[0]:
            column = REACH + pick(is_low("gx", link), -past, nx - 1 + past)
            to = pl.ds(TOP + pick(low_y, -rows, ny), rows)
            cells[field, column, to, :] = corner[pl.ds(zero + offset, rows), :]

    def at(ref, *index, start, count):
        return ref[(*index, pl.ds(zero + start, count), slice(None))]

    for a in range(-3, nx + 3):
        get = functools.partial(at, cells, start=TOP - 4, count=tall)
        z = get(ZV, a + REACH)
        divergence = 0.5 * (
            get(XV, a + REACH + 1)
            - get(XV, a + REACH - 1)
            + (at(cells, YV, a + REACH, start=TOP - 3, count=tall) - at(cells, YV, a + REACH, start=TOP - 5, count=tall))
            + (up(z) - down(z))
        )
        per_mass = 0.4 * get(ENERGY, a + REACH) + 0.5 * jnp.square(jnp.minimum(divergence, 0.0))
        stress[a + 3] = get(DENSITY, a + REACH) * per_mass
        if -2 <= a < nx + 2:
            growth[a + 2] = dt * divergence
            heat[a + 2] = per_mass

    for a in range(-2, nx + 2):
        get = functools.partial(at, cells, start=TOP - 2, count=wide)
        density = get(DENSITY, a + REACH)
        grown = at(growth, a + 2, start=2, count=wide)
        centre = at(stress, a + 3, start=2, count=wide)
        scale = half / density
        density_one = density / (1.0 + grown)
        energy = get(ENERGY, a + REACH) - at(heat, a + 2, start=2, count=wide) * grown
        passive[0, a + 2] = density_one
        passive[1, a + 2] = density_one * energy
        x_one = get(XV, a + REACH) - scale * (
            at(stress, a + 4, start=2, count=wide) - at(stress, a + 2, start=2, count=wide)
        )
        state[0, a + 2] = x_one
        speed[a + 2] = x_one
        state[1, a + 2] = get(YV, a + REACH) - scale * (
            at(stress, a + 3, start=3, count=wide) - at(stress, a + 3, start=1, count=wide)
        )
        state[2, a + 2] = get(ZV, a + REACH) - scale * (up(centre) - down(centre))
        if 0 <= a < nx:
            energy_one[a, 0:wide] = energy

    sweep_x(state, speed, swept, (0, 1, 2), half)
    for a in range(nx):
        speed_y[a, 0:wide] = swept[1, a, 0:wide]

    peak = jnp.zeros((wide, nz), jnp.float32)
    for a in range(nx):
        below, here = at(swept, 1, a, start=1, count=wide), at(swept, 1, a, start=2, count=wide)
        moved = sweep_y(zero, swept, work, a, (0, 1, 2), face_factors(below, here, half), wide)
        speed_z[a] = moved[2]
        final = sweep_z(moved, face_factors(down(moved[2]), moved[2], half))
        for field in range(3):
            flows[field, a] = final[field][:ny]
        peak = jnp.maximum(
            peak,
            jnp.sqrt(0.56 * at(energy_one, a, start=2, count=wide))
            + jnp.abs(final[0])
            + jnp.abs(final[1])
            + jnp.abs(final[2]),
        )
    row = lax.broadcasted_iota(jnp.int32, peak.shape, 0)
    peak = jnp.max(jnp.where(row < ny, peak, 0.0), axis=0, keepdims=True)
    peak_ref[...] = peak


def carry_kernel(nx, ny, zero_ref, dt_ref, *refs):
    state, speed, speed_y, speed_z, flows, density_out, energy_out = refs[:7]
    flow_outs, swept, work, written = refs[7:10], refs[10], refs[11], refs[12]
    zero = zero_ref[0]
    half = 0.5 * dt_ref[0]
    wide = ny + 4
    copies = [pltpu.make_async_copy(flows.at[k], flow_outs[k], written.at[k]) for k in range(3)]
    for copy in copies:
        copy.start()
    sweep_x(state, speed, swept, (0, 1), half)
    for a in range(nx):
        below, here = speed_y[a, pl.ds(zero + 1, wide)], speed_y[a, pl.ds(zero + 2, wide)]
        moved = sweep_y(zero, swept, work, a, (0, 1), face_factors(below, here, half), wide)
        final = sweep_z(moved, face_factors(down(speed_z[a]), speed_z[a], half))
        density_out[a] = final[0][:ny]
        energy_out[a] = final[1][:ny]
    for copy in copies:
        copy.wait()


def all_max(row):
    axes = ("gx", "gy")
    count, stride = lax.axis_size(axes), 1
    while stride < count:
        if count & (count - 1):
            pairs = [(i, (i + stride) % count) for i in range(count)]
        else:
            pairs = [(i, i ^ stride) for i in range(count)]
        row = jnp.maximum(row, lax.ppermute(row, axes, pairs))
        stride *= 2
    return row


def body(density0, energy0, x_velocity, y_velocity, z_velocity, time_increment):
    nx, ny, nz = density0.shape
    fields = (density0, energy0, x_velocity, y_velocity, z_velocity)
    zero = jnp.zeros((1,), jnp.int32)
    wide, tall = ny + 4, ny + 12

    def array(*shape):
        return jax.ShapeDtypeStruct((*shape, nz), jnp.float32)

    def scratch(*shape):
        return pltpu.VMEM((*shape, nz), jnp.float32)

    def limit(mebibytes):
        return pltpu.CompilerParams(vmem_limit_bytes=mebibytes * 1024 * 1024)

    x_edge, y_edge = array(len(x_layers()) * ny), array(y_layers(nx)[1])
    own, *edges = pl.pallas_call(
        functools.partial(pack_kernel, nx, ny),
        out_shape=[array(5, nx, ny), x_edge, x_edge, y_edge, y_edge],
        in_specs=[SMEM] + [HBM] * 5,
        out_specs=[VMEM] * 5,
        scratch_shapes=[pltpu.SemaphoreType.DMA((5,))],
        compiler_params=limit(4),
        name="pack",
    )(zero, *[pltpu.with_memory_space_constraint(field, pltpu.HBM) for field in fields])
    edges = [exchanged(edge, axis, link) for edge, (axis, link) in zip(edges, itertools.product(("gx", "gy"), LINKS))]
    corners = pl.pallas_call(
        functools.partial(corner_kernel, ny),
        out_shape=[array(corner_layers()[1])] * 2,
        in_specs=[SMEM] + [VMEM] * 2,
        out_specs=[VMEM] * 2,
        compiler_params=limit(4),
        name="corners",
    )(zero, edges[0], edges[1])
    corners = [exchanged(corner, "gy", link) for corner, link in zip(corners, LINKS)]
    increment = time_increment.reshape(1)
    passed = [array(2, nx + 4, wide), array(nx + 4, wide), array(nx, wide + 8), array(nx, wide), array(3, nx, ny)]
    *passed, peak = pl.pallas_call(
        functools.partial(step_kernel, nx, ny),
        out_shape=passed + [array(1)],
        in_specs=[SMEM, SMEM] + [VMEM] * 7,
        out_specs=[VMEM] * 6,
        scratch_shapes=[
            scratch(5, nx + 8, ny + 20),
            scratch(nx + 6, tall),
            scratch(nx + 4, tall),
            scratch(nx + 4, tall),
            scratch(3, nx + 4, wide),
            scratch(nx, wide + 8),
            scratch(3, nx, wide + 8),
            scratch(2, 3, nx, wide + 8),
        ],
        compiler_params=limit(12),
        name="step",
    )(zero, increment, own, *edges, *corners)
    outs = pl.pallas_call(
        functools.partial(carry_kernel, nx, ny),
        out_shape=[array(nx, ny)] * 5,
        in_specs=[SMEM, SMEM] + [VMEM] * 5,
        out_specs=[VMEM] * 2 + [HBM] * 3,
        scratch_shapes=[
            scratch(2, nx, wide + 8),
            scratch(2, 2, nx, wide + 8),
            pltpu.SemaphoreType.DMA((3,)),
        ],
        compiler_params=limit(8),
        cost_estimate=pl.CostEstimate(flops=10**7, bytes_accessed=4 * 10**6, transcendentals=0),
        name="carry",
    )(zero, increment, *passed)
    return (*outs, 0.3 / jnp.max(all_max(peak)))


def solution(mesh):
    cells = P("gx", "gy", None)
    return jax.shard_map(
        body,
        mesh=mesh,
        in_specs=(cells,) * 5 + (P(),),
        out_specs=(cells,) * 5 + (P(),),
        check_vma=False,
    )
```

```python
import functools

import jax
import jax.numpy as jnp
from jax import lax
from jax.experimental import pallas as pl
from jax.experimental.pallas import tpu as pltpu
from jax.sharding import PartitionSpec as P

DENSITY, ENERGY, XV, YV, ZV = range(5)
REACH = 4
NEAR, FAR = "near", "far"
LINKS = (FAR, NEAR)
TOP = 8
VMEM = pl.BlockSpec(memory_space=pltpu.VMEM)
HBM = pl.BlockSpec(memory_space=pltpu.HBM)
SMEM = pl.BlockSpec(memory_space=pltpu.SMEM)


def ghost_rows(field, past):
    if field == YV:
        return (4, 4, 4, 3, 0)[past]
    return (3, 3, 3, 3, 2)[past] if field == XV else (3, 3, 3, 2, 0)[past]


def x_layers():
    return [(field, past) for field in range(5) for past in range(1, REACH + 1) if ghost_rows(field, past)]


def y_layers(nx):
    found, offset = [], 0
    for a in range(nx):
        for field in range(5):
            found.append((field, a, ghost_rows(field, 0), offset))
            offset += ghost_rows(field, 0)
    return found, -(-offset // 8) * 8


def split_rows(ny):
    return [(0, REACH), (ny - REACH, REACH)], [(REACH, ny - 2 * REACH)]


def corner_layers():
    found, offset = [], 0
    for link in LINKS:
        for number, (field, past) in enumerate(x_layers()):
            rows = ghost_rows(field, past)
            found.append((link, number, field, past, rows, offset))
            offset += rows
    return found, -(-offset // 8) * 8


def is_low(axis, link):
    odd = lax.rem(lax.axis_index(axis), 2)
    return odd if link == NEAR else 1 - odd


def exchanged(value, axis, link):
    count = lax.axis_size(axis)
    partner = [i ^ 1 if link == NEAR else ((i - 1) ^ 1) + 1 for i in range(count)]
    return lax.ppermute(value, axis, [(i, j % count) for i, j in enumerate(partner)])


def pick(flag, one, other):
    return flag * one + (1 - flag) * other


def pack_kernel(nx, ny, zero_ref, *refs):
    fields, own, x_outer, x_inner, y_edges, arrived = refs[:5], refs[5], refs[6:8], refs[8:10], refs[10:12], refs[-1]
    zero = zero_ref[0]
    copies = [pltpu.make_async_copy(fields[field], own.at[field], arrived.at[field]) for field in range(5)]
    for copy in copies:
        copy.start()
    for current, copy in enumerate(copies):
        copy.wait()
        for k, link in enumerate(LINKS):
            low = is_low("gx", link)
            for number, (field, past) in enumerate(x_layers()):
                if field == current:
                    column = pick(low, past - 1, nx - past)
                    for edge, pieces in zip((x_outer[k], x_inner[k]), split_rows(ny)):
                        offset = number * sum(rows for _, rows in pieces)
                        for first, rows in pieces:
                            edge[pl.ds(zero + offset, rows), :] = own[field, column, pl.ds(zero + first, rows), :]
                            offset += rows
        for link, edge in zip(LINKS, y_edges):
            low = is_low("gy", link)
            for field, a, rows, offset in y_layers(nx)[0]:
                if field == current:
                    edge[pl.ds(zero + offset, rows), :] = own[field, a, pl.ds(pick(low, 0, ny - rows), rows), :]


def corner_kernel(zero_ref, far_ref, near_ref, y_near, far_out, near_out):
    zero = zero_ref[0]
    start = y_near.shape[0]
    near_out[0:start, :] = y_near[...]
    for link_y, out, start in ((FAR, far_out, 0), (NEAR, near_out, start)):
        low = is_low("gy", link_y)
        for link, number, _, _, rows, offset in corner_layers()[0]:
            edge = far_ref if link == FAR else near_ref
            first = number * 2 * REACH + pick(low, 0, 2 * REACH - rows)
            out[pl.ds(zero + (start + offset), rows), :] = edge[pl.ds(first, rows), :]


def limited(above, below):
    return jnp.minimum(jnp.maximum(above, jnp.minimum(below, 0.0)), jnp.maximum(below, 0.0))


def face_factors(v_minus, v, half_increment):
    courant = half_increment * (v_minus + v)
    size = jnp.abs(courant)
    return courant, 0.5 * size * (1.0 - size), courant > 0.0


def face_flux(factors, f_minus, f, s_minus, s):
    courant, slope_factor, upward = factors
    return courant * jnp.where(upward, f_minus, f) + slope_factor * jnp.where(upward, s_minus, s)


def up(value):
    return pltpu.roll(value, value.shape[-1] - 1, value.ndim - 1)


def down(value):
    return pltpu.roll(value, 1, value.ndim - 1)


def sweep_x(state, speed, swept, fields, half):
    for part in range(0, state.shape[2], 8):
        rows = pl.ds(part, 8)
        before = [state[field, 1, rows] for field in fields]
        here = [state[field, 2, rows] for field in fields]
        steps = [h - b for h, b in zip(here, before)]
        slopes = [limited(st, b - state[field, 0, rows]) for field, st, b in zip(fields, steps, before)]
        lower = None
        for a in range(swept.shape[1] + 1):
            factors = face_factors(speed[a + 1, rows], speed[a + 2, rows], half)
            fluxes = []
            for k, field in enumerate(fields):
                after = state[field, a + 3, rows]
                step = after - here[k]
                slope = limited(step, steps[k])
                fluxes.append(face_flux(factors, before[k], here[k], slopes[k], slope))
                if lower is not None:
                    swept[field, a - 1, rows] = before[k] - (fluxes[k] - lower[k])
                before[k], here[k], steps[k], slopes[k] = here[k], after, step, slope
            lower = fluxes


def sweep_y(zero, swept, work, a, fields, factors, wide):
    moved = []
    for field in fields:
        below = swept[field, a, pl.ds(zero + 1, wide)]
        here = swept[field, a, pl.ds(zero + 2, wide)]
        slope = limited(here - below, below - swept[field, a, 0:wide])
        work[0, field, a, 0:wide] = slope
        flux = face_flux(factors, below, here, slope, work[0, field, a, pl.ds(zero + 1, wide)])
        work[1, field, a, 0:wide] = flux
        moved.append(here - (work[1, field, a, pl.ds(zero + 1, wide)] - flux))
    return moved


def sweep_z(moved, factors):
    final = []
    for value in moved:
        below = down(value)
        step = value - below
        slope = limited(up(step), step)
        flux = face_flux(factors, below, value, down(slope), slope)
        final.append(value - (up(flux) - flux))
    return final


def step_kernel(nx, ny, zero_ref, dt_ref, *refs):
    own, x_outer, x_inner, (y_far, far, near) = refs[0], refs[1:3], refs[3:5], refs[5:8]
    passive, speed, speed_y, speed_z, flows, peak_ref = refs[8:14]
    cells, stress, growth, heat, state, energy_one, swept, work = refs[14:]
    nz = own.shape[-1]
    zero = zero_ref[0]
    dt = dt_ref[0]
    half = 0.5 * dt
    wide = ny + 4
    tall = ny + 12

    for field in range(5):
        for a in range(nx):
            cells[field, a + REACH, pl.ds(TOP, ny), :] = own[field, a]
    for k, link in enumerate(LINKS):
        low = is_low("gx", link)
        for number, (field, past) in enumerate(x_layers()):
            column = REACH + pick(low, -past, nx - 1 + past)
            for edge, pieces in zip((x_outer[k], x_inner[k]), split_rows(ny)):
                offset = number * sum(rows for _, rows in pieces)
                for first, rows in pieces:
                    cells[field, column, pl.ds(zero + (TOP + first), rows), :] = edge[pl.ds(zero + offset, rows), :]
                    offset += rows
    for link_y, edge, corner, start in ((FAR, y_far, far, 0), (NEAR, near, near, y_layers(nx)[1])):
        low_y = is_low("gy", link_y)
        for field, a, rows, offset in y_layers(nx)[0]:
            to = pl.ds(TOP + pick(low_y, -rows, ny), rows)
            cells[field, a + REACH, to, :] = edge[pl.ds(zero + offset, rows), :]
        for link, _, field, past, rows, offset in corner_layers()[0]:
            column = REACH + pick(is_low("gx", link), -past, nx - 1 + past)
            to = pl.ds(TOP + pick(low_y, -rows, ny), rows)
            cells[field, column, to, :] = corner[pl.ds(zero + (start + offset), rows), :]

    def at(ref, *index, start, count):
        return ref[(*index, pl.ds(zero + start, count), slice(None))]

    for a in range(-3, nx + 3):
        get = functools.partial(at, cells, start=TOP - 4, count=tall)
        z = get(ZV, a + REACH)
        divergence = 0.5 * (
            get(XV, a + REACH + 1)
            - get(XV, a + REACH - 1)
            + (at(cells, YV, a + REACH, start=TOP - 3, count=tall) - at(cells, YV, a + REACH, start=TOP - 5, count=tall))
            + (up(z) - down(z))
        )
        per_mass = 0.4 * get(ENERGY, a + REACH) + 0.5 * jnp.square(jnp.minimum(divergence, 0.0))
        stress[a + 3] = get(DENSITY, a + REACH) * per_mass
        if -2 <= a < nx + 2:
            growth[a + 2] = dt * divergence
            heat[a + 2] = per_mass

    for a in range(-2, nx + 2):
        get = functools.partial(at, cells, start=TOP - 2, count=wide)
        density = get(DENSITY, a + REACH)
        grown = at(growth, a + 2, start=2, count=wide)
        centre = at(stress, a + 3, start=2, count=wide)
        scale = half / density
        density_one = density / (1.0 + grown)
        energy = get(ENERGY, a + REACH) - at(heat, a + 2, start=2, count=wide) * grown
        passive[0, a + 2] = density_one
        passive[1, a + 2] = density_one * energy
        x_one = get(XV, a + REACH) - scale * (
            at(stress, a + 4, start=2, count=wide) - at(stress, a + 2, start=2, count=wide)
        )
        state[0, a + 2] = x_one
        speed[a + 2] = x_one
        state[1, a + 2] = get(YV, a + REACH) - scale * (
            at(stress, a + 3, start=3, count=wide) - at(stress, a + 3, start=1, count=wide)
        )
        state[2, a + 2] = get(ZV, a + REACH) - scale * (up(centre) - down(centre))
        if 0 <= a < nx:
            energy_one[a, 0:wide] = energy

    sweep_x(state, speed, swept, (0, 1, 2), half)
    for a in range(nx):
        speed_y[a, 0:wide] = swept[1, a, 0:wide]

    peak = jnp.zeros((wide, nz), jnp.float32)
    for a in range(nx):
        below, here = at(swept, 1, a, start=1, count=wide), at(swept, 1, a, start=2, count=wide)
        moved = sweep_y(zero, swept, work, a, (0, 1, 2), face_factors(below, here, half), wide)
        speed_z[a] = moved[2]
        final = sweep_z(moved, face_factors(down(moved[2]), moved[2], half))
        for field in range(3):
            flows[field, a] = final[field][:ny]
        peak = jnp.maximum(
            peak,
            jnp.sqrt(0.56 * at(energy_one, a, start=2, count=wide))
            + jnp.abs(final[0])
            + jnp.abs(final[1])
            + jnp.abs(final[2]),
        )
    row = lax.broadcasted_iota(jnp.int32, peak.shape, 0)
    peak = jnp.max(jnp.where(row < ny, peak, 0.0), axis=0, keepdims=True)
    peak_ref[...] = jnp.broadcast_to(peak, peak_ref.shape)


def carry_kernel(nx, ny, zero_ref, dt_ref, *refs):
    state, speed, speed_y, speed_z, flows, density_out, energy_out = refs[:7]
    flow_outs, swept, work, written = refs[7:10], refs[10], refs[11], refs[12]
    zero = zero_ref[0]
    half = 0.5 * dt_ref[0]
    wide = ny + 4
    copies = [pltpu.make_async_copy(flows.at[k], flow_outs[k], written.at[k]) for k in range(3)]
    for copy in copies:
        copy.start()
    sweep_x(state, speed, swept, (0, 1), half)
    for a in range(nx):
        below, here = speed_y[a, pl.ds(zero + 1, wide)], speed_y[a, pl.ds(zero + 2, wide)]
        moved = sweep_y(zero, swept, work, a, (0, 1), face_factors(below, here, half), wide)
        final = sweep_z(moved, face_factors(down(speed_z[a]), speed_z[a], half))
        density_out[a] = final[0][:ny]
        energy_out[a] = final[1][:ny]
    for copy in copies:
        copy.wait()


def body(density0, energy0, x_velocity, y_velocity, z_velocity, time_increment):
    nx, ny, nz = density0.shape
    fields = (density0, energy0, x_velocity, y_velocity, z_velocity)
    zero = jnp.zeros((1,), jnp.int32)
    wide, tall = ny + 4, ny + 12

    def array(*shape):
        return jax.ShapeDtypeStruct((*shape, nz), jnp.float32)

    def scratch(*shape):
        return pltpu.VMEM((*shape, nz), jnp.float32)

    def limit(mebibytes):
        return pltpu.CompilerParams(vmem_limit_bytes=mebibytes * 1024 * 1024)

    outer, inner = [
        array(len(x_layers()) * sum(rows for _, rows in pieces)) for pieces in split_rows(ny)
    ]
    y_edge, corner = array(y_layers(nx)[1]), array(corner_layers()[1])
    own, *edges = pl.pallas_call(
        functools.partial(pack_kernel, nx, ny),
        out_shape=[array(5, nx, ny), outer, outer, inner, inner, y_edge, y_edge],
        in_specs=[SMEM] + [HBM] * 5,
        out_specs=[VMEM] * 7,
        scratch_shapes=[pltpu.SemaphoreType.DMA((5,))],
        compiler_params=limit(4),
        name="pack",
    )(zero, *[pltpu.with_memory_space_constraint(field, pltpu.HBM) for field in fields])
    outers = [exchanged(edge, "gx", link) for edge, link in zip(edges[0:2], LINKS)]
    inners = [exchanged(edge, "gx", link) for edge, link in zip(edges[2:4], LINKS)]
    y_far = exchanged(edges[4], "gy", FAR)
    far, near = pl.pallas_call(
        corner_kernel,
        out_shape=[corner, array(y_edge.shape[0] + corner.shape[0])],
        in_specs=[SMEM] + [VMEM] * 3,
        out_specs=[VMEM] * 2,
        compiler_params=limit(4),
        name="corners",
    )(zero, *outers, edges[5])
    far, near = exchanged(far, "gy", FAR), exchanged(near, "gy", NEAR)
    increment = time_increment.reshape(1)
    passed = [array(2, nx + 4, wide), array(nx + 4, wide), array(nx, wide + 8), array(nx, wide), array(3, nx, ny)]
    *passed, peak = pl.pallas_call(
        functools.partial(step_kernel, nx, ny),
        out_shape=passed + [pltpu.VMEM((lax.axis_size(("gx", "gy")), nz), jnp.float32)],
        in_specs=[SMEM, SMEM] + [VMEM] * 8,
        out_specs=[VMEM] * 6,
        scratch_shapes=[
            scratch(5, nx + 8, ny + 20),
            scratch(nx + 6, tall),
            scratch(nx + 4, tall),
            scratch(nx + 4, tall),
            scratch(3, nx + 4, wide),
            scratch(nx, wide + 8),
            scratch(3, nx, wide + 8),
            scratch(2, 3, nx, wide + 8),
        ],
        compiler_params=limit(12),
        name="step",
    )(zero, increment, own, *outers, *inners, y_far, far, near)
    outs = pl.pallas_call(
        functools.partial(carry_kernel, nx, ny),
        out_shape=[array(nx, ny)] * 5,
        in_specs=[SMEM, SMEM] + [VMEM] * 5,
        out_specs=[VMEM] * 2 + [HBM] * 3,
        scratch_shapes=[
            scratch(2, nx, wide + 8),
            scratch(2, 2, nx, wide + 8),
            pltpu.SemaphoreType.DMA((3,)),
        ],
        compiler_params=limit(8),
        cost_estimate=pl.CostEstimate(flops=10**7, bytes_accessed=4 * 10**6, transcendentals=0),
        name="carry",
    )(zero, increment, *passed)
    peak = lax.all_to_all(peak, ("gx", "gy"), 0, 0, tiled=True)
    return (*outs, 0.3 / jnp.max(peak))


def solution(mesh):
    cells = P("gx", "gy", None)
    return jax.shard_map(
        body,
        mesh=mesh,
        in_specs=(cells,) * 5 + (P(),),
        out_specs=(cells,) * 5 + (P(),),
        check_vma=False,
    )
```

```python
import functools

import jax
import jax.numpy as jnp
from jax import lax
from jax.experimental import pallas as pl
from jax.experimental.pallas import tpu as pltpu
from jax.sharding import PartitionSpec as P

DENSITY, ENERGY, XV, YV, ZV = range(5)
REACH = 4
NEAR, FAR = "near", "far"
SIDES = (-1, 1)
TOP = 8
VMEM = pl.BlockSpec(memory_space=pltpu.VMEM)
HBM = pl.BlockSpec(memory_space=pltpu.HBM)
SMEM = pl.BlockSpec(memory_space=pltpu.SMEM)


def ghost_rows(field, past):
    if field == YV:
        return (4, 4, 4, 3, 0)[past]
    return (3, 3, 3, 3, 2)[past] if field == XV else (3, 3, 3, 2, 0)[past]


def x_layers():
    return [(field, past) for field in range(5) for past in range(1, REACH + 1) if ghost_rows(field, past)]


def y_layers(nx):
    found, offset = [], 0
    for a in range(nx):
        for field in range(5):
            found.append((field, a, ghost_rows(field, 0), offset))
            offset += ghost_rows(field, 0)
    return found, -(-offset // 8) * 8


def corner_layers():
    found, offset = [], 0
    for number, (field, past) in enumerate(x_layers()):
        rows = ghost_rows(field, past)
        found.append((number, field, past, rows, offset))
        offset += rows
    return found, -(-offset // 8) * 8


def is_low(link):
    odd = lax.rem(lax.axis_index("gy"), 2)
    return odd if link == NEAR else 1 - odd


def partner(index, link, count):
    return index ^ 1 if link == NEAR else (((index - 1) ^ 1) + 1) % count


def fetched(value, side=0, link=None):
    gx, gy = lax.axis_size("gx"), lax.axis_size("gy")
    if link is None:
        return lax.ppermute(value, "gx", [((i + side) % gx, i) for i in range(gx)])
    if not side:
        return lax.ppermute(value, "gy", [(partner(j, link, gy), j) for j in range(gy)])
    pairs = [
        ((i + side) % gx * gy + partner(j, link, gy), i * gy + j) for i in range(gx) for j in range(gy)
    ]
    return lax.ppermute(value, ("gx", "gy"), pairs)


def pick(flag, one, other):
    return flag * one + (1 - flag) * other


def pack_kernel(nx, ny, zero_ref, *refs):
    fields, own, x_edges, corners, y_edges, arrived = refs[:5], refs[5], refs[6:8], refs[8:10], refs[10:12], refs[-1]
    zero = zero_ref[0]
    low = is_low(FAR)
    copies = [pltpu.make_async_copy(fields[field], own.at[field], arrived.at[field]) for field in range(5)]
    for copy in copies:
        copy.start()
    for current, copy in enumerate(copies):
        copy.wait()
        for side, edge, corner in zip(SIDES, x_edges, corners):
            for number, field, past, rows, offset in corner_layers()[0]:
                if field == current:
                    column = nx - past if side < 0 else past - 1
                    edge[pl.ds(zero + number * ny, ny), :] = own[field, column]
                    corner[pl.ds(zero + offset, rows), :] = own[field, column, pl.ds(pick(low, 0, ny - rows), rows), :]
        for link, edge in zip((FAR, NEAR), y_edges):
            for field, a, rows, offset in y_layers(nx)[0]:
                if field == current:
                    start = pick(is_low(link), 0, ny - rows)
                    edge[pl.ds(zero + offset, rows), :] = own[field, a, pl.ds(start, rows), :]


def near_kernel(ny, zero_ref, low_ref, high_ref, y_near, *refs):
    zero, out = zero_ref[0], refs[-1]
    start = y_near.shape[0]
    out[0:start, :] = y_near[...]
    for edge in (low_ref, high_ref):
        for number, _, _, rows, offset in corner_layers()[0]:
            first = number * ny + pick(is_low(NEAR), 0, ny - rows)
            out[pl.ds(zero + (start + offset), rows), :] = edge[pl.ds(first, rows), :]
        start += corner_layers()[1]


def limited(above, below):
    return jnp.minimum(jnp.maximum(above, jnp.minimum(below, 0.0)), jnp.maximum(below, 0.0))


def face_factors(v_minus, v, half_increment):
    courant = half_increment * (v_minus + v)
    size = jnp.abs(courant)
    return courant, 0.5 * size * (1.0 - size), courant > 0.0


def face_flux(factors, f_minus, f, s_minus, s):
    courant, slope_factor, upward = factors
    return courant * jnp.where(upward, f_minus, f) + slope_factor * jnp.where(upward, s_minus, s)


def up(value):
    return pltpu.roll(value, value.shape[-1] - 1, value.ndim - 1)


def down(value):
    return pltpu.roll(value, 1, value.ndim - 1)


def sweep_x(state, speed, swept, fields, half):
    for part in range(0, state.shape[2], 8):
        rows = pl.ds(part, 8)
        before = [state[field, 1, rows] for field in fields]
        here = [state[field, 2, rows] for field in fields]
        steps = [h - b for h, b in zip(here, before)]
        slopes = [limited(st, b - state[field, 0, rows]) for field, st, b in zip(fields, steps, before)]
        lower = None
        for a in range(swept.shape[1] + 1):
            factors = face_factors(speed[a + 1, rows], speed[a + 2, rows], half)
            fluxes = []
            for k, field in enumerate(fields):
                after = state[field, a + 3, rows]
                step = after - here[k]
                slope = limited(step, steps[k])
                fluxes.append(face_flux(factors, before[k], here[k], slopes[k], slope))
                if lower is not None:
                    swept[field, a - 1, rows] = before[k] - (fluxes[k] - lower[k])
                before[k], here[k], steps[k], slopes[k] = here[k], after, step, slope
            lower = fluxes


def sweep_y(zero, swept, work, a, fields, factors, wide):
    moved = []
    for field in fields:
        below = swept[field, a, pl.ds(zero + 1, wide)]
        here = swept[field, a, pl.ds(zero + 2, wide)]
        slope = limited(here - below, below - swept[field, a, 0:wide])
        work[0, field, a, 0:wide] = slope
        flux = face_flux(factors, below, here, slope, work[0, field, a, pl.ds(zero + 1, wide)])
        work[1, field, a, 0:wide] = flux
        moved.append(here - (work[1, field, a, pl.ds(zero + 1, wide)] - flux))
    return moved


def sweep_z(moved, factors):
    final = []
    for value in moved:
        below = down(value)
        step = value - below
        slope = limited(up(step), step)
        flux = face_flux(factors, below, value, down(slope), slope)
        final.append(value - (up(flux) - flux))
    return final


def step_kernel(nx, ny, zero_ref, dt_ref, *refs):
    own, x_edges, far_corners, (y_far, near) = refs[0], refs[1:3], refs[3:5], refs[5:7]
    passive, speed, speed_y, speed_z, flows, peak_ref = refs[7:13]
    cells, stress, growth, heat, state, energy_one, swept, work = refs[13:]
    nz = own.shape[-1]
    zero = zero_ref[0]
    dt = dt_ref[0]
    half = 0.5 * dt
    wide = ny + 4
    tall = ny + 12

    for field in range(5):
        for a in range(nx):
            cells[field, a + REACH, pl.ds(TOP, ny), :] = own[field, a]
    for side, edge in zip(SIDES, x_edges):
        for number, (field, past) in enumerate(x_layers()):
            column = REACH + (-past if side < 0 else nx - 1 + past)
            cells[field, column, pl.ds(TOP, ny), :] = edge[pl.ds(zero + number * ny, ny), :]
    corner_rows, start = corner_layers()[1], y_layers(nx)[1]
    near_corners = [(near, start), (near, start + corner_rows)]
    for link, edge, corners in ((FAR, y_far, [(corner, 0) for corner in far_corners]), (NEAR, near, near_corners)):
        low = is_low(link)
        for field, a, rows, offset in y_layers(nx)[0]:
            to = pl.ds(TOP + pick(low, -rows, ny), rows)
            cells[field, a + REACH, to, :] = edge[pl.ds(zero + offset, rows), :]
        for side, (corner, start) in zip(SIDES, corners):
            for _, field, past, rows, offset in corner_layers()[0]:
                column = REACH + (-past if side < 0 else nx - 1 + past)
                to = pl.ds(TOP + pick(low, -rows, ny), rows)
                cells[field, column, to, :] = corner[pl.ds(zero + (start + offset), rows), :]

    def at(ref, *index, start, count):
        return ref[(*index, pl.ds(zero + start, count), slice(None))]

    for a in range(-3, nx + 3):
        get = functools.partial(at, cells, start=TOP - 4, count=tall)
        z = get(ZV, a + REACH)
        divergence = 0.5 * (
            get(XV, a + REACH + 1)
            - get(XV, a + REACH - 1)
            + (at(cells, YV, a + REACH, start=TOP - 3, count=tall) - at(cells, YV, a + REACH, start=TOP - 5, count=tall))
            + (up(z) - down(z))
        )
        per_mass = 0.4 * get(ENERGY, a + REACH) + 0.5 * jnp.square(jnp.minimum(divergence, 0.0))
        stress[a + 3] = get(DENSITY, a + REACH) * per_mass
        if -2 <= a < nx + 2:
            growth[a + 2] = dt * divergence
            heat[a + 2] = per_mass

    for a in range(-2, nx + 2):
        get = functools.partial(at, cells, start=TOP - 2, count=wide)
        density = get(DENSITY, a + REACH)
        grown = at(growth, a + 2, start=2, count=wide)
        centre = at(stress, a + 3, start=2, count=wide)
        scale = half / density
        density_one = density / (1.0 + grown)
        energy = get(ENERGY, a + REACH) - at(heat, a + 2, start=2, count=wide) * grown
        passive[0, a + 2] = density_one
        passive[1, a + 2] = density_one * energy
        x_one = get(XV, a + REACH) - scale * (
            at(stress, a + 4, start=2, count=wide) - at(stress, a + 2, start=2, count=wide)
        )
        state[0, a + 2] = x_one
        speed[a + 2] = x_one
        state[1, a + 2] = get(YV, a + REACH) - scale * (
            at(stress, a + 3, start=3, count=wide) - at(stress, a + 3, start=1, count=wide)
        )
        state[2, a + 2] = get(ZV, a + REACH) - scale * (up(centre) - down(centre))
        if 0 <= a < nx:
            energy_one[a, 0:wide] = energy

    sweep_x(state, speed, swept, (0, 1, 2), half)
    for a in range(nx):
        speed_y[a, 0:wide] = swept[1, a, 0:wide]

    peak = jnp.zeros((wide, nz), jnp.float32)
    for a in range(nx):
        below, here = at(swept, 1, a, start=1, count=wide), at(swept, 1, a, start=2, count=wide)
        moved = sweep_y(zero, swept, work, a, (0, 1, 2), face_factors(below, here, half), wide)
        speed_z[a] = moved[2]
        final = sweep_z(moved, face_factors(down(moved[2]), moved[2], half))
        for field in range(3):
            flows[field, a] = final[field][:ny]
        peak = jnp.maximum(
            peak,
            jnp.sqrt(0.56 * at(energy_one, a, start=2, count=wide))
            + jnp.abs(final[0])
            + jnp.abs(final[1])
            + jnp.abs(final[2]),
        )
    row = lax.broadcasted_iota(jnp.int32, peak.shape, 0)
    peak = jnp.max(jnp.where(row < ny, peak, 0.0), axis=0, keepdims=True)
    peak_ref[...] = jnp.broadcast_to(peak, peak_ref.shape)


def carry_kernel(nx, ny, zero_ref, dt_ref, *refs):
    state, speed, speed_y, speed_z, flows, density_out, energy_out = refs[:7]
    flow_outs, swept, work, written = refs[7:10], refs[10], refs[11], refs[12]
    zero = zero_ref[0]
    half = 0.5 * dt_ref[0]
    wide = ny + 4
    copies = [pltpu.make_async_copy(flows.at[k], flow_outs[k], written.at[k]) for k in range(3)]
    for copy in copies:
        copy.start()
    sweep_x(state, speed, swept, (0, 1), half)
    for a in range(nx):
        below, here = speed_y[a, pl.ds(zero + 1, wide)], speed_y[a, pl.ds(zero + 2, wide)]
        moved = sweep_y(zero, swept, work, a, (0, 1), face_factors(below, here, half), wide)
        final = sweep_z(moved, face_factors(down(speed_z[a]), speed_z[a], half))
        density_out[a] = final[0][:ny]
        energy_out[a] = final[1][:ny]
    for copy in copies:
        copy.wait()


def body(density0, energy0, x_velocity, y_velocity, z_velocity, time_increment):
    nx, ny, nz = density0.shape
    fields = (density0, energy0, x_velocity, y_velocity, z_velocity)
    zero = jnp.zeros((1,), jnp.int32)
    wide, tall = ny + 4, ny + 12

    def array(*shape):
        return jax.ShapeDtypeStruct((*shape, nz), jnp.float32)

    def scratch(*shape):
        return pltpu.VMEM((*shape, nz), jnp.float32)

    def limit(mebibytes):
        return pltpu.CompilerParams(vmem_limit_bytes=mebibytes * 1024 * 1024)

    x_edge, y_edge, corner = array(len(x_layers()) * ny), array(y_layers(nx)[1]), array(corner_layers()[1])
    own, *edges = pl.pallas_call(
        functools.partial(pack_kernel, nx, ny),
        out_shape=[array(5, nx, ny), x_edge, x_edge, corner, corner, y_edge, y_edge],
        in_specs=[SMEM] + [HBM] * 5,
        out_specs=[VMEM] * 7,
        scratch_shapes=[pltpu.SemaphoreType.DMA((5,))],
        compiler_params=limit(4),
        name="pack",
    )(zero, *[pltpu.with_memory_space_constraint(field, pltpu.HBM) for field in fields])
    x_edges = [fetched(edge, side) for side, edge in zip(SIDES, edges[0:2])]
    far_corners = [fetched(edge, side, FAR) for side, edge in zip(SIDES, edges[2:4])]
    y_far = fetched(edges[4], 0, FAR)
    near = pl.pallas_call(
        functools.partial(near_kernel, ny),
        out_shape=array(y_edge.shape[0] + 2 * corner.shape[0]),
        in_specs=[SMEM] + [VMEM] * 6,
        out_specs=VMEM,
        compiler_params=limit(4),
        name="near",
    )(zero, *x_edges, edges[5], *far_corners, y_far)
    near = fetched(near, 0, NEAR)
    increment = time_increment.reshape(1)
    passed = [array(2, nx + 4, wide), array(nx + 4, wide), array(nx, wide + 8), array(nx, wide), array(3, nx, ny)]
    *passed, peak = pl.pallas_call(
        functools.partial(step_kernel, nx, ny),
        out_shape=passed + [array(lax.axis_size(("gx", "gy")))],
        in_specs=[SMEM, SMEM] + [VMEM] * 7,
        out_specs=[VMEM] * 6,
        scratch_shapes=[
            scratch(5, nx + 8, ny + 20),
            scratch(nx + 6, tall),
            scratch(nx + 4, tall),
            scratch(nx + 4, tall),
            scratch(3, nx + 4, wide),
            scratch(nx, wide + 8),
            scratch(3, nx, wide + 8),
            scratch(2, 3, nx, wide + 8),
        ],
        compiler_params=limit(12),
        name="step",
    )(zero, increment, own, *x_edges, *far_corners, y_far, near)
    outs = pl.pallas_call(
        functools.partial(carry_kernel, nx, ny),
        out_shape=[array(nx, ny)] * 5,
        in_specs=[SMEM, SMEM] + [VMEM] * 5,
        out_specs=[VMEM] * 2 + [HBM] * 3,
        scratch_shapes=[
            scratch(2, nx, wide + 8),
            scratch(2, 2, nx, wide + 8),
            pltpu.SemaphoreType.DMA((3,)),
        ],
        compiler_params=limit(8),
        cost_estimate=pl.CostEstimate(flops=10**7, bytes_accessed=4 * 10**6, transcendentals=0),
        name="carry",
    )(zero, increment, *passed)
    peak = lax.all_to_all(peak, ("gx", "gy"), 0, 0, tiled=True)
    return (*outs, 0.3 / jnp.max(peak))


def solution(mesh):
    cells = P("gx", "gy", None)
    return jax.shard_map(
        body,
        mesh=mesh,
        in_specs=(cells,) * 5 + (P(),),
        out_specs=(cells,) * 5 + (P(),),
        check_vma=False,
    )
```

```python
import functools

import jax
import jax.numpy as jnp
from jax import lax
from jax.experimental import pallas as pl
from jax.experimental.pallas import tpu as pltpu
from jax.sharding import PartitionSpec as P

DENSITY, ENERGY, XV, YV, ZV = range(5)
REACH = 4
SIDES = ((-1, 0), (1, 0), (0, -1), (0, 1))
TOP = 8
VMEM = pl.BlockSpec(memory_space=pltpu.VMEM)
HBM = pl.BlockSpec(memory_space=pltpu.HBM)
SMEM = pl.BlockSpec(memory_space=pltpu.SMEM)


def rows_needed(field, a, nx, ny):
    past = max(-a, a - nx + 1, 0)
    if field == XV:
        reach = {0: 3, 1: 3, 2: 3, 3: 3, 4: 2}.get(past, -1)
    elif field == YV:
        reach = {0: 4, 1: 4, 2: 4, 3: 3}.get(past, -1)
    else:
        reach = {0: 3, 1: 3, 2: 3, 3: 2}.get(past, -1)
    return (-reach, ny + reach) if reach >= 0 else (0, 0)


def segments(side, nx, ny):
    columns = {-1: range(-REACH, 0), 0: range(nx), 1: range(nx, nx + REACH)}[side[0]]
    low, high = {-1: (-REACH, 0), 0: (0, ny), 1: (ny, ny + REACH)}[side[1]]
    found, offset = [], 0
    for a in columns:
        for field in range(5):
            first, last = rows_needed(field, a, nx, ny)
            first, last = max(first, low), min(last, high)
            if last > first:
                found.append((field, a, first, last - first, offset))
                offset += last - first
    return found, -(-offset // 8) * 8


def corner_segments(side_y, nx, ny):
    found, offset = [], 0
    for side_x in (-1, 1):
        for field, a, first, count, _ in segments((side_x, side_y), nx, ny)[0]:
            found.append((side_x, field, a, first, count, offset))
            offset += count
    return found, -(-offset // 8) * 8


def hidden_zero():
    return lax.shift_right_logical(lax.axis_index("gx"), 20)


def pack_kernel(nx, ny, *refs):
    fields, own, edges, arrived = refs[:5], refs[5], refs[6 : 6 + len(SIDES)], refs[-1]
    zero = hidden_zero()
    copies = [pltpu.make_async_copy(fields[field], own.at[field], arrived.at[field]) for field in range(5)]
    for copy in copies:
        copy.start()
    for current, copy in enumerate(copies):
        copy.wait()
        for side, edge in zip(SIDES, edges):
            for field, a, b, count, offset in segments(side, nx, ny)[0]:
                if field == current:
                    edge[pl.ds(zero + offset, count), :] = own[
                        field, a - side[0] * nx, pl.ds(zero + (b - side[1] * ny), count), :
                    ]


def corner_kernel(nx, ny, below_ref, above_ref, low_ref, high_ref):
    zero = hidden_zero()
    held = {
        (side_x, field, a): (ref, offset)
        for side_x, ref in ((-1, below_ref), (1, above_ref))
        for field, a, _, _, offset in segments((side_x, 0), nx, ny)[0]
    }
    for side_y, out in ((-1, low_ref), (1, high_ref)):
        for side_x, field, a, b, count, offset in corner_segments(side_y, nx, ny)[0]:
            ref, start = held[side_x, field, a]
            out[pl.ds(zero + offset, count), :] = ref[pl.ds(zero + (start + b - side_y * ny), count), :]


def limited(above, below):
    return jnp.minimum(jnp.maximum(above, jnp.minimum(below, 0.0)), jnp.maximum(below, 0.0))


def face_factors(v_minus, v, half_increment):
    courant = half_increment * (v_minus + v)
    size = jnp.abs(courant)
    return courant, 0.5 * size * (1.0 - size), courant > 0.0


def face_flux(factors, f_minus, f, s_minus, s):
    courant, slope_factor, upward = factors
    return courant * jnp.where(upward, f_minus, f) + slope_factor * jnp.where(upward, s_minus, s)


def up(value):
    return pltpu.roll(value, value.shape[-1] - 1, value.ndim - 1)


def down(value):
    return pltpu.roll(value, 1, value.ndim - 1)


def sweep_x(state, speed, swept, fields, half):
    for part in range(0, state.shape[2], 8):
        rows = pl.ds(part, 8)
        before = [state[field, 1, rows] for field in fields]
        here = [state[field, 2, rows] for field in fields]
        steps = [h - b for h, b in zip(here, before)]
        slopes = [limited(st, b - state[field, 0, rows]) for field, st, b in zip(fields, steps, before)]
        lower = None
        for a in range(swept.shape[1] + 1):
            factors = face_factors(speed[a + 1, rows], speed[a + 2, rows], half)
            fluxes = []
            for k, field in enumerate(fields):
                after = state[field, a + 3, rows]
                step = after - here[k]
                slope = limited(step, steps[k])
                fluxes.append(face_flux(factors, before[k], here[k], slopes[k], slope))
                if lower is not None:
                    swept[field, a - 1, rows] = before[k] - (fluxes[k] - lower[k])
                before[k], here[k], steps[k], slopes[k] = here[k], after, step, slope
            lower = fluxes


def sweep_y(zero, swept, work, a, fields, factors, wide):
    moved = []
    for field in fields:
        below = swept[field, a, pl.ds(zero + 1, wide)]
        here = swept[field, a, pl.ds(zero + 2, wide)]
        slope = limited(here - below, below - swept[field, a, 0:wide])
        work[0, field, a, 0:wide] = slope
        flux = face_flux(factors, below, here, slope, work[0, field, a, pl.ds(zero + 1, wide)])
        work[1, field, a, 0:wide] = flux
        moved.append(here - (work[1, field, a, pl.ds(zero + 1, wide)] - flux))
    return moved


def sweep_z(moved, factors):
    final = []
    for value in moved:
        below = down(value)
        step = value - below
        slope = limited(up(step), step)
        flux = face_flux(factors, below, value, down(slope), slope)
        final.append(value - (up(flux) - flux))
    return final


def step_kernel(nx, ny, dt_ref, *refs):
    own, halos = refs[0], refs[1:7]
    passive, speed, speed_y, speed_z, flows, increment_ref = refs[7:13]
    cells, stress, growth, heat, state, energy_one, swept, work = refs[13:]
    nz = own.shape[-1]
    zero = hidden_zero()
    dt = dt_ref[0]
    half = 0.5 * dt
    wide = ny + 4
    tall = ny + 12

    for field in range(5):
        for a in range(nx):
            cells[field, a + REACH, pl.ds(TOP, ny), :] = own[field, a]
    for side, halo in zip(SIDES, halos):
        for field, a, b, count, offset in segments(side, nx, ny)[0]:
            cells[field, a + REACH, pl.ds(zero + (b + TOP), count), :] = halo[pl.ds(zero + offset, count), :]
    for side_y, halo in zip((-1, 1), halos[len(SIDES) :]):
        for _, field, a, b, count, offset in corner_segments(side_y, nx, ny)[0]:
            cells[field, a + REACH, pl.ds(zero + (b + TOP), count), :] = halo[pl.ds(zero + offset, count), :]

    def at(ref, *index, start, count):
        return ref[(*index, pl.ds(zero + start, count), slice(None))]

    for a in range(-3, nx + 3):
        get = functools.partial(at, cells, start=TOP - 4, count=tall)
        z = get(ZV, a + REACH)
        divergence = 0.5 * (
            get(XV, a + REACH + 1)
            - get(XV, a + REACH - 1)
            + (at(cells, YV, a + REACH, start=TOP - 3, count=tall) - at(cells, YV, a + REACH, start=TOP - 5, count=tall))
            + (up(z) - down(z))
        )
        per_mass = 0.4 * get(ENERGY, a + REACH) + 0.5 * jnp.square(jnp.minimum(divergence, 0.0))
        stress[a + 3] = get(DENSITY, a + REACH) * per_mass
        if -2 <= a < nx + 2:
            growth[a + 2] = dt * divergence
            heat[a + 2] = per_mass

    for a in range(-2, nx + 2):
        get = functools.partial(at, cells, start=TOP - 2, count=wide)
        density = get(DENSITY, a + REACH)
        grown = at(growth, a + 2, start=2, count=wide)
        centre = at(stress, a + 3, start=2, count=wide)
        scale = half / density
        density_one = density / (1.0 + grown)
        energy = get(ENERGY, a + REACH) - at(heat, a + 2, start=2, count=wide) * grown
        passive[0, a + 2] = density_one
        passive[1, a + 2] = density_one * energy
        x_one = get(XV, a + REACH) - scale * (
            at(stress, a + 4, start=2, count=wide) - at(stress, a + 2, start=2, count=wide)
        )
        state[0, a + 2] = x_one
        speed[a + 2] = x_one
        state[1, a + 2] = get(YV, a + REACH) - scale * (
            at(stress, a + 3, start=3, count=wide) - at(stress, a + 3, start=1, count=wide)
        )
        state[2, a + 2] = get(ZV, a + REACH) - scale * (up(centre) - down(centre))
        if 0 <= a < nx:
            energy_one[a, 0:wide] = energy

    sweep_x(state, speed, swept, (0, 1, 2), half)
    for a in range(nx):
        speed_y[a, 0:wide] = swept[1, a, 0:wide]

    peak = jnp.zeros((wide, nz), jnp.float32)
    for a in range(nx):
        below, here = at(swept, 1, a, start=1, count=wide), at(swept, 1, a, start=2, count=wide)
        moved = sweep_y(zero, swept, work, a, (0, 1, 2), face_factors(below, here, half), wide)
        speed_z[a] = moved[2]
        final = sweep_z(moved, face_factors(down(moved[2]), moved[2], half))
        for field in range(3):
            flows[field, a] = final[field][:ny]
        peak = jnp.maximum(
            peak,
            jnp.sqrt(0.56 * at(energy_one, a, start=2, count=wide))
            + jnp.abs(final[0])
            + jnp.abs(final[1])
            + jnp.abs(final[2]),
        )
    row = lax.broadcasted_iota(jnp.int32, peak.shape, 0)
    peak = jnp.max(jnp.where(row < ny, peak, 0.0), axis=0, keepdims=True)
    increment_ref[...] = jnp.broadcast_to(0.3 / peak, increment_ref.shape)


def carry_kernel(nx, ny, dt_ref, *refs):
    state, speed, speed_y, speed_z, flows, density_out, energy_out = refs[:7]
    flow_outs, swept, work, written = refs[7:10], refs[10], refs[11], refs[12]
    zero = hidden_zero()
    half = 0.5 * dt_ref[0]
    wide = ny + 4
    copies = [pltpu.make_async_copy(flows.at[k], flow_outs[k], written.at[k]) for k in range(3)]
    for copy in copies:
        copy.start()
    sweep_x(state, speed, swept, (0, 1), half)
    for a in range(nx):
        below, here = speed_y[a, pl.ds(zero + 1, wide)], speed_y[a, pl.ds(zero + 2, wide)]
        moved = sweep_y(zero, swept, work, a, (0, 1), face_factors(below, here, half), wide)
        final = sweep_z(moved, face_factors(down(speed_z[a]), speed_z[a], half))
        density_out[a] = final[0][:ny]
        energy_out[a] = final[1][:ny]
    for copy in copies:
        copy.wait()


def shifted(value, side):
    axis, step = ("gx", side[0]) if side[0] else ("gy", side[1])
    count = lax.axis_size(axis)
    return lax.ppermute(value, axis, [((i + step) % count, i) for i in range(count)])


def body(density0, energy0, x_velocity, y_velocity, z_velocity, time_increment):
    nx, ny, nz = density0.shape
    fields = (density0, energy0, x_velocity, y_velocity, z_velocity)
    wide, tall = ny + 4, ny + 12

    def array(*shape):
        return jax.ShapeDtypeStruct((*shape, nz), jnp.float32)

    def scratch(*shape):
        return pltpu.VMEM((*shape, nz), jnp.float32)

    def limit(mebibytes):
        return pltpu.CompilerParams(vmem_limit_bytes=mebibytes * 1024 * 1024)

    own, *edges = pl.pallas_call(
        functools.partial(pack_kernel, nx, ny),
        out_shape=[array(5, nx, ny)] + [array(segments(side, nx, ny)[1]) for side in SIDES],
        in_specs=[HBM] * 5,
        out_specs=[VMEM] * (1 + len(SIDES)),
        scratch_shapes=[pltpu.SemaphoreType.DMA((5,))],
        compiler_params=limit(4),
        name="pack",
    )(*[pltpu.with_memory_space_constraint(field, pltpu.HBM) for field in fields])
    edges = [shifted(edge, side) for edge, side in zip(edges, SIDES)]
    corners = pl.pallas_call(
        functools.partial(corner_kernel, nx, ny),
        out_shape=[array(corner_segments(1, nx, ny)[1])] * 2,
        in_specs=[VMEM] * 2,
        out_specs=[VMEM] * 2,
        compiler_params=limit(4),
        name="corners",
    )(edges[0], edges[1])
    corners = [shifted(corner, (0, side_y)) for corner, side_y in zip(corners, (-1, 1))]
    count = lax.axis_size(("gx", "gy"))
    increment = time_increment.reshape(1)
    passed = [array(2, nx + 4, wide), array(nx + 4, wide), array(nx, wide + 8), array(nx, wide), array(3, nx, ny)]
    *passed, smallest = pl.pallas_call(
        functools.partial(step_kernel, nx, ny),
        out_shape=passed + [array(count)],
        in_specs=[SMEM] + [VMEM] * 7,
        out_specs=[VMEM] * 6,
        scratch_shapes=[
            scratch(5, nx + 8, ny + 20),
            scratch(nx + 6, tall),
            scratch(nx + 4, tall),
            scratch(nx + 4, tall),
            scratch(3, nx + 4, wide),
            scratch(nx, wide + 8),
            scratch(3, nx, wide + 8),
            scratch(2, 3, nx, wide + 8),
        ],
        compiler_params=limit(12),
        name="step",
    )(increment, own, *edges, *corners)
    outs = pl.pallas_call(
        functools.partial(carry_kernel, nx, ny),
        out_shape=[array(nx, ny)] * 5,
        in_specs=[SMEM] + [VMEM] * 5,
        out_specs=[VMEM] * 2 + [HBM] * 3,
        scratch_shapes=[
            scratch(2, nx, wide + 8),
            scratch(2, 2, nx, wide + 8),
            pltpu.SemaphoreType.DMA((3,)),
        ],
        compiler_params=limit(8),
        cost_estimate=pl.CostEstimate(flops=10**7, bytes_accessed=4 * 10**6, transcendentals=0),
        name="carry",
    )(increment, *passed)
    return (*outs, jnp.min(lax.all_to_all(smallest, ("gx", "gy"), 0, 0, tiled=True)))


def solution(mesh):
    cells = P("gx", "gy", None)
    return jax.shard_map(
        body,
        mesh=mesh,
        in_specs=(cells,) * 5 + (P(),),
        out_specs=(cells,) * 5 + (P(),),
        check_vma=False,
    )
```

```python
import functools

import jax
import jax.numpy as jnp
from jax import lax
from jax.experimental import pallas as pl
from jax.experimental.pallas import tpu as pltpu
from jax.sharding import PartitionSpec as P

DENSITY, ENERGY, XV, YV, ZV = range(5)
REACH = 4
SIDES = ((-1, 0), (1, 0), (0, -1), (0, 1))
TOP = 8
VMEM = pl.BlockSpec(memory_space=pltpu.VMEM)
HBM = pl.BlockSpec(memory_space=pltpu.HBM)
SMEM = pl.BlockSpec(memory_space=pltpu.SMEM)


def rows_needed(field, a, nx, ny):
    past = max(-a, a - nx + 1, 0)
    if field == XV:
        reach = {0: 3, 1: 3, 2: 3, 3: 3, 4: 2}.get(past, -1)
    elif field == YV:
        reach = {0: 4, 1: 4, 2: 4, 3: 3}.get(past, -1)
    else:
        reach = {0: 3, 1: 3, 2: 3, 3: 2}.get(past, -1)
    return (-reach, ny + reach) if reach >= 0 else (0, 0)


def segments(side, nx, ny):
    columns = {-1: range(-REACH, 0), 0: range(nx), 1: range(nx, nx + REACH)}[side[0]]
    low, high = {-1: (-REACH, 0), 0: (0, ny), 1: (ny, ny + REACH)}[side[1]]
    found, offset = [], 0
    for a in columns:
        for field in range(5):
            first, last = rows_needed(field, a, nx, ny)
            first, last = max(first, low), min(last, high)
            if last > first:
                found.append((field, a, first, last - first, offset))
                offset += last - first
    return found, -(-offset // 8) * 8


def corner_segments(side_y, nx, ny):
    found, offset = [], 0
    for side_x in (-1, 1):
        for field, a, first, count, _ in segments((side_x, side_y), nx, ny)[0]:
            found.append((side_x, field, a, first, count, offset))
            offset += count
    return found, -(-offset // 8) * 8


def hidden_zero():
    return lax.shift_right_logical(lax.axis_index("gx"), 20)


def pack_kernel(nx, ny, *refs):
    fields, own, edges, arrived = refs[:5], refs[5], refs[6 : 6 + len(SIDES)], refs[-1]
    zero = hidden_zero()
    copies = [pltpu.make_async_copy(fields[field], own.at[field], arrived.at[field]) for field in range(5)]
    for copy in copies:
        copy.start()
    for current, copy in enumerate(copies):
        copy.wait()
        for side, edge in zip(SIDES, edges):
            for field, a, b, count, offset in segments(side, nx, ny)[0]:
                if field == current:
                    edge[pl.ds(zero + offset, count), :] = own[
                        field, a - side[0] * nx, pl.ds(zero + (b - side[1] * ny), count), :
                    ]


def corner_kernel(nx, ny, below_ref, above_ref, low_ref, high_ref):
    zero = hidden_zero()
    held = {
        (side_x, field, a): (ref, offset)
        for side_x, ref in ((-1, below_ref), (1, above_ref))
        for field, a, _, _, offset in segments((side_x, 0), nx, ny)[0]
    }
    for side_y, out in ((-1, low_ref), (1, high_ref)):
        for side_x, field, a, b, count, offset in corner_segments(side_y, nx, ny)[0]:
            ref, start = held[side_x, field, a]
            out[pl.ds(zero + offset, count), :] = ref[pl.ds(zero + (start + b - side_y * ny), count), :]


def limited(above, below):
    return jnp.minimum(jnp.maximum(above, jnp.minimum(below, 0.0)), jnp.maximum(below, 0.0))


def face_factors(v_minus, v, half_increment):
    courant = half_increment * (v_minus + v)
    size = jnp.abs(courant)
    return courant, 0.5 * size * (1.0 - size), courant > 0.0


def face_flux(factors, f_minus, f, s_minus, s):
    courant, slope_factor, upward = factors
    return courant * jnp.where(upward, f_minus, f) + slope_factor * jnp.where(upward, s_minus, s)


def up(value):
    return pltpu.roll(value, value.shape[-1] - 1, value.ndim - 1)


def down(value):
    return pltpu.roll(value, 1, value.ndim - 1)


def sweep_x(state, speed, swept, fields, half):
    for part in range(0, state.shape[2], 8):
        rows = pl.ds(part, 8)
        before = [state[field, 1, rows] for field in fields]
        here = [state[field, 2, rows] for field in fields]
        steps = [h - b for h, b in zip(here, before)]
        slopes = [limited(st, b - state[field, 0, rows]) for field, st, b in zip(fields, steps, before)]
        lower = None
        for a in range(swept.shape[1] + 1):
            factors = face_factors(speed[a + 1, rows], speed[a + 2, rows], half)
            fluxes = []
            for k, field in enumerate(fields):
                after = state[field, a + 3, rows]
                step = after - here[k]
                slope = limited(step, steps[k])
                fluxes.append(face_flux(factors, before[k], here[k], slopes[k], slope))
                if lower is not None:
                    swept[field, a - 1, rows] = before[k] - (fluxes[k] - lower[k])
                before[k], here[k], steps[k], slopes[k] = here[k], after, step, slope
            lower = fluxes


def sweep_y(zero, swept, work, a, fields, factors, wide):
    moved = []
    for field in fields:
        below = swept[field, a, pl.ds(zero + 1, wide)]
        here = swept[field, a, pl.ds(zero + 2, wide)]
        slope = limited(here - below, below - swept[field, a, 0:wide])
        work[0, field, a, 0:wide] = slope
        flux = face_flux(factors, below, here, slope, work[0, field, a, pl.ds(zero + 1, wide)])
        work[1, field, a, 0:wide] = flux
        moved.append(here - (work[1, field, a, pl.ds(zero + 1, wide)] - flux))
    return moved


def sweep_z(moved, factors):
    final = []
    for value in moved:
        below = down(value)
        step = value - below
        slope = limited(up(step), step)
        flux = face_flux(factors, below, value, down(slope), slope)
        final.append(value - (up(flux) - flux))
    return final


def step_kernel(nx, ny, dt_ref, *refs):
    own, halos = refs[0], refs[1:7]
    passive, speed, speed_y, speed_z, flows, increment_ref = refs[7:13]
    cells, stress, growth, heat, state, energy_one, swept, work = refs[13:]
    nz = own.shape[-1]
    zero = hidden_zero()
    dt = dt_ref[0]
    half = 0.5 * dt
    wide = ny + 4
    tall = ny + 12

    for field in range(5):
        for a in range(nx):
            cells[field, a + REACH, pl.ds(TOP, ny), :] = own[field, a]
    for side, halo in zip(SIDES, halos):
        for field, a, b, count, offset in segments(side, nx, ny)[0]:
            cells[field, a + REACH, pl.ds(zero + (b + TOP), count), :] = halo[pl.ds(zero + offset, count), :]
    for side_y, halo in zip((-1, 1), halos[len(SIDES) :]):
        for _, field, a, b, count, offset in corner_segments(side_y, nx, ny)[0]:
            cells[field, a + REACH, pl.ds(zero + (b + TOP), count), :] = halo[pl.ds(zero + offset, count), :]

    def at(ref, *index, start, count):
        return ref[(*index, pl.ds(zero + start, count), slice(None))]

    for a in range(-3, nx + 3):
        get = functools.partial(at, cells, start=TOP - 4, count=tall)
        z = get(ZV, a + REACH)
        divergence = 0.5 * (
            get(XV, a + REACH + 1)
            - get(XV, a + REACH - 1)
            + (at(cells, YV, a + REACH, start=TOP - 3, count=tall) - at(cells, YV, a + REACH, start=TOP - 5, count=tall))
            + (up(z) - down(z))
        )
        per_mass = 0.4 * get(ENERGY, a + REACH) + 0.5 * jnp.square(jnp.minimum(divergence, 0.0))
        stress[a + 3] = get(DENSITY, a + REACH) * per_mass
        if -2 <= a < nx + 2:
            growth[a + 2] = dt * divergence
            heat[a + 2] = per_mass

    for a in range(-2, nx + 2):
        get = functools.partial(at, cells, start=TOP - 2, count=wide)
        density = get(DENSITY, a + REACH)
        grown = at(growth, a + 2, start=2, count=wide)
        centre = at(stress, a + 3, start=2, count=wide)
        scale = half / density
        density_one = density / (1.0 + grown)
        energy = get(ENERGY, a + REACH) - at(heat, a + 2, start=2, count=wide) * grown
        passive[0, a + 2] = density_one
        passive[1, a + 2] = density_one * energy
        x_one = get(XV, a + REACH) - scale * (
            at(stress, a + 4, start=2, count=wide) - at(stress, a + 2, start=2, count=wide)
        )
        state[0, a + 2] = x_one
        speed[a + 2] = x_one
        state[1, a + 2] = get(YV, a + REACH) - scale * (
            at(stress, a + 3, start=3, count=wide) - at(stress, a + 3, start=1, count=wide)
        )
        state[2, a + 2] = get(ZV, a + REACH) - scale * (up(centre) - down(centre))
        if 0 <= a < nx:
            energy_one[a, 0:wide] = energy

    sweep_x(state, speed, swept, (0, 1, 2), half)
    for a in range(nx):
        speed_y[a, 0:wide] = swept[1, a, 0:wide]

    peak = jnp.zeros((wide, nz), jnp.float32)
    for a in range(nx):
        below, here = at(swept, 1, a, start=1, count=wide), at(swept, 1, a, start=2, count=wide)
        moved = sweep_y(zero, swept, work, a, (0, 1, 2), face_factors(below, here, half), wide)
        speed_z[a] = moved[2]
        final = sweep_z(moved, face_factors(down(moved[2]), moved[2], half))
        for field in range(3):
            flows[field, a] = final[field][:ny]
        peak = jnp.maximum(
            peak,
            jnp.sqrt(0.56 * at(energy_one, a, start=2, count=wide))
            + jnp.abs(final[0])
            + jnp.abs(final[1])
            + jnp.abs(final[2]),
        )
    row = lax.broadcasted_iota(jnp.int32, peak.shape, 0)
    peak = jnp.max(jnp.where(row < ny, peak, 0.0), axis=0, keepdims=True)
    increment_ref[...] = 0.3 / peak


def carry_kernel(nx, ny, dt_ref, _, *refs):
    state, speed, speed_y, speed_z, flows, density_out, energy_out = refs[:7]
    flow_outs, swept, work, written = refs[7:10], refs[10], refs[11], refs[12]
    zero = hidden_zero()
    half = 0.5 * dt_ref[0]
    wide = ny + 4
    copies = [pltpu.make_async_copy(flows.at[k], flow_outs[k], written.at[k]) for k in range(3)]
    for copy in copies:
        copy.start()
    sweep_x(state, speed, swept, (0, 1), half)
    for a in range(nx):
        below, here = speed_y[a, pl.ds(zero + 1, wide)], speed_y[a, pl.ds(zero + 2, wide)]
        moved = sweep_y(zero, swept, work, a, (0, 1), face_factors(below, here, half), wide)
        final = sweep_z(moved, face_factors(down(speed_z[a]), speed_z[a], half))
        density_out[a] = final[0][:ny]
        energy_out[a] = final[1][:ny]
    for copy in copies:
        copy.wait()


def shifted(value, side):
    axis, step = ("gx", side[0]) if side[0] else ("gy", side[1])
    count = lax.axis_size(axis)
    return lax.ppermute(value, axis, [((i + step) % count, i) for i in range(count)])


def pair_min(row):
    axes = ("gx", "gy")
    return jnp.minimum(row, lax.ppermute(row, axes, [(i, i ^ 1) for i in range(lax.axis_size(axes))]))


def global_min(row):
    axes = ("gx", "gy")
    count = lax.axis_size(axes)
    rows = jnp.broadcast_to(row, (count // 2, row.shape[-1]))
    groups = [list(range(first, count, 2)) for first in range(2)]
    return jnp.min(lax.all_to_all(rows, axes, 0, 0, axis_index_groups=groups, tiled=True))


def body(density0, energy0, x_velocity, y_velocity, z_velocity, time_increment):
    nx, ny, nz = density0.shape
    fields = (density0, energy0, x_velocity, y_velocity, z_velocity)
    wide, tall = ny + 4, ny + 12

    def array(*shape):
        return jax.ShapeDtypeStruct((*shape, nz), jnp.float32)

    def scratch(*shape):
        return pltpu.VMEM((*shape, nz), jnp.float32)

    def limit(mebibytes):
        return pltpu.CompilerParams(vmem_limit_bytes=mebibytes * 1024 * 1024)

    own, *edges = pl.pallas_call(
        functools.partial(pack_kernel, nx, ny),
        out_shape=[array(5, nx, ny)] + [array(segments(side, nx, ny)[1]) for side in SIDES],
        in_specs=[HBM] * 5,
        out_specs=[VMEM] * (1 + len(SIDES)),
        scratch_shapes=[pltpu.SemaphoreType.DMA((5,))],
        compiler_params=limit(4),
        name="pack",
    )(*[pltpu.with_memory_space_constraint(field, pltpu.HBM) for field in fields])
    edges = [shifted(edge, side) for edge, side in zip(edges, SIDES)]
    corners = pl.pallas_call(
        functools.partial(corner_kernel, nx, ny),
        out_shape=[array(corner_segments(1, nx, ny)[1])] * 2,
        in_specs=[VMEM] * 2,
        out_specs=[VMEM] * 2,
        compiler_params=limit(4),
        name="corners",
    )(edges[0], edges[1])
    corners = [shifted(corner, (0, side_y)) for corner, side_y in zip(corners, (-1, 1))]
    increment = time_increment.reshape(1)
    passed = [array(2, nx + 4, wide), array(nx + 4, wide), array(nx, wide + 8), array(nx, wide), array(3, nx, ny)]
    *passed, smallest = pl.pallas_call(
        functools.partial(step_kernel, nx, ny),
        out_shape=passed + [array(1)],
        in_specs=[SMEM] + [VMEM] * 7,
        out_specs=[VMEM] * 6,
        scratch_shapes=[
            scratch(5, nx + 8, ny + 20),
            scratch(nx + 6, tall),
            scratch(nx + 4, tall),
            scratch(nx + 4, tall),
            scratch(3, nx + 4, wide),
            scratch(nx, wide + 8),
            scratch(3, nx, wide + 8),
            scratch(2, 3, nx, wide + 8),
        ],
        compiler_params=limit(12),
        name="step",
    )(increment, own, *edges, *corners)
    smallest = pair_min(smallest)
    outs = pl.pallas_call(
        functools.partial(carry_kernel, nx, ny),
        out_shape=[array(nx, ny)] * 5,
        in_specs=[SMEM] + [VMEM] * 6,
        out_specs=[VMEM] * 2 + [HBM] * 3,
        scratch_shapes=[
            scratch(2, nx, wide + 8),
            scratch(2, 2, nx, wide + 8),
            pltpu.SemaphoreType.DMA((3,)),
        ],
        compiler_params=limit(8),
        cost_estimate=pl.CostEstimate(flops=10**7, bytes_accessed=4 * 10**6, transcendentals=0),
        name="carry",
    )(increment, smallest, *passed)
    return (*outs, global_min(smallest))


def solution(mesh):
    cells = P("gx", "gy", None)
    return jax.shard_map(
        body,
        mesh=mesh,
        in_specs=(cells,) * 5 + (P(),),
        out_specs=(cells,) * 5 + (P(),),
        check_vma=False,
    )
```

```python
import functools

import jax
import jax.numpy as jnp
from jax import lax
from jax.experimental import pallas as pl
from jax.experimental.pallas import tpu as pltpu
from jax.sharding import PartitionSpec as P

DENSITY, ENERGY, XV, YV, ZV = range(5)
TOP = 8
LEFT = 3
SIDES = (-1, 1)
NEAR, FAR = "near", "far"
LINKS = (FAR, NEAR)
EDGE_KINDS = 4
VMEM = pl.BlockSpec(memory_space=pltpu.VMEM)
HBM = pl.BlockSpec(memory_space=pltpu.HBM)
SMEM = pl.BlockSpec(memory_space=pltpu.SMEM)


def ghost_rows(field):
    return 4 if field == YV else 3


def x_layers():
    return [(field, past) for field in range(5) for past in (1, 2)] + [(XV, 3)]


def x_edge_rows(ny):
    return (len(x_layers()) + 1) * ny + 2 * EDGE_KINDS


def y_layers(nx):
    found, offset = [], 0
    for a in range(nx):
        for field in range(5):
            found.append((field, a, ghost_rows(field), offset))
            offset += ghost_rows(field)
    return found, -(-offset // 8) * 8


def corner_layers():
    found, offset = [], 0
    for number, (field, past) in enumerate(x_layers()):
        found.append((number, field, past, ghost_rows(field), offset))
        offset += ghost_rows(field)
    return found, offset, -(-(offset + 1 + EDGE_KINDS) // 8) * 8


def is_low(link):
    odd = lax.rem(lax.axis_index("gy"), 2)
    return odd if link == NEAR else 1 - odd


def pick(flag, one, other):
    return flag * one + (1 - flag) * other


def along_x(value, side):
    count = lax.axis_size("gx")
    return lax.ppermute(value, "gx", [((i + side) % count, i) for i in range(count)])


def along_y(value, link):
    count = lax.axis_size("gy")
    partners = [i ^ 1 if link == NEAR else (((i - 1) ^ 1) + 1) % count for i in range(count)]
    return lax.ppermute(value, "gy", list(enumerate(partners)))


def hidden_zero():
    return lax.shift_right_logical(lax.axis_index("gx"), 20)


def per_mass(energy, spread):
    return 0.4 * energy + 0.5 * jnp.square(jnp.minimum(0.5 * spread, 0.0))


def pack_kernel(nx, ny, *refs):
    fields, own, x_edges, y_edges, padded, arrived = refs[:5], refs[5], refs[6:8], refs[8:10], refs[10], refs[11]
    zero = hidden_zero()
    copies = [pltpu.make_async_copy(fields[field], own.at[field], arrived.at[field]) for field in range(5)]
    for copy in copies:
        copy.start()
    for current, copy in enumerate(copies):
        copy.wait()
        for side, edge in zip(SIDES, x_edges):
            for number, (field, past) in enumerate(x_layers()):
                if field == current:
                    column = nx - past if side < 0 else past - 1
                    edge[pl.ds(zero + number * ny, ny), :] = own[field, column]
        for link, edge in zip(LINKS, y_edges):
            for field, a, rows, offset in y_layers(nx)[0]:
                if field == current:
                    start = pick(is_low(link), 0, ny - rows)
                    edge[pl.ds(zero + offset, rows), :] = own[field, a, pl.ds(start, rows), :]
    for k, (side, edge) in enumerate(zip(SIDES, x_edges)):
        a = nx - 3 if side < 0 else 2
        offset = len(x_layers()) * ny
        padded[k] = jnp.zeros_like(padded[k])
        padded[k, pl.ds(TOP, ny), :] = own[YV, a]
        spread = own[XV, a + 1] - own[XV, a - 1]
        spread += padded[k, pl.ds(zero + (TOP + 1), ny), :] - padded[k, pl.ds(zero + (TOP - 1), ny), :]
        spread += up(own[ZV, a]) - down(own[ZV, a])
        edge[pl.ds(zero + offset, ny), :] = own[DENSITY, a] * per_mass(own[ENERGY, a], spread)
        offset += ny
        padded[k, pl.ds(TOP, ny), :] = spread
        for row in (0, ny - 1):
            for value in (own[DENSITY, a, pl.ds(row, 1), :], own[ENERGY, a, pl.ds(row, 1), :],
                          padded[k, pl.ds(TOP + row, 1), :], own[YV, a, pl.ds(row, 1), :]):
                edge[pl.ds(zero + offset, 1), :] = value
                offset += 1


def corner_kernel(ny, *refs):
    x_edges, outs = refs[:2], refs[2:]
    zero = hidden_zero()
    columns, singles, rows_of_corner = corner_layers()
    for link, out in zip(LINKS, outs):
        low = is_low(link)
        for k, edge in enumerate(x_edges):
            base = zero + k * rows_of_corner
            for number, _, _, rows, offset in columns:
                out[pl.ds(base + offset, rows), :] = edge[pl.ds(number * ny + pick(low, 0, ny - rows), rows), :]
            number = len(x_layers())
            out[pl.ds(base + singles, 1), :] = edge[pl.ds(number * ny + pick(low, 1, ny - 2), 1), :]
            first = (number + 1) * ny + pick(low, 0, EDGE_KINDS)
            out[pl.ds(base + (singles + 1), EDGE_KINDS), :] = edge[pl.ds(first, EDGE_KINDS), :]


def limited(above, below):
    return jnp.minimum(jnp.maximum(above, jnp.minimum(below, 0.0)), jnp.maximum(below, 0.0))


def face_factors(v_minus, v, half_increment):
    courant = half_increment * (v_minus + v)
    size = jnp.abs(courant)
    return courant, 0.5 * size * (1.0 - size), courant > 0.0


def face_flux(factors, f_minus, f, s_minus, s):
    courant, slope_factor, upward = factors
    return courant * jnp.where(upward, f_minus, f) + slope_factor * jnp.where(upward, s_minus, s)


def up(value):
    return pltpu.roll(value, value.shape[-1] - 1, value.ndim - 1)


def down(value):
    return pltpu.roll(value, 1, value.ndim - 1)


def sweep_x(state, speed, swept, fields, half):
    for part in range(0, state.shape[2], 8):
        rows = pl.ds(part, 8)
        before = [state[field, 1, rows] for field in fields]
        here = [state[field, 2, rows] for field in fields]
        steps = [h - b for h, b in zip(here, before)]
        slopes = [limited(st, b - state[field, 0, rows]) for field, st, b in zip(fields, steps, before)]
        lower = None
        for a in range(swept.shape[1] + 1):
            factors = face_factors(speed[a + 1, rows], speed[a + 2, rows], half)
            fluxes = []
            for k, field in enumerate(fields):
                after = state[field, a + 3, rows]
                step = after - here[k]
                slope = limited(step, steps[k])
                fluxes.append(face_flux(factors, before[k], here[k], slopes[k], slope))
                if lower is not None:
                    swept[field, a - 1, rows] = before[k] - (fluxes[k] - lower[k])
                before[k], here[k], steps[k], slopes[k] = here[k], after, step, slope
            lower = fluxes


def sweep_y(zero, swept, work, a, fields, factors, wide):
    moved = []
    for field in fields:
        below = swept[field, a, pl.ds(zero + 1, wide)]
        here = swept[field, a, pl.ds(zero + 2, wide)]
        slope = limited(here - below, below - swept[field, a, 0:wide])
        work[0, field, a, 0:wide] = slope
        flux = face_flux(factors, below, here, slope, work[0, field, a, pl.ds(zero + 1, wide)])
        work[1, field, a, 0:wide] = flux
        moved.append(here - (work[1, field, a, pl.ds(zero + 1, wide)] - flux))
    return moved


def sweep_z(moved, factors):
    final = []
    for value in moved:
        below = down(value)
        step = value - below
        slope = limited(up(step), step)
        flux = face_flux(factors, below, value, down(slope), slope)
        final.append(value - (up(flux) - flux))
    return final


def step_kernel(nx, ny, dt_ref, *refs):
    own, x_edges, y_edges, corners = refs[0], refs[1:3], refs[3:5], refs[5:7]
    passive, speed, speed_y, speed_z, flows, increment_ref = refs[7:13]
    cells, third, stress, growth, heat, state, energy_one, swept, work = refs[13:]
    nz = own.shape[-1]
    zero = hidden_zero()
    dt = dt_ref[0]
    half = 0.5 * dt
    wide = ny + 4
    tall = ny + 12

    for field in range(5):
        for a in range(nx):
            cells[field, a + LEFT, pl.ds(TOP, ny), :] = own[field, a]
    columns, singles, rows_of_corner = corner_layers()
    for k, (side, edge) in enumerate(zip(SIDES, x_edges)):
        for number, (field, past) in enumerate(x_layers()):
            column = LEFT + (-past if side < 0 else nx - 1 + past)
            cells[field, column, pl.ds(TOP, ny), :] = edge[pl.ds(zero + number * ny, ny), :]
        offset = len(x_layers()) * ny
        third[k, EDGE_KINDS, pl.ds(TOP, ny), :] = edge[pl.ds(zero + offset, ny), :]
        offset += ny
        for row in (0, ny - 1):
            for kind in range(EDGE_KINDS):
                third[k, kind, pl.ds(TOP + row, 1), :] = edge[pl.ds(zero + offset, 1), :]
                offset += 1
    for link, edge, corner in zip(LINKS, y_edges, corners):
        low = is_low(link)
        for field, a, rows, offset in y_layers(nx)[0]:
            to = pl.ds(TOP + pick(low, -rows, ny), rows)
            cells[field, a + LEFT, to, :] = edge[pl.ds(zero + offset, rows), :]
        for k, side in enumerate(SIDES):
            base = zero + k * rows_of_corner
            for _, field, past, rows, offset in columns:
                column = LEFT + (-past if side < 0 else nx - 1 + past)
                to = pl.ds(TOP + pick(low, -rows, ny), rows)
                cells[field, column, to, :] = corner[pl.ds(base + offset, rows), :]
            third[k, EDGE_KINDS, pl.ds(TOP + pick(low, -2, ny + 1), 1), :] = corner[pl.ds(base + singles, 1), :]
            for kind in range(EDGE_KINDS):
                to = pl.ds(TOP + pick(low, -1, ny), 1)
                third[k, kind, to, :] = corner[pl.ds(base + (singles + 1 + kind), 1), :]

    def at(ref, *index, start, count):
        return ref[(*index, pl.ds(zero + start, count), slice(None))]

    row = lax.broadcasted_iota(jnp.int32, (tall, nz), 0) - 4
    for k, a in enumerate((-3, nx + 2)):
        above = at(third, k, 3, start=TOP - 3, count=tall)
        below = at(third, k, 3, start=TOP - 5, count=tall)
        spread = at(third, k, 2, start=TOP - 4, count=tall)
        spread += jnp.where((row == -1) | (row == ny - 1), above, -below)
        density, energy = [at(third, k, kind, start=TOP - 4, count=tall) for kind in range(2)]
        split = (row == -1) | (row == 0) | (row == ny - 1) | (row == ny)
        whole = at(third, k, EDGE_KINDS, start=TOP - 4, count=tall)
        stress[a + 3] = jnp.where(split, density * per_mass(energy, spread), whole)

    for a in range(-2, nx + 2):
        get = functools.partial(at, cells, start=TOP - 4, count=tall)
        z = get(ZV, a + LEFT)
        spread = (
            get(XV, a + LEFT + 1)
            - get(XV, a + LEFT - 1)
            + (at(cells, YV, a + LEFT, start=TOP - 3, count=tall) - at(cells, YV, a + LEFT, start=TOP - 5, count=tall))
            + (up(z) - down(z))
        )
        heat[a + 2] = per_mass(get(ENERGY, a + LEFT), spread)
        stress[a + 3] = get(DENSITY, a + LEFT) * heat[a + 2]
        growth[a + 2] = half * spread

    for a in range(-2, nx + 2):
        get = functools.partial(at, cells, start=TOP - 2, count=wide)
        density = get(DENSITY, a + LEFT)
        grown = at(growth, a + 2, start=2, count=wide)
        centre = at(stress, a + 3, start=2, count=wide)
        scale = half / density
        density_one = density / (1.0 + grown)
        energy = get(ENERGY, a + LEFT) - at(heat, a + 2, start=2, count=wide) * grown
        passive[0, a + 2] = density_one
        passive[1, a + 2] = density_one * energy
        x_one = get(XV, a + LEFT) - scale * (
            at(stress, a + 4, start=2, count=wide) - at(stress, a + 2, start=2, count=wide)
        )
        state[0, a + 2] = x_one
        speed[a + 2] = x_one
        state[1, a + 2] = get(YV, a + LEFT) - scale * (
            at(stress, a + 3, start=3, count=wide) - at(stress, a + 3, start=1, count=wide)
        )
        state[2, a + 2] = get(ZV, a + LEFT) - scale * (up(centre) - down(centre))
        if 0 <= a < nx:
            energy_one[a, 0:wide] = energy

    sweep_x(state, speed, swept, (0, 1, 2), half)
    for a in range(nx):
        speed_y[a, 0:wide] = swept[1, a, 0:wide]

    peak = jnp.zeros((wide, nz), jnp.float32)
    for a in range(nx):
        below, here = at(swept, 1, a, start=1, count=wide), at(swept, 1, a, start=2, count=wide)
        moved = sweep_y(zero, swept, work, a, (0, 1, 2), face_factors(below, here, half), wide)
        speed_z[a] = moved[2]
        final = sweep_z(moved, face_factors(down(moved[2]), moved[2], half))
        for field in range(3):
            flows[field, a] = final[field][:ny]
        peak = jnp.maximum(
            peak,
            jnp.sqrt(0.56 * at(energy_one, a, start=2, count=wide))
            + jnp.abs(final[0])
            + jnp.abs(final[1])
            + jnp.abs(final[2]),
        )
    row = lax.broadcasted_iota(jnp.int32, peak.shape, 0)
    peak = jnp.max(jnp.where(row < ny, peak, 0.0), axis=0, keepdims=True)
    increment_ref[...] = jnp.broadcast_to(0.3 / peak, increment_ref.shape)


def carry_kernel(nx, ny, dt_ref, *refs):
    state, speed, speed_y, speed_z, flows, density_out, energy_out = refs[:7]
    flow_outs, swept, work, written = refs[7:10], refs[10], refs[11], refs[12]
    zero = hidden_zero()
    half = 0.5 * dt_ref[0]
    wide = ny + 4
    copies = [pltpu.make_async_copy(flows.at[k], flow_outs[k], written.at[k]) for k in range(3)]
    for copy in copies:
        copy.start()
    sweep_x(state, speed, swept, (0, 1), half)
    for a in range(nx):
        below, here = speed_y[a, pl.ds(zero + 1, wide)], speed_y[a, pl.ds(zero + 2, wide)]
        moved = sweep_y(zero, swept, work, a, (0, 1), face_factors(below, here, half), wide)
        final = sweep_z(moved, face_factors(down(speed_z[a]), speed_z[a], half))
        density_out[a] = final[0][:ny]
        energy_out[a] = final[1][:ny]
    for copy in copies:
        copy.wait()


def body(density0, energy0, x_velocity, y_velocity, z_velocity, time_increment):
    nx, ny, nz = density0.shape
    fields = (density0, energy0, x_velocity, y_velocity, z_velocity)
    wide, tall = ny + 4, ny + 12

    def array(*shape):
        return jax.ShapeDtypeStruct((*shape, nz), jnp.float32)

    def scratch(*shape):
        return pltpu.VMEM((*shape, nz), jnp.float32)

    def limit(mebibytes):
        return pltpu.CompilerParams(vmem_limit_bytes=mebibytes * 1024 * 1024)

    x_edge, y_edge, corner = array(x_edge_rows(ny)), array(y_layers(nx)[1]), array(2 * corner_layers()[2])
    own, *edges = pl.pallas_call(
        functools.partial(pack_kernel, nx, ny),
        out_shape=[array(5, nx, ny), x_edge, x_edge, y_edge, y_edge],
        in_specs=[HBM] * 5,
        out_specs=[VMEM] * 5,
        scratch_shapes=[scratch(2, ny + 20), pltpu.SemaphoreType.DMA((5,))],
        compiler_params=limit(4),
        name="pack",
    )(*[pltpu.with_memory_space_constraint(field, pltpu.HBM) for field in fields])
    x_edges = [along_x(edge, side) for edge, side in zip(edges[:2], SIDES)]
    y_edges = [along_y(edge, link) for edge, link in zip(edges[2:], LINKS)]
    corners = pl.pallas_call(
        functools.partial(corner_kernel, ny),
        out_shape=[corner] * 2,
        in_specs=[VMEM] * 2,
        out_specs=[VMEM] * 2,
        compiler_params=limit(4),
        name="corners",
    )(*x_edges)
    corners = [along_y(corner, link) for corner, link in zip(corners, LINKS)]
    increment = time_increment.reshape(1)
    passed = [array(2, nx + 4, wide), array(nx + 4, wide), array(nx, wide + 8), array(nx, wide), array(3, nx, ny)]
    *passed, smallest = pl.pallas_call(
        functools.partial(step_kernel, nx, ny),
        out_shape=passed + [array(lax.axis_size(("gx", "gy")))],
        in_specs=[SMEM] + [VMEM] * 7,
        out_specs=[VMEM] * 6,
        scratch_shapes=[
            scratch(5, nx + 6, ny + 20),
            scratch(2, EDGE_KINDS + 1, ny + 20),
            scratch(nx + 6, tall),
            scratch(nx + 4, tall),
            scratch(nx + 4, tall),
            scratch(3, nx + 4, wide),
            scratch(nx, wide + 8),
            scratch(3, nx, wide + 8),
            scratch(2, 3, nx, wide + 8),
        ],
        compiler_params=limit(12),
        name="step",
    )(increment, own, *x_edges, *y_edges, *corners)
    outs = pl.pallas_call(
        functools.partial(carry_kernel, nx, ny),
        out_shape=[array(nx, ny)] * 5,
        in_specs=[SMEM] + [VMEM] * 5,
        out_specs=[VMEM] * 2 + [HBM] * 3,
        scratch_shapes=[
            scratch(2, nx, wide + 8),
            scratch(2, 2, nx, wide + 8),
            pltpu.SemaphoreType.DMA((3,)),
        ],
        compiler_params=limit(8),
        cost_estimate=pl.CostEstimate(flops=10**7, bytes_accessed=4 * 10**6, transcendentals=0),
        name="carry",
    )(increment, *passed)
    return (*outs, jnp.min(lax.all_to_all(smallest, ("gx", "gy"), 0, 0, tiled=True)))


def solution(mesh):
    cells = P("gx", "gy", None)
    return jax.shard_map(
        body,
        mesh=mesh,
        in_specs=(cells,) * 5 + (P(),),
        out_specs=(cells,) * 5 + (P(),),
        check_vma=False,
    )
```

```python
import functools

import jax
import jax.numpy as jnp
from jax import lax
from jax.experimental import pallas as pl
from jax.experimental.pallas import tpu as pltpu
from jax.sharding import PartitionSpec as P

DENSITY, ENERGY, XV, YV, ZV = range(5)
TOP = 8
LEFT = 3
SIDES = (-1, 1)
NEAR, FAR = "near", "far"
LINKS = (FAR, NEAR)
EDGE_KINDS = 4
VMEM = pl.BlockSpec(memory_space=pltpu.VMEM)
HBM = pl.BlockSpec(memory_space=pltpu.HBM)
SMEM = pl.BlockSpec(memory_space=pltpu.SMEM)


def ghost_rows(field):
    return 4 if field == YV else 3


def x_layers():
    return [(field, past) for field in range(5) for past in (1, 2)] + [(XV, 3)]


def x_edge_rows(ny):
    return (len(x_layers()) + 1) * ny + 2 * EDGE_KINDS


def y_layers(nx):
    found, offset = [], 0
    for a in range(nx):
        for field in range(5):
            found.append((field, a, ghost_rows(field), offset))
            offset += ghost_rows(field)
    return found, -(-offset // 8) * 8


def corner_layers():
    found, offset = [], 0
    for number, (field, past) in enumerate(x_layers()):
        found.append((number, field, past, ghost_rows(field), offset))
        offset += ghost_rows(field)
    return found, offset, -(-(offset + 1 + EDGE_KINDS) // 8) * 8


def is_low(link):
    odd = lax.rem(lax.axis_index("gy"), 2)
    return odd if link == NEAR else 1 - odd


def pick(flag, one, other):
    return flag * one + (1 - flag) * other


def along_x(value, side):
    count = lax.axis_size("gx")
    return lax.ppermute(value, "gx", [((i + side) % count, i) for i in range(count)])


def along_y(value, link):
    count = lax.axis_size("gy")
    partners = [i ^ 1 if link == NEAR else (((i - 1) ^ 1) + 1) % count for i in range(count)]
    return lax.ppermute(value, "gy", list(enumerate(partners)))


def hidden_zero():
    return lax.shift_right_logical(lax.axis_index("gx"), 20)


def per_mass(energy, spread):
    return 0.4 * energy + 0.5 * jnp.square(jnp.minimum(0.5 * spread, 0.0))


def pack_kernel(nx, ny, *refs):
    fields, own, x_edges, y_edges, padded, arrived = refs[:5], refs[5], refs[6:8], refs[8:10], refs[10], refs[11]
    zero = hidden_zero()
    copies = [pltpu.make_async_copy(fields[field], own.at[field], arrived.at[field]) for field in range(5)]
    for copy in copies:
        copy.start()
    for current, copy in enumerate(copies):
        copy.wait()
        for side, edge in zip(SIDES, x_edges):
            for number, (field, past) in enumerate(x_layers()):
                if field == current:
                    column = nx - past if side < 0 else past - 1
                    edge[pl.ds(zero + number * ny, ny), :] = own[field, column]
        for link, edge in zip(LINKS, y_edges):
            for field, a, rows, offset in y_layers(nx)[0]:
                if field == current:
                    start = pick(is_low(link), 0, ny - rows)
                    edge[pl.ds(zero + offset, rows), :] = own[field, a, pl.ds(start, rows), :]
    for k, (side, edge) in enumerate(zip(SIDES, x_edges)):
        a = nx - 3 if side < 0 else 2
        offset = len(x_layers()) * ny
        padded[k] = jnp.zeros_like(padded[k])
        padded[k, pl.ds(TOP, ny), :] = own[YV, a]
        spread = own[XV, a + 1] - own[XV, a - 1]
        spread += padded[k, pl.ds(zero + (TOP + 1), ny), :] - padded[k, pl.ds(zero + (TOP - 1), ny), :]
        spread += up(own[ZV, a]) - down(own[ZV, a])
        edge[pl.ds(zero + offset, ny), :] = own[DENSITY, a] * per_mass(own[ENERGY, a], spread)
        offset += ny
        padded[k, pl.ds(TOP, ny), :] = spread
        for row in (0, ny - 1):
            for value in (own[DENSITY, a, pl.ds(row, 1), :], own[ENERGY, a, pl.ds(row, 1), :],
                          padded[k, pl.ds(TOP + row, 1), :], own[YV, a, pl.ds(row, 1), :]):
                edge[pl.ds(zero + offset, 1), :] = value
                offset += 1


def corner_kernel(ny, *refs):
    x_edges, outs = refs[:2], refs[2:]
    zero = hidden_zero()
    columns, singles, rows_of_corner = corner_layers()
    for link, out in zip(LINKS, outs):
        low = is_low(link)
        for k, edge in enumerate(x_edges):
            base = zero + k * rows_of_corner
            for number, _, _, rows, offset in columns:
                out[pl.ds(base + offset, rows), :] = edge[pl.ds(number * ny + pick(low, 0, ny - rows), rows), :]
            number = len(x_layers())
            out[pl.ds(base + singles, 1), :] = edge[pl.ds(number * ny + pick(low, 1, ny - 2), 1), :]
            first = (number + 1) * ny + pick(low, 0, EDGE_KINDS)
            out[pl.ds(base + (singles + 1), EDGE_KINDS), :] = edge[pl.ds(first, EDGE_KINDS), :]


def limited(above, below):
    return jnp.minimum(jnp.maximum(above, jnp.minimum(below, 0.0)), jnp.maximum(below, 0.0))


def face_factors(v_minus, v, half_increment):
    courant = half_increment * (v_minus + v)
    size = jnp.abs(courant)
    return courant, 0.5 * size * (1.0 - size), courant > 0.0


def face_flux(factors, f_minus, f, s_minus, s):
    courant, slope_factor, upward = factors
    return courant * jnp.where(upward, f_minus, f) + slope_factor * jnp.where(upward, s_minus, s)


def up(value):
    return pltpu.roll(value, value.shape[-1] - 1, value.ndim - 1)


def down(value):
    return pltpu.roll(value, 1, value.ndim - 1)


def sweep_x(state, speed, swept, fields, half):
    for part in range(0, state.shape[2], 8):
        rows = pl.ds(part, 8)
        before = [state[field, 1, rows] for field in fields]
        here = [state[field, 2, rows] for field in fields]
        steps = [h - b for h, b in zip(here, before)]
        slopes = [limited(st, b - state[field, 0, rows]) for field, st, b in zip(fields, steps, before)]
        lower = None
        for a in range(swept.shape[1] + 1):
            factors = face_factors(speed[a + 1, rows], speed[a + 2, rows], half)
            fluxes = []
            for k, field in enumerate(fields):
                after = state[field, a + 3, rows]
                step = after - here[k]
                slope = limited(step, steps[k])
                fluxes.append(face_flux(factors, before[k], here[k], slopes[k], slope))
                if lower is not None:
                    swept[field, a - 1, rows] = before[k] - (fluxes[k] - lower[k])
                before[k], here[k], steps[k], slopes[k] = here[k], after, step, slope
            lower = fluxes


def sweep_y(zero, swept, work, a, fields, factors, wide):
    moved = []
    for field in fields:
        below = swept[field, a, pl.ds(zero + 1, wide)]
        here = swept[field, a, pl.ds(zero + 2, wide)]
        slope = limited(here - below, below - swept[field, a, 0:wide])
        work[0, field, a, 0:wide] = slope
        flux = face_flux(factors, below, here, slope, work[0, field, a, pl.ds(zero + 1, wide)])
        work[1, field, a, 0:wide] = flux
        moved.append(here - (work[1, field, a, pl.ds(zero + 1, wide)] - flux))
    return moved


def sweep_z(moved, factors):
    final = []
    for value in moved:
        below = down(value)
        step = value - below
        slope = limited(up(step), step)
        flux = face_flux(factors, below, value, down(slope), slope)
        final.append(value - (up(flux) - flux))
    return final


def step_kernel(nx, ny, dt_ref, *refs):
    own, x_edges, y_edges, corners = refs[0], refs[1:3], refs[3:5], refs[5:7]
    passive, speed, speed_y, speed_z, flows, increment_ref = refs[7:13]
    cells, third, stress, growth, heat, state, energy_one, swept, work = refs[13:]
    nz = own.shape[-1]
    zero = hidden_zero()
    dt = dt_ref[0]
    half = 0.5 * dt
    wide = ny + 4
    tall = ny + 12

    for field in range(5):
        for a in range(nx):
            cells[field, a + LEFT, pl.ds(TOP, ny), :] = own[field, a]
    columns, singles, rows_of_corner = corner_layers()
    for k, (side, edge) in enumerate(zip(SIDES, x_edges)):
        for number, (field, past) in enumerate(x_layers()):
            column = LEFT + (-past if side < 0 else nx - 1 + past)
            cells[field, column, pl.ds(TOP, ny), :] = edge[pl.ds(zero + number * ny, ny), :]
        offset = len(x_layers()) * ny
        third[k, EDGE_KINDS, pl.ds(TOP, ny), :] = edge[pl.ds(zero + offset, ny), :]
        offset += ny
        for row in (0, ny - 1):
            for kind in range(EDGE_KINDS):
                third[k, kind, pl.ds(TOP + row, 1), :] = edge[pl.ds(zero + offset, 1), :]
                offset += 1
    for link, edge, corner in zip(LINKS, y_edges, corners):
        low = is_low(link)
        for field, a, rows, offset in y_layers(nx)[0]:
            to = pl.ds(TOP + pick(low, -rows, ny), rows)
            cells[field, a + LEFT, to, :] = edge[pl.ds(zero + offset, rows), :]
        for k, side in enumerate(SIDES):
            base = zero + k * rows_of_corner
            for _, field, past, rows, offset in columns:
                column = LEFT + (-past if side < 0 else nx - 1 + past)
                to = pl.ds(TOP + pick(low, -rows, ny), rows)
                cells[field, column, to, :] = corner[pl.ds(base + offset, rows), :]
            third[k, EDGE_KINDS, pl.ds(TOP + pick(low, -2, ny + 1), 1), :] = corner[pl.ds(base + singles, 1), :]
            for kind in range(EDGE_KINDS):
                to = pl.ds(TOP + pick(low, -1, ny), 1)
                third[k, kind, to, :] = corner[pl.ds(base + (singles + 1 + kind), 1), :]

    def at(ref, *index, start, count):
        return ref[(*index, pl.ds(zero + start, count), slice(None))]

    row = lax.broadcasted_iota(jnp.int32, (tall, nz), 0) - 4
    for k, a in enumerate((-3, nx + 2)):
        above = at(third, k, 3, start=TOP - 3, count=tall)
        below = at(third, k, 3, start=TOP - 5, count=tall)
        spread = at(third, k, 2, start=TOP - 4, count=tall)
        spread += jnp.where((row == -1) | (row == ny - 1), above, -below)
        density, energy = [at(third, k, kind, start=TOP - 4, count=tall) for kind in range(2)]
        split = (row == -1) | (row == 0) | (row == ny - 1) | (row == ny)
        whole = at(third, k, EDGE_KINDS, start=TOP - 4, count=tall)
        stress[a + 3] = jnp.where(split, density * per_mass(energy, spread), whole)

    for a in range(-2, nx + 2):
        get = functools.partial(at, cells, start=TOP - 4, count=tall)
        z = get(ZV, a + LEFT)
        spread = (
            get(XV, a + LEFT + 1)
            - get(XV, a + LEFT - 1)
            + (at(cells, YV, a + LEFT, start=TOP - 3, count=tall) - at(cells, YV, a + LEFT, start=TOP - 5, count=tall))
            + (up(z) - down(z))
        )
        heat[a + 2] = per_mass(get(ENERGY, a + LEFT), spread)
        stress[a + 3] = get(DENSITY, a + LEFT) * heat[a + 2]
        growth[a + 2] = half * spread

    for a in range(-2, nx + 2):
        get = functools.partial(at, cells, start=TOP - 2, count=wide)
        density = get(DENSITY, a + LEFT)
        grown = at(growth, a + 2, start=2, count=wide)
        centre = at(stress, a + 3, start=2, count=wide)
        scale = half / density
        density_one = density / (1.0 + grown)
        energy = get(ENERGY, a + LEFT) - at(heat, a + 2, start=2, count=wide) * grown
        passive[0, a + 2] = density_one
        passive[1, a + 2] = density_one * energy
        x_one = get(XV, a + LEFT) - scale * (
            at(stress, a + 4, start=2, count=wide) - at(stress, a + 2, start=2, count=wide)
        )
        state[0, a + 2] = x_one
        speed[a + 2] = x_one
        state[1, a + 2] = get(YV, a + LEFT) - scale * (
            at(stress, a + 3, start=3, count=wide) - at(stress, a + 3, start=1, count=wide)
        )
        state[2, a + 2] = get(ZV, a + LEFT) - scale * (up(centre) - down(centre))
        if 0 <= a < nx:
            energy_one[a, 0:wide] = energy

    sweep_x(state, speed, swept, (0, 1, 2), half)
    for a in range(nx):
        speed_y[a, 0:wide] = swept[1, a, 0:wide]

    peak = jnp.zeros((wide, nz), jnp.float32)
    for a in range(nx):
        below, here = at(swept, 1, a, start=1, count=wide), at(swept, 1, a, start=2, count=wide)
        moved = sweep_y(zero, swept, work, a, (0, 1, 2), face_factors(below, here, half), wide)
        speed_z[a] = moved[2]
        final = sweep_z(moved, face_factors(down(moved[2]), moved[2], half))
        for field in range(3):
            flows[field, a] = final[field][:ny]
        peak = jnp.maximum(
            peak,
            jnp.sqrt(0.56 * at(energy_one, a, start=2, count=wide))
            + jnp.abs(final[0])
            + jnp.abs(final[1])
            + jnp.abs(final[2]),
        )
    row = lax.broadcasted_iota(jnp.int32, peak.shape, 0)
    peak = jnp.max(jnp.where(row < ny, peak, 0.0), axis=0, keepdims=True)
    increment_ref[...] = jnp.broadcast_to(0.3 / peak, increment_ref.shape)


def carry_kernel(nx, ny, dt_ref, *refs):
    state, speed, speed_y, speed_z, flows, density_out, energy_out = refs[:7]
    flow_outs, swept, work, written = refs[7:10], refs[10], refs[11], refs[12]
    zero = hidden_zero()
    half = 0.5 * dt_ref[0]
    wide = ny + 4
    copies = [pltpu.make_async_copy(flows.at[k], flow_outs[k], written.at[k]) for k in range(3)]
    for copy in copies:
        copy.start()
    sweep_x(state, speed, swept, (0, 1), half)
    for a in range(nx):
        below, here = speed_y[a, pl.ds(zero + 1, wide)], speed_y[a, pl.ds(zero + 2, wide)]
        moved = sweep_y(zero, swept, work, a, (0, 1), face_factors(below, here, half), wide)
        final = sweep_z(moved, face_factors(down(speed_z[a]), speed_z[a], half))
        density_out[a] = final[0][:ny]
        energy_out[a] = final[1][:ny]
    for copy in copies:
        copy.wait()


def body(density0, energy0, x_velocity, y_velocity, z_velocity, time_increment):
    nx, ny, nz = density0.shape
    fields = (density0, energy0, x_velocity, y_velocity, z_velocity)
    wide, tall = ny + 4, ny + 12

    def array(*shape):
        return jax.ShapeDtypeStruct((*shape, nz), jnp.float32)

    def scratch(*shape):
        return pltpu.VMEM((*shape, nz), jnp.float32)

    def limit(mebibytes):
        return pltpu.CompilerParams(vmem_limit_bytes=mebibytes * 1024 * 1024)

    x_edge, y_edge, corner = array(x_edge_rows(ny)), array(y_layers(nx)[1]), array(2 * corner_layers()[2])
    own, *edges = pl.pallas_call(
        functools.partial(pack_kernel, nx, ny),
        out_shape=[array(5, nx, ny), x_edge, x_edge, y_edge, y_edge],
        in_specs=[HBM] * 5,
        out_specs=[VMEM] * 5,
        scratch_shapes=[scratch(2, ny + 20), pltpu.SemaphoreType.DMA((5,))],
        compiler_params=limit(4),
        name="pack",
    )(*[pltpu.with_memory_space_constraint(field, pltpu.HBM) for field in fields])
    x_edges = [along_x(edge, side) for edge, side in zip(edges[:2], SIDES)]
    y_edges = [along_y(edge, link) for edge, link in zip(edges[2:], LINKS)]
    corners = pl.pallas_call(
        functools.partial(corner_kernel, ny),
        out_shape=[corner] * 2,
        in_specs=[VMEM] * 2,
        out_specs=[VMEM] * 2,
        compiler_params=limit(4),
        name="corners",
    )(*x_edges)
    corners = [along_y(corner, link) for corner, link in zip(corners, LINKS)]
    increment = time_increment.reshape(1)
    passed = [array(2, nx + 4, wide), array(nx + 4, wide), array(nx, wide + 8), array(nx, wide), array(3, nx, ny)]
    *passed, smallest = pl.pallas_call(
        functools.partial(step_kernel, nx, ny),
        out_shape=passed + [array(8)],
        in_specs=[SMEM] + [VMEM] * 7,
        out_specs=[VMEM] * 6,
        scratch_shapes=[
            scratch(5, nx + 6, ny + 20),
            scratch(2, EDGE_KINDS + 1, ny + 20),
            scratch(nx + 6, tall),
            scratch(nx + 4, tall),
            scratch(nx + 4, tall),
            scratch(3, nx + 4, wide),
            scratch(nx, wide + 8),
            scratch(3, nx, wide + 8),
            scratch(2, 3, nx, wide + 8),
        ],
        compiler_params=limit(12),
        name="step",
    )(increment, own, *x_edges, *y_edges, *corners)
    outs = pl.pallas_call(
        functools.partial(carry_kernel, nx, ny),
        out_shape=[array(nx, ny)] * 5,
        in_specs=[SMEM] + [VMEM] * 5,
        out_specs=[VMEM] * 2 + [HBM] * 3,
        scratch_shapes=[
            scratch(2, nx, wide + 8),
            scratch(2, 2, nx, wide + 8),
            pltpu.SemaphoreType.DMA((3,)),
        ],
        compiler_params=limit(8),
        cost_estimate=pl.CostEstimate(flops=10**7, bytes_accessed=4 * 10**6, transcendentals=0),
        name="carry",
    )(increment, *passed)
    return (*outs, jnp.min(lax.all_gather(smallest, ("gx", "gy"), tiled=True)))


def solution(mesh):
    cells = P("gx", "gy", None)
    return jax.shard_map(
        body,
        mesh=mesh,
        in_specs=(cells,) * 5 + (P(),),
        out_specs=(cells,) * 5 + (P(),),
        check_vma=False,
    )
```

```python
import functools

import jax
import jax.numpy as jnp
from jax import lax
from jax.experimental import pallas as pl
from jax.experimental.pallas import tpu as pltpu
from jax.sharding import PartitionSpec as P

DENSITY, ENERGY, XV, YV, ZV = range(5)
TOP = 8
LEFT = 3
SIDES = (-1, 1)
NEAR, FAR = "near", "far"
LINKS = (FAR, NEAR)
EDGE_KINDS = 4
VMEM = pl.BlockSpec(memory_space=pltpu.VMEM)
HBM = pl.BlockSpec(memory_space=pltpu.HBM)
SMEM = pl.BlockSpec(memory_space=pltpu.SMEM)


def ghost_rows(field):
    return 4 if field == YV else 3


def x_layers():
    return [(field, past) for field in range(5) for past in (1, 2)] + [(XV, 3)]


def x_edge_rows(ny):
    return (len(x_layers()) + 1) * ny + 2 * EDGE_KINDS


def y_layers(nx):
    found, offset = [], 0
    for a in range(nx):
        for field in range(5):
            found.append((field, a, ghost_rows(field), offset))
            offset += ghost_rows(field)
    return found, -(-offset // 8) * 8


def corner_layers():
    found, offset = [], 0
    for number, (field, past) in enumerate(x_layers()):
        found.append((number, field, past, ghost_rows(field), offset))
        offset += ghost_rows(field)
    return found, offset, -(-(offset + 1 + EDGE_KINDS) // 8) * 8


def is_low(link):
    odd = lax.rem(lax.axis_index("gy"), 2)
    return odd if link == NEAR else 1 - odd


def pick(flag, one, other):
    return flag * one + (1 - flag) * other


def along_x(value, side):
    count = lax.axis_size("gx")
    return lax.ppermute(value, "gx", [((i + side) % count, i) for i in range(count)])


def along_y(value, link):
    count = lax.axis_size("gy")
    partners = [i ^ 1 if link == NEAR else (((i - 1) ^ 1) + 1) % count for i in range(count)]
    return lax.ppermute(value, "gy", list(enumerate(partners)))


def hidden_zero():
    return lax.shift_right_logical(lax.axis_index("gx"), 20)


def per_mass(energy, spread):
    return 0.4 * energy + 0.5 * jnp.square(jnp.minimum(0.5 * spread, 0.0))


def pack_kernel(nx, ny, *refs):
    fields, own, x_edges, y_edges, padded, arrived = refs[:5], refs[5], refs[6:8], refs[8:10], refs[10], refs[11]
    zero = hidden_zero()
    copies = [pltpu.make_async_copy(fields[field], own.at[field], arrived.at[field]) for field in range(5)]
    for copy in copies:
        copy.start()
    for current, copy in enumerate(copies):
        copy.wait()
        for side, edge in zip(SIDES, x_edges):
            for number, (field, past) in enumerate(x_layers()):
                if field == current:
                    column = nx - past if side < 0 else past - 1
                    edge[pl.ds(zero + number * ny, ny), :] = own[field, column]
        for link, edge in zip(LINKS, y_edges):
            for field, a, rows, offset in y_layers(nx)[0]:
                if field == current:
                    start = pick(is_low(link), 0, ny - rows)
                    edge[pl.ds(zero + offset, rows), :] = own[field, a, pl.ds(start, rows), :]
    for k, (side, edge) in enumerate(zip(SIDES, x_edges)):
        a = nx - 3 if side < 0 else 2
        offset = len(x_layers()) * ny
        padded[k] = jnp.zeros_like(padded[k])
        padded[k, pl.ds(TOP, ny), :] = own[YV, a]
        spread = own[XV, a + 1] - own[XV, a - 1]
        spread += padded[k, pl.ds(zero + (TOP + 1), ny), :] - padded[k, pl.ds(zero + (TOP - 1), ny), :]
        spread += up(own[ZV, a]) - down(own[ZV, a])
        edge[pl.ds(zero + offset, ny), :] = own[DENSITY, a] * per_mass(own[ENERGY, a], spread)
        offset += ny
        padded[k, pl.ds(TOP, ny), :] = spread
        for row in (0, ny - 1):
            for value in (own[DENSITY, a, pl.ds(row, 1), :], own[ENERGY, a, pl.ds(row, 1), :],
                          padded[k, pl.ds(TOP + row, 1), :], own[YV, a, pl.ds(row, 1), :]):
                edge[pl.ds(zero + offset, 1), :] = value
                offset += 1


def corner_kernel(ny, *refs):
    x_edges, outs = refs[:2], refs[2:]
    zero = hidden_zero()
    columns, singles, rows_of_corner = corner_layers()
    for link, out in zip(LINKS, outs):
        low = is_low(link)
        for k, edge in enumerate(x_edges):
            base = zero + k * rows_of_corner
            for number, _, _, rows, offset in columns:
                out[pl.ds(base + offset, rows), :] = edge[pl.ds(number * ny + pick(low, 0, ny - rows), rows), :]
            number = len(x_layers())
            out[pl.ds(base + singles, 1), :] = edge[pl.ds(number * ny + pick(low, 1, ny - 2), 1), :]
            first = (number + 1) * ny + pick(low, 0, EDGE_KINDS)
            out[pl.ds(base + (singles + 1), EDGE_KINDS), :] = edge[pl.ds(first, EDGE_KINDS), :]


def limited(above, below):
    return jnp.minimum(jnp.maximum(above, jnp.minimum(below, 0.0)), jnp.maximum(below, 0.0))


def face_factors(v_minus, v, half_increment):
    courant = half_increment * (v_minus + v)
    size = jnp.abs(courant)
    return courant, 0.5 * size * (1.0 - size), courant > 0.0


def face_flux(factors, f_minus, f, s_minus, s):
    courant, slope_factor, upward = factors
    return courant * jnp.where(upward, f_minus, f) + slope_factor * jnp.where(upward, s_minus, s)


def up(value):
    return pltpu.roll(value, value.shape[-1] - 1, value.ndim - 1)


def down(value):
    return pltpu.roll(value, 1, value.ndim - 1)


def place(pieces, a):
    for ref, first, last, number in pieces:
        if first <= a < last:
            return ref, a - first + number
    raise ValueError(a)


def read(zero, pieces, a, start, count, *field):
    ref, number = place(pieces, a)
    return ref[(*field, number, pl.ds(zero + start, count), slice(None))]


def write(pieces, a, value, *field):
    ref, number = place(pieces, a)
    ref[(*field, number, pl.ds(0, value.shape[0]), slice(None))] = value


def sweep_x(state, speed, swept, fields, first, last, wide, half):
    for part in range(0, wide, 8):
        before = [state(field, first - 1, part) for field in fields]
        here = [state(field, first, part) for field in fields]
        steps = [h - b for h, b in zip(here, before)]
        slopes = [limited(st, b - state(field, first - 2, part)) for field, st, b in zip(fields, steps, before)]
        lower = None
        for a in range(first, last + 1):
            factors = face_factors(speed(a - 1, part), speed(a, part), half)
            fluxes = []
            for k, field in enumerate(fields):
                after = state(field, a + 1, part)
                step = after - here[k]
                slope = limited(step, steps[k])
                fluxes.append(face_flux(factors, before[k], here[k], slopes[k], slope))
                if lower is not None:
                    swept[field, a - 1 - first, pl.ds(part, 8)] = before[k] - (fluxes[k] - lower[k])
                before[k], here[k], steps[k], slopes[k] = here[k], after, step, slope
            lower = fluxes


def sweep_y(zero, swept, work, number, fields, factors, wide):
    moved = []
    for field in fields:
        below = swept[field, number, pl.ds(zero + 1, wide)]
        here = swept[field, number, pl.ds(zero + 2, wide)]
        slope = limited(here - below, below - swept[field, number, 0:wide])
        work[0, field, number, 0:wide] = slope
        flux = face_flux(factors, below, here, slope, work[0, field, number, pl.ds(zero + 1, wide)])
        work[1, field, number, 0:wide] = flux
        moved.append(here - (work[1, field, number, pl.ds(zero + 1, wide)] - flux))
    return moved


def sweep_z(moved, factors):
    final = []
    for value in moved:
        below = down(value)
        step = value - below
        slope = limited(up(step), step)
        flux = face_flux(factors, below, value, down(slope), slope)
        final.append(value - (up(flux) - flux))
    return final


def spread_columns(zero, columns, tall, half, cells, stress, heat, growth):
    for a in columns:
        z = read(zero, cells, a, TOP - 4, tall, ZV)
        spread = (
            read(zero, cells, a + 1, TOP - 4, tall, XV)
            - read(zero, cells, a - 1, TOP - 4, tall, XV)
            + (read(zero, cells, a, TOP - 3, tall, YV) - read(zero, cells, a, TOP - 5, tall, YV))
            + (up(z) - down(z))
        )
        warmth = per_mass(read(zero, cells, a, TOP - 4, tall, ENERGY), spread)
        write(heat, a, warmth)
        write(stress, a, read(zero, cells, a, TOP - 4, tall, DENSITY) * warmth)
        write(growth, a, half * spread)


def advance_columns(zero, columns, wide, half, cells, stress, heat, growth, passive, state, energies, nx):
    for a in columns:
        density, energy, x, y, z = [read(zero, cells, a, TOP - 2, wide, field) for field in range(5)]
        grown = read(zero, growth, a, 2, wide)
        centre = read(zero, stress, a, 2, wide)
        scale = half / density
        density_one = density / (1.0 + grown)
        energy = energy - read(zero, heat, a, 2, wide) * grown
        write(passive, a, density_one, 0)
        write(passive, a, density_one * energy, 1)
        write(state, a, x - scale * (read(zero, stress, a + 1, 2, wide) - read(zero, stress, a - 1, 2, wide)), 0)
        write(state, a, y - scale * (read(zero, stress, a, 3, wide) - read(zero, stress, a, 1, wide)), 1)
        write(state, a, z - scale * (up(centre) - down(centre)), 2)
        if 0 <= a < nx:
            write(energies, a, energy)


def flow_columns(zero, first, last, ny, half, state, energies, swept, work, speed_y, speed_z, flows):
    wide = ny + 4
    sweep_x(
        lambda field, a, part: read(zero, state, a, part, 8, field),
        lambda a, part: read(zero, state, a, part, 8, 0),
        swept, (0, 1, 2), first, last, wide, half,
    )
    peak = None
    for a in range(first, last):
        number = a - first
        write(speed_y, a, swept[1, number, 0:wide])
        below, here = [swept[1, number, pl.ds(zero + start, wide)] for start in (1, 2)]
        moved = sweep_y(zero, swept, work, number, (0, 1, 2), face_factors(below, here, half), wide)
        write(speed_z, a, moved[2])
        final = sweep_z(moved, face_factors(down(moved[2]), moved[2], half))
        for field in range(3):
            write(flows, a, final[field][:ny], field)
        signal = (
            jnp.sqrt(0.56 * read(zero, energies, a, 2, wide))
            + jnp.abs(final[0])
            + jnp.abs(final[1])
            + jnp.abs(final[2])
        )
        peak = signal if peak is None else jnp.maximum(peak, signal)
    return peak


def inner_kernel(nx, ny, dt_ref, *refs):
    own, y_edges = refs[0], refs[1:3]
    cells, stress, state, passive, energies, speed_y, speed_z, flows, peak_ref = refs[3:12]
    heat, growth, swept, work = refs[12:]
    zero = hidden_zero()
    half = 0.5 * dt_ref[0]
    for field in range(5):
        for a in range(nx):
            cells[field, a, pl.ds(TOP, ny), :] = own[field, a]
    for link, edge in zip(LINKS, y_edges):
        low = is_low(link)
        for field, a, rows, offset in y_layers(nx)[0]:
            cells[field, a, pl.ds(TOP + pick(low, -rows, ny), rows), :] = edge[pl.ds(zero + offset, rows), :]
    cells = [(cells, 0, nx, 0)]
    stress, heat, growth = [[(ref, 1, nx - 1, 0)] for ref in (stress, heat, growth)]
    state, passive, energies = [[(ref, 2, nx - 2, 0)] for ref in (state, passive, energies)]
    speed_y, speed_z, flows = [[(ref, 4, nx - 4, 0)] for ref in (speed_y, speed_z, flows)]
    spread_columns(zero, range(1, nx - 1), ny + 12, half, cells, stress, heat, growth)
    advance_columns(
        zero, range(2, nx - 2), ny + 4, half, cells, stress, heat, growth, passive, state, energies, nx
    )
    peak_ref[...] = flow_columns(
        zero, 4, nx - 4, ny, half, state, energies, swept, work, speed_y, speed_z, flows
    )


def outer_pieces(ref, nx, reach, inside):
    return [(ref, -reach, inside, 0), (ref, nx - inside, nx + reach, reach + inside)]


def outer_kernel(nx, ny, dt_ref, *refs):
    x_edges, corners = refs[0:2], refs[2:4]
    cells_in, stress_in, state_in, energies_in, peak_in = refs[4:9]
    state_out, passive_out, speed_y, speed_z, flows, increment_ref = refs[9:15]
    beyond, third, stress_out, heat, growth, energies_out, swept, work = refs[15:]
    nz = increment_ref.shape[-1]
    zero = hidden_zero()
    half = 0.5 * dt_ref[0]
    wide, tall = ny + 4, ny + 12

    columns, singles, rows_of_corner = corner_layers()
    for k, (side, edge) in enumerate(zip(SIDES, x_edges)):
        for number, (field, past) in enumerate(x_layers()):
            column = LEFT - past if side < 0 else LEFT - 1 + past
            beyond[field, column, pl.ds(TOP, ny), :] = edge[pl.ds(zero + number * ny, ny), :]
        offset = len(x_layers()) * ny
        third[k, EDGE_KINDS, pl.ds(TOP, ny), :] = edge[pl.ds(zero + offset, ny), :]
        offset += ny
        for row in (0, ny - 1):
            for kind in range(EDGE_KINDS):
                third[k, kind, pl.ds(TOP + row, 1), :] = edge[pl.ds(zero + offset, 1), :]
                offset += 1
    for link, corner in zip(LINKS, corners):
        low = is_low(link)
        for k, side in enumerate(SIDES):
            base = zero + k * rows_of_corner
            for _, field, past, rows, offset in columns:
                column = LEFT - past if side < 0 else LEFT - 1 + past
                to = pl.ds(TOP + pick(low, -rows, ny), rows)
                beyond[field, column, to, :] = corner[pl.ds(base + offset, rows), :]
            third[k, EDGE_KINDS, pl.ds(TOP + pick(low, -2, ny + 1), 1), :] = corner[pl.ds(base + singles, 1), :]
            for kind in range(EDGE_KINDS):
                to = pl.ds(TOP + pick(low, -1, ny), 1)
                third[k, kind, to, :] = corner[pl.ds(base + (singles + 1 + kind), 1), :]

    cells = [(cells_in, 0, nx, 0)] + outer_pieces(beyond, nx, LEFT, 0)
    stress = outer_pieces(stress_out, nx, 3, 2) + [(stress_in, 2, nx - 2, 1)]
    heat, growth = outer_pieces(heat, nx, 2, 2), outer_pieces(growth, nx, 2, 2)
    state = outer_pieces(state_out, nx, 2, 2) + [(state_in, 2, nx - 2, 0)]
    passive = outer_pieces(passive_out, nx, 2, 2)
    energies = outer_pieces(energies_out, nx, 0, 2) + [(energies_in, 2, nx - 2, 0)]
    speed_y, speed_z, flows = [outer_pieces(ref, nx, 0, 4) for ref in (speed_y, speed_z, flows)]

    row = lax.broadcasted_iota(jnp.int32, (tall, nz), 0) - 4
    for k, a in enumerate((-3, nx + 2)):
        above, below = [third[k, 3, pl.ds(zero + start, tall)] for start in (TOP - 3, TOP - 5)]
        density, energy, spread, _, whole = [third[k, kind, pl.ds(zero + TOP - 4, tall)] for kind in range(5)]
        spread += jnp.where((row == -1) | (row == ny - 1), above, -below)
        split = (row == -1) | (row == 0) | (row == ny - 1) | (row == ny)
        write(stress, a, jnp.where(split, density * per_mass(energy, spread), whole))

    ends = (*range(-2, 2), *range(nx - 2, nx + 2))
    spread_columns(zero, ends, tall, half, cells, stress, heat, growth)
    advance_columns(zero, ends, wide, half, cells, stress, heat, growth, passive, state, energies, nx)
    peak = peak_in[...]
    for k, first in enumerate((0, nx - 4)):
        peak = jnp.maximum(
            peak,
            flow_columns(
                zero, first, first + 4, ny, half, state, energies, swept.at[k], work.at[k], speed_y, speed_z, flows
            ),
        )
    peak = jnp.max(jnp.where(row[4 : 4 + wide] < ny, peak, 0.0), axis=0, keepdims=True)
    increment_ref[...] = jnp.broadcast_to(0.3 / peak, increment_ref.shape)


def carry_kernel(nx, ny, dt_ref, *refs):
    state_in, passive_in, speed_y_in, speed_z_in, flows_in = refs[0:5]
    state_out, passive_out, speed_y_out, speed_z_out, flows_out = refs[5:10]
    density_out, energy_out, flow_outs, swept, work, written = refs[10], refs[11], refs[12:15], refs[15], refs[16], refs[17]
    zero = hidden_zero()
    half = 0.5 * dt_ref[0]
    wide = ny + 4
    copies = []
    for k in range(3):
        for piece, (ref, first, last, number) in enumerate([(flows_in, 4, nx - 4, 0)] + outer_pieces(flows_out, nx, 0, 4)):
            source = ref.at[k, pl.ds(number, last - first)]
            copies.append(
                pltpu.make_async_copy(source, flow_outs[k].at[pl.ds(first, last - first)], written.at[k, piece])
            )
    for copy in copies:
        copy.start()
    state = outer_pieces(state_out, nx, 2, 2) + [(state_in, 2, nx - 2, 0)]
    passive = outer_pieces(passive_out, nx, 2, 2) + [(passive_in, 2, nx - 2, 0)]
    speed_y = outer_pieces(speed_y_out, nx, 0, 4) + [(speed_y_in, 4, nx - 4, 0)]
    speed_z = outer_pieces(speed_z_out, nx, 0, 4) + [(speed_z_in, 4, nx - 4, 0)]
    sweep_x(
        lambda field, a, part: read(zero, passive, a, part, 8, field),
        lambda a, part: read(zero, state, a, part, 8, 0),
        swept, (0, 1), 0, nx, wide, half,
    )
    for a in range(nx):
        below, here = [read(zero, speed_y, a, start, wide) for start in (1, 2)]
        moved = sweep_y(zero, swept, work, a, (0, 1), face_factors(below, here, half), wide)
        along = read(zero, speed_z, a, 0, wide)
        final = sweep_z(moved, face_factors(down(along), along, half))
        density_out[a] = final[0][:ny]
        energy_out[a] = final[1][:ny]
    for copy in copies:
        copy.wait()


def body(density0, energy0, x_velocity, y_velocity, z_velocity, time_increment):
    nx, ny, nz = density0.shape
    fields = (density0, energy0, x_velocity, y_velocity, z_velocity)
    wide, tall = ny + 4, ny + 12

    def array(*shape):
        return jax.ShapeDtypeStruct((*shape, nz), jnp.float32)

    def scratch(*shape):
        return pltpu.VMEM((*shape, nz), jnp.float32)

    def limit(mebibytes):
        return pltpu.CompilerParams(vmem_limit_bytes=mebibytes * 1024 * 1024)

    x_edge, y_edge, corner = array(x_edge_rows(ny)), array(y_layers(nx)[1]), array(2 * corner_layers()[2])
    own, *edges = pl.pallas_call(
        functools.partial(pack_kernel, nx, ny),
        out_shape=[array(5, nx, ny), x_edge, x_edge, y_edge, y_edge],
        in_specs=[HBM] * 5,
        out_specs=[VMEM] * 5,
        scratch_shapes=[scratch(2, ny + 20), pltpu.SemaphoreType.DMA((5,))],
        compiler_params=limit(4),
        name="pack",
    )(*[pltpu.with_memory_space_constraint(field, pltpu.HBM) for field in fields])
    x_edges = [along_x(edge, side) for edge, side in zip(edges[:2], SIDES)]
    y_edges = [along_y(edge, link) for edge, link in zip(edges[2:], LINKS)]
    corners = pl.pallas_call(
        functools.partial(corner_kernel, ny),
        out_shape=[corner] * 2,
        in_specs=[VMEM] * 2,
        out_specs=[VMEM] * 2,
        compiler_params=limit(4),
        name="corners",
    )(*x_edges)
    corners = [along_y(corner, link) for corner, link in zip(corners, LINKS)]
    increment = time_increment.reshape(1)
    passed_in = [array(3, nx - 4, wide), array(2, nx - 4, wide), array(nx - 8, wide + 8), array(nx - 8, wide), array(3, nx - 8, ny)]
    passed_out = [array(3, 8, wide), array(2, 8, wide), array(8, wide + 8), array(8, wide), array(3, 8, ny)]
    cells, stress, state_in, passive_in, energies, *rest_in, peak = pl.pallas_call(
        functools.partial(inner_kernel, nx, ny),
        out_shape=[
            array(5, nx, ny + 20),
            array(nx - 2, tall),
            *passed_in[:2],
            array(nx - 4, wide + 8),
            *passed_in[2:],
            array(wide),
        ],
        in_specs=[SMEM] + [VMEM] * 3,
        out_specs=[VMEM] * 9,
        scratch_shapes=[
            scratch(nx - 2, tall),
            scratch(nx - 2, tall),
            scratch(3, nx - 8, wide + 8),
            scratch(2, 3, nx - 8, wide + 8),
        ],
        compiler_params=limit(8),
        cost_estimate=pl.CostEstimate(flops=5 * 10**6, bytes_accessed=2 * 10**6, transcendentals=0),
        name="inner",
    )(increment, own, *y_edges)
    *outer, smallest = pl.pallas_call(
        functools.partial(outer_kernel, nx, ny),
        out_shape=passed_out + [array(lax.axis_size(("gx", "gy")))],
        in_specs=[SMEM] + [VMEM] * 9,
        out_specs=[VMEM] * 6,
        scratch_shapes=[
            scratch(5, 2 * LEFT, ny + 20),
            scratch(2, EDGE_KINDS + 1, ny + 20),
            scratch(10, tall),
            scratch(8, tall),
            scratch(8, tall),
            scratch(4, wide + 8),
            scratch(2, 3, 4, wide + 8),
            scratch(2, 2, 3, 4, wide + 8),
        ],
        compiler_params=limit(8),
        name="outer",
    )(increment, *x_edges, *corners, cells, stress, state_in, energies, peak)
    outs = pl.pallas_call(
        functools.partial(carry_kernel, nx, ny),
        out_shape=[array(nx, ny)] * 5,
        in_specs=[SMEM] + [VMEM] * 10,
        out_specs=[VMEM] * 2 + [HBM] * 3,
        scratch_shapes=[
            scratch(2, nx, wide + 8),
            scratch(2, 2, nx, wide + 8),
            pltpu.SemaphoreType.DMA((3, 3)),
        ],
        compiler_params=limit(8),
        cost_estimate=pl.CostEstimate(flops=10**7, bytes_accessed=4 * 10**6, transcendentals=0),
        name="carry",
    )(increment, state_in, passive_in, *rest_in, *outer)
    return (*outs, jnp.min(lax.all_to_all(smallest, ("gx", "gy"), 0, 0, tiled=True)))


def solution(mesh):
    cells = P("gx", "gy", None)
    return jax.shard_map(
        body,
        mesh=mesh,
        in_specs=(cells,) * 5 + (P(),),
        out_specs=(cells,) * 5 + (P(),),
        check_vma=False,
    )
```

```python
import functools

import jax
import jax.numpy as jnp
from jax import lax
from jax.experimental import pallas as pl
from jax.experimental.pallas import tpu as pltpu
from jax.sharding import PartitionSpec as P

DENSITY, ENERGY, XV, YV, ZV = range(5)
TOP = 8
LEFT = 3
SIDES = (-1, 1)
NEAR, FAR = "near", "far"
LINKS = (FAR, NEAR)
EDGE_KINDS = 4
VMEM = pl.BlockSpec(memory_space=pltpu.VMEM)
HBM = pl.BlockSpec(memory_space=pltpu.HBM)
SMEM = pl.BlockSpec(memory_space=pltpu.SMEM)


def ghost_rows(field):
    return 4 if field == YV else 3


def x_layers():
    return [(field, past) for field in range(5) for past in (1, 2)] + [(XV, 3)]


def x_edge_rows(ny):
    return (len(x_layers()) + 1) * ny + 2 * EDGE_KINDS


def y_layers(nx):
    found, offset = [], 0
    for a in range(nx):
        for field in range(5):
            found.append((field, a, ghost_rows(field), offset))
            offset += ghost_rows(field)
    return found, -(-offset // 8) * 8


def corner_layers():
    found, offset = [], 0
    for number, (field, past) in enumerate(x_layers()):
        found.append((number, field, past, ghost_rows(field), offset))
        offset += ghost_rows(field)
    return found, offset, -(-(offset + 1 + EDGE_KINDS) // 8) * 8


def is_low(link):
    odd = lax.rem(lax.axis_index("gy"), 2)
    return odd if link == NEAR else 1 - odd


def pick(flag, one, other):
    return flag * one + (1 - flag) * other


def along_x(value, side):
    count = lax.axis_size("gx")
    return lax.ppermute(value, "gx", [((i + side) % count, i) for i in range(count)])


def along_y(value, link):
    count = lax.axis_size("gy")
    partners = [i ^ 1 if link == NEAR else (((i - 1) ^ 1) + 1) % count for i in range(count)]
    return lax.ppermute(value, "gy", list(enumerate(partners)))


def hidden_zero():
    return lax.shift_right_logical(lax.axis_index("gx"), 20)


def per_mass(energy, spread):
    return 0.4 * energy + 0.5 * jnp.square(jnp.minimum(0.5 * spread, 0.0))


def x_pack_kernel(nx, ny, *refs):
    fields, x_edges, near, padded, arrived = refs[:5], refs[5:7], refs[7], refs[8], refs[9]
    zero = hidden_zero()
    copies = [
        pltpu.make_async_copy(
            fields[field].at[pl.ds(first, 4)], near.at[field, pl.ds(4 * k, 4)], arrived.at[field, k]
        )
        for field in range(5)
        for k, first in enumerate((nx - 4, 0))
    ]
    for copy in copies:
        copy.start()
    for current in range(5):
        for k, (side, edge) in enumerate(zip(SIDES, x_edges)):
            copies[2 * current + k].wait()
            for number, (field, past) in enumerate(x_layers()):
                if field == current:
                    edge[pl.ds(zero + number * ny, ny), :] = near[field, 4 - past if side < 0 else 3 + past]
    for k, (side, edge) in enumerate(zip(SIDES, x_edges)):
        a = 1 if side < 0 else 6
        offset = len(x_layers()) * ny
        padded[k] = jnp.zeros_like(padded[k])
        padded[k, pl.ds(TOP, ny), :] = near[YV, a]
        spread = near[XV, a + 1] - near[XV, a - 1]
        spread += padded[k, pl.ds(zero + (TOP + 1), ny), :] - padded[k, pl.ds(zero + (TOP - 1), ny), :]
        spread += up(near[ZV, a]) - down(near[ZV, a])
        edge[pl.ds(zero + offset, ny), :] = near[DENSITY, a] * per_mass(near[ENERGY, a], spread)
        offset += ny
        padded[k, pl.ds(TOP, ny), :] = spread
        for row in (0, ny - 1):
            for value in (near[DENSITY, a, pl.ds(row, 1), :], near[ENERGY, a, pl.ds(row, 1), :],
                          padded[k, pl.ds(TOP + row, 1), :], near[YV, a, pl.ds(row, 1), :]):
                edge[pl.ds(zero + offset, 1), :] = value
                offset += 1


def y_pack_kernel(nx, ny, *refs):
    fields, own, y_edges, arrived = refs[:5], refs[5], refs[6:8], refs[8]
    zero = hidden_zero()
    copies = [pltpu.make_async_copy(fields[field], own.at[field], arrived.at[field]) for field in range(5)]
    for copy in copies:
        copy.start()
    for current, copy in enumerate(copies):
        copy.wait()
        for link, edge in zip(LINKS, y_edges):
            for field, a, rows, offset in y_layers(nx)[0]:
                if field == current:
                    start = pick(is_low(link), 0, ny - rows)
                    edge[pl.ds(zero + offset, rows), :] = own[field, a, pl.ds(start, rows), :]


def corner_kernel(ny, *refs):
    x_edges, outs = refs[:2], refs[2:]
    zero = hidden_zero()
    columns, singles, rows_of_corner = corner_layers()
    for link, out in zip(LINKS, outs):
        low = is_low(link)
        for k, edge in enumerate(x_edges):
            base = zero + k * rows_of_corner
            for number, _, _, rows, offset in columns:
                out[pl.ds(base + offset, rows), :] = edge[pl.ds(number * ny + pick(low, 0, ny - rows), rows), :]
            number = len(x_layers())
            out[pl.ds(base + singles, 1), :] = edge[pl.ds(number * ny + pick(low, 1, ny - 2), 1), :]
            first = (number + 1) * ny + pick(low, 0, EDGE_KINDS)
            out[pl.ds(base + (singles + 1), EDGE_KINDS), :] = edge[pl.ds(first, EDGE_KINDS), :]


def limited(above, below):
    return jnp.minimum(jnp.maximum(above, jnp.minimum(below, 0.0)), jnp.maximum(below, 0.0))


def face_factors(v_minus, v, half_increment):
    courant = half_increment * (v_minus + v)
    size = jnp.abs(courant)
    return courant, 0.5 * size * (1.0 - size), courant > 0.0


def face_flux(factors, f_minus, f, s_minus, s):
    courant, slope_factor, upward = factors
    return courant * jnp.where(upward, f_minus, f) + slope_factor * jnp.where(upward, s_minus, s)


def up(value):
    return pltpu.roll(value, value.shape[-1] - 1, value.ndim - 1)


def down(value):
    return pltpu.roll(value, 1, value.ndim - 1)


def place(pieces, a):
    for ref, first, last, number in pieces:
        if first <= a < last:
            return ref, a - first + number
    raise ValueError(a)


def read(zero, pieces, a, start, count, *field):
    ref, number = place(pieces, a)
    return ref[(*field, number, pl.ds(zero + start, count), slice(None))]


def write(pieces, a, value, *field):
    ref, number = place(pieces, a)
    ref[(*field, number, pl.ds(0, value.shape[0]), slice(None))] = value


def sweep_x(state, speed, swept, fields, first, last, wide, half):
    for part in range(0, wide, 8):
        before = [state(field, first - 1, part) for field in fields]
        here = [state(field, first, part) for field in fields]
        steps = [h - b for h, b in zip(here, before)]
        slopes = [limited(st, b - state(field, first - 2, part)) for field, st, b in zip(fields, steps, before)]
        lower = None
        for a in range(first, last + 1):
            factors = face_factors(speed(a - 1, part), speed(a, part), half)
            fluxes = []
            for k, field in enumerate(fields):
                after = state(field, a + 1, part)
                step = after - here[k]
                slope = limited(step, steps[k])
                fluxes.append(face_flux(factors, before[k], here[k], slopes[k], slope))
                if lower is not None:
                    swept[field, a - 1 - first, pl.ds(part, 8)] = before[k] - (fluxes[k] - lower[k])
                before[k], here[k], steps[k], slopes[k] = here[k], after, step, slope
            lower = fluxes


def sweep_y(zero, swept, work, numbers, fields, factors, wide):
    cases = [(number, field) for number in numbers for field in fields]

    def rows(number, field, start):
        return swept[field, number, pl.ds(zero + start, wide)]

    for number, field in cases:
        below = rows(number, field, 1)
        slope = limited(rows(number, field, 2) - below, below - rows(number, field, 0))
        work[0, field, number, 0:wide] = slope
    for number, field in cases:
        slope, above = [work[0, field, number, pl.ds(zero + start, wide)] for start in (0, 1)]
        flux = face_flux(factors[number], rows(number, field, 1), rows(number, field, 2), slope, above)
        work[1, field, number, 0:wide] = flux
    moved = {}
    for number, field in cases:
        flux, above = [work[1, field, number, pl.ds(zero + start, wide)] for start in (0, 1)]
        moved[number, field] = rows(number, field, 2) - (above - flux)
    return [[moved[number, field] for field in fields] for number in numbers]


def sweep_z(moved, factors):
    final = []
    for value in moved:
        below = down(value)
        step = value - below
        slope = limited(up(step), step)
        flux = face_flux(factors, below, value, down(slope), slope)
        final.append(value - (up(flux) - flux))
    return final


def spread_columns(zero, columns, tall, half, cells, stress, heat, growth):
    for a in columns:
        z = read(zero, cells, a, TOP - 4, tall, ZV)
        spread = (
            read(zero, cells, a + 1, TOP - 4, tall, XV)
            - read(zero, cells, a - 1, TOP - 4, tall, XV)
            + (read(zero, cells, a, TOP - 3, tall, YV) - read(zero, cells, a, TOP - 5, tall, YV))
            + (up(z) - down(z))
        )
        warmth = per_mass(read(zero, cells, a, TOP - 4, tall, ENERGY), spread)
        write(heat, a, warmth)
        write(stress, a, read(zero, cells, a, TOP - 4, tall, DENSITY) * warmth)
        write(growth, a, half * spread)


def advance_columns(zero, columns, wide, half, cells, stress, heat, growth, passive, state, energies, nx):
    for a in columns:
        density, energy, x, y, z = [read(zero, cells, a, TOP - 2, wide, field) for field in range(5)]
        grown = read(zero, growth, a, 2, wide)
        centre = read(zero, stress, a, 2, wide)
        scale = half / density
        density_one = density / (1.0 + grown)
        energy = energy - read(zero, heat, a, 2, wide) * grown
        write(passive, a, density_one, 0)
        write(passive, a, density_one * energy, 1)
        write(state, a, x - scale * (read(zero, stress, a + 1, 2, wide) - read(zero, stress, a - 1, 2, wide)), 0)
        write(state, a, y - scale * (read(zero, stress, a, 3, wide) - read(zero, stress, a, 1, wide)), 1)
        write(state, a, z - scale * (up(centre) - down(centre)), 2)
        if 0 <= a < nx:
            write(energies, a, energy)


def flow_columns(zero, first, last, ny, half, state, energies, swept, work, speed_y, speed_z, flows):
    wide = ny + 4
    sweep_x(
        lambda field, a, part: read(zero, state, a, part, 8, field),
        lambda a, part: read(zero, state, a, part, 8, 0),
        swept, (0, 1, 2), first, last, wide, half,
    )
    numbers = range(last - first)
    factors = []
    for number in numbers:
        below, here = [swept[1, number, pl.ds(zero + start, wide)] for start in (1, 2)]
        factors.append(face_factors(below, here, half))
        write(speed_y, first + number, swept[1, number, 0:wide])
    peak = None
    for a, moved in zip(range(first, last), sweep_y(zero, swept, work, numbers, (0, 1, 2), factors, wide)):
        write(speed_z, a, moved[2])
        final = sweep_z(moved, face_factors(down(moved[2]), moved[2], half))
        for field in range(3):
            write(flows, a, final[field][:ny], field)
        signal = (
            jnp.sqrt(0.56 * read(zero, energies, a, 2, wide))
            + jnp.abs(final[0])
            + jnp.abs(final[1])
            + jnp.abs(final[2])
        )
        peak = signal if peak is None else jnp.maximum(peak, signal)
    return peak


def inner_kernel(nx, ny, dt_ref, *refs):
    own, y_edges = refs[0], refs[1:3]
    cells, stress, state, passive, energies, speed_y, speed_z, flows, peak_ref = refs[3:12]
    heat, growth, swept, work = refs[12:]
    zero = hidden_zero()
    half = 0.5 * dt_ref[0]
    for field in range(5):
        for a in range(nx):
            cells[field, a, pl.ds(TOP, ny), :] = own[field, a]
    for link, edge in zip(LINKS, y_edges):
        low = is_low(link)
        for field, a, rows, offset in y_layers(nx)[0]:
            cells[field, a, pl.ds(TOP + pick(low, -rows, ny), rows), :] = edge[pl.ds(zero + offset, rows), :]
    cells = [(cells, 0, nx, 0)]
    stress, heat, growth = [[(ref, 1, nx - 1, 0)] for ref in (stress, heat, growth)]
    state, passive, energies = [[(ref, 2, nx - 2, 0)] for ref in (state, passive, energies)]
    speed_y, speed_z, flows = [[(ref, 4, nx - 4, 0)] for ref in (speed_y, speed_z, flows)]
    spread_columns(zero, range(1, nx - 1), ny + 12, half, cells, stress, heat, growth)
    advance_columns(
        zero, range(2, nx - 2), ny + 4, half, cells, stress, heat, growth, passive, state, energies, nx
    )
    peak_ref[...] = flow_columns(
        zero, 4, nx - 4, ny, half, state, energies, swept, work, speed_y, speed_z, flows
    )


def outer_pieces(ref, nx, reach, inside):
    return [(ref, -reach, inside, 0), (ref, nx - inside, nx + reach, reach + inside)]


def outer_kernel(nx, ny, dt_ref, *refs):
    x_edges, corners = refs[0:2], refs[2:4]
    cells_in, stress_in, state_in, energies_in, peak_in = refs[4:9]
    state_out, passive_out, speed_y, speed_z, flows, increment_ref = refs[9:15]
    beyond, third, stress_out, heat, growth, energies_out, swept, work = refs[15:]
    nz = increment_ref.shape[-1]
    zero = hidden_zero()
    half = 0.5 * dt_ref[0]
    wide, tall = ny + 4, ny + 12

    columns, singles, rows_of_corner = corner_layers()
    for k, (side, edge) in enumerate(zip(SIDES, x_edges)):
        for number, (field, past) in enumerate(x_layers()):
            column = LEFT - past if side < 0 else LEFT - 1 + past
            beyond[field, column, pl.ds(TOP, ny), :] = edge[pl.ds(zero + number * ny, ny), :]
        offset = len(x_layers()) * ny
        third[k, EDGE_KINDS, pl.ds(TOP, ny), :] = edge[pl.ds(zero + offset, ny), :]
        offset += ny
        for row in (0, ny - 1):
            for kind in range(EDGE_KINDS):
                third[k, kind, pl.ds(TOP + row, 1), :] = edge[pl.ds(zero + offset, 1), :]
                offset += 1
    for link, corner in zip(LINKS, corners):
        low = is_low(link)
        for k, side in enumerate(SIDES):
            base = zero + k * rows_of_corner
            for _, field, past, rows, offset in columns:
                column = LEFT - past if side < 0 else LEFT - 1 + past
                to = pl.ds(TOP + pick(low, -rows, ny), rows)
                beyond[field, column, to, :] = corner[pl.ds(base + offset, rows), :]
            third[k, EDGE_KINDS, pl.ds(TOP + pick(low, -2, ny + 1), 1), :] = corner[pl.ds(base + singles, 1), :]
            for kind in range(EDGE_KINDS):
                to = pl.ds(TOP + pick(low, -1, ny), 1)
                third[k, kind, to, :] = corner[pl.ds(base + (singles + 1 + kind), 1), :]

    cells = [(cells_in, 0, nx, 0)] + outer_pieces(beyond, nx, LEFT, 0)
    stress = outer_pieces(stress_out, nx, 3, 2) + [(stress_in, 2, nx - 2, 1)]
    heat, growth = outer_pieces(heat, nx, 2, 2), outer_pieces(growth, nx, 2, 2)
    state = outer_pieces(state_out, nx, 2, 2) + [(state_in, 2, nx - 2, 0)]
    passive = outer_pieces(passive_out, nx, 2, 2)
    energies = outer_pieces(energies_out, nx, 0, 2) + [(energies_in, 2, nx - 2, 0)]
    speed_y, speed_z, flows = [outer_pieces(ref, nx, 0, 4) for ref in (speed_y, speed_z, flows)]

    row = lax.broadcasted_iota(jnp.int32, (tall, nz), 0) - 4
    for k, a in enumerate((-3, nx + 2)):
        above, below = [third[k, 3, pl.ds(zero + start, tall)] for start in (TOP - 3, TOP - 5)]
        density, energy, spread, _, whole = [third[k, kind, pl.ds(zero + TOP - 4, tall)] for kind in range(5)]
        spread += jnp.where((row == -1) | (row == ny - 1), above, -below)
        split = (row == -1) | (row == 0) | (row == ny - 1) | (row == ny)
        write(stress, a, jnp.where(split, density * per_mass(energy, spread), whole))

    ends = (*range(-2, 2), *range(nx - 2, nx + 2))
    spread_columns(zero, ends, tall, half, cells, stress, heat, growth)
    advance_columns(zero, ends, wide, half, cells, stress, heat, growth, passive, state, energies, nx)
    peak = peak_in[...]
    for k, first in enumerate((0, nx - 4)):
        peak = jnp.maximum(
            peak,
            flow_columns(
                zero, first, first + 4, ny, half, state, energies, swept.at[k], work.at[k], speed_y, speed_z, flows
            ),
        )
    peak = jnp.max(jnp.where(row[4 : 4 + wide] < ny, peak, 0.0), axis=0, keepdims=True)
    increment_ref[...] = jnp.broadcast_to(0.3 / peak, increment_ref.shape)


def carry_kernel(nx, ny, dt_ref, *refs):
    state_in, passive_in, speed_y_in, speed_z_in, flows_in = refs[0:5]
    state_out, passive_out, speed_y_out, speed_z_out, flows_out = refs[5:10]
    density_out, energy_out, flow_outs, swept, work, written = refs[10], refs[11], refs[12:15], refs[15], refs[16], refs[17]
    zero = hidden_zero()
    half = 0.5 * dt_ref[0]
    wide = ny + 4
    copies = []
    for k in range(3):
        for piece, (ref, first, last, number) in enumerate([(flows_in, 4, nx - 4, 0)] + outer_pieces(flows_out, nx, 0, 4)):
            source = ref.at[k, pl.ds(number, last - first)]
            copies.append(
                pltpu.make_async_copy(source, flow_outs[k].at[pl.ds(first, last - first)], written.at[k, piece])
            )
    for copy in copies:
        copy.start()
    state = outer_pieces(state_out, nx, 2, 2) + [(state_in, 2, nx - 2, 0)]
    passive = outer_pieces(passive_out, nx, 2, 2) + [(passive_in, 2, nx - 2, 0)]
    speed_y = outer_pieces(speed_y_out, nx, 0, 4) + [(speed_y_in, 4, nx - 4, 0)]
    speed_z = outer_pieces(speed_z_out, nx, 0, 4) + [(speed_z_in, 4, nx - 4, 0)]
    sweep_x(
        lambda field, a, part: read(zero, passive, a, part, 8, field),
        lambda a, part: read(zero, state, a, part, 8, 0),
        swept, (0, 1), 0, nx, wide, half,
    )
    factors = [face_factors(*[read(zero, speed_y, a, start, wide) for start in (1, 2)], half) for a in range(nx)]
    for a, moved in enumerate(sweep_y(zero, swept, work, range(nx), (0, 1), factors, wide)):
        along = read(zero, speed_z, a, 0, wide)
        final = sweep_z(moved, face_factors(down(along), along, half))
        density_out[a] = final[0][:ny]
        energy_out[a] = final[1][:ny]
    for copy in copies:
        copy.wait()


def body(density0, energy0, x_velocity, y_velocity, z_velocity, time_increment):
    nx, ny, nz = density0.shape
    fields = (density0, energy0, x_velocity, y_velocity, z_velocity)
    wide, tall = ny + 4, ny + 12

    def array(*shape):
        return jax.ShapeDtypeStruct((*shape, nz), jnp.float32)

    def scratch(*shape):
        return pltpu.VMEM((*shape, nz), jnp.float32)

    def limit(mebibytes):
        return pltpu.CompilerParams(vmem_limit_bytes=mebibytes * 1024 * 1024)

    x_edge, y_edge, corner = array(x_edge_rows(ny)), array(y_layers(nx)[1]), array(2 * corner_layers()[2])
    placed = [pltpu.with_memory_space_constraint(field, pltpu.HBM) for field in fields]
    x_edges = pl.pallas_call(
        functools.partial(x_pack_kernel, nx, ny),
        out_shape=[x_edge] * 2,
        in_specs=[HBM] * 5,
        out_specs=[VMEM] * 2,
        scratch_shapes=[scratch(5, 8, ny), scratch(2, ny + 20), pltpu.SemaphoreType.DMA((5, 2))],
        compiler_params=limit(4),
        name="x_pack",
    )(*placed)
    x_edges = [along_x(edge, side) for edge, side in zip(x_edges, SIDES)]
    own, *y_edges = pl.pallas_call(
        functools.partial(y_pack_kernel, nx, ny),
        out_shape=[array(5, nx, ny), y_edge, y_edge],
        in_specs=[HBM] * 5,
        out_specs=[VMEM] * 3,
        scratch_shapes=[pltpu.SemaphoreType.DMA((5,))],
        compiler_params=limit(4),
        name="y_pack",
    )(*placed)
    y_edges = [along_y(edge, link) for edge, link in zip(y_edges, LINKS)]
    corners = pl.pallas_call(
        functools.partial(corner_kernel, ny),
        out_shape=[corner] * 2,
        in_specs=[VMEM] * 2,
        out_specs=[VMEM] * 2,
        compiler_params=limit(4),
        name="corners",
    )(*x_edges)
    corners = [along_y(corner, link) for corner, link in zip(corners, LINKS)]
    increment = time_increment.reshape(1)
    passed_in = [array(3, nx - 4, wide), array(2, nx - 4, wide), array(nx - 8, wide + 8), array(nx - 8, wide), array(3, nx - 8, ny)]
    passed_out = [array(3, 8, wide), array(2, 8, wide), array(8, wide + 8), array(8, wide), array(3, 8, ny)]
    cells, stress, state_in, passive_in, energies, *rest_in, peak = pl.pallas_call(
        functools.partial(inner_kernel, nx, ny),
        out_shape=[
            array(5, nx, ny + 20),
            array(nx - 2, tall),
            *passed_in[:2],
            array(nx - 4, wide + 8),
            *passed_in[2:],
            array(wide),
        ],
        in_specs=[SMEM] + [VMEM] * 3,
        out_specs=[VMEM] * 9,
        scratch_shapes=[
            scratch(nx - 2, tall),
            scratch(nx - 2, tall),
            scratch(3, nx - 8, wide + 8),
            scratch(2, 3, nx - 8, wide + 8),
        ],
        compiler_params=limit(8),
        cost_estimate=pl.CostEstimate(flops=5 * 10**6, bytes_accessed=2 * 10**6, transcendentals=0),
        name="inner",
    )(increment, own, *y_edges)
    *outer, smallest = pl.pallas_call(
        functools.partial(outer_kernel, nx, ny),
        out_shape=passed_out + [array(lax.axis_size(("gx", "gy")))],
        in_specs=[SMEM] + [VMEM] * 9,
        out_specs=[VMEM] * 6,
        scratch_shapes=[
            scratch(5, 2 * LEFT, ny + 20),
            scratch(2, EDGE_KINDS + 1, ny + 20),
            scratch(10, tall),
            scratch(8, tall),
            scratch(8, tall),
            scratch(4, wide + 8),
            scratch(2, 3, 4, wide + 8),
            scratch(2, 2, 3, 4, wide + 8),
        ],
        compiler_params=limit(8),
        name="outer",
    )(increment, *x_edges, *corners, cells, stress, state_in, energies, peak)
    outs = pl.pallas_call(
        functools.partial(carry_kernel, nx, ny),
        out_shape=[array(nx, ny)] * 5,
        in_specs=[SMEM] + [VMEM] * 10,
        out_specs=[VMEM] * 2 + [HBM] * 3,
        scratch_shapes=[
            scratch(2, nx, wide + 8),
            scratch(2, 2, nx, wide + 8),
            pltpu.SemaphoreType.DMA((3, 3)),
        ],
        compiler_params=limit(8),
        cost_estimate=pl.CostEstimate(flops=10**7, bytes_accessed=4 * 10**6, transcendentals=0),
        name="carry",
    )(increment, state_in, passive_in, *rest_in, *outer)
    return (*outs, jnp.min(lax.all_to_all(smallest, ("gx", "gy"), 0, 0, tiled=True)))


def solution(mesh):
    cells = P("gx", "gy", None)
    return jax.shard_map(
        body,
        mesh=mesh,
        in_specs=(cells,) * 5 + (P(),),
        out_specs=(cells,) * 5 + (P(),),
        check_vma=False,
    )
```

```python
import functools

import jax
import jax.numpy as jnp
from jax import lax
from jax.experimental import pallas as pl
from jax.experimental.pallas import tpu as pltpu
from jax.sharding import PartitionSpec as P

DENSITY, ENERGY, XV, YV, ZV = range(5)
TOP = 8
LEFT = 3
SIDES = (-1, 1)
NEAR, FAR = "near", "far"
LINKS = (FAR, NEAR)
EDGE_KINDS = 4
VMEM = pl.BlockSpec(memory_space=pltpu.VMEM)
HBM = pl.BlockSpec(memory_space=pltpu.HBM)
SMEM = pl.BlockSpec(memory_space=pltpu.SMEM)


def ghost_rows(field):
    return 4 if field == YV else 3


def x_layers():
    return [(field, past) for field in range(5) for past in (1, 2)] + [(XV, 3)]


def x_edge_rows(ny):
    return (len(x_layers()) + 1) * ny + 2 * EDGE_KINDS


def y_layers(nx):
    found, offset = [], 0
    for a in range(nx):
        for field in range(5):
            found.append((field, a, ghost_rows(field), offset))
            offset += ghost_rows(field)
    return found, -(-offset // 8) * 8


def corner_layers():
    found, offset = [], 0
    for number, (field, past) in enumerate(x_layers()):
        found.append((number, field, past, ghost_rows(field), offset))
        offset += ghost_rows(field)
    return found, offset, -(-(offset + 1 + EDGE_KINDS) // 8) * 8


def is_low(link):
    odd = lax.rem(lax.axis_index("gy"), 2)
    return odd if link == NEAR else 1 - odd


def pick(flag, one, other):
    return flag * one + (1 - flag) * other


def along_x(value, side):
    count = lax.axis_size("gx")
    return lax.ppermute(value, "gx", [((i + side) % count, i) for i in range(count)])


def along_y(value, link):
    count = lax.axis_size("gy")
    partners = [i ^ 1 if link == NEAR else (((i - 1) ^ 1) + 1) % count for i in range(count)]
    return lax.ppermute(value, "gy", list(enumerate(partners)))


def hidden_zero():
    return lax.shift_right_logical(lax.axis_index("gx"), 20)


def per_mass(energy, spread):
    return 0.4 * energy + 0.5 * jnp.square(jnp.minimum(0.5 * spread, 0.0))


def x_pack_kernel(nx, ny, *refs):
    fields, own, x_edges, padded, arrived = refs[:5], refs[5], refs[6:8], refs[8], refs[9]
    zero = hidden_zero()
    copies = [pltpu.make_async_copy(fields[field], own.at[field], arrived.at[field]) for field in range(5)]
    for copy in copies:
        copy.start()
    for current, copy in enumerate(copies):
        copy.wait()
        for side, edge in zip(SIDES, x_edges):
            for number, (field, past) in enumerate(x_layers()):
                if field == current:
                    edge[pl.ds(zero + number * ny, ny), :] = own[field, nx - past if side < 0 else past - 1]
    for k, (side, edge) in enumerate(zip(SIDES, x_edges)):
        a = nx - 3 if side < 0 else 2
        offset = len(x_layers()) * ny
        padded[k] = jnp.zeros_like(padded[k])
        padded[k, pl.ds(TOP, ny), :] = own[YV, a]
        spread = own[XV, a + 1] - own[XV, a - 1]
        spread += padded[k, pl.ds(zero + (TOP + 1), ny), :] - padded[k, pl.ds(zero + (TOP - 1), ny), :]
        spread += up(own[ZV, a]) - down(own[ZV, a])
        edge[pl.ds(zero + offset, ny), :] = own[DENSITY, a] * per_mass(own[ENERGY, a], spread)
        offset += ny
        padded[k, pl.ds(TOP, ny), :] = spread
        for row in (0, ny - 1):
            for value in (own[DENSITY, a, pl.ds(row, 1), :], own[ENERGY, a, pl.ds(row, 1), :],
                          padded[k, pl.ds(TOP + row, 1), :], own[YV, a, pl.ds(row, 1), :]):
                edge[pl.ds(zero + offset, 1), :] = value
                offset += 1


def y_pack_kernel(nx, ny, own, *y_edges):
    zero = hidden_zero()
    for link, edge in zip(LINKS, y_edges):
        low = is_low(link)
        for field, a, rows, offset in y_layers(nx)[0]:
            edge[pl.ds(zero + offset, rows), :] = own[field, a, pl.ds(pick(low, 0, ny - rows), rows), :]


def corner_kernel(ny, *refs):
    x_edges, outs = refs[:2], refs[2:]
    zero = hidden_zero()
    columns, singles, rows_of_corner = corner_layers()
    for link, out in zip(LINKS, outs):
        low = is_low(link)
        for k, edge in enumerate(x_edges):
            base = zero + k * rows_of_corner
            for number, _, _, rows, offset in columns:
                out[pl.ds(base + offset, rows), :] = edge[pl.ds(number * ny + pick(low, 0, ny - rows), rows), :]
            number = len(x_layers())
            out[pl.ds(base + singles, 1), :] = edge[pl.ds(number * ny + pick(low, 1, ny - 2), 1), :]
            first = (number + 1) * ny + pick(low, 0, EDGE_KINDS)
            out[pl.ds(base + (singles + 1), EDGE_KINDS), :] = edge[pl.ds(first, EDGE_KINDS), :]


def limited(above, below):
    return jnp.minimum(jnp.maximum(above, jnp.minimum(below, 0.0)), jnp.maximum(below, 0.0))


def face_factors(v_minus, v, half_increment):
    courant = half_increment * (v_minus + v)
    size = jnp.abs(courant)
    return courant, 0.5 * size * (1.0 - size), courant > 0.0


def face_flux(factors, f_minus, f, s_minus, s):
    courant, slope_factor, upward = factors
    return courant * jnp.where(upward, f_minus, f) + slope_factor * jnp.where(upward, s_minus, s)


def up(value):
    return pltpu.roll(value, value.shape[-1] - 1, value.ndim - 1)


def down(value):
    return pltpu.roll(value, 1, value.ndim - 1)


def place(pieces, a):
    for ref, first, last, number in pieces:
        if first <= a < last:
            return ref, a - first + number
    raise ValueError(a)


def read(zero, pieces, a, start, count, *field):
    ref, number = place(pieces, a)
    return ref[(*field, number, pl.ds(zero + start, count), slice(None))]


def write(pieces, a, value, *field):
    ref, number = place(pieces, a)
    ref[(*field, number, pl.ds(0, value.shape[0]), slice(None))] = value


def sweep_x(state, speed, swept, fields, first, last, wide, half):
    for part in range(0, wide, 8):
        before = [state(field, first - 1, part) for field in fields]
        here = [state(field, first, part) for field in fields]
        steps = [h - b for h, b in zip(here, before)]
        slopes = [limited(st, b - state(field, first - 2, part)) for field, st, b in zip(fields, steps, before)]
        lower = None
        for a in range(first, last + 1):
            factors = face_factors(speed(a - 1, part), speed(a, part), half)
            fluxes = []
            for k, field in enumerate(fields):
                after = state(field, a + 1, part)
                step = after - here[k]
                slope = limited(step, steps[k])
                fluxes.append(face_flux(factors, before[k], here[k], slopes[k], slope))
                if lower is not None:
                    swept[field, a - 1 - first, pl.ds(part, 8)] = before[k] - (fluxes[k] - lower[k])
                before[k], here[k], steps[k], slopes[k] = here[k], after, step, slope
            lower = fluxes


def sweep_y(zero, swept, work, numbers, fields, factors, wide):
    cases = [(number, field) for number in numbers for field in fields]

    def rows(number, field, start):
        return swept[field, number, pl.ds(zero + start, wide)]

    for number, field in cases:
        below = rows(number, field, 1)
        slope = limited(rows(number, field, 2) - below, below - rows(number, field, 0))
        work[0, field, number, 0:wide] = slope
    for number, field in cases:
        slope, above = [work[0, field, number, pl.ds(zero + start, wide)] for start in (0, 1)]
        flux = face_flux(factors[number], rows(number, field, 1), rows(number, field, 2), slope, above)
        work[1, field, number, 0:wide] = flux
    moved = {}
    for number, field in cases:
        flux, above = [work[1, field, number, pl.ds(zero + start, wide)] for start in (0, 1)]
        moved[number, field] = rows(number, field, 2) - (above - flux)
    return [[moved[number, field] for field in fields] for number in numbers]


def sweep_z(moved, factors):
    final = []
    for value in moved:
        below = down(value)
        step = value - below
        slope = limited(up(step), step)
        flux = face_flux(factors, below, value, down(slope), slope)
        final.append(value - (up(flux) - flux))
    return final


def spread_columns(zero, columns, tall, half, cells, stress, heat, growth):
    for a in columns:
        z = read(zero, cells, a, TOP - 4, tall, ZV)
        spread = (
            read(zero, cells, a + 1, TOP - 4, tall, XV)
            - read(zero, cells, a - 1, TOP - 4, tall, XV)
            + (read(zero, cells, a, TOP - 3, tall, YV) - read(zero, cells, a, TOP - 5, tall, YV))
            + (up(z) - down(z))
        )
        warmth = per_mass(read(zero, cells, a, TOP - 4, tall, ENERGY), spread)
        write(heat, a, warmth)
        write(stress, a, read(zero, cells, a, TOP - 4, tall, DENSITY) * warmth)
        write(growth, a, half * spread)


def advance_columns(zero, columns, wide, half, cells, stress, heat, growth, passive, state, energies, nx):
    for a in columns:
        density, energy, x, y, z = [read(zero, cells, a, TOP - 2, wide, field) for field in range(5)]
        grown = read(zero, growth, a, 2, wide)
        centre = read(zero, stress, a, 2, wide)
        scale = half / density
        density_one = density / (1.0 + grown)
        energy = energy - read(zero, heat, a, 2, wide) * grown
        write(passive, a, density_one, 0)
        write(passive, a, density_one * energy, 1)
        write(state, a, x - scale * (read(zero, stress, a + 1, 2, wide) - read(zero, stress, a - 1, 2, wide)), 0)
        write(state, a, y - scale * (read(zero, stress, a, 3, wide) - read(zero, stress, a, 1, wide)), 1)
        write(state, a, z - scale * (up(centre) - down(centre)), 2)
        if 0 <= a < nx:
            write(energies, a, energy)


def flow_columns(zero, first, last, ny, half, state, energies, swept, work, speed_y, speed_z, flows):
    wide = ny + 4
    sweep_x(
        lambda field, a, part: read(zero, state, a, part, 8, field),
        lambda a, part: read(zero, state, a, part, 8, 0),
        swept, (0, 1, 2), first, last, wide, half,
    )
    numbers = range(last - first)
    factors = []
    for number in numbers:
        below, here = [swept[1, number, pl.ds(zero + start, wide)] for start in (1, 2)]
        factors.append(face_factors(below, here, half))
        write(speed_y, first + number, swept[1, number, 0:wide])
    peak = None
    for a, moved in zip(range(first, last), sweep_y(zero, swept, work, numbers, (0, 1, 2), factors, wide)):
        write(speed_z, a, moved[2])
        final = sweep_z(moved, face_factors(down(moved[2]), moved[2], half))
        for field in range(3):
            write(flows, a, final[field][:ny], field)
        signal = (
            jnp.sqrt(0.56 * read(zero, energies, a, 2, wide))
            + jnp.abs(final[0])
            + jnp.abs(final[1])
            + jnp.abs(final[2])
        )
        peak = signal if peak is None else jnp.maximum(peak, signal)
    return peak


def inner_kernel(nx, ny, dt_ref, *refs):
    own, y_edges = refs[0], refs[1:3]
    cells, stress, state, passive, energies, speed_y, speed_z, flows, peak_ref = refs[3:12]
    heat, growth, swept, work = refs[12:]
    zero = hidden_zero()
    half = 0.5 * dt_ref[0]
    for field in range(5):
        for a in range(nx):
            cells[field, a, pl.ds(TOP, ny), :] = own[field, a]
    for link, edge in zip(LINKS, y_edges):
        low = is_low(link)
        for field, a, rows, offset in y_layers(nx)[0]:
            cells[field, a, pl.ds(TOP + pick(low, -rows, ny), rows), :] = edge[pl.ds(zero + offset, rows), :]
    cells = [(cells, 0, nx, 0)]
    stress, heat, growth = [[(ref, 1, nx - 1, 0)] for ref in (stress, heat, growth)]
    state, passive, energies = [[(ref, 2, nx - 2, 0)] for ref in (state, passive, energies)]
    speed_y, speed_z, flows = [[(ref, 4, nx - 4, 0)] for ref in (speed_y, speed_z, flows)]
    spread_columns(zero, range(1, nx - 1), ny + 12, half, cells, stress, heat, growth)
    advance_columns(
        zero, range(2, nx - 2), ny + 4, half, cells, stress, heat, growth, passive, state, energies, nx
    )
    peak_ref[...] = flow_columns(
        zero, 4, nx - 4, ny, half, state, energies, swept, work, speed_y, speed_z, flows
    )


def outer_pieces(ref, nx, reach, inside):
    return [(ref, -reach, inside, 0), (ref, nx - inside, nx + reach, reach + inside)]


def outer_kernel(nx, ny, dt_ref, *refs):
    x_edges, corners = refs[0:2], refs[2:4]
    cells_in, stress_in, state_in, energies_in, peak_in = refs[4:9]
    state_out, passive_out, speed_y, speed_z, flows, increment_ref = refs[9:15]
    beyond, third, stress_out, heat, growth, energies_out, swept, work = refs[15:]
    nz = increment_ref.shape[-1]
    zero = hidden_zero()
    half = 0.5 * dt_ref[0]
    wide, tall = ny + 4, ny + 12

    columns, singles, rows_of_corner = corner_layers()
    for k, (side, edge) in enumerate(zip(SIDES, x_edges)):
        for number, (field, past) in enumerate(x_layers()):
            column = LEFT - past if side < 0 else LEFT - 1 + past
            beyond[field, column, pl.ds(TOP, ny), :] = edge[pl.ds(zero + number * ny, ny), :]
        offset = len(x_layers()) * ny
        third[k, EDGE_KINDS, pl.ds(TOP, ny), :] = edge[pl.ds(zero + offset, ny), :]
        offset += ny
        for row in (0, ny - 1):
            for kind in range(EDGE_KINDS):
                third[k, kind, pl.ds(TOP + row, 1), :] = edge[pl.ds(zero + offset, 1), :]
                offset += 1
    for link, corner in zip(LINKS, corners):
        low = is_low(link)
        for k, side in enumerate(SIDES):
            base = zero + k * rows_of_corner
            for _, field, past, rows, offset in columns:
                column = LEFT - past if side < 0 else LEFT - 1 + past
                to = pl.ds(TOP + pick(low, -rows, ny), rows)
                beyond[field, column, to, :] = corner[pl.ds(base + offset, rows), :]
            third[k, EDGE_KINDS, pl.ds(TOP + pick(low, -2, ny + 1), 1), :] = corner[pl.ds(base + singles, 1), :]
            for kind in range(EDGE_KINDS):
                to = pl.ds(TOP + pick(low, -1, ny), 1)
                third[k, kind, to, :] = corner[pl.ds(base + (singles + 1 + kind), 1), :]

    cells = [(cells_in, 0, nx, 0)] + outer_pieces(beyond, nx, LEFT, 0)
    stress = outer_pieces(stress_out, nx, 3, 2) + [(stress_in, 2, nx - 2, 1)]
    heat, growth = outer_pieces(heat, nx, 2, 2), outer_pieces(growth, nx, 2, 2)
    state = outer_pieces(state_out, nx, 2, 2) + [(state_in, 2, nx - 2, 0)]
    passive = outer_pieces(passive_out, nx, 2, 2)
    energies = outer_pieces(energies_out, nx, 0, 2) + [(energies_in, 2, nx - 2, 0)]
    speed_y, speed_z, flows = [outer_pieces(ref, nx, 0, 4) for ref in (speed_y, speed_z, flows)]

    row = lax.broadcasted_iota(jnp.int32, (tall, nz), 0) - 4
    for k, a in enumerate((-3, nx + 2)):
        above, below = [third[k, 3, pl.ds(zero + start, tall)] for start in (TOP - 3, TOP - 5)]
        density, energy, spread, _, whole = [third[k, kind, pl.ds(zero + TOP - 4, tall)] for kind in range(5)]
        spread += jnp.where((row == -1) | (row == ny - 1), above, -below)
        split = (row == -1) | (row == 0) | (row == ny - 1) | (row == ny)
        write(stress, a, jnp.where(split, density * per_mass(energy, spread), whole))

    ends = (*range(-2, 2), *range(nx - 2, nx + 2))
    spread_columns(zero, ends, tall, half, cells, stress, heat, growth)
    advance_columns(zero, ends, wide, half, cells, stress, heat, growth, passive, state, energies, nx)
    peak = peak_in[...]
    for k, first in enumerate((0, nx - 4)):
        peak = jnp.maximum(
            peak,
            flow_columns(
                zero, first, first + 4, ny, half, state, energies, swept.at[k], work.at[k], speed_y, speed_z, flows
            ),
        )
    peak = jnp.max(jnp.where(row[4 : 4 + wide] < ny, peak, 0.0), axis=0, keepdims=True)
    increment_ref[...] = jnp.broadcast_to(0.3 / peak, increment_ref.shape)


def carry_kernel(nx, ny, dt_ref, *refs):
    state_in, passive_in, speed_y_in, speed_z_in, flows_in = refs[0:5]
    state_out, passive_out, speed_y_out, speed_z_out, flows_out = refs[5:10]
    density_out, energy_out, flow_outs, swept, work, written = refs[10], refs[11], refs[12:15], refs[15], refs[16], refs[17]
    zero = hidden_zero()
    half = 0.5 * dt_ref[0]
    wide = ny + 4
    copies = []
    for k in range(3):
        for piece, (ref, first, last, number) in enumerate([(flows_in, 4, nx - 4, 0)] + outer_pieces(flows_out, nx, 0, 4)):
            source = ref.at[k, pl.ds(number, last - first)]
            copies.append(
                pltpu.make_async_copy(source, flow_outs[k].at[pl.ds(first, last - first)], written.at[k, piece])
            )
    for copy in copies:
        copy.start()
    state = outer_pieces(state_out, nx, 2, 2) + [(state_in, 2, nx - 2, 0)]
    passive = outer_pieces(passive_out, nx, 2, 2) + [(passive_in, 2, nx - 2, 0)]
    speed_y = outer_pieces(speed_y_out, nx, 0, 4) + [(speed_y_in, 4, nx - 4, 0)]
    speed_z = outer_pieces(speed_z_out, nx, 0, 4) + [(speed_z_in, 4, nx - 4, 0)]
    sweep_x(
        lambda field, a, part: read(zero, passive, a, part, 8, field),
        lambda a, part: read(zero, state, a, part, 8, 0),
        swept, (0, 1), 0, nx, wide, half,
    )
    factors = [face_factors(*[read(zero, speed_y, a, start, wide) for start in (1, 2)], half) for a in range(nx)]
    for a, moved in enumerate(sweep_y(zero, swept, work, range(nx), (0, 1), factors, wide)):
        along = read(zero, speed_z, a, 0, wide)
        final = sweep_z(moved, face_factors(down(along), along, half))
        density_out[a] = final[0][:ny]
        energy_out[a] = final[1][:ny]
    for copy in copies:
        copy.wait()


def body(density0, energy0, x_velocity, y_velocity, z_velocity, time_increment):
    nx, ny, nz = density0.shape
    fields = (density0, energy0, x_velocity, y_velocity, z_velocity)
    wide, tall = ny + 4, ny + 12

    def array(*shape):
        return jax.ShapeDtypeStruct((*shape, nz), jnp.float32)

    def scratch(*shape):
        return pltpu.VMEM((*shape, nz), jnp.float32)

    def limit(mebibytes):
        return pltpu.CompilerParams(vmem_limit_bytes=mebibytes * 1024 * 1024)

    x_edge, y_edge, corner = array(x_edge_rows(ny)), array(y_layers(nx)[1]), array(2 * corner_layers()[2])
    own, *x_edges = pl.pallas_call(
        functools.partial(x_pack_kernel, nx, ny),
        out_shape=[array(5, nx, ny), x_edge, x_edge],
        in_specs=[HBM] * 5,
        out_specs=[VMEM] * 3,
        scratch_shapes=[scratch(2, ny + 20), pltpu.SemaphoreType.DMA((5,))],
        compiler_params=limit(4),
        name="x_pack",
    )(*[pltpu.with_memory_space_constraint(field, pltpu.HBM) for field in fields])
    x_edges = [along_x(edge, side) for edge, side in zip(x_edges, SIDES)]
    y_edges = pl.pallas_call(
        functools.partial(y_pack_kernel, nx, ny),
        out_shape=[y_edge] * 2,
        in_specs=[VMEM],
        out_specs=[VMEM] * 2,
        compiler_params=limit(4),
        name="y_pack",
    )(own)
    y_edges = [along_y(edge, link) for edge, link in zip(y_edges, LINKS)]
    corners = pl.pallas_call(
        functools.partial(corner_kernel, ny),
        out_shape=[corner] * 2,
        in_specs=[VMEM] * 2,
        out_specs=[VMEM] * 2,
        compiler_params=limit(4),
        name="corners",
    )(*x_edges)
    corners = [along_y(corner, link) for corner, link in zip(corners, LINKS)]
    increment = time_increment.reshape(1)
    passed_in = [array(3, nx - 4, wide), array(2, nx - 4, wide), array(nx - 8, wide + 8), array(nx - 8, wide), array(3, nx - 8, ny)]
    passed_out = [array(3, 8, wide), array(2, 8, wide), array(8, wide + 8), array(8, wide), array(3, 8, ny)]
    cells, stress, state_in, passive_in, energies, *rest_in, peak = pl.pallas_call(
        functools.partial(inner_kernel, nx, ny),
        out_shape=[
            array(5, nx, ny + 20),
            array(nx - 2, tall),
            *passed_in[:2],
            array(nx - 4, wide + 8),
            *passed_in[2:],
            array(wide),
        ],
        in_specs=[SMEM] + [VMEM] * 3,
        out_specs=[VMEM] * 9,
        scratch_shapes=[
            scratch(nx - 2, tall),
            scratch(nx - 2, tall),
            scratch(3, nx - 8, wide + 8),
            scratch(2, 3, nx - 8, wide + 8),
        ],
        compiler_params=limit(8),
        cost_estimate=pl.CostEstimate(flops=5 * 10**6, bytes_accessed=2 * 10**6, transcendentals=0),
        name="inner",
    )(increment, own, *y_edges)
    *outer, smallest = pl.pallas_call(
        functools.partial(outer_kernel, nx, ny),
        out_shape=passed_out + [array(lax.axis_size(("gx", "gy")))],
        in_specs=[SMEM] + [VMEM] * 9,
        out_specs=[VMEM] * 6,
        scratch_shapes=[
            scratch(5, 2 * LEFT, ny + 20),
            scratch(2, EDGE_KINDS + 1, ny + 20),
            scratch(10, tall),
            scratch(8, tall),
            scratch(8, tall),
            scratch(4, wide + 8),
            scratch(2, 3, 4, wide + 8),
            scratch(2, 2, 3, 4, wide + 8),
        ],
        compiler_params=limit(8),
        name="outer",
    )(increment, *x_edges, *corners, cells, stress, state_in, energies, peak)
    outs = pl.pallas_call(
        functools.partial(carry_kernel, nx, ny),
        out_shape=[array(nx, ny)] * 5,
        in_specs=[SMEM] + [VMEM] * 10,
        out_specs=[VMEM] * 2 + [HBM] * 3,
        scratch_shapes=[
            scratch(2, nx, wide + 8),
            scratch(2, 2, nx, wide + 8),
            pltpu.SemaphoreType.DMA((3, 3)),
        ],
        compiler_params=limit(8),
        cost_estimate=pl.CostEstimate(flops=10**7, bytes_accessed=4 * 10**6, transcendentals=0),
        name="carry",
    )(increment, state_in, passive_in, *rest_in, *outer)
    return (*outs, jnp.min(lax.all_to_all(smallest, ("gx", "gy"), 0, 0, tiled=True)))


def solution(mesh):
    cells = P("gx", "gy", None)
    return jax.shard_map(
        body,
        mesh=mesh,
        in_specs=(cells,) * 5 + (P(),),
        out_specs=(cells,) * 5 + (P(),),
        check_vma=False,
    )
```

```python
import functools

import jax
import jax.numpy as jnp
from jax import lax
from jax.experimental import pallas as pl
from jax.experimental.pallas import tpu as pltpu
from jax.sharding import PartitionSpec as P

DENSITY, ENERGY, XV, YV, ZV = range(5)
TOP = 8
LEFT = 3
SIDES = (-1, 1)
NEAR, FAR = "near", "far"
LINKS = (FAR, NEAR)
EDGE_KINDS = 4
VMEM = pl.BlockSpec(memory_space=pltpu.VMEM)
HBM = pl.BlockSpec(memory_space=pltpu.HBM)
SMEM = pl.BlockSpec(memory_space=pltpu.SMEM)


def ghost_rows(field):
    return 4 if field == YV else 3


def x_layers():
    return [(field, past) for field in range(5) for past in (1, 2)] + [(XV, 3)]


def x_edge_rows(ny):
    return (len(x_layers()) + 1) * ny + 2 * EDGE_KINDS


def y_layers(nx):
    found, offset = [], 0
    for a in range(nx):
        for field in range(5):
            found.append((field, a, ghost_rows(field), offset))
            offset += ghost_rows(field)
    return found, -(-offset // 8) * 8


def corner_layers():
    found, offset = [], 0
    for number, (field, past) in enumerate(x_layers()):
        found.append((number, field, past, ghost_rows(field), offset))
        offset += ghost_rows(field)
    return found, offset, -(-(offset + 1 + EDGE_KINDS) // 8) * 8


def is_low(link):
    odd = lax.rem(lax.axis_index("gy"), 2)
    return odd if link == NEAR else 1 - odd


def pick(flag, one, other):
    return flag * one + (1 - flag) * other


def along_x(value, side):
    count = lax.axis_size("gx")
    return lax.ppermute(value, "gx", [((i + side) % count, i) for i in range(count)])


def along_y(value, link):
    count = lax.axis_size("gy")
    partners = [i ^ 1 if link == NEAR else (((i - 1) ^ 1) + 1) % count for i in range(count)]
    return lax.ppermute(value, "gy", list(enumerate(partners)))


def hidden_zero():
    return lax.shift_right_logical(lax.axis_index("gx"), 20)


def per_mass(energy, spread):
    return 0.4 * energy + 0.5 * jnp.square(jnp.minimum(0.5 * spread, 0.0))


def x_pack_kernel(nx, ny, *refs):
    fields, x_edges, near, padded, arrived = refs[:5], refs[5:7], refs[7], refs[8], refs[9]
    zero = hidden_zero()
    copies = [
        pltpu.make_async_copy(
            fields[field].at[pl.ds(first, 4)], near.at[field, pl.ds(4 * k, 4)], arrived.at[field, k]
        )
        for field in range(5)
        for k, first in enumerate((nx - 4, 0))
    ]
    for copy in copies:
        copy.start()
    for current in range(5):
        for k, (side, edge) in enumerate(zip(SIDES, x_edges)):
            copies[2 * current + k].wait()
            for number, (field, past) in enumerate(x_layers()):
                if field == current:
                    edge[pl.ds(zero + number * ny, ny), :] = near[field, 4 - past if side < 0 else 3 + past]
    for k, (side, edge) in enumerate(zip(SIDES, x_edges)):
        a = 1 if side < 0 else 6
        offset = len(x_layers()) * ny
        padded[k] = jnp.zeros_like(padded[k])
        padded[k, pl.ds(TOP, ny), :] = near[YV, a]
        spread = near[XV, a + 1] - near[XV, a - 1]
        spread += padded[k, pl.ds(zero + (TOP + 1), ny), :] - padded[k, pl.ds(zero + (TOP - 1), ny), :]
        spread += up(near[ZV, a]) - down(near[ZV, a])
        edge[pl.ds(zero + offset, ny), :] = near[DENSITY, a] * per_mass(near[ENERGY, a], spread)
        offset += ny
        padded[k, pl.ds(TOP, ny), :] = spread
        for row in (0, ny - 1):
            for value in (near[DENSITY, a, pl.ds(row, 1), :], near[ENERGY, a, pl.ds(row, 1), :],
                          padded[k, pl.ds(TOP + row, 1), :], near[YV, a, pl.ds(row, 1), :]):
                edge[pl.ds(zero + offset, 1), :] = value
                offset += 1


def y_pack_kernel(nx, ny, *refs):
    fields, own, y_edges, arrived = refs[:5], refs[5], refs[6:8], refs[8]
    zero = hidden_zero()
    copies = [pltpu.make_async_copy(fields[field], own.at[field], arrived.at[field]) for field in range(5)]
    for copy in copies:
        copy.start()
    for current, copy in enumerate(copies):
        copy.wait()
        for link, edge in zip(LINKS, y_edges):
            for field, a, rows, offset in y_layers(nx)[0]:
                if field == current:
                    start = pick(is_low(link), 0, ny - rows)
                    edge[pl.ds(zero + offset, rows), :] = own[field, a, pl.ds(start, rows), :]


def corner_kernel(ny, *refs):
    x_edges, outs = refs[:2], refs[2:]
    zero = hidden_zero()
    columns, singles, rows_of_corner = corner_layers()
    for link, out in zip(LINKS, outs):
        low = is_low(link)
        for k, edge in enumerate(x_edges):
            base = zero + k * rows_of_corner
            for number, _, _, rows, offset in columns:
                out[pl.ds(base + offset, rows), :] = edge[pl.ds(number * ny + pick(low, 0, ny - rows), rows), :]
            number = len(x_layers())
            out[pl.ds(base + singles, 1), :] = edge[pl.ds(number * ny + pick(low, 1, ny - 2), 1), :]
            first = (number + 1) * ny + pick(low, 0, EDGE_KINDS)
            out[pl.ds(base + (singles + 1), EDGE_KINDS), :] = edge[pl.ds(first, EDGE_KINDS), :]


def limited(above, below):
    return jnp.minimum(jnp.maximum(above, jnp.minimum(below, 0.0)), jnp.maximum(below, 0.0))


def face_factors(v_minus, v, half_increment):
    courant = half_increment * (v_minus + v)
    size = jnp.abs(courant)
    return courant, 0.5 * size * (1.0 - size), courant > 0.0


def face_flux(factors, f_minus, f, s_minus, s):
    courant, slope_factor, upward = factors
    return courant * jnp.where(upward, f_minus, f) + slope_factor * jnp.where(upward, s_minus, s)


def up(value):
    return pltpu.roll(value, value.shape[-1] - 1, value.ndim - 1)


def down(value):
    return pltpu.roll(value, 1, value.ndim - 1)


def place(pieces, a):
    for ref, first, last, number in pieces:
        if first <= a < last:
            return ref, a - first + number
    raise ValueError(a)


def read(zero, pieces, a, start, count, *field):
    ref, number = place(pieces, a)
    return ref[(*field, number, pl.ds(zero + start, count), slice(None))]


def write(pieces, a, value, *field):
    ref, number = place(pieces, a)
    ref[(*field, number, pl.ds(0, value.shape[0]), slice(None))] = value


def sweep_x(state, speed, swept, fields, first, last, wide, half):
    for part in range(0, wide, 8):
        before = [state(field, first - 1, part) for field in fields]
        here = [state(field, first, part) for field in fields]
        steps = [h - b for h, b in zip(here, before)]
        slopes = [limited(st, b - state(field, first - 2, part)) for field, st, b in zip(fields, steps, before)]
        lower = None
        for a in range(first, last + 1):
            factors = face_factors(speed(a - 1, part), speed(a, part), half)
            fluxes = []
            for k, field in enumerate(fields):
                after = state(field, a + 1, part)
                step = after - here[k]
                slope = limited(step, steps[k])
                fluxes.append(face_flux(factors, before[k], here[k], slopes[k], slope))
                if lower is not None:
                    swept[field, a - 1 - first, pl.ds(part, 8)] = before[k] - (fluxes[k] - lower[k])
                before[k], here[k], steps[k], slopes[k] = here[k], after, step, slope
            lower = fluxes


def sweep_y(zero, swept, work, numbers, fields, factors, wide):
    cases = [(number, field) for number in numbers for field in fields]

    def rows(number, field, start):
        return swept[field, number, pl.ds(zero + start, wide)]

    for number, field in cases:
        start = [rows(number, field, first) for first in range(4)]
        steps = [after - before for before, after in zip(start, start[1:])]
        slopes = [limited(after, before) for before, after in zip(steps, steps[1:])]
        work[field, number, 0:wide] = face_flux(factors[number], start[1], start[2], *slopes)
    moved = {}
    for number, field in cases:
        flux, above = [work[field, number, pl.ds(zero + start, wide)] for start in (0, 1)]
        moved[number, field] = rows(number, field, 2) - (above - flux)
    return [[moved[number, field] for field in fields] for number in numbers]


def sweep_z(moved, factors):
    final = []
    for value in moved:
        below, above = down(value), up(value)
        step = value - below
        slopes = limited(step, below - pltpu.roll(value, 2, 1)), limited(above - value, step)
        flux = face_flux(factors, below, value, *slopes)
        final.append(value - (up(flux) - flux))
    return final


def spread_columns(zero, columns, tall, half, cells, stress, heat, growth):
    for a in columns:
        z = read(zero, cells, a, TOP - 4, tall, ZV)
        spread = (
            read(zero, cells, a + 1, TOP - 4, tall, XV)
            - read(zero, cells, a - 1, TOP - 4, tall, XV)
            + (read(zero, cells, a, TOP - 3, tall, YV) - read(zero, cells, a, TOP - 5, tall, YV))
            + (up(z) - down(z))
        )
        warmth = per_mass(read(zero, cells, a, TOP - 4, tall, ENERGY), spread)
        write(heat, a, warmth)
        write(stress, a, read(zero, cells, a, TOP - 4, tall, DENSITY) * warmth)
        write(growth, a, half * spread)


def advance_columns(zero, columns, wide, half, cells, stress, heat, growth, passive, state, energies, nx):
    for a in columns:
        density, energy, x, y, z = [read(zero, cells, a, TOP - 2, wide, field) for field in range(5)]
        grown = read(zero, growth, a, 2, wide)
        centre = read(zero, stress, a, 2, wide)
        scale = half / density
        density_one = density / (1.0 + grown)
        energy = energy - read(zero, heat, a, 2, wide) * grown
        write(passive, a, density_one, 0)
        write(passive, a, density_one * energy, 1)
        write(state, a, x - scale * (read(zero, stress, a + 1, 2, wide) - read(zero, stress, a - 1, 2, wide)), 0)
        write(state, a, y - scale * (read(zero, stress, a, 3, wide) - read(zero, stress, a, 1, wide)), 1)
        write(state, a, z - scale * (up(centre) - down(centre)), 2)
        if 0 <= a < nx:
            write(energies, a, energy)


def flow_columns(zero, first, last, ny, half, state, energies, swept, work, speed_y, speed_z, flows):
    wide = ny + 4
    sweep_x(
        lambda field, a, part: read(zero, state, a, part, 8, field),
        lambda a, part: read(zero, state, a, part, 8, 0),
        swept, (0, 1, 2), first, last, wide, half,
    )
    numbers = range(last - first)
    factors = []
    for number in numbers:
        below, here = [swept[1, number, pl.ds(zero + start, wide)] for start in (1, 2)]
        factors.append(face_factors(below, here, half))
        write(speed_y, first + number, swept[1, number, 0:wide])
    peak = None
    for a, moved in zip(range(first, last), sweep_y(zero, swept, work, numbers, (0, 1, 2), factors, wide)):
        write(speed_z, a, moved[2])
        final = sweep_z(moved, face_factors(down(moved[2]), moved[2], half))
        for field in range(3):
            write(flows, a, final[field][:ny], field)
        signal = (
            jnp.sqrt(0.56 * read(zero, energies, a, 2, wide))
            + jnp.abs(final[0])
            + jnp.abs(final[1])
            + jnp.abs(final[2])
        )
        peak = signal if peak is None else jnp.maximum(peak, signal)
    return peak


def inner_kernel(nx, ny, dt_ref, *refs):
    own, y_edges = refs[0], refs[1:3]
    cells, stress, state, passive, energies, speed_y, speed_z, flows, peak_ref = refs[3:12]
    heat, growth, swept, work = refs[12:]
    zero = hidden_zero()
    half = 0.5 * dt_ref[0]
    for field in range(5):
        for a in range(nx):
            cells[field, a, pl.ds(TOP, ny), :] = own[field, a]
    for link, edge in zip(LINKS, y_edges):
        low = is_low(link)
        for field, a, rows, offset in y_layers(nx)[0]:
            cells[field, a, pl.ds(TOP + pick(low, -rows, ny), rows), :] = edge[pl.ds(zero + offset, rows), :]
    cells = [(cells, 0, nx, 0)]
    stress, heat, growth = [[(ref, 1, nx - 1, 0)] for ref in (stress, heat, growth)]
    state, passive, energies = [[(ref, 2, nx - 2, 0)] for ref in (state, passive, energies)]
    speed_y, speed_z, flows = [[(ref, 4, nx - 4, 0)] for ref in (speed_y, speed_z, flows)]
    spread_columns(zero, range(1, nx - 1), ny + 12, half, cells, stress, heat, growth)
    advance_columns(
        zero, range(2, nx - 2), ny + 4, half, cells, stress, heat, growth, passive, state, energies, nx
    )
    peak_ref[...] = flow_columns(
        zero, 4, nx - 4, ny, half, state, energies, swept, work, speed_y, speed_z, flows
    )


def outer_pieces(ref, nx, reach, inside):
    return [(ref, -reach, inside, 0), (ref, nx - inside, nx + reach, reach + inside)]


def outer_kernel(nx, ny, dt_ref, *refs):
    x_edges, corners = refs[0:2], refs[2:4]
    cells_in, stress_in, state_in, energies_in, peak_in = refs[4:9]
    state_out, passive_out, speed_y, speed_z, flows, increment_ref = refs[9:15]
    beyond, third, stress_out, heat, growth, energies_out = refs[15:21]
    swept, work = refs[21:23], refs[23:25]
    nz = increment_ref.shape[-1]
    zero = hidden_zero()
    half = 0.5 * dt_ref[0]
    wide, tall = ny + 4, ny + 12

    columns, singles, rows_of_corner = corner_layers()
    for k, (side, edge) in enumerate(zip(SIDES, x_edges)):
        for number, (field, past) in enumerate(x_layers()):
            column = LEFT - past if side < 0 else LEFT - 1 + past
            beyond[field, column, pl.ds(TOP, ny), :] = edge[pl.ds(zero + number * ny, ny), :]
        offset = len(x_layers()) * ny
        third[k, EDGE_KINDS, pl.ds(TOP, ny), :] = edge[pl.ds(zero + offset, ny), :]
        offset += ny
        for row in (0, ny - 1):
            for kind in range(EDGE_KINDS):
                third[k, kind, pl.ds(TOP + row, 1), :] = edge[pl.ds(zero + offset, 1), :]
                offset += 1
    for link, corner in zip(LINKS, corners):
        low = is_low(link)
        for k, side in enumerate(SIDES):
            base = zero + k * rows_of_corner
            for _, field, past, rows, offset in columns:
                column = LEFT - past if side < 0 else LEFT - 1 + past
                to = pl.ds(TOP + pick(low, -rows, ny), rows)
                beyond[field, column, to, :] = corner[pl.ds(base + offset, rows), :]
            third[k, EDGE_KINDS, pl.ds(TOP + pick(low, -2, ny + 1), 1), :] = corner[pl.ds(base + singles, 1), :]
            for kind in range(EDGE_KINDS):
                to = pl.ds(TOP + pick(low, -1, ny), 1)
                third[k, kind, to, :] = corner[pl.ds(base + (singles + 1 + kind), 1), :]

    cells = [(cells_in, 0, nx, 0)] + outer_pieces(beyond, nx, LEFT, 0)
    stress = outer_pieces(stress_out, nx, 3, 2) + [(stress_in, 2, nx - 2, 1)]
    heat, growth = outer_pieces(heat, nx, 2, 2), outer_pieces(growth, nx, 2, 2)
    state = outer_pieces(state_out, nx, 2, 2) + [(state_in, 2, nx - 2, 0)]
    passive = outer_pieces(passive_out, nx, 2, 2)
    energies = outer_pieces(energies_out, nx, 0, 2) + [(energies_in, 2, nx - 2, 0)]
    speed_y, speed_z, flows = [outer_pieces(ref, nx, 0, 4) for ref in (speed_y, speed_z, flows)]

    row = lax.broadcasted_iota(jnp.int32, (tall, nz), 0) - 4
    for k, a in enumerate((-3, nx + 2)):
        above, below = [third[k, 3, pl.ds(zero + start, tall)] for start in (TOP - 3, TOP - 5)]
        density, energy, spread, _, whole = [third[k, kind, pl.ds(zero + TOP - 4, tall)] for kind in range(5)]
        spread += jnp.where((row == -1) | (row == ny - 1), above, -below)
        split = (row == -1) | (row == 0) | (row == ny - 1) | (row == ny)
        write(stress, a, jnp.where(split, density * per_mass(energy, spread), whole))

    ends = (*range(-2, 2), *range(nx - 2, nx + 2))
    spread_columns(zero, ends, tall, half, cells, stress, heat, growth)
    advance_columns(zero, ends, wide, half, cells, stress, heat, growth, passive, state, energies, nx)
    peak = peak_in[...]
    for k, first in enumerate((0, nx - 4)):
        peak = jnp.maximum(
            peak,
            flow_columns(
                zero, first, first + 4, ny, half, state, energies, swept[k], work[k], speed_y, speed_z, flows
            ),
        )
    peak = jnp.max(jnp.where(row[4 : 4 + wide] < ny, peak, 0.0), axis=0, keepdims=True)
    increment_ref[...] = jnp.broadcast_to(0.3 / peak, increment_ref.shape)


def carry_kernel(nx, ny, dt_ref, *refs):
    state_in, passive_in, speed_y_in, speed_z_in, flows_in = refs[0:5]
    state_out, passive_out, speed_y_out, speed_z_out, flows_out = refs[5:10]
    density_out, energy_out, flow_outs, swept, work, written = refs[10], refs[11], refs[12:15], refs[15], refs[16], refs[17]
    zero = hidden_zero()
    half = 0.5 * dt_ref[0]
    wide = ny + 4
    copies = []
    for k in range(3):
        for piece, (ref, first, last, number) in enumerate([(flows_in, 4, nx - 4, 0)] + outer_pieces(flows_out, nx, 0, 4)):
            source = ref.at[k, pl.ds(number, last - first)]
            copies.append(
                pltpu.make_async_copy(source, flow_outs[k].at[pl.ds(first, last - first)], written.at[k, piece])
            )
    for copy in copies:
        copy.start()
    state = outer_pieces(state_out, nx, 2, 2) + [(state_in, 2, nx - 2, 0)]
    passive = outer_pieces(passive_out, nx, 2, 2) + [(passive_in, 2, nx - 2, 0)]
    speed_y = outer_pieces(speed_y_out, nx, 0, 4) + [(speed_y_in, 4, nx - 4, 0)]
    speed_z = outer_pieces(speed_z_out, nx, 0, 4) + [(speed_z_in, 4, nx - 4, 0)]
    sweep_x(
        lambda field, a, part: read(zero, passive, a, part, 8, field),
        lambda a, part: read(zero, state, a, part, 8, 0),
        swept, (0, 1), 0, nx, wide, half,
    )
    factors = [face_factors(*[read(zero, speed_y, a, start, wide) for start in (1, 2)], half) for a in range(nx)]
    for a, moved in enumerate(sweep_y(zero, swept, work, range(nx), (0, 1), factors, wide)):
        along = read(zero, speed_z, a, 0, wide)
        final = sweep_z(moved, face_factors(down(along), along, half))
        density_out[a] = final[0][:ny]
        energy_out[a] = final[1][:ny]
    for copy in copies:
        copy.wait()


def body(density0, energy0, x_velocity, y_velocity, z_velocity, time_increment):
    nx, ny, nz = density0.shape
    fields = (density0, energy0, x_velocity, y_velocity, z_velocity)
    wide, tall = ny + 4, ny + 12

    def array(*shape):
        return jax.ShapeDtypeStruct((*shape, nz), jnp.float32)

    def scratch(*shape):
        return pltpu.VMEM((*shape, nz), jnp.float32)

    def limit(mebibytes):
        return pltpu.CompilerParams(vmem_limit_bytes=mebibytes * 1024 * 1024)

    x_edge, y_edge, corner = array(x_edge_rows(ny)), array(y_layers(nx)[1]), array(2 * corner_layers()[2])
    placed = [pltpu.with_memory_space_constraint(field, pltpu.HBM) for field in fields]
    x_edges = pl.pallas_call(
        functools.partial(x_pack_kernel, nx, ny),
        out_shape=[x_edge] * 2,
        in_specs=[HBM] * 5,
        out_specs=[VMEM] * 2,
        scratch_shapes=[scratch(5, 8, ny), scratch(2, ny + 20), pltpu.SemaphoreType.DMA((5, 2))],
        compiler_params=limit(4),
        name="x_pack",
    )(*placed)
    x_edges = [along_x(edge, side) for edge, side in zip(x_edges, SIDES)]
    own, *y_edges = pl.pallas_call(
        functools.partial(y_pack_kernel, nx, ny),
        out_shape=[array(5, nx, ny), y_edge, y_edge],
        in_specs=[HBM] * 5,
        out_specs=[VMEM] * 3,
        scratch_shapes=[pltpu.SemaphoreType.DMA((5,))],
        compiler_params=limit(4),
        name="y_pack",
    )(*placed)
    y_edges = [along_y(edge, link) for edge, link in zip(y_edges, LINKS)]
    corners = pl.pallas_call(
        functools.partial(corner_kernel, ny),
        out_shape=[corner] * 2,
        in_specs=[VMEM] * 2,
        out_specs=[VMEM] * 2,
        compiler_params=limit(4),
        name="corners",
    )(*x_edges)
    corners = [along_y(corner, link) for corner, link in zip(corners, LINKS)]
    increment = time_increment.reshape(1)
    passed_in = [array(3, nx - 4, wide), array(2, nx - 4, wide), array(nx - 8, wide + 8), array(nx - 8, wide), array(3, nx - 8, ny)]
    passed_out = [array(3, 8, wide), array(2, 8, wide), array(8, wide + 8), array(8, wide), array(3, 8, ny)]
    cells, stress, state_in, passive_in, energies, *rest_in, peak = pl.pallas_call(
        functools.partial(inner_kernel, nx, ny),
        out_shape=[
            array(5, nx, ny + 20),
            array(nx - 2, tall),
            *passed_in[:2],
            array(nx - 4, wide + 8),
            *passed_in[2:],
            array(wide),
        ],
        in_specs=[SMEM] + [VMEM] * 3,
        out_specs=[VMEM] * 9,
        scratch_shapes=[
            scratch(nx - 2, tall),
            scratch(nx - 2, tall),
            scratch(3, nx - 8, wide + 8),
            scratch(3, nx - 8, wide + 8),
        ],
        compiler_params=limit(8),
        cost_estimate=pl.CostEstimate(flops=5 * 10**6, bytes_accessed=2 * 10**6, transcendentals=0),
        name="inner",
    )(increment, own, *y_edges)
    *outer, smallest = pl.pallas_call(
        functools.partial(outer_kernel, nx, ny),
        out_shape=passed_out + [array(lax.axis_size(("gx", "gy")))],
        in_specs=[SMEM] + [VMEM] * 9,
        out_specs=[VMEM] * 6,
        scratch_shapes=[
            scratch(5, 2 * LEFT, ny + 20),
            scratch(2, EDGE_KINDS + 1, ny + 20),
            scratch(10, tall),
            scratch(8, tall),
            scratch(8, tall),
            scratch(4, wide + 8),
            scratch(3, 4, wide + 8),
            scratch(3, 4, wide + 8),
            scratch(3, 4, wide + 8),
            scratch(3, 4, wide + 8),
        ],
        compiler_params=limit(8),
        name="outer",
    )(increment, *x_edges, *corners, cells, stress, state_in, energies, peak)
    outs = pl.pallas_call(
        functools.partial(carry_kernel, nx, ny),
        out_shape=[array(nx, ny)] * 5,
        in_specs=[SMEM] + [VMEM] * 10,
        out_specs=[VMEM] * 2 + [HBM] * 3,
        scratch_shapes=[
            scratch(2, nx, wide + 8),
            scratch(2, nx, wide + 8),
            pltpu.SemaphoreType.DMA((3, 3)),
        ],
        compiler_params=limit(8),
        cost_estimate=pl.CostEstimate(flops=10**7, bytes_accessed=4 * 10**6, transcendentals=0),
        name="carry",
    )(increment, state_in, passive_in, *rest_in, *outer)
    return (*outs, jnp.min(lax.all_to_all(smallest, ("gx", "gy"), 0, 0, tiled=True)))


def solution(mesh):
    cells = P("gx", "gy", None)
    return jax.shard_map(
        body,
        mesh=mesh,
        in_specs=(cells,) * 5 + (P(),),
        out_specs=(cells,) * 5 + (P(),),
        check_vma=False,
    )
```

```python
import functools

import jax
import jax.numpy as jnp
from jax import lax
from jax.experimental import pallas as pl
from jax.experimental.pallas import tpu as pltpu
from jax.sharding import PartitionSpec as P

DENSITY, ENERGY, XV, YV, ZV = range(5)
TOP = 8
LEFT = 3
SIDES = (-1, 1)
NEAR, FAR = "near", "far"
LINKS = (FAR, NEAR)
EDGE_KINDS = 4
VMEM = pl.BlockSpec(memory_space=pltpu.VMEM)
HBM = pl.BlockSpec(memory_space=pltpu.HBM)
SMEM = pl.BlockSpec(memory_space=pltpu.SMEM)


def ghost_rows(field):
    return 4 if field == YV else 3


def x_layers():
    return [(field, past) for field in range(5) for past in (1, 2)] + [(XV, 3)]


def x_edge_rows(ny):
    return (len(x_layers()) + 1) * ny + 2 * EDGE_KINDS


def y_layers(nx):
    found, offset = [], 0
    for a in range(nx):
        for field in range(5):
            found.append((field, a, ghost_rows(field), offset))
            offset += ghost_rows(field)
    return found, (offset // 8 + 2) * 8


def corner_layers():
    found, offset = [], 0
    for number, (field, past) in enumerate(x_layers()):
        found.append((number, field, past, ghost_rows(field), offset))
        offset += ghost_rows(field)
    return found, offset, -(-(offset + 1 + EDGE_KINDS) // 8) * 8


def is_low(link):
    odd = lax.rem(lax.axis_index("gy"), 2)
    return odd if link == NEAR else 1 - odd


def pick(flag, one, other):
    return flag * one + (1 - flag) * other


def along_x(value, side):
    count = lax.axis_size("gx")
    return lax.ppermute(value, "gx", [((i + side) % count, i) for i in range(count)])


def along_y(value, link):
    count = lax.axis_size("gy")
    partners = [i ^ 1 if link == NEAR else (((i - 1) ^ 1) + 1) % count for i in range(count)]
    return lax.ppermute(value, "gy", list(enumerate(partners)))


def hidden_zero():
    return lax.shift_right_logical(lax.axis_index("gx"), 20)


def span(zero, start, count, total):
    return pl.ds(start if start + -(-count // 8) * 8 > total else zero + start, count)


def per_mass(energy, spread):
    return 0.4 * energy + 0.5 * jnp.square(jnp.minimum(0.5 * spread, 0.0))


def x_pack_kernel(nx, ny, *refs):
    fields, x_edges, near, padded, arrived = refs[:5], refs[5:7], refs[7], refs[8], refs[9]
    zero = hidden_zero()
    copies = [
        pltpu.make_async_copy(
            fields[field].at[pl.ds(first, 4)], near.at[field, pl.ds(4 * k, 4)], arrived.at[field, k]
        )
        for field in range(5)
        for k, first in enumerate((nx - 4, 0))
    ]
    for copy in copies:
        copy.start()
    for current in range(5):
        for k, (side, edge) in enumerate(zip(SIDES, x_edges)):
            copies[2 * current + k].wait()
            for number, (field, past) in enumerate(x_layers()):
                if field == current:
                    edge[pl.ds(zero + number * ny, ny), :] = near[field, 4 - past if side < 0 else 3 + past]
    for k, (side, edge) in enumerate(zip(SIDES, x_edges)):
        a = 1 if side < 0 else 6
        offset = len(x_layers()) * ny
        padded[k] = jnp.zeros_like(padded[k])
        padded[k, pl.ds(TOP, ny), :] = near[YV, a]
        spread = near[XV, a + 1] - near[XV, a - 1]
        spread += padded[k, pl.ds(zero + (TOP + 1), ny), :] - padded[k, pl.ds(zero + (TOP - 1), ny), :]
        spread += up(near[ZV, a]) - down(near[ZV, a])
        edge[pl.ds(zero + offset, ny), :] = near[DENSITY, a] * per_mass(near[ENERGY, a], spread)
        offset += ny
        padded[k, pl.ds(TOP, ny), :] = spread
        for row in (0, ny - 1):
            for value in (near[DENSITY, a, pl.ds(row, 1), :], near[ENERGY, a, pl.ds(row, 1), :],
                          padded[k, pl.ds(TOP + row, 1), :], near[YV, a, pl.ds(row, 1), :]):
                edge[pl.ds(offset, 1), :] = value
                offset += 1


def y_pack_kernel(nx, ny, *refs):
    fields, own, y_edges, arrived = refs[:5], refs[5], refs[6:8], refs[8]
    zero = hidden_zero()
    copies = [
        pltpu.make_async_copy(fields[field], own.at[field, pl.ds(0, nx), pl.ds(0, ny), :], arrived.at[field])
        for field in range(5)
    ]
    for copy in copies:
        copy.start()
    for current, copy in enumerate(copies):
        copy.wait()
        for link, edge in zip(LINKS, y_edges):
            for field, a, rows, offset in y_layers(nx)[0]:
                if field == current:
                    start = pick(is_low(link), 0, ny - rows)
                    edge[pl.ds(zero + offset, rows), :] = own[field, a, pl.ds(start, rows), :]


def corner_kernel(ny, *refs):
    x_edges, outs = refs[:2], refs[2:]
    zero = hidden_zero()
    columns, singles, rows_of_corner = corner_layers()
    for link, out in zip(LINKS, outs):
        low = is_low(link)
        for k, edge in enumerate(x_edges):
            base, total = k * rows_of_corner, out.shape[0]
            for number, _, _, rows, offset in columns:
                out[span(zero, base + offset, rows, total), :] = edge[pl.ds(number * ny + pick(low, 0, ny - rows), rows), :]
            number = len(x_layers())
            out[span(zero, base + singles, 1, total), :] = edge[pl.ds(number * ny + pick(low, 1, ny - 2), 1), :]
            first, last = [
                edge[pl.ds((number + 1) * ny + k * EDGE_KINDS, EDGE_KINDS), :] for k in range(2)
            ]
            out[span(zero, base + singles + 1, EDGE_KINDS, total), :] = jnp.where(low == 1, first, last)


def limited(above, below):
    return jnp.minimum(jnp.maximum(above, jnp.minimum(below, 0.0)), jnp.maximum(below, 0.0))


def face_factors(v_minus, v, half_increment):
    courant = half_increment * (v_minus + v)
    size = jnp.abs(courant)
    return courant, 0.5 * size * (1.0 - size), courant > 0.0


def face_flux(factors, f_minus, f, s_minus, s):
    courant, slope_factor, upward = factors
    return courant * jnp.where(upward, f_minus, f) + slope_factor * jnp.where(upward, s_minus, s)


def up(value):
    return pltpu.roll(value, value.shape[-1] - 1, value.ndim - 1)


def down(value):
    return pltpu.roll(value, 1, value.ndim - 1)


def place(pieces, a):
    for ref, first, last, number in pieces:
        if first <= a < last:
            return ref, a - first + number
    raise ValueError(a)


def read(zero, pieces, a, start, count, *field):
    ref, number = place(pieces, a)
    return ref[(*field, number, pl.ds(zero + start, count), slice(None))]


def write(pieces, a, value, *field):
    ref, number = place(pieces, a)
    ref[(*field, number, pl.ds(0, value.shape[0]), slice(None))] = value


def sweep_x(state, speed, swept, fields, first, last, wide, half):
    for part in range(0, wide, 8):
        before = [state(field, first - 1, part) for field in fields]
        here = [state(field, first, part) for field in fields]
        steps = [h - b for h, b in zip(here, before)]
        slopes = [limited(st, b - state(field, first - 2, part)) for field, st, b in zip(fields, steps, before)]
        lower = None
        for a in range(first, last + 1):
            factors = face_factors(speed(a - 1, part), speed(a, part), half)
            fluxes = []
            for k, field in enumerate(fields):
                after = state(field, a + 1, part)
                step = after - here[k]
                slope = limited(step, steps[k])
                fluxes.append(face_flux(factors, before[k], here[k], slopes[k], slope))
                if lower is not None:
                    swept[field, a - 1 - first, pl.ds(part, 8)] = before[k] - (fluxes[k] - lower[k])
                before[k], here[k], steps[k], slopes[k] = here[k], after, step, slope
            lower = fluxes


def sweep_y(zero, swept, work, numbers, fields, factors, wide):
    cases = [(number, field) for number in numbers for field in fields]

    def rows(number, field, start):
        return swept[field, number, pl.ds(zero + start, wide)]

    for number, field in cases:
        start = [rows(number, field, first) for first in range(4)]
        steps = [after - before for before, after in zip(start, start[1:])]
        slopes = [limited(after, before) for before, after in zip(steps, steps[1:])]
        work[field, number, 0:wide] = face_flux(factors[number], start[1], start[2], *slopes)
    moved = {}
    for number, field in cases:
        flux, above = [work[field, number, pl.ds(zero + start, wide)] for start in (0, 1)]
        moved[number, field] = rows(number, field, 2) - (above - flux)
    return [[moved[number, field] for field in fields] for number in numbers]


def sweep_z(moved, factors):
    final = []
    for value in moved:
        below, above = down(value), up(value)
        step = value - below
        slopes = limited(step, below - pltpu.roll(value, 2, 1)), limited(above - value, step)
        flux = face_flux(factors, below, value, *slopes)
        final.append(value - (up(flux) - flux))
    return final


def spread_columns(zero, columns, tall, half, cells, stress, heat, growth):
    for a in columns:
        z = read(zero, cells, a, TOP - 4, tall, ZV)
        spread = (
            read(zero, cells, a + 1, TOP - 4, tall, XV)
            - read(zero, cells, a - 1, TOP - 4, tall, XV)
            + (read(zero, cells, a, TOP - 3, tall, YV) - read(zero, cells, a, TOP - 5, tall, YV))
            + (up(z) - down(z))
        )
        warmth = per_mass(read(zero, cells, a, TOP - 4, tall, ENERGY), spread)
        write(heat, a, warmth)
        write(stress, a, read(zero, cells, a, TOP - 4, tall, DENSITY) * warmth)
        write(growth, a, half * spread)


def advance_columns(zero, columns, wide, half, cells, stress, heat, growth, passive, state, energies, nx):
    for a in columns:
        density, energy, x, y, z = [read(zero, cells, a, TOP - 2, wide, field) for field in range(5)]
        grown = read(zero, growth, a, 2, wide)
        centre = read(zero, stress, a, 2, wide)
        scale = half / density
        density_one = density / (1.0 + grown)
        energy = energy - read(zero, heat, a, 2, wide) * grown
        write(passive, a, density_one, 0)
        write(passive, a, density_one * energy, 1)
        write(state, a, x - scale * (read(zero, stress, a + 1, 2, wide) - read(zero, stress, a - 1, 2, wide)), 0)
        write(state, a, y - scale * (read(zero, stress, a, 3, wide) - read(zero, stress, a, 1, wide)), 1)
        write(state, a, z - scale * (up(centre) - down(centre)), 2)
        if 0 <= a < nx:
            write(energies, a, energy)


def flow_columns(zero, first, last, ny, half, state, energies, swept, work, speed_y, speed_z, flows):
    wide = ny + 4
    sweep_x(
        lambda field, a, part: read(zero, state, a, part, 8, field),
        lambda a, part: read(zero, state, a, part, 8, 0),
        swept, (0, 1, 2), first, last, wide, half,
    )
    numbers = range(last - first)
    factors = []
    for number in numbers:
        below, here = [swept[1, number, pl.ds(zero + start, wide)] for start in (1, 2)]
        factors.append(face_factors(below, here, half))
        write(speed_y, first + number, swept[1, number, 0:wide])
    peak = None
    for a, moved in zip(range(first, last), sweep_y(zero, swept, work, numbers, (0, 1, 2), factors, wide)):
        write(speed_z, a, moved[2])
        final = sweep_z(moved, face_factors(down(moved[2]), moved[2], half))
        for field in range(3):
            write(flows, a, final[field][:ny], field)
        signal = (
            jnp.sqrt(0.56 * read(zero, energies, a, 2, wide))
            + jnp.abs(final[0])
            + jnp.abs(final[1])
            + jnp.abs(final[2])
        )
        peak = signal if peak is None else jnp.maximum(peak, signal)
    return peak


def inner_kernel(nx, ny, dt_ref, *refs):
    own, y_edges = refs[0], refs[1:3]
    cells, stress, state, passive, energies, speed_y, speed_z, flows, peak_ref = refs[3:12]
    heat, growth, swept, work = refs[12:]
    zero = hidden_zero()
    half = 0.5 * dt_ref[0]
    for field in range(5):
        for a in range(nx):
            cells[field, a, pl.ds(TOP, ny), :] = own[field, a, pl.ds(0, ny), :]
    for link, edge in zip(LINKS, y_edges):
        low = is_low(link)
        for field, a, rows, offset in y_layers(nx)[0]:
            cells[field, a, pl.ds(TOP + pick(low, -rows, ny), rows), :] = edge[pl.ds(zero + offset, rows), :]
    cells = [(cells, 0, nx, 0)]
    stress, heat, growth = [[(ref, 1, nx - 1, 0)] for ref in (stress, heat, growth)]
    state, passive, energies = [[(ref, 2, nx - 2, 0)] for ref in (state, passive, energies)]
    speed_y, speed_z, flows = [[(ref, 4, nx - 4, 0)] for ref in (speed_y, speed_z, flows)]
    spread_columns(zero, range(1, nx - 1), ny + 12, half, cells, stress, heat, growth)
    advance_columns(
        zero, range(2, nx - 2), ny + 4, half, cells, stress, heat, growth, passive, state, energies, nx
    )
    peak_ref[...] = flow_columns(
        zero, 4, nx - 4, ny, half, state, energies, swept, work, speed_y, speed_z, flows
    )


def outer_pieces(ref, nx, reach, inside):
    return [(ref, -reach, inside, 0), (ref, nx - inside, nx + reach, reach + inside)]


def outer_kernel(nx, ny, dt_ref, *refs):
    x_edges, corners = refs[0:2], refs[2:4]
    cells_in, stress_in, state_in, energies_in, peak_in = refs[4:9]
    state_out, passive_out, speed_y, speed_z, flows, increment_ref = refs[9:15]
    beyond, third, stress_out, heat, growth, energies_out = refs[15:21]
    swept, work = refs[21:23], refs[23:25]
    nz = increment_ref.shape[-1]
    zero = hidden_zero()
    half = 0.5 * dt_ref[0]
    wide, tall = ny + 4, ny + 12

    columns, singles, rows_of_corner = corner_layers()
    for k, (side, edge) in enumerate(zip(SIDES, x_edges)):
        for number, (field, past) in enumerate(x_layers()):
            column = LEFT - past if side < 0 else LEFT - 1 + past
            beyond[field, column, pl.ds(TOP, ny), :] = edge[pl.ds(zero + number * ny, ny), :]
        offset = len(x_layers()) * ny
        third[k, EDGE_KINDS, pl.ds(TOP, ny), :] = edge[pl.ds(zero + offset, ny), :]
        offset += ny
        for row in (0, ny - 1):
            for kind in range(EDGE_KINDS):
                third[k, kind, pl.ds(TOP + row, 1), :] = edge[pl.ds(offset, 1), :]
                offset += 1
    for link, corner in zip(LINKS, corners):
        low = is_low(link)
        for k, side in enumerate(SIDES):
            base, total = k * rows_of_corner, corner.shape[0]
            for _, field, past, rows, offset in columns:
                column = LEFT - past if side < 0 else LEFT - 1 + past
                to = pl.ds(TOP + pick(low, -rows, ny), rows)
                beyond[field, column, to, :] = corner[span(zero, base + offset, rows, total), :]
            to = pl.ds(TOP + pick(low, -2, ny + 1), 1)
            third[k, EDGE_KINDS, to, :] = corner[span(zero, base + singles, 1, total), :]
            for kind in range(EDGE_KINDS):
                to = pl.ds(TOP + pick(low, -1, ny), 1)
                third[k, kind, to, :] = corner[span(zero, base + singles + 1 + kind, 1, total), :]

    cells = [(cells_in, 0, nx, 0)] + outer_pieces(beyond, nx, LEFT, 0)
    stress = outer_pieces(stress_out, nx, 3, 2) + [(stress_in, 2, nx - 2, 1)]
    heat, growth = outer_pieces(heat, nx, 2, 2), outer_pieces(growth, nx, 2, 2)
    state = outer_pieces(state_out, nx, 2, 2) + [(state_in, 2, nx - 2, 0)]
    passive = outer_pieces(passive_out, nx, 2, 2)
    energies = outer_pieces(energies_out, nx, 0, 2) + [(energies_in, 2, nx - 2, 0)]
    speed_y, speed_z, flows = [outer_pieces(ref, nx, 0, 4) for ref in (speed_y, speed_z, flows)]

    row = lax.broadcasted_iota(jnp.int32, (tall, nz), 0) - 4
    for k, a in enumerate((-3, nx + 2)):
        above, below = [third[k, 3, pl.ds(zero + start, tall)] for start in (TOP - 3, TOP - 5)]
        density, energy, spread, _, whole = [third[k, kind, pl.ds(zero + TOP - 4, tall)] for kind in range(5)]
        spread += jnp.where((row == -1) | (row == ny - 1), above, -below)
        split = (row == -1) | (row == 0) | (row == ny - 1) | (row == ny)
        write(stress, a, jnp.where(split, density * per_mass(energy, spread), whole))

    ends = (*range(-2, 2), *range(nx - 2, nx + 2))
    spread_columns(zero, ends, tall, half, cells, stress, heat, growth)
    advance_columns(zero, ends, wide, half, cells, stress, heat, growth, passive, state, energies, nx)
    peak = peak_in[...]
    for k, first in enumerate((0, nx - 4)):
        peak = jnp.maximum(
            peak,
            flow_columns(
                zero, first, first + 4, ny, half, state, energies, swept[k], work[k], speed_y, speed_z, flows
            ),
        )
    peak = jnp.max(jnp.where(row[4 : 4 + wide] < ny, peak, 0.0), axis=0, keepdims=True)
    increment_ref[...] = jnp.broadcast_to(0.3 / peak, increment_ref.shape)


def carry_kernel(nx, ny, dt_ref, *refs):
    state_in, passive_in, speed_y_in, speed_z_in, flows_in = refs[0:5]
    state_out, passive_out, speed_y_out, speed_z_out, flows_out = refs[5:10]
    density_out, energy_out, flow_outs, swept, work, written = refs[10], refs[11], refs[12:15], refs[15], refs[16], refs[17]
    zero = hidden_zero()
    half = 0.5 * dt_ref[0]
    wide = ny + 4
    copies = []
    for k in range(3):
        for piece, (ref, first, last, number) in enumerate([(flows_in, 4, nx - 4, 0)] + outer_pieces(flows_out, nx, 0, 4)):
            source = ref.at[k, pl.ds(number, last - first)]
            copies.append(
                pltpu.make_async_copy(source, flow_outs[k].at[pl.ds(first, last - first)], written.at[k, piece])
            )
    for copy in copies:
        copy.start()
    state = outer_pieces(state_out, nx, 2, 2) + [(state_in, 2, nx - 2, 0)]
    passive = outer_pieces(passive_out, nx, 2, 2) + [(passive_in, 2, nx - 2, 0)]
    speed_y = outer_pieces(speed_y_out, nx, 0, 4) + [(speed_y_in, 4, nx - 4, 0)]
    speed_z = outer_pieces(speed_z_out, nx, 0, 4) + [(speed_z_in, 4, nx - 4, 0)]
    sweep_x(
        lambda field, a, part: read(zero, passive, a, part, 8, field),
        lambda a, part: read(zero, state, a, part, 8, 0),
        swept, (0, 1), 0, nx, wide, half,
    )
    factors = [face_factors(*[read(zero, speed_y, a, start, wide) for start in (1, 2)], half) for a in range(nx)]
    for a, moved in enumerate(sweep_y(zero, swept, work, range(nx), (0, 1), factors, wide)):
        along = read(zero, speed_z, a, 0, wide)
        final = sweep_z(moved, face_factors(down(along), along, half))
        density_out[a] = final[0][:ny]
        energy_out[a] = final[1][:ny]
    for copy in copies:
        copy.wait()


def body(density0, energy0, x_velocity, y_velocity, z_velocity, time_increment):
    nx, ny, nz = density0.shape
    fields = (density0, energy0, x_velocity, y_velocity, z_velocity)
    wide, tall = ny + 4, ny + 12

    def array(*shape):
        return jax.ShapeDtypeStruct((*shape, nz), jnp.float32)

    def scratch(*shape):
        return pltpu.VMEM((*shape, nz), jnp.float32)

    def limit(mebibytes):
        return pltpu.CompilerParams(vmem_limit_bytes=mebibytes * 1024 * 1024)

    x_edge, y_edge, corner = array(x_edge_rows(ny)), array(y_layers(nx)[1]), array(2 * corner_layers()[2])
    placed = [pltpu.with_memory_space_constraint(field, pltpu.HBM) for field in fields]
    x_edges = pl.pallas_call(
        functools.partial(x_pack_kernel, nx, ny),
        out_shape=[x_edge] * 2,
        in_specs=[HBM] * 5,
        out_specs=[VMEM] * 2,
        scratch_shapes=[scratch(5, 8, ny), scratch(2, ny + 20), pltpu.SemaphoreType.DMA((5, 2))],
        compiler_params=limit(4),
        name="x_pack",
    )(*placed)
    x_edges = [along_x(edge, side) for edge, side in zip(x_edges, SIDES)]
    own, *y_edges = pl.pallas_call(
        functools.partial(y_pack_kernel, nx, ny),
        out_shape=[array(5, nx, ny + 12), y_edge, y_edge],
        in_specs=[HBM] * 5,
        out_specs=[VMEM] * 3,
        scratch_shapes=[pltpu.SemaphoreType.DMA((5,))],
        compiler_params=limit(4),
        name="y_pack",
    )(*placed)
    y_edges = [along_y(edge, link) for edge, link in zip(y_edges, LINKS)]
    corners = pl.pallas_call(
        functools.partial(corner_kernel, ny),
        out_shape=[corner] * 2,
        in_specs=[VMEM] * 2,
        out_specs=[VMEM] * 2,
        compiler_params=limit(4),
        name="corners",
    )(*x_edges)
    corners = [along_y(corner, link) for corner, link in zip(corners, LINKS)]
    increment = time_increment.reshape(1)
    passed_in = [array(3, nx - 4, wide), array(2, nx - 4, wide), array(nx - 8, wide + 8), array(nx - 8, wide), array(3, nx - 8, ny)]
    passed_out = [array(3, 8, wide), array(2, 8, wide), array(8, wide + 8), array(8, wide), array(3, 8, ny)]
    cells, stress, state_in, passive_in, energies, *rest_in, peak = pl.pallas_call(
        functools.partial(inner_kernel, nx, ny),
        out_shape=[
            array(5, nx, ny + 20),
            array(nx - 2, tall),
            *passed_in[:2],
            array(nx - 4, wide + 8),
            *passed_in[2:],
            array(wide),
        ],
        in_specs=[SMEM] + [VMEM] * 3,
        out_specs=[VMEM] * 9,
        scratch_shapes=[
            scratch(nx - 2, tall),
            scratch(nx - 2, tall),
            scratch(3, nx - 8, wide + 8),
            scratch(3, nx - 8, wide + 8),
        ],
        compiler_params=limit(8),
        cost_estimate=pl.CostEstimate(flops=5 * 10**6, bytes_accessed=2 * 10**6, transcendentals=0),
        name="inner",
    )(increment, own, *y_edges)
    *outer, smallest = pl.pallas_call(
        functools.partial(outer_kernel, nx, ny),
        out_shape=passed_out + [array(lax.axis_size(("gx", "gy")))],
        in_specs=[SMEM] + [VMEM] * 9,
        out_specs=[VMEM] * 6,
        scratch_shapes=[
            scratch(5, 2 * LEFT, ny + 20),
            scratch(2, EDGE_KINDS + 1, ny + 20),
            scratch(10, tall),
            scratch(8, tall),
            scratch(8, tall),
            scratch(4, wide + 8),
            scratch(3, 4, wide + 8),
            scratch(3, 4, wide + 8),
            scratch(3, 4, wide + 8),
            scratch(3, 4, wide + 8),
        ],
        compiler_params=limit(8),
        name="outer",
    )(increment, *x_edges, *corners, cells, stress, state_in, energies, peak)
    outs = pl.pallas_call(
        functools.partial(carry_kernel, nx, ny),
        out_shape=[array(nx, ny)] * 5,
        in_specs=[SMEM] + [VMEM] * 10,
        out_specs=[VMEM] * 2 + [HBM] * 3,
        scratch_shapes=[
            scratch(2, nx, wide + 8),
            scratch(2, nx, wide + 8),
            pltpu.SemaphoreType.DMA((3, 3)),
        ],
        compiler_params=limit(8),
        cost_estimate=pl.CostEstimate(flops=10**7, bytes_accessed=4 * 10**6, transcendentals=0),
        name="carry",
    )(increment, state_in, passive_in, *rest_in, *outer)
    return (*outs, jnp.min(lax.all_to_all(smallest, ("gx", "gy"), 0, 0, tiled=True)))


def solution(mesh):
    cells = P("gx", "gy", None)
    return jax.shard_map(
        body,
        mesh=mesh,
        in_specs=(cells,) * 5 + (P(),),
        out_specs=(cells,) * 5 + (P(),),
        check_vma=False,
    )
```

```python
import functools

import jax
import jax.numpy as jnp
from jax import lax
from jax.experimental import pallas as pl
from jax.experimental.pallas import tpu as pltpu
from jax.sharding import PartitionSpec as P

DENSITY, ENERGY, XV, YV, ZV = range(5)
TOP = 8
LEFT = 3
SIDES = (-1, 1)
NEAR, FAR = "near", "far"
LINKS = (FAR, NEAR)
EDGE_KINDS = 4
VMEM = pl.BlockSpec(memory_space=pltpu.VMEM)
HBM = pl.BlockSpec(memory_space=pltpu.HBM)
SMEM = pl.BlockSpec(memory_space=pltpu.SMEM)


def ghost_rows(field):
    return 4 if field == YV else 3


def x_layers():
    return [(field, past) for field in range(5) for past in (1, 2)] + [(XV, 3)]


def x_edge_rows(ny):
    return (len(x_layers()) + 1) * ny + 2 * EDGE_KINDS


def y_layers(nx):
    found, offset = [], 0
    for a in range(nx):
        for field in range(5):
            found.append((field, a, ghost_rows(field), offset))
            offset += ghost_rows(field)
    return found, (offset // 8 + 2) * 8


def corner_layers():
    found, offset = [], 0
    for number, (field, past) in enumerate(x_layers()):
        found.append((number, field, past, ghost_rows(field), offset))
        offset += ghost_rows(field)
    return found, offset, -(-(offset + 1 + EDGE_KINDS) // 8) * 8


def is_low(link):
    odd = lax.rem(lax.axis_index("gy"), 2)
    return odd if link == NEAR else 1 - odd


def pick(flag, one, other):
    return flag * one + (1 - flag) * other


def along_x(value, side):
    count = lax.axis_size("gx")
    return lax.ppermute(value, "gx", [((i + side) % count, i) for i in range(count)])


def along_y(value, link):
    count = lax.axis_size("gy")
    partners = [i ^ 1 if link == NEAR else (((i - 1) ^ 1) + 1) % count for i in range(count)]
    return lax.ppermute(value, "gy", list(enumerate(partners)))


def hidden_zero():
    return lax.shift_right_logical(lax.axis_index("gx"), 20)


def span(zero, start, count, total):
    return pl.ds(start if start + -(-count // 8) * 8 > total else zero + start, count)


def per_mass(energy, spread):
    return 0.4 * energy + 0.5 * jnp.square(jnp.minimum(0.5 * spread, 0.0))


def x_pack_kernel(nx, ny, *refs):
    fields, x_edges, near, padded, arrived = refs[:5], refs[5:7], refs[7], refs[8], refs[9]
    zero = hidden_zero()
    order = (ZV, YV, XV, ENERGY, DENSITY)
    copies = {
        (field, k): pltpu.make_async_copy(
            fields[field].at[pl.ds(first, 4)], near.at[field, pl.ds(4 * k, 4)], arrived.at[field, k]
        )
        for field in order
        for k, first in enumerate((nx - 4, 0))
    }
    for copy in copies.values():
        copy.start()
    thirds = (1, 6)
    for current in order:
        for k, (side, edge) in enumerate(zip(SIDES, x_edges)):
            copies[current, k].wait()
            if current == ZV:
                padded[k] = jnp.zeros_like(padded[k])
                padded[2 + k, pl.ds(TOP, ny), :] = up(near[ZV, thirds[k]]) - down(near[ZV, thirds[k]])
            if current == YV:
                padded[k, pl.ds(TOP, ny), :] = near[YV, thirds[k]]
            for number, (field, past) in enumerate(x_layers()):
                if field == current:
                    edge[pl.ds(zero + number * ny, ny), :] = near[field, 4 - past if side < 0 else 3 + past]
    for k, edge in enumerate(x_edges):
        a = thirds[k]
        offset = len(x_layers()) * ny
        spread = near[XV, a + 1] - near[XV, a - 1]
        spread += padded[k, pl.ds(zero + (TOP + 1), ny), :] - padded[k, pl.ds(zero + (TOP - 1), ny), :]
        spread += padded[2 + k, pl.ds(TOP, ny), :]
        edge[pl.ds(zero + offset, ny), :] = near[DENSITY, a] * per_mass(near[ENERGY, a], spread)
        offset += ny
        padded[2 + k, pl.ds(TOP, ny), :] = spread
        for row in (0, ny - 1):
            for value in (near[DENSITY, a, pl.ds(row, 1), :], near[ENERGY, a, pl.ds(row, 1), :],
                          padded[2 + k, pl.ds(TOP + row, 1), :], near[YV, a, pl.ds(row, 1), :]):
                edge[pl.ds(offset, 1), :] = value
                offset += 1


def y_pack_kernel(nx, ny, *refs):
    fields, own, y_edges, arrived = refs[:5], refs[5], refs[6:8], refs[8]
    zero = hidden_zero()
    copies = [
        pltpu.make_async_copy(fields[field], own.at[field, pl.ds(0, nx), pl.ds(0, ny), :], arrived.at[field])
        for field in range(5)
    ]
    for copy in copies:
        copy.start()
    for current, copy in enumerate(copies):
        copy.wait()
        for link, edge in zip(LINKS, y_edges):
            for field, a, rows, offset in y_layers(nx)[0]:
                if field == current:
                    start = pick(is_low(link), 0, ny - rows)
                    edge[pl.ds(zero + offset, rows), :] = own[field, a, pl.ds(start, rows), :]


def corner_kernel(ny, *refs):
    x_edges, outs = refs[:2], refs[2:]
    zero = hidden_zero()
    columns, singles, rows_of_corner = corner_layers()
    for link, out in zip(LINKS, outs):
        low = is_low(link)
        for k, edge in enumerate(x_edges):
            base, total = k * rows_of_corner, out.shape[0]
            for number, _, _, rows, offset in columns:
                out[span(zero, base + offset, rows, total), :] = edge[pl.ds(number * ny + pick(low, 0, ny - rows), rows), :]
            number = len(x_layers())
            out[span(zero, base + singles, 1, total), :] = edge[pl.ds(number * ny + pick(low, 1, ny - 2), 1), :]
            first, last = [
                edge[pl.ds((number + 1) * ny + k * EDGE_KINDS, EDGE_KINDS), :] for k in range(2)
            ]
            out[span(zero, base + singles + 1, EDGE_KINDS, total), :] = jnp.where(low == 1, first, last)


def limited(above, below):
    return jnp.minimum(jnp.maximum(above, jnp.minimum(below, 0.0)), jnp.maximum(below, 0.0))


def face_factors(v_minus, v, half_increment):
    courant = half_increment * (v_minus + v)
    size = jnp.abs(courant)
    return courant, 0.5 * size * (1.0 - size), courant > 0.0


def face_flux(factors, f_minus, f, s_minus, s):
    courant, slope_factor, upward = factors
    return courant * jnp.where(upward, f_minus, f) + slope_factor * jnp.where(upward, s_minus, s)


def up(value):
    return pltpu.roll(value, value.shape[-1] - 1, value.ndim - 1)


def down(value):
    return pltpu.roll(value, 1, value.ndim - 1)


def place(pieces, a):
    for ref, first, last, number in pieces:
        if first <= a < last:
            return ref, a - first + number
    raise ValueError(a)


def read(zero, pieces, a, start, count, *field):
    ref, number = place(pieces, a)
    return ref[(*field, number, pl.ds(zero + start, count), slice(None))]


def write(pieces, a, value, *field):
    ref, number = place(pieces, a)
    ref[(*field, number, pl.ds(0, value.shape[0]), slice(None))] = value


def sweep_x(state, speed, swept, fields, first, last, wide, half):
    for part in range(0, wide, 8):
        before = [state(field, first - 1, part) for field in fields]
        here = [state(field, first, part) for field in fields]
        steps = [h - b for h, b in zip(here, before)]
        slopes = [limited(st, b - state(field, first - 2, part)) for field, st, b in zip(fields, steps, before)]
        lower = None
        for a in range(first, last + 1):
            factors = face_factors(speed(a - 1, part), speed(a, part), half)
            fluxes = []
            for k, field in enumerate(fields):
                after = state(field, a + 1, part)
                step = after - here[k]
                slope = limited(step, steps[k])
                fluxes.append(face_flux(factors, before[k], here[k], slopes[k], slope))
                if lower is not None:
                    swept[field, a - 1 - first, pl.ds(part, 8)] = before[k] - (fluxes[k] - lower[k])
                before[k], here[k], steps[k], slopes[k] = here[k], after, step, slope
            lower = fluxes


def sweep_y(zero, swept, work, numbers, fields, factors, wide):
    cases = [(number, field) for number in numbers for field in fields]

    def rows(number, field, start):
        return swept[field, number, pl.ds(zero + start, wide)]

    for number, field in cases:
        start = [rows(number, field, first) for first in range(4)]
        steps = [after - before for before, after in zip(start, start[1:])]
        slopes = [limited(after, before) for before, after in zip(steps, steps[1:])]
        work[field, number, 0:wide] = face_flux(factors[number], start[1], start[2], *slopes)
    moved = {}
    for number, field in cases:
        flux, above = [work[field, number, pl.ds(zero + start, wide)] for start in (0, 1)]
        moved[number, field] = rows(number, field, 2) - (above - flux)
    return [[moved[number, field] for field in fields] for number in numbers]


def sweep_z(moved, factors):
    final = []
    for value in moved:
        below, above = down(value), up(value)
        step = value - below
        slopes = limited(step, below - pltpu.roll(value, 2, 1)), limited(above - value, step)
        flux = face_flux(factors, below, value, *slopes)
        final.append(value - (up(flux) - flux))
    return final


def spread_columns(zero, columns, tall, half, cells, stress, heat, growth):
    for a in columns:
        z = read(zero, cells, a, TOP - 4, tall, ZV)
        spread = (
            read(zero, cells, a + 1, TOP - 4, tall, XV)
            - read(zero, cells, a - 1, TOP - 4, tall, XV)
            + (read(zero, cells, a, TOP - 3, tall, YV) - read(zero, cells, a, TOP - 5, tall, YV))
            + (up(z) - down(z))
        )
        warmth = per_mass(read(zero, cells, a, TOP - 4, tall, ENERGY), spread)
        write(heat, a, warmth)
        write(stress, a, read(zero, cells, a, TOP - 4, tall, DENSITY) * warmth)
        write(growth, a, half * spread)


def advance_columns(zero, columns, wide, half, cells, stress, heat, growth, passive, state, energies, nx):
    for a in columns:
        density, energy, x, y, z = [read(zero, cells, a, TOP - 2, wide, field) for field in range(5)]
        grown = read(zero, growth, a, 2, wide)
        centre = read(zero, stress, a, 2, wide)
        scale = half / density
        density_one = density / (1.0 + grown)
        energy = energy - read(zero, heat, a, 2, wide) * grown
        write(passive, a, density_one, 0)
        write(passive, a, density_one * energy, 1)
        write(state, a, x - scale * (read(zero, stress, a + 1, 2, wide) - read(zero, stress, a - 1, 2, wide)), 0)
        write(state, a, y - scale * (read(zero, stress, a, 3, wide) - read(zero, stress, a, 1, wide)), 1)
        write(state, a, z - scale * (up(centre) - down(centre)), 2)
        if 0 <= a < nx:
            write(energies, a, energy)


def flow_columns(zero, first, last, ny, half, state, energies, swept, work, speed_y, speed_z, flows):
    wide = ny + 4
    sweep_x(
        lambda field, a, part: read(zero, state, a, part, 8, field),
        lambda a, part: read(zero, state, a, part, 8, 0),
        swept, (0, 1, 2), first, last, wide, half,
    )
    numbers = range(last - first)
    factors = []
    for number in numbers:
        below, here = [swept[1, number, pl.ds(zero + start, wide)] for start in (1, 2)]
        factors.append(face_factors(below, here, half))
        write(speed_y, first + number, swept[1, number, 0:wide])
    peak = None
    for a, moved in zip(range(first, last), sweep_y(zero, swept, work, numbers, (0, 1, 2), factors, wide)):
        write(speed_z, a, moved[2])
        final = sweep_z(moved, face_factors(down(moved[2]), moved[2], half))
        for field in range(3):
            write(flows, a, final[field][:ny], field)
        signal = (
            jnp.sqrt(0.56 * read(zero, energies, a, 2, wide))
            + jnp.abs(final[0])
            + jnp.abs(final[1])
            + jnp.abs(final[2])
        )
        peak = signal if peak is None else jnp.maximum(peak, signal)
    return peak


def inner_kernel(nx, ny, dt_ref, *refs):
    own, y_edges = refs[0], refs[1:3]
    cells, stress, state, passive, energies, speed_y, speed_z, flows, peak_ref = refs[3:12]
    heat, growth, swept, work = refs[12:]
    zero = hidden_zero()
    half = 0.5 * dt_ref[0]
    for field in range(5):
        for a in range(nx):
            cells[field, a, pl.ds(TOP, ny), :] = own[field, a, pl.ds(0, ny), :]
    for link, edge in zip(LINKS, y_edges):
        low = is_low(link)
        for field, a, rows, offset in y_layers(nx)[0]:
            cells[field, a, pl.ds(TOP + pick(low, -rows, ny), rows), :] = edge[pl.ds(zero + offset, rows), :]
    cells = [(cells, 0, nx, 0)]
    stress, heat, growth = [[(ref, 1, nx - 1, 0)] for ref in (stress, heat, growth)]
    state, passive, energies = [[(ref, 2, nx - 2, 0)] for ref in (state, passive, energies)]
    speed_y, speed_z, flows = [[(ref, 4, nx - 4, 0)] for ref in (speed_y, speed_z, flows)]
    spread_columns(zero, range(1, nx - 1), ny + 12, half, cells, stress, heat, growth)
    advance_columns(
        zero, range(2, nx - 2), ny + 4, half, cells, stress, heat, growth, passive, state, energies, nx
    )
    peak_ref[...] = flow_columns(
        zero, 4, nx - 4, ny, half, state, energies, swept, work, speed_y, speed_z, flows
    )


def outer_pieces(ref, nx, reach, inside):
    return [(ref, -reach, inside, 0), (ref, nx - inside, nx + reach, reach + inside)]


def outer_kernel(nx, ny, dt_ref, *refs):
    x_edges, corners = refs[0:2], refs[2:4]
    cells_in, stress_in, state_in, energies_in, peak_in = refs[4:9]
    state_out, passive_out, speed_y, speed_z, flows, increment_ref = refs[9:15]
    beyond, third, stress_out, heat, growth, energies_out = refs[15:21]
    swept, work = refs[21:23], refs[23:25]
    nz = increment_ref.shape[-1]
    zero = hidden_zero()
    half = 0.5 * dt_ref[0]
    wide, tall = ny + 4, ny + 12

    columns, singles, rows_of_corner = corner_layers()
    for k, (side, edge) in enumerate(zip(SIDES, x_edges)):
        for number, (field, past) in enumerate(x_layers()):
            column = LEFT - past if side < 0 else LEFT - 1 + past
            beyond[field, column, pl.ds(TOP, ny), :] = edge[pl.ds(zero + number * ny, ny), :]
        offset = len(x_layers()) * ny
        third[k, EDGE_KINDS, pl.ds(TOP, ny), :] = edge[pl.ds(zero + offset, ny), :]
        offset += ny
        for row in (0, ny - 1):
            for kind in range(EDGE_KINDS):
                third[k, kind, pl.ds(TOP + row, 1), :] = edge[pl.ds(offset, 1), :]
                offset += 1
    for link, corner in zip(LINKS, corners):
        low = is_low(link)
        for k, side in enumerate(SIDES):
            base, total = k * rows_of_corner, corner.shape[0]
            for _, field, past, rows, offset in columns:
                column = LEFT - past if side < 0 else LEFT - 1 + past
                to = pl.ds(TOP + pick(low, -rows, ny), rows)
                beyond[field, column, to, :] = corner[span(zero, base + offset, rows, total), :]
            to = pl.ds(TOP + pick(low, -2, ny + 1), 1)
            third[k, EDGE_KINDS, to, :] = corner[span(zero, base + singles, 1, total), :]
            for kind in range(EDGE_KINDS):
                to = pl.ds(TOP + pick(low, -1, ny), 1)
                third[k, kind, to, :] = corner[span(zero, base + singles + 1 + kind, 1, total), :]

    cells = [(cells_in, 0, nx, 0)] + outer_pieces(beyond, nx, LEFT, 0)
    stress = outer_pieces(stress_out, nx, 3, 2) + [(stress_in, 2, nx - 2, 1)]
    heat, growth = outer_pieces(heat, nx, 2, 2), outer_pieces(growth, nx, 2, 2)
    state = outer_pieces(state_out, nx, 2, 2) + [(state_in, 2, nx - 2, 0)]
    passive = outer_pieces(passive_out, nx, 2, 2)
    energies = outer_pieces(energies_out, nx, 0, 2) + [(energies_in, 2, nx - 2, 0)]
    speed_y, speed_z, flows = [outer_pieces(ref, nx, 0, 4) for ref in (speed_y, speed_z, flows)]

    row = lax.broadcasted_iota(jnp.int32, (tall, nz), 0) - 4
    for k, a in enumerate((-3, nx + 2)):
        above, below = [third[k, 3, pl.ds(zero + start, tall)] for start in (TOP - 3, TOP - 5)]
        density, energy, spread, _, whole = [third[k, kind, pl.ds(zero + TOP - 4, tall)] for kind in range(5)]
        spread += jnp.where((row == -1) | (row == ny - 1), above, -below)
        split = (row == -1) | (row == 0) | (row == ny - 1) | (row == ny)
        write(stress, a, jnp.where(split, density * per_mass(energy, spread), whole))

    ends = (*range(-2, 2), *range(nx - 2, nx + 2))
    spread_columns(zero, ends, tall, half, cells, stress, heat, growth)
    advance_columns(zero, ends, wide, half, cells, stress, heat, growth, passive, state, energies, nx)
    peak = peak_in[...]
    for k, first in enumerate((0, nx - 4)):
        peak = jnp.maximum(
            peak,
            flow_columns(
                zero, first, first + 4, ny, half, state, energies, swept[k], work[k], speed_y, speed_z, flows
            ),
        )
    peak = jnp.max(jnp.where(row[4 : 4 + wide] < ny, peak, 0.0), axis=0, keepdims=True)
    increment_ref[...] = jnp.broadcast_to(0.3 / peak, increment_ref.shape)


def carry_kernel(nx, ny, dt_ref, *refs):
    state_in, passive_in, speed_y_in, speed_z_in, flows_in = refs[0:5]
    state_out, passive_out, speed_y_out, speed_z_out, flows_out = refs[5:10]
    density_out, energy_out, flow_outs, swept, work, written = refs[10], refs[11], refs[12:15], refs[15], refs[16], refs[17]
    zero = hidden_zero()
    half = 0.5 * dt_ref[0]
    wide = ny + 4
    copies = []
    for k in range(3):
        for piece, (ref, first, last, number) in enumerate([(flows_in, 4, nx - 4, 0)] + outer_pieces(flows_out, nx, 0, 4)):
            source = ref.at[k, pl.ds(number, last - first)]
            copies.append(
                pltpu.make_async_copy(source, flow_outs[k].at[pl.ds(first, last - first)], written.at[k, piece])
            )
    for copy in copies:
        copy.start()
    state = outer_pieces(state_out, nx, 2, 2) + [(state_in, 2, nx - 2, 0)]
    passive = outer_pieces(passive_out, nx, 2, 2) + [(passive_in, 2, nx - 2, 0)]
    speed_y = outer_pieces(speed_y_out, nx, 0, 4) + [(speed_y_in, 4, nx - 4, 0)]
    speed_z = outer_pieces(speed_z_out, nx, 0, 4) + [(speed_z_in, 4, nx - 4, 0)]
    sweep_x(
        lambda field, a, part: read(zero, passive, a, part, 8, field),
        lambda a, part: read(zero, state, a, part, 8, 0),
        swept, (0, 1), 0, nx, wide, half,
    )
    factors = [face_factors(*[read(zero, speed_y, a, start, wide) for start in (1, 2)], half) for a in range(nx)]
    for a, moved in enumerate(sweep_y(zero, swept, work, range(nx), (0, 1), factors, wide)):
        along = read(zero, speed_z, a, 0, wide)
        final = sweep_z(moved, face_factors(down(along), along, half))
        density_out[a] = final[0][:ny]
        energy_out[a] = final[1][:ny]
    for copy in copies:
        copy.wait()


def body(density0, energy0, x_velocity, y_velocity, z_velocity, time_increment):
    nx, ny, nz = density0.shape
    fields = (density0, energy0, x_velocity, y_velocity, z_velocity)
    wide, tall = ny + 4, ny + 12

    def array(*shape):
        return jax.ShapeDtypeStruct((*shape, nz), jnp.float32)

    def scratch(*shape):
        return pltpu.VMEM((*shape, nz), jnp.float32)

    def limit(mebibytes):
        return pltpu.CompilerParams(vmem_limit_bytes=mebibytes * 1024 * 1024)

    x_edge, y_edge, corner = array(x_edge_rows(ny)), array(y_layers(nx)[1]), array(2 * corner_layers()[2])
    placed = [pltpu.with_memory_space_constraint(field, pltpu.HBM) for field in fields]
    x_edges = pl.pallas_call(
        functools.partial(x_pack_kernel, nx, ny),
        out_shape=[x_edge] * 2,
        in_specs=[HBM] * 5,
        out_specs=[VMEM] * 2,
        scratch_shapes=[scratch(5, 8, ny), scratch(4, ny + 20), pltpu.SemaphoreType.DMA((5, 2))],
        compiler_params=limit(4),
        name="x_pack",
    )(*placed)
    x_edges = [along_x(edge, side) for edge, side in zip(x_edges, SIDES)]
    own, *y_edges = pl.pallas_call(
        functools.partial(y_pack_kernel, nx, ny),
        out_shape=[array(5, nx, ny + 12), y_edge, y_edge],
        in_specs=[HBM] * 5,
        out_specs=[VMEM] * 3,
        scratch_shapes=[pltpu.SemaphoreType.DMA((5,))],
        compiler_params=limit(4),
        name="y_pack",
    )(*placed)
    y_edges = [along_y(edge, link) for edge, link in zip(y_edges, LINKS)]
    corners = pl.pallas_call(
        functools.partial(corner_kernel, ny),
        out_shape=[corner] * 2,
        in_specs=[VMEM] * 2,
        out_specs=[VMEM] * 2,
        compiler_params=limit(4),
        name="corners",
    )(*x_edges)
    corners = [along_y(corner, link) for corner, link in zip(corners, LINKS)]
    increment = time_increment.reshape(1)
    passed_in = [array(3, nx - 4, wide), array(2, nx - 4, wide), array(nx - 8, wide + 8), array(nx - 8, wide), array(3, nx - 8, ny)]
    passed_out = [array(3, 8, wide), array(2, 8, wide), array(8, wide + 8), array(8, wide), array(3, 8, ny)]
    cells, stress, state_in, passive_in, energies, *rest_in, peak = pl.pallas_call(
        functools.partial(inner_kernel, nx, ny),
        out_shape=[
            array(5, nx, ny + 20),
            array(nx - 2, tall),
            *passed_in[:2],
            array(nx - 4, wide + 8),
            *passed_in[2:],
            array(wide),
        ],
        in_specs=[SMEM] + [VMEM] * 3,
        out_specs=[VMEM] * 9,
        scratch_shapes=[
            scratch(nx - 2, tall),
            scratch(nx - 2, tall),
            scratch(3, nx - 8, wide + 8),
            scratch(3, nx - 8, wide + 8),
        ],
        compiler_params=limit(8),
        cost_estimate=pl.CostEstimate(flops=5 * 10**6, bytes_accessed=2 * 10**6, transcendentals=0),
        name="inner",
    )(increment, own, *y_edges)
    *outer, smallest = pl.pallas_call(
        functools.partial(outer_kernel, nx, ny),
        out_shape=passed_out + [array(lax.axis_size(("gx", "gy")))],
        in_specs=[SMEM] + [VMEM] * 9,
        out_specs=[VMEM] * 6,
        scratch_shapes=[
            scratch(5, 2 * LEFT, ny + 20),
            scratch(2, EDGE_KINDS + 1, ny + 20),
            scratch(10, tall),
            scratch(8, tall),
            scratch(8, tall),
            scratch(4, wide + 8),
            scratch(3, 4, wide + 8),
            scratch(3, 4, wide + 8),
            scratch(3, 4, wide + 8),
            scratch(3, 4, wide + 8),
        ],
        compiler_params=limit(8),
        name="outer",
    )(increment, *x_edges, *corners, cells, stress, state_in, energies, peak)
    outs = pl.pallas_call(
        functools.partial(carry_kernel, nx, ny),
        out_shape=[array(nx, ny)] * 5,
        in_specs=[SMEM] + [VMEM] * 10,
        out_specs=[VMEM] * 2 + [HBM] * 3,
        scratch_shapes=[
            scratch(2, nx, wide + 8),
            scratch(2, nx, wide + 8),
            pltpu.SemaphoreType.DMA((3, 3)),
        ],
        compiler_params=limit(8),
        cost_estimate=pl.CostEstimate(flops=10**7, bytes_accessed=4 * 10**6, transcendentals=0),
        name="carry",
    )(increment, state_in, passive_in, *rest_in, *outer)
    return (*outs, jnp.min(lax.all_to_all(smallest, ("gx", "gy"), 0, 0, tiled=True)))


def solution(mesh):
    cells = P("gx", "gy", None)
    return jax.shard_map(
        body,
        mesh=mesh,
        in_specs=(cells,) * 5 + (P(),),
        out_specs=(cells,) * 5 + (P(),),
        check_vma=False,
    )
```

```python
import functools

import jax
import jax.numpy as jnp
from jax import lax
from jax.experimental import pallas as pl
from jax.experimental.pallas import tpu as pltpu
from jax.sharding import PartitionSpec as P

DENSITY, ENERGY, XV, YV, ZV = range(5)
TOP = 8
LEFT = 3
SIDES = (-1, 1)
NEAR, FAR = "near", "far"
LINKS = (FAR, NEAR)
EDGE_KINDS = 4
VMEM = pl.BlockSpec(memory_space=pltpu.VMEM)
HBM = pl.BlockSpec(memory_space=pltpu.HBM)
SMEM = pl.BlockSpec(memory_space=pltpu.SMEM)


def ghost_rows(field):
    return 4 if field == YV else 3


def x_layers():
    return [(field, past) for field in range(5) for past in (1, 2)] + [(XV, 3)]


def x_edge_rows(ny):
    return (len(x_layers()) + 1) * ny + 2 * EDGE_KINDS


def y_layers(nx):
    found, offset = [], 0
    for a in range(nx):
        for field in range(5):
            found.append((field, a, ghost_rows(field), offset))
            offset += ghost_rows(field)
    return found, (offset // 8 + 2) * 8


def corner_layers():
    found, offset = [], 0
    for number, (field, past) in enumerate(x_layers()):
        found.append((number, field, past, ghost_rows(field), offset))
        offset += ghost_rows(field)
    return found, offset, -(-(offset + 1 + EDGE_KINDS) // 8) * 8


def is_low(link):
    odd = lax.rem(lax.axis_index("gy"), 2)
    return odd if link == NEAR else 1 - odd


def pick(flag, one, other):
    return flag * one + (1 - flag) * other


def along_x(value, side):
    count = lax.axis_size("gx")
    return lax.ppermute(value, "gx", [((i + side) % count, i) for i in range(count)])


def along_y(value, link):
    count = lax.axis_size("gy")
    partners = [i ^ 1 if link == NEAR else (((i - 1) ^ 1) + 1) % count for i in range(count)]
    return lax.ppermute(value, "gy", list(enumerate(partners)))


def hidden_zero():
    return lax.shift_right_logical(lax.axis_index("gx"), 20)


def span(zero, start, count, total):
    return pl.ds(start if start + -(-count // 8) * 8 > total else zero + start, count)


def per_mass(energy, spread):
    return 0.4 * energy + 0.5 * jnp.square(jnp.minimum(0.5 * spread, 0.0))


def x_pack_kernel(nx, ny, *refs):
    fields, x_edges, near, padded, arrived = refs[:5], refs[5:7], refs[7], refs[8], refs[9]
    zero = hidden_zero()
    order = (ZV, YV, XV, ENERGY, DENSITY)
    copies = {
        (field, k): pltpu.make_async_copy(
            fields[field].at[pl.ds(first, 4)], near.at[field, pl.ds(4 * k, 4)], arrived.at[field, k]
        )
        for field in order
        for k, first in enumerate((nx - 4, 0))
    }
    for copy in copies.values():
        copy.start()
    thirds = (1, 6)
    for current in order:
        for k, (side, edge) in enumerate(zip(SIDES, x_edges)):
            copies[current, k].wait()
            if current == ZV:
                padded[k] = jnp.zeros_like(padded[k])
                padded[2 + k, pl.ds(TOP, ny), :] = up(near[ZV, thirds[k]]) - down(near[ZV, thirds[k]])
            if current == YV:
                padded[k, pl.ds(TOP, ny), :] = near[YV, thirds[k]]
            for number, (field, past) in enumerate(x_layers()):
                if field == current:
                    edge[pl.ds(zero + number * ny, ny), :] = near[field, 4 - past if side < 0 else 3 + past]
    for k, edge in enumerate(x_edges):
        a = thirds[k]
        offset = len(x_layers()) * ny
        spread = near[XV, a + 1] - near[XV, a - 1]
        spread += padded[k, pl.ds(zero + (TOP + 1), ny), :] - padded[k, pl.ds(zero + (TOP - 1), ny), :]
        spread += padded[2 + k, pl.ds(TOP, ny), :]
        edge[pl.ds(zero + offset, ny), :] = near[DENSITY, a] * per_mass(near[ENERGY, a], spread)
        offset += ny
        padded[2 + k, pl.ds(TOP, ny), :] = spread
        for row in (0, ny - 1):
            for value in (near[DENSITY, a, pl.ds(row, 1), :], near[ENERGY, a, pl.ds(row, 1), :],
                          padded[2 + k, pl.ds(TOP + row, 1), :], near[YV, a, pl.ds(row, 1), :]):
                edge[pl.ds(offset, 1), :] = value
                offset += 1


def y_pack_kernel(nx, ny, *refs):
    fields, own, y_edges, arrived = refs[:5], refs[5], refs[6:8], refs[8]
    zero = hidden_zero()
    copies = [
        pltpu.make_async_copy(fields[field], own.at[field, pl.ds(0, nx), pl.ds(0, ny), :], arrived.at[field])
        for field in range(5)
    ]
    for copy in copies:
        copy.start()
    for current, copy in enumerate(copies):
        copy.wait()
        for link, edge in zip(LINKS, y_edges):
            for field, a, rows, offset in y_layers(nx)[0]:
                if field == current:
                    start = pick(is_low(link), 0, ny - rows)
                    edge[pl.ds(zero + offset, rows), :] = own[field, a, pl.ds(start, rows), :]


def corner_kernel(ny, *refs):
    x_edges, outs = refs[:2], refs[2:]
    zero = hidden_zero()
    columns, singles, rows_of_corner = corner_layers()
    for link, out in zip(LINKS, outs):
        low = is_low(link)
        for k, edge in enumerate(x_edges):
            base, total = k * rows_of_corner, out.shape[0]
            for number, _, _, rows, offset in columns:
                out[span(zero, base + offset, rows, total), :] = edge[pl.ds(number * ny + pick(low, 0, ny - rows), rows), :]
            number = len(x_layers())
            out[span(zero, base + singles, 1, total), :] = edge[pl.ds(number * ny + pick(low, 1, ny - 2), 1), :]
            first, last = [
                edge[pl.ds((number + 1) * ny + k * EDGE_KINDS, EDGE_KINDS), :] for k in range(2)
            ]
            out[span(zero, base + singles + 1, EDGE_KINDS, total), :] = jnp.where(low == 1, first, last)


def limited(above, below):
    return jnp.minimum(jnp.maximum(above, jnp.minimum(below, 0.0)), jnp.maximum(below, 0.0))


def face_factors(v_minus, v, half_increment):
    courant = half_increment * (v_minus + v)
    size = jnp.abs(courant)
    return courant, 0.5 * size * (1.0 - size), courant > 0.0


def face_flux(factors, f_minus, f, s_minus, s):
    courant, slope_factor, upward = factors
    return courant * jnp.where(upward, f_minus, f) + slope_factor * jnp.where(upward, s_minus, s)


def up(value):
    return pltpu.roll(value, value.shape[-1] - 1, value.ndim - 1)


def down(value):
    return pltpu.roll(value, 1, value.ndim - 1)


def place(pieces, a):
    for ref, first, last, number in pieces:
        if first <= a < last:
            return ref, a - first + number
    raise ValueError(a)


def read(zero, pieces, a, start, count, *field):
    ref, number = place(pieces, a)
    return ref[(*field, number, pl.ds(zero + start, count), slice(None))]


def write(pieces, a, value, *field):
    ref, number = place(pieces, a)
    ref[(*field, number, pl.ds(0, value.shape[0]), slice(None))] = value


def sweep_x(state, speed, swept, fields, first, last, wide, half):
    for part in range(0, wide, 8):
        before = [state(field, first - 1, part) for field in fields]
        here = [state(field, first, part) for field in fields]
        steps = [h - b for h, b in zip(here, before)]
        slopes = [limited(st, b - state(field, first - 2, part)) for field, st, b in zip(fields, steps, before)]
        lower = None
        for a in range(first, last + 1):
            factors = face_factors(speed(a - 1, part), speed(a, part), half)
            fluxes = []
            for k, field in enumerate(fields):
                after = state(field, a + 1, part)
                step = after - here[k]
                slope = limited(step, steps[k])
                fluxes.append(face_flux(factors, before[k], here[k], slopes[k], slope))
                if lower is not None:
                    swept[field, a - 1 - first, pl.ds(part, 8)] = before[k] - (fluxes[k] - lower[k])
                before[k], here[k], steps[k], slopes[k] = here[k], after, step, slope
            lower = fluxes


def sweep_y(zero, columns, fields, wide):
    def rows(swept, number, field, start):
        return swept[field, number, pl.ds(zero + start, wide)]

    for swept, work, number, factors in columns:
        for field in fields:
            start = [rows(swept, number, field, first) for first in range(4)]
            steps = [after - before for before, after in zip(start, start[1:])]
            slopes = [limited(after, before) for before, after in zip(steps, steps[1:])]
            work[field, number, 0:wide] = face_flux(factors, start[1], start[2], *slopes)
    moved = []
    for swept, work, number, _ in columns:
        moved.append([])
        for field in fields:
            flux, above = [work[field, number, pl.ds(zero + start, wide)] for start in (0, 1)]
            moved[-1].append(rows(swept, number, field, 2) - (above - flux))
    return moved


def sweep_z(moved, factors):
    final = []
    for value in moved:
        below, above = down(value), up(value)
        step = value - below
        slopes = limited(step, below - pltpu.roll(value, 2, 1)), limited(above - value, step)
        flux = face_flux(factors, below, value, *slopes)
        final.append(value - (up(flux) - flux))
    return final


def spread_columns(zero, columns, tall, half, cells, stress, heat, growth):
    for a in columns:
        z = read(zero, cells, a, TOP - 4, tall, ZV)
        spread = (
            read(zero, cells, a + 1, TOP - 4, tall, XV)
            - read(zero, cells, a - 1, TOP - 4, tall, XV)
            + (read(zero, cells, a, TOP - 3, tall, YV) - read(zero, cells, a, TOP - 5, tall, YV))
            + (up(z) - down(z))
        )
        warmth = per_mass(read(zero, cells, a, TOP - 4, tall, ENERGY), spread)
        write(heat, a, warmth)
        write(stress, a, read(zero, cells, a, TOP - 4, tall, DENSITY) * warmth)
        write(growth, a, half * spread)


def advance_columns(zero, columns, wide, half, cells, stress, heat, growth, passive, state, roots, nx):
    for a in columns:
        density, energy, x, y, z = [read(zero, cells, a, TOP - 2, wide, field) for field in range(5)]
        grown = read(zero, growth, a, 2, wide)
        centre = read(zero, stress, a, 2, wide)
        scale = half / density
        density_one = density / (1.0 + grown)
        energy = energy - read(zero, heat, a, 2, wide) * grown
        write(passive, a, density_one, 0)
        write(passive, a, density_one * energy, 1)
        write(state, a, x - scale * (read(zero, stress, a + 1, 2, wide) - read(zero, stress, a - 1, 2, wide)), 0)
        write(state, a, y - scale * (read(zero, stress, a, 3, wide) - read(zero, stress, a, 1, wide)), 1)
        write(state, a, z - scale * (up(centre) - down(centre)), 2)
        if 0 <= a < nx:
            write(roots, a, jnp.sqrt(0.56 * energy))


def flow_columns(zero, groups, ny, half, state, roots, speed_y, speed_z, flows):
    wide = ny + 4
    columns, names = [], []
    for first, last, swept, work in groups:
        sweep_x(
            lambda field, a, part: read(zero, state, a, part, 8, field),
            lambda a, part: read(zero, state, a, part, 8, 0),
            swept, (0, 1, 2), first, last, wide, half,
        )
    for first, last, swept, work in groups:
        for a in range(first, last):
            below, here = [swept[1, a - first, pl.ds(zero + start, wide)] for start in (1, 2)]
            columns.append((swept, work, a - first, face_factors(below, here, half)))
            names.append(a)
            write(speed_y, a, swept[1, a - first, 0:wide])
    peak = None
    for a, moved in zip(names, sweep_y(zero, columns, (0, 1, 2), wide)):
        write(speed_z, a, moved[2])
        final = sweep_z(moved, face_factors(down(moved[2]), moved[2], half))
        for field in range(3):
            write(flows, a, final[field][:ny], field)
        signal = read(zero, roots, a, 2, wide) + jnp.abs(final[0]) + jnp.abs(final[1]) + jnp.abs(final[2])
        peak = signal if peak is None else jnp.maximum(peak, signal)
    return peak


def inner_kernel(nx, ny, dt_ref, *refs):
    own, y_edges = refs[0], refs[1:3]
    cells, stress, state, passive, roots, speed_y, speed_z, flows, peak_ref = refs[3:12]
    heat, growth, swept, work = refs[12:]
    zero = hidden_zero()
    half = 0.5 * dt_ref[0]
    for field in range(5):
        for a in range(nx):
            cells[field, a, pl.ds(TOP, ny), :] = own[field, a, pl.ds(0, ny), :]
    for link, edge in zip(LINKS, y_edges):
        low = is_low(link)
        for field, a, rows, offset in y_layers(nx)[0]:
            cells[field, a, pl.ds(TOP + pick(low, -rows, ny), rows), :] = edge[pl.ds(zero + offset, rows), :]
    cells = [(cells, 0, nx, 0)]
    stress, heat, growth = [[(ref, 1, nx - 1, 0)] for ref in (stress, heat, growth)]
    state, passive, roots = [[(ref, 2, nx - 2, 0)] for ref in (state, passive, roots)]
    speed_y, speed_z, flows = [[(ref, 4, nx - 4, 0)] for ref in (speed_y, speed_z, flows)]
    spread_columns(zero, range(1, nx - 1), ny + 12, half, cells, stress, heat, growth)
    advance_columns(
        zero, range(2, nx - 2), ny + 4, half, cells, stress, heat, growth, passive, state, roots, nx
    )
    peak_ref[...] = flow_columns(
        zero, [(4, nx - 4, swept, work)], ny, half, state, roots, speed_y, speed_z, flows
    )


def outer_pieces(ref, nx, reach, inside):
    return [(ref, -reach, inside, 0), (ref, nx - inside, nx + reach, reach + inside)]


def outer_kernel(nx, ny, dt_ref, *refs):
    x_edges, corners = refs[0:2], refs[2:4]
    cells_in, stress_in, state_in, roots_in, peak_in = refs[4:9]
    state_out, passive_out, speed_y, speed_z, flows, increment_ref = refs[9:15]
    beyond, third, stress_out, heat, growth, roots_out = refs[15:21]
    swept, work = refs[21:23], refs[23:25]
    nz = increment_ref.shape[-1]
    zero = hidden_zero()
    half = 0.5 * dt_ref[0]
    wide, tall = ny + 4, ny + 12

    columns, singles, rows_of_corner = corner_layers()
    for k, (side, edge) in enumerate(zip(SIDES, x_edges)):
        for number, (field, past) in enumerate(x_layers()):
            column = LEFT - past if side < 0 else LEFT - 1 + past
            beyond[field, column, pl.ds(TOP, ny), :] = edge[pl.ds(zero + number * ny, ny), :]
        offset = len(x_layers()) * ny
        third[k, EDGE_KINDS, pl.ds(TOP, ny), :] = edge[pl.ds(zero + offset, ny), :]
        offset += ny
        for row in (0, ny - 1):
            for kind in range(EDGE_KINDS):
                third[k, kind, pl.ds(TOP + row, 1), :] = edge[pl.ds(offset, 1), :]
                offset += 1
    for link, corner in zip(LINKS, corners):
        low = is_low(link)
        for k, side in enumerate(SIDES):
            base, total = k * rows_of_corner, corner.shape[0]
            for _, field, past, rows, offset in columns:
                column = LEFT - past if side < 0 else LEFT - 1 + past
                to = pl.ds(TOP + pick(low, -rows, ny), rows)
                beyond[field, column, to, :] = corner[span(zero, base + offset, rows, total), :]
            to = pl.ds(TOP + pick(low, -2, ny + 1), 1)
            third[k, EDGE_KINDS, to, :] = corner[span(zero, base + singles, 1, total), :]
            for kind in range(EDGE_KINDS):
                to = pl.ds(TOP + pick(low, -1, ny), 1)
                third[k, kind, to, :] = corner[span(zero, base + singles + 1 + kind, 1, total), :]

    cells = [(cells_in, 0, nx, 0)] + outer_pieces(beyond, nx, LEFT, 0)
    stress = outer_pieces(stress_out, nx, 3, 2) + [(stress_in, 2, nx - 2, 1)]
    heat, growth = outer_pieces(heat, nx, 2, 2), outer_pieces(growth, nx, 2, 2)
    state = outer_pieces(state_out, nx, 2, 2) + [(state_in, 2, nx - 2, 0)]
    passive = outer_pieces(passive_out, nx, 2, 2)
    roots = outer_pieces(roots_out, nx, 0, 2) + [(roots_in, 2, nx - 2, 0)]
    speed_y, speed_z, flows = [outer_pieces(ref, nx, 0, 4) for ref in (speed_y, speed_z, flows)]

    row = lax.broadcasted_iota(jnp.int32, (tall, nz), 0) - 4
    for k, a in enumerate((-3, nx + 2)):
        above, below = [third[k, 3, pl.ds(zero + start, tall)] for start in (TOP - 3, TOP - 5)]
        density, energy, spread, _, whole = [third[k, kind, pl.ds(zero + TOP - 4, tall)] for kind in range(5)]
        spread += jnp.where((row == -1) | (row == ny - 1), above, -below)
        split = (row == -1) | (row == 0) | (row == ny - 1) | (row == ny)
        write(stress, a, jnp.where(split, density * per_mass(energy, spread), whole))

    ends = (*range(-2, 2), *range(nx - 2, nx + 2))
    spread_columns(zero, ends, tall, half, cells, stress, heat, growth)
    advance_columns(zero, ends, wide, half, cells, stress, heat, growth, passive, state, roots, nx)
    groups = [(first, first + 4, swept[k], work[k]) for k, first in enumerate((0, nx - 4))]
    peak = flow_columns(zero, groups, ny, half, state, roots, speed_y, speed_z, flows)
    peak = jnp.maximum(peak, peak_in[...])
    peak = jnp.max(jnp.where(row[4 : 4 + wide] < ny, peak, 0.0), axis=0, keepdims=True)
    increment_ref[...] = jnp.broadcast_to(0.3 / peak, increment_ref.shape)


def carry_kernel(nx, ny, dt_ref, *refs):
    state_in, passive_in, speed_y_in, speed_z_in, flows_in = refs[0:5]
    state_out, passive_out, speed_y_out, speed_z_out, flows_out = refs[5:10]
    density_out, energy_out, flow_outs, swept, work, written = refs[10], refs[11], refs[12:15], refs[15], refs[16], refs[17]
    zero = hidden_zero()
    half = 0.5 * dt_ref[0]
    wide = ny + 4
    copies = []
    for k in range(3):
        for piece, (ref, first, last, number) in enumerate([(flows_in, 4, nx - 4, 0)] + outer_pieces(flows_out, nx, 0, 4)):
            source = ref.at[k, pl.ds(number, last - first)]
            copies.append(
                pltpu.make_async_copy(source, flow_outs[k].at[pl.ds(first, last - first)], written.at[k, piece])
            )
    for copy in copies:
        copy.start()
    state = outer_pieces(state_out, nx, 2, 2) + [(state_in, 2, nx - 2, 0)]
    passive = outer_pieces(passive_out, nx, 2, 2) + [(passive_in, 2, nx - 2, 0)]
    speed_y = outer_pieces(speed_y_out, nx, 0, 4) + [(speed_y_in, 4, nx - 4, 0)]
    speed_z = outer_pieces(speed_z_out, nx, 0, 4) + [(speed_z_in, 4, nx - 4, 0)]
    sweep_x(
        lambda field, a, part: read(zero, passive, a, part, 8, field),
        lambda a, part: read(zero, state, a, part, 8, 0),
        swept, (0, 1), 0, nx, wide, half,
    )
    factors = [face_factors(*[read(zero, speed_y, a, start, wide) for start in (1, 2)], half) for a in range(nx)]
    columns = [(swept, work, a, factors[a]) for a in range(nx)]
    for a, moved in enumerate(sweep_y(zero, columns, (0, 1), wide)):
        along = read(zero, speed_z, a, 0, wide)
        final = sweep_z(moved, face_factors(down(along), along, half))
        density_out[a] = final[0][:ny]
        energy_out[a] = final[1][:ny]
    for copy in copies:
        copy.wait()


def body(density0, energy0, x_velocity, y_velocity, z_velocity, time_increment):
    nx, ny, nz = density0.shape
    fields = (density0, energy0, x_velocity, y_velocity, z_velocity)
    wide, tall = ny + 4, ny + 12

    def array(*shape):
        return jax.ShapeDtypeStruct((*shape, nz), jnp.float32)

    def scratch(*shape):
        return pltpu.VMEM((*shape, nz), jnp.float32)

    def limit(mebibytes):
        return pltpu.CompilerParams(vmem_limit_bytes=mebibytes * 1024 * 1024)

    x_edge, y_edge, corner = array(x_edge_rows(ny)), array(y_layers(nx)[1]), array(2 * corner_layers()[2])
    placed = [pltpu.with_memory_space_constraint(field, pltpu.HBM) for field in fields]
    x_edges = pl.pallas_call(
        functools.partial(x_pack_kernel, nx, ny),
        out_shape=[x_edge] * 2,
        in_specs=[HBM] * 5,
        out_specs=[VMEM] * 2,
        scratch_shapes=[scratch(5, 8, ny), scratch(4, ny + 20), pltpu.SemaphoreType.DMA((5, 2))],
        compiler_params=limit(4),
        name="x_pack",
    )(*placed)
    x_edges = [along_x(edge, side) for edge, side in zip(x_edges, SIDES)]
    own, *y_edges = pl.pallas_call(
        functools.partial(y_pack_kernel, nx, ny),
        out_shape=[array(5, nx, ny + 12), y_edge, y_edge],
        in_specs=[HBM] * 5,
        out_specs=[VMEM] * 3,
        scratch_shapes=[pltpu.SemaphoreType.DMA((5,))],
        compiler_params=limit(4),
        name="y_pack",
    )(*placed)
    y_edges = [along_y(edge, link) for edge, link in zip(y_edges, LINKS)]
    corners = pl.pallas_call(
        functools.partial(corner_kernel, ny),
        out_shape=[corner] * 2,
        in_specs=[VMEM] * 2,
        out_specs=[VMEM] * 2,
        compiler_params=limit(4),
        name="corners",
    )(*x_edges)
    corners = [along_y(corner, link) for corner, link in zip(corners, LINKS)]
    increment = time_increment.reshape(1)
    passed_in = [array(3, nx - 4, wide), array(2, nx - 4, wide), array(nx - 8, wide + 8), array(nx - 8, wide), array(3, nx - 8, ny)]
    passed_out = [array(3, 8, wide), array(2, 8, wide), array(8, wide + 8), array(8, wide), array(3, 8, ny)]
    cells, stress, state_in, passive_in, roots, *rest_in, peak = pl.pallas_call(
        functools.partial(inner_kernel, nx, ny),
        out_shape=[
            array(5, nx, ny + 20),
            array(nx - 2, tall),
            *passed_in[:2],
            array(nx - 4, wide + 8),
            *passed_in[2:],
            array(wide),
        ],
        in_specs=[SMEM] + [VMEM] * 3,
        out_specs=[VMEM] * 9,
        scratch_shapes=[
            scratch(nx - 2, tall),
            scratch(nx - 2, tall),
            scratch(3, nx - 8, wide + 8),
            scratch(3, nx - 8, wide + 8),
        ],
        compiler_params=limit(8),
        cost_estimate=pl.CostEstimate(flops=5 * 10**6, bytes_accessed=2 * 10**6, transcendentals=0),
        name="inner",
    )(increment, own, *y_edges)
    *outer, smallest = pl.pallas_call(
        functools.partial(outer_kernel, nx, ny),
        out_shape=passed_out + [array(lax.axis_size(("gx", "gy")))],
        in_specs=[SMEM] + [VMEM] * 9,
        out_specs=[VMEM] * 6,
        scratch_shapes=[
            scratch(5, 2 * LEFT, ny + 20),
            scratch(2, EDGE_KINDS + 1, ny + 20),
            scratch(10, tall),
            scratch(8, tall),
            scratch(8, tall),
            scratch(4, wide + 8),
            scratch(3, 4, wide + 8),
            scratch(3, 4, wide + 8),
            scratch(3, 4, wide + 8),
            scratch(3, 4, wide + 8),
        ],
        compiler_params=limit(8),
        name="outer",
    )(increment, *x_edges, *corners, cells, stress, state_in, roots, peak)
    outs = pl.pallas_call(
        functools.partial(carry_kernel, nx, ny),
        out_shape=[array(nx, ny)] * 5,
        in_specs=[SMEM] + [VMEM] * 10,
        out_specs=[VMEM] * 2 + [HBM] * 3,
        scratch_shapes=[
            scratch(2, nx, wide + 8),
            scratch(2, nx, wide + 8),
            pltpu.SemaphoreType.DMA((3, 3)),
        ],
        compiler_params=limit(8),
        cost_estimate=pl.CostEstimate(flops=10**7, bytes_accessed=4 * 10**6, transcendentals=0),
        name="carry",
    )(increment, state_in, passive_in, *rest_in, *outer)
    return (*outs, jnp.min(lax.all_to_all(smallest, ("gx", "gy"), 0, 0, tiled=True)))


def solution(mesh):
    cells = P("gx", "gy", None)
    return jax.shard_map(
        body,
        mesh=mesh,
        in_specs=(cells,) * 5 + (P(),),
        out_specs=(cells,) * 5 + (P(),),
        check_vma=False,
    )
```

```python
import functools

import jax
import jax.numpy as jnp
from jax import lax
from jax.experimental import pallas as pl
from jax.experimental.pallas import tpu as pltpu
from jax.sharding import PartitionSpec as P

DENSITY, ENERGY, XV, YV, ZV = range(5)
TOP = 8
LEFT = 3
SIDES = (-1, 1)
NEAR, FAR = "near", "far"
LINKS = (FAR, NEAR)
EDGE_KINDS = 4
VMEM = pl.BlockSpec(memory_space=pltpu.VMEM)
HBM = pl.BlockSpec(memory_space=pltpu.HBM)
SMEM = pl.BlockSpec(memory_space=pltpu.SMEM)


def ghost_rows(field):
    return 4 if field == YV else 3


def x_layers():
    return [(field, past) for field in range(5) for past in (1, 2)] + [(XV, 3)]


def x_edge_rows(ny):
    return (len(x_layers()) + 1) * ny + 2 * EDGE_KINDS


def y_layers(nx):
    found, offset = [], 0
    for a in range(nx):
        for field in range(5):
            found.append((field, a, ghost_rows(field), offset))
            offset += ghost_rows(field)
    return found, (offset // 8 + 2) * 8


def corner_layers():
    found, offset = [], 0
    for number, (field, past) in enumerate(x_layers()):
        found.append((number, field, past, ghost_rows(field), offset))
        offset += ghost_rows(field)
    return found, offset, -(-(offset + 1 + EDGE_KINDS) // 8) * 8


def is_low(link):
    odd = lax.rem(lax.axis_index("gy"), 2)
    return odd if link == NEAR else 1 - odd


def pick(flag, one, other):
    return flag * one + (1 - flag) * other


def along_x(value, side):
    count = lax.axis_size("gx")
    return lax.ppermute(value, "gx", [((i + side) % count, i) for i in range(count)])


def along_y(value, link):
    count = lax.axis_size("gy")
    partners = [i ^ 1 if link == NEAR else (((i - 1) ^ 1) + 1) % count for i in range(count)]
    return lax.ppermute(value, "gy", list(enumerate(partners)))


def hidden_zero():
    return lax.shift_right_logical(lax.axis_index("gx"), 20)


def span(zero, start, count, total):
    return pl.ds(start if start + -(-count // 8) * 8 > total else zero + start, count)


def per_mass(energy, spread):
    return 0.4 * energy + 0.5 * jnp.square(jnp.minimum(0.5 * spread, 0.0))


def x_pack_kernel(nx, ny, *refs):
    fields, x_edges, near, padded, arrived = refs[:5], refs[5:7], refs[7], refs[8], refs[9]
    zero = hidden_zero()
    order = (ZV, YV, XV, ENERGY, DENSITY)
    copies = {}
    for field in order:
        width = 4 if field == XV else 3
        for k, (first, place_at) in enumerate(((nx - width, 4 - width), (0, 4))):
            copies[field, k] = pltpu.make_async_copy(
                fields[field].at[pl.ds(first, width)], near.at[field, pl.ds(place_at, width)], arrived.at[field, k]
            )
    for copy in copies.values():
        copy.start()
    thirds = (1, 6)
    for current in order:
        for k, (side, edge) in enumerate(zip(SIDES, x_edges)):
            copies[current, k].wait()
            if current == ZV:
                padded[k] = jnp.zeros_like(padded[k])
                padded[2 + k, pl.ds(TOP, ny), :] = up(near[ZV, thirds[k]]) - down(near[ZV, thirds[k]])
            if current == YV:
                padded[k, pl.ds(TOP, ny), :] = near[YV, thirds[k]]
            for number, (field, past) in enumerate(x_layers()):
                if field == current:
                    edge[pl.ds(zero + number * ny, ny), :] = near[field, 4 - past if side < 0 else 3 + past]
    for k, edge in enumerate(x_edges):
        a = thirds[k]
        offset = len(x_layers()) * ny
        spread = near[XV, a + 1] - near[XV, a - 1]
        spread += padded[k, pl.ds(zero + (TOP + 1), ny), :] - padded[k, pl.ds(zero + (TOP - 1), ny), :]
        spread += padded[2 + k, pl.ds(TOP, ny), :]
        edge[pl.ds(zero + offset, ny), :] = near[DENSITY, a] * per_mass(near[ENERGY, a], spread)
        offset += ny
        padded[2 + k, pl.ds(TOP, ny), :] = spread
        for row in (0, ny - 1):
            for value in (near[DENSITY, a, pl.ds(row, 1), :], near[ENERGY, a, pl.ds(row, 1), :],
                          padded[2 + k, pl.ds(TOP + row, 1), :], near[YV, a, pl.ds(row, 1), :]):
                edge[pl.ds(offset, 1), :] = value
                offset += 1


def y_pack_kernel(nx, ny, *refs):
    fields, own, y_edges, arrived = refs[:5], refs[5], refs[6:8], refs[8]
    zero = hidden_zero()
    copies = [
        pltpu.make_async_copy(fields[field], own.at[field, pl.ds(0, nx), pl.ds(0, ny), :], arrived.at[field])
        for field in range(5)
    ]
    for copy in copies:
        copy.start()
    for current, copy in enumerate(copies):
        copy.wait()
        for link, edge in zip(LINKS, y_edges):
            for field, a, rows, offset in y_layers(nx)[0]:
                if field == current:
                    start = pick(is_low(link), 0, ny - rows)
                    edge[pl.ds(zero + offset, rows), :] = own[field, a, pl.ds(start, rows), :]


def corner_kernel(ny, *refs):
    x_edges, outs = refs[:2], refs[2:]
    zero = hidden_zero()
    columns, singles, rows_of_corner = corner_layers()
    for link, out in zip(LINKS, outs):
        low = is_low(link)
        for k, edge in enumerate(x_edges):
            base, total = k * rows_of_corner, out.shape[0]
            for number, _, _, rows, offset in columns:
                out[span(zero, base + offset, rows, total), :] = edge[pl.ds(number * ny + pick(low, 0, ny - rows), rows), :]
            number = len(x_layers())
            out[span(zero, base + singles, 1, total), :] = edge[pl.ds(number * ny + pick(low, 1, ny - 2), 1), :]
            first, last = [
                edge[pl.ds((number + 1) * ny + k * EDGE_KINDS, EDGE_KINDS), :] for k in range(2)
            ]
            out[span(zero, base + singles + 1, EDGE_KINDS, total), :] = jnp.where(low == 1, first, last)


def limited(above, below):
    return jnp.minimum(jnp.maximum(above, jnp.minimum(below, 0.0)), jnp.maximum(below, 0.0))


def face_factors(v_minus, v, half_increment):
    courant = half_increment * (v_minus + v)
    size = jnp.abs(courant)
    return courant, 0.5 * size * (1.0 - size), courant > 0.0


def face_flux(factors, f_minus, f, s_minus, s):
    courant, slope_factor, upward = factors
    return courant * jnp.where(upward, f_minus, f) + slope_factor * jnp.where(upward, s_minus, s)


def up(value):
    return pltpu.roll(value, value.shape[-1] - 1, value.ndim - 1)


def down(value):
    return pltpu.roll(value, 1, value.ndim - 1)


def place(pieces, a):
    for ref, first, last, number in pieces:
        if first <= a < last:
            return ref, a - first + number
    raise ValueError(a)


def read(zero, pieces, a, start, count, *field):
    ref, number = place(pieces, a)
    return ref[(*field, number, pl.ds(zero + start, count), slice(None))]


def write(pieces, a, value, *field):
    ref, number = place(pieces, a)
    ref[(*field, number, pl.ds(0, value.shape[0]), slice(None))] = value


def sweep_x(state, speed, swept, fields, first, last, wide, half):
    for part in range(0, wide, 8):
        before = [state(field, first - 1, part) for field in fields]
        here = [state(field, first, part) for field in fields]
        steps = [h - b for h, b in zip(here, before)]
        slopes = [limited(st, b - state(field, first - 2, part)) for field, st, b in zip(fields, steps, before)]
        lower = None
        for a in range(first, last + 1):
            factors = face_factors(speed(a - 1, part), speed(a, part), half)
            fluxes = []
            for k, field in enumerate(fields):
                after = state(field, a + 1, part)
                step = after - here[k]
                slope = limited(step, steps[k])
                fluxes.append(face_flux(factors, before[k], here[k], slopes[k], slope))
                if lower is not None:
                    swept[field, a - 1 - first, pl.ds(part, 8)] = before[k] - (fluxes[k] - lower[k])
                before[k], here[k], steps[k], slopes[k] = here[k], after, step, slope
            lower = fluxes


def sweep_y(zero, swept, work, numbers, fields, factors, wide):
    cases = [(number, field) for number in numbers for field in fields]

    def rows(number, field, start):
        return swept[field, number, pl.ds(zero + start, wide)]

    for number, field in cases:
        start = [rows(number, field, first) for first in range(4)]
        steps = [after - before for before, after in zip(start, start[1:])]
        slopes = [limited(after, before) for before, after in zip(steps, steps[1:])]
        work[field, number, 0:wide] = face_flux(factors[number], start[1], start[2], *slopes)
    moved = {}
    for number, field in cases:
        flux, above = [work[field, number, pl.ds(zero + start, wide)] for start in (0, 1)]
        moved[number, field] = rows(number, field, 2) - (above - flux)
    return [[moved[number, field] for field in fields] for number in numbers]


def sweep_z(moved, factors):
    final = []
    for value in moved:
        below, above = down(value), up(value)
        step = value - below
        slopes = limited(step, below - pltpu.roll(value, 2, 1)), limited(above - value, step)
        flux = face_flux(factors, below, value, *slopes)
        final.append(value - (up(flux) - flux))
    return final


def spread_columns(zero, columns, tall, half, cells, stress, heat, growth):
    for a in columns:
        z = read(zero, cells, a, TOP - 4, tall, ZV)
        spread = (
            read(zero, cells, a + 1, TOP - 4, tall, XV)
            - read(zero, cells, a - 1, TOP - 4, tall, XV)
            + (read(zero, cells, a, TOP - 3, tall, YV) - read(zero, cells, a, TOP - 5, tall, YV))
            + (up(z) - down(z))
        )
        warmth = per_mass(read(zero, cells, a, TOP - 4, tall, ENERGY), spread)
        write(heat, a, warmth)
        write(stress, a, read(zero, cells, a, TOP - 4, tall, DENSITY) * warmth)
        write(growth, a, half * spread)


def advance_columns(zero, columns, wide, half, cells, stress, heat, growth, passive, state, energies, nx):
    for a in columns:
        density, energy, x, y, z = [read(zero, cells, a, TOP - 2, wide, field) for field in range(5)]
        grown = read(zero, growth, a, 2, wide)
        centre = read(zero, stress, a, 2, wide)
        scale = half / density
        density_one = density / (1.0 + grown)
        energy = energy - read(zero, heat, a, 2, wide) * grown
        write(passive, a, density_one, 0)
        write(passive, a, density_one * energy, 1)
        write(state, a, x - scale * (read(zero, stress, a + 1, 2, wide) - read(zero, stress, a - 1, 2, wide)), 0)
        write(state, a, y - scale * (read(zero, stress, a, 3, wide) - read(zero, stress, a, 1, wide)), 1)
        write(state, a, z - scale * (up(centre) - down(centre)), 2)
        if 0 <= a < nx:
            write(energies, a, energy)


def flow_columns(zero, first, last, ny, half, state, energies, swept, work, speed_y, speed_z, flows):
    wide = ny + 4
    sweep_x(
        lambda field, a, part: read(zero, state, a, part, 8, field),
        lambda a, part: read(zero, state, a, part, 8, 0),
        swept, (0, 1, 2), first, last, wide, half,
    )
    numbers = range(last - first)
    factors = []
    for number in numbers:
        below, here = [swept[1, number, pl.ds(zero + start, wide)] for start in (1, 2)]
        factors.append(face_factors(below, here, half))
        write(speed_y, first + number, swept[1, number, 0:wide])
    peak = None
    for a, moved in zip(range(first, last), sweep_y(zero, swept, work, numbers, (0, 1, 2), factors, wide)):
        write(speed_z, a, moved[2])
        final = sweep_z(moved, face_factors(down(moved[2]), moved[2], half))
        for field in range(3):
            write(flows, a, final[field][:ny], field)
        signal = (
            jnp.sqrt(0.56 * read(zero, energies, a, 2, wide))
            + jnp.abs(final[0])
            + jnp.abs(final[1])
            + jnp.abs(final[2])
        )
        peak = signal if peak is None else jnp.maximum(peak, signal)
    return peak


def inner_kernel(nx, ny, dt_ref, *refs):
    own, y_edges = refs[0], refs[1:3]
    cells, stress, state, passive, energies, speed_y, speed_z, flows, peak_ref = refs[3:12]
    heat, growth, swept, work = refs[12:]
    zero = hidden_zero()
    half = 0.5 * dt_ref[0]
    for field in range(5):
        for a in range(nx):
            cells[field, a, pl.ds(TOP, ny), :] = own[field, a, pl.ds(0, ny), :]
    for link, edge in zip(LINKS, y_edges):
        low = is_low(link)
        for field, a, rows, offset in y_layers(nx)[0]:
            cells[field, a, pl.ds(TOP + pick(low, -rows, ny), rows), :] = edge[pl.ds(zero + offset, rows), :]
    cells = [(cells, 0, nx, 0)]
    stress, heat, growth = [[(ref, 1, nx - 1, 0)] for ref in (stress, heat, growth)]
    state, passive, energies = [[(ref, 2, nx - 2, 0)] for ref in (state, passive, energies)]
    speed_y, speed_z, flows = [[(ref, 4, nx - 4, 0)] for ref in (speed_y, speed_z, flows)]
    spread_columns(zero, range(1, nx - 1), ny + 12, half, cells, stress, heat, growth)
    advance_columns(
        zero, range(2, nx - 2), ny + 4, half, cells, stress, heat, growth, passive, state, energies, nx
    )
    peak_ref[...] = flow_columns(
        zero, 4, nx - 4, ny, half, state, energies, swept, work, speed_y, speed_z, flows
    )


def outer_pieces(ref, nx, reach, inside):
    return [(ref, -reach, inside, 0), (ref, nx - inside, nx + reach, reach + inside)]


def outer_kernel(nx, ny, dt_ref, *refs):
    x_edges, corners = refs[0:2], refs[2:4]
    cells_in, stress_in, state_in, energies_in, peak_in = refs[4:9]
    state_out, passive_out, speed_y, speed_z, flows, increment_ref = refs[9:15]
    beyond, third, stress_out, heat, growth, energies_out = refs[15:21]
    swept, work = refs[21:23], refs[23:25]
    nz = increment_ref.shape[-1]
    zero = hidden_zero()
    half = 0.5 * dt_ref[0]
    wide, tall = ny + 4, ny + 12

    columns, singles, rows_of_corner = corner_layers()
    for k, (side, edge) in enumerate(zip(SIDES, x_edges)):
        for number, (field, past) in enumerate(x_layers()):
            column = LEFT - past if side < 0 else LEFT - 1 + past
            beyond[field, column, pl.ds(TOP, ny), :] = edge[pl.ds(zero + number * ny, ny), :]
        offset = len(x_layers()) * ny
        third[k, EDGE_KINDS, pl.ds(TOP, ny), :] = edge[pl.ds(zero + offset, ny), :]
        offset += ny
        for row in (0, ny - 1):
            for kind in range(EDGE_KINDS):
                third[k, kind, pl.ds(TOP + row, 1), :] = edge[pl.ds(offset, 1), :]
                offset += 1
    for link, corner in zip(LINKS, corners):
        low = is_low(link)
        for k, side in enumerate(SIDES):
            base, total = k * rows_of_corner, corner.shape[0]
            for _, field, past, rows, offset in columns:
                column = LEFT - past if side < 0 else LEFT - 1 + past
                to = pl.ds(TOP + pick(low, -rows, ny), rows)
                beyond[field, column, to, :] = corner[span(zero, base + offset, rows, total), :]
            to = pl.ds(TOP + pick(low, -2, ny + 1), 1)
            third[k, EDGE_KINDS, to, :] = corner[span(zero, base + singles, 1, total), :]
            for kind in range(EDGE_KINDS):
                to = pl.ds(TOP + pick(low, -1, ny), 1)
                third[k, kind, to, :] = corner[span(zero, base + singles + 1 + kind, 1, total), :]

    cells = [(cells_in, 0, nx, 0)] + outer_pieces(beyond, nx, LEFT, 0)
    stress = outer_pieces(stress_out, nx, 3, 2) + [(stress_in, 2, nx - 2, 1)]
    heat, growth = outer_pieces(heat, nx, 2, 2), outer_pieces(growth, nx, 2, 2)
    state = outer_pieces(state_out, nx, 2, 2) + [(state_in, 2, nx - 2, 0)]
    passive = outer_pieces(passive_out, nx, 2, 2)
    energies = outer_pieces(energies_out, nx, 0, 2) + [(energies_in, 2, nx - 2, 0)]
    speed_y, speed_z, flows = [outer_pieces(ref, nx, 0, 4) for ref in (speed_y, speed_z, flows)]

    row = lax.broadcasted_iota(jnp.int32, (tall, nz), 0) - 4
    for k, a in enumerate((-3, nx + 2)):
        above, below = [third[k, 3, pl.ds(zero + start, tall)] for start in (TOP - 3, TOP - 5)]
        density, energy, spread, _, whole = [third[k, kind, pl.ds(zero + TOP - 4, tall)] for kind in range(5)]
        spread += jnp.where((row == -1) | (row == ny - 1), above, -below)
        split = (row == -1) | (row == 0) | (row == ny - 1) | (row == ny)
        write(stress, a, jnp.where(split, density * per_mass(energy, spread), whole))

    ends = (*range(-2, 2), *range(nx - 2, nx + 2))
    spread_columns(zero, ends, tall, half, cells, stress, heat, growth)
    advance_columns(zero, ends, wide, half, cells, stress, heat, growth, passive, state, energies, nx)
    peak = peak_in[...]
    for k, first in enumerate((0, nx - 4)):
        peak = jnp.maximum(
            peak,
            flow_columns(
                zero, first, first + 4, ny, half, state, energies, swept[k], work[k], speed_y, speed_z, flows
            ),
        )
    peak = jnp.max(jnp.where(row[4 : 4 + wide] < ny, peak, 0.0), axis=0, keepdims=True)
    increment_ref[...] = jnp.broadcast_to(0.3 / peak, increment_ref.shape)


def carry_kernel(nx, ny, dt_ref, *refs):
    state_in, passive_in, speed_y_in, speed_z_in, flows_in = refs[0:5]
    state_out, passive_out, speed_y_out, speed_z_out, flows_out = refs[5:10]
    density_out, energy_out, flow_outs, swept, work, written = refs[10], refs[11], refs[12:15], refs[15], refs[16], refs[17]
    zero = hidden_zero()
    half = 0.5 * dt_ref[0]
    wide = ny + 4
    copies = []
    for k in range(3):
        for piece, (ref, first, last, number) in enumerate([(flows_in, 4, nx - 4, 0)] + outer_pieces(flows_out, nx, 0, 4)):
            source = ref.at[k, pl.ds(number, last - first)]
            copies.append(
                pltpu.make_async_copy(source, flow_outs[k].at[pl.ds(first, last - first)], written.at[k, piece])
            )
    for copy in copies:
        copy.start()
    state = outer_pieces(state_out, nx, 2, 2) + [(state_in, 2, nx - 2, 0)]
    passive = outer_pieces(passive_out, nx, 2, 2) + [(passive_in, 2, nx - 2, 0)]
    speed_y = outer_pieces(speed_y_out, nx, 0, 4) + [(speed_y_in, 4, nx - 4, 0)]
    speed_z = outer_pieces(speed_z_out, nx, 0, 4) + [(speed_z_in, 4, nx - 4, 0)]
    sweep_x(
        lambda field, a, part: read(zero, passive, a, part, 8, field),
        lambda a, part: read(zero, state, a, part, 8, 0),
        swept, (0, 1), 0, nx, wide, half,
    )
    factors = [face_factors(*[read(zero, speed_y, a, start, wide) for start in (1, 2)], half) for a in range(nx)]
    for a, moved in enumerate(sweep_y(zero, swept, work, range(nx), (0, 1), factors, wide)):
        along = read(zero, speed_z, a, 0, wide)
        final = sweep_z(moved, face_factors(down(along), along, half))
        density_out[a] = final[0][:ny]
        energy_out[a] = final[1][:ny]
    for copy in copies:
        copy.wait()


def body(density0, energy0, x_velocity, y_velocity, z_velocity, time_increment):
    nx, ny, nz = density0.shape
    fields = (density0, energy0, x_velocity, y_velocity, z_velocity)
    wide, tall = ny + 4, ny + 12

    def array(*shape):
        return jax.ShapeDtypeStruct((*shape, nz), jnp.float32)

    def scratch(*shape):
        return pltpu.VMEM((*shape, nz), jnp.float32)

    def limit(mebibytes):
        return pltpu.CompilerParams(vmem_limit_bytes=mebibytes * 1024 * 1024)

    x_edge, y_edge, corner = array(x_edge_rows(ny)), array(y_layers(nx)[1]), array(2 * corner_layers()[2])
    placed = [pltpu.with_memory_space_constraint(field, pltpu.HBM) for field in fields]
    x_edges = pl.pallas_call(
        functools.partial(x_pack_kernel, nx, ny),
        out_shape=[x_edge] * 2,
        in_specs=[HBM] * 5,
        out_specs=[VMEM] * 2,
        scratch_shapes=[scratch(5, 8, ny), scratch(4, ny + 20), pltpu.SemaphoreType.DMA((5, 2))],
        compiler_params=limit(4),
        name="x_pack",
    )(*placed)
    x_edges = [along_x(edge, side) for edge, side in zip(x_edges, SIDES)]
    own, *y_edges = pl.pallas_call(
        functools.partial(y_pack_kernel, nx, ny),
        out_shape=[array(5, nx, ny + 12), y_edge, y_edge],
        in_specs=[HBM] * 5,
        out_specs=[VMEM] * 3,
        scratch_shapes=[pltpu.SemaphoreType.DMA((5,))],
        compiler_params=limit(4),
        name="y_pack",
    )(*placed)
    y_edges = [along_y(edge, link) for edge, link in zip(y_edges, LINKS)]
    corners = pl.pallas_call(
        functools.partial(corner_kernel, ny),
        out_shape=[corner] * 2,
        in_specs=[VMEM] * 2,
        out_specs=[VMEM] * 2,
        compiler_params=limit(4),
        name="corners",
    )(*x_edges)
    corners = [along_y(corner, link) for corner, link in zip(corners, LINKS)]
    increment = time_increment.reshape(1)
    passed_in = [array(3, nx - 4, wide), array(2, nx - 4, wide), array(nx - 8, wide + 8), array(nx - 8, wide), array(3, nx - 8, ny)]
    passed_out = [array(3, 8, wide), array(2, 8, wide), array(8, wide + 8), array(8, wide), array(3, 8, ny)]
    cells, stress, state_in, passive_in, energies, *rest_in, peak = pl.pallas_call(
        functools.partial(inner_kernel, nx, ny),
        out_shape=[
            array(5, nx, ny + 20),
            array(nx - 2, tall),
            *passed_in[:2],
            array(nx - 4, wide + 8),
            *passed_in[2:],
            array(wide),
        ],
        in_specs=[SMEM] + [VMEM] * 3,
        out_specs=[VMEM] * 9,
        scratch_shapes=[
            scratch(nx - 2, tall),
            scratch(nx - 2, tall),
            scratch(3, nx - 8, wide + 8),
            scratch(3, nx - 8, wide + 8),
        ],
        compiler_params=limit(8),
        cost_estimate=pl.CostEstimate(flops=5 * 10**6, bytes_accessed=2 * 10**6, transcendentals=0),
        name="inner",
    )(increment, own, *y_edges)
    *outer, smallest = pl.pallas_call(
        functools.partial(outer_kernel, nx, ny),
        out_shape=passed_out + [array(lax.axis_size(("gx", "gy")))],
        in_specs=[SMEM] + [VMEM] * 9,
        out_specs=[VMEM] * 6,
        scratch_shapes=[
            scratch(5, 2 * LEFT, ny + 20),
            scratch(2, EDGE_KINDS + 1, ny + 20),
            scratch(10, tall),
            scratch(8, tall),
            scratch(8, tall),
            scratch(4, wide + 8),
            scratch(3, 4, wide + 8),
            scratch(3, 4, wide + 8),
            scratch(3, 4, wide + 8),
            scratch(3, 4, wide + 8),
        ],
        compiler_params=limit(8),
        name="outer",
    )(increment, *x_edges, *corners, cells, stress, state_in, energies, peak)
    outs = pl.pallas_call(
        functools.partial(carry_kernel, nx, ny),
        out_shape=[array(nx, ny)] * 5,
        in_specs=[SMEM] + [VMEM] * 10,
        out_specs=[VMEM] * 2 + [HBM] * 3,
        scratch_shapes=[
            scratch(2, nx, wide + 8),
            scratch(2, nx, wide + 8),
            pltpu.SemaphoreType.DMA((3, 3)),
        ],
        compiler_params=limit(8),
        cost_estimate=pl.CostEstimate(flops=10**7, bytes_accessed=4 * 10**6, transcendentals=0),
        name="carry",
    )(increment, state_in, passive_in, *rest_in, *outer)
    return (*outs, jnp.min(lax.all_to_all(smallest, ("gx", "gy"), 0, 0, tiled=True)))


def solution(mesh):
    cells = P("gx", "gy", None)
    return jax.shard_map(
        body,
        mesh=mesh,
        in_specs=(cells,) * 5 + (P(),),
        out_specs=(cells,) * 5 + (P(),),
        check_vma=False,
    )
```

```python
import functools

import jax
import jax.numpy as jnp
from jax import lax
from jax.experimental import pallas as pl
from jax.experimental.pallas import tpu as pltpu
from jax.sharding import PartitionSpec as P

DENSITY, ENERGY, XV, YV, ZV = range(5)
TOP = 8
LEFT = 3
SIDES = (-1, 1)
NEAR, FAR = "near", "far"
LINKS = (FAR, NEAR)
EDGE_KINDS = 4
VMEM = pl.BlockSpec(memory_space=pltpu.VMEM)
HBM = pl.BlockSpec(memory_space=pltpu.HBM)
SMEM = pl.BlockSpec(memory_space=pltpu.SMEM)


def ghost_rows(field):
    return 4 if field == YV else 3


def x_layers():
    return [(field, past) for field in range(5) for past in (1, 2)] + [(XV, 3)]


def x_edge_rows(ny):
    return (len(x_layers()) + 1) * ny + 2 * EDGE_KINDS


def y_layers(nx):
    found, offset = [], 0
    for a in range(nx):
        for field in range(5):
            found.append((field, a, ghost_rows(field), offset))
            offset += ghost_rows(field)
    return found, (offset // 8 + 2) * 8


def corner_layers():
    found, offset = [], 0
    for number, (field, past) in enumerate(x_layers()):
        found.append((number, field, past, ghost_rows(field), offset))
        offset += ghost_rows(field)
    return found, offset, -(-(offset + 1 + EDGE_KINDS) // 8) * 8


def is_low(link):
    odd = lax.rem(lax.axis_index("gy"), 2)
    return odd if link == NEAR else 1 - odd


def pick(flag, one, other):
    return flag * one + (1 - flag) * other


def along_x(value, side):
    count = lax.axis_size("gx")
    return lax.ppermute(value, "gx", [((i + side) % count, i) for i in range(count)])


def along_y(value, link):
    count = lax.axis_size("gy")
    partners = [i ^ 1 if link == NEAR else (((i - 1) ^ 1) + 1) % count for i in range(count)]
    return lax.ppermute(value, "gy", list(enumerate(partners)))


def hidden_zero():
    return lax.shift_right_logical(lax.axis_index("gx"), 20)


def span(zero, start, count, total):
    return pl.ds(start if start + -(-count // 8) * 8 > total else zero + start, count)


def per_mass(energy, spread):
    return 0.4 * energy + 0.5 * jnp.square(jnp.minimum(0.5 * spread, 0.0))


def x_pack_kernel(nx, ny, *refs):
    fields, x_edges, near, padded, arrived = refs[:5], refs[5:7], refs[7], refs[8], refs[9]
    zero = hidden_zero()
    order = (ZV, YV, XV, ENERGY, DENSITY)
    copies = {}
    for field in order:
        width = 4 if field == XV else 3
        for k, (first, place_at) in enumerate(((nx - width, 4 - width), (0, 4))):
            copies[field, k] = pltpu.make_async_copy(
                fields[field].at[pl.ds(first, width)], near.at[field, pl.ds(place_at, width)], arrived.at[field, k]
            )
    for copy in copies.values():
        copy.start()
    thirds = (1, 6)
    for k in range(2):
        padded[k] = jnp.zeros_like(padded[k])
    for current in order:
        for k, (side, edge) in enumerate(zip(SIDES, x_edges)):
            copies[current, k].wait()
            if current == ZV:
                padded[2 + k, pl.ds(TOP, ny), :] = up(near[ZV, thirds[k]]) - down(near[ZV, thirds[k]])
            if current == YV:
                padded[k, pl.ds(TOP, ny), :] = near[YV, thirds[k]]
            if current == ENERGY:
                a = thirds[k]
                spread = near[XV, a + 1] - near[XV, a - 1]
                spread += padded[k, pl.ds(zero + (TOP + 1), ny), :] - padded[k, pl.ds(zero + (TOP - 1), ny), :]
                spread += padded[2 + k, pl.ds(TOP, ny), :]
                padded[2 + k, pl.ds(TOP, ny), :] = spread
                padded[4 + k, pl.ds(TOP, ny), :] = per_mass(near[ENERGY, a], spread)
            for number, (field, past) in enumerate(x_layers()):
                if field == current:
                    edge[pl.ds(zero + number * ny, ny), :] = near[field, 4 - past if side < 0 else 3 + past]
    for k, edge in enumerate(x_edges):
        a = thirds[k]
        offset = len(x_layers()) * ny
        edge[pl.ds(zero + offset, ny), :] = near[DENSITY, a] * padded[4 + k, pl.ds(TOP, ny), :]
        offset += ny
        for row in (0, ny - 1):
            for value in (near[DENSITY, a, pl.ds(row, 1), :], near[ENERGY, a, pl.ds(row, 1), :],
                          padded[2 + k, pl.ds(TOP + row, 1), :], near[YV, a, pl.ds(row, 1), :]):
                edge[pl.ds(offset, 1), :] = value
                offset += 1


def y_pack_kernel(nx, ny, *refs):
    fields, own, y_edges, arrived = refs[:5], refs[5], refs[6:8], refs[8]
    zero = hidden_zero()
    copies = [
        pltpu.make_async_copy(fields[field], own.at[field, pl.ds(0, nx), pl.ds(0, ny), :], arrived.at[field])
        for field in range(5)
    ]
    for copy in copies:
        copy.start()
    for current, copy in enumerate(copies):
        copy.wait()
        for link, edge in zip(LINKS, y_edges):
            for field, a, rows, offset in y_layers(nx)[0]:
                if field == current:
                    start = pick(is_low(link), 0, ny - rows)
                    edge[pl.ds(zero + offset, rows), :] = own[field, a, pl.ds(start, rows), :]


def corner_kernel(ny, *refs):
    x_edges, outs = refs[:2], refs[2:]
    zero = hidden_zero()
    columns, singles, rows_of_corner = corner_layers()
    for link, out in zip(LINKS, outs):
        low = is_low(link)
        for k, edge in enumerate(x_edges):
            base, total = k * rows_of_corner, out.shape[0]
            for number, _, _, rows, offset in columns:
                out[span(zero, base + offset, rows, total), :] = edge[pl.ds(number * ny + pick(low, 0, ny - rows), rows), :]
            number = len(x_layers())
            out[span(zero, base + singles, 1, total), :] = edge[pl.ds(number * ny + pick(low, 1, ny - 2), 1), :]
            first, last = [
                edge[pl.ds((number + 1) * ny + k * EDGE_KINDS, EDGE_KINDS), :] for k in range(2)
            ]
            out[span(zero, base + singles + 1, EDGE_KINDS, total), :] = jnp.where(low == 1, first, last)


def limited(above, below):
    return jnp.minimum(jnp.maximum(above, jnp.minimum(below, 0.0)), jnp.maximum(below, 0.0))


def face_factors(v_minus, v, half_increment):
    courant = half_increment * (v_minus + v)
    size = jnp.abs(courant)
    return courant, 0.5 * size * (1.0 - size), courant > 0.0


def face_flux(factors, f_minus, f, s_minus, s):
    courant, slope_factor, upward = factors
    return courant * jnp.where(upward, f_minus, f) + slope_factor * jnp.where(upward, s_minus, s)


def up(value):
    return pltpu.roll(value, value.shape[-1] - 1, value.ndim - 1)


def down(value):
    return pltpu.roll(value, 1, value.ndim - 1)


def place(pieces, a):
    for ref, first, last, number in pieces:
        if first <= a < last:
            return ref, a - first + number
    raise ValueError(a)


def read(zero, pieces, a, start, count, *field):
    ref, number = place(pieces, a)
    return ref[(*field, number, pl.ds(zero + start, count), slice(None))]


def write(pieces, a, value, *field):
    ref, number = place(pieces, a)
    ref[(*field, number, pl.ds(0, value.shape[0]), slice(None))] = value


def sweep_x(state, speed, swept, fields, first, last, wide, half):
    for part in range(0, wide, 8):
        before = [state(field, first - 1, part) for field in fields]
        here = [state(field, first, part) for field in fields]
        steps = [h - b for h, b in zip(here, before)]
        slopes = [limited(st, b - state(field, first - 2, part)) for field, st, b in zip(fields, steps, before)]
        lower = None
        for a in range(first, last + 1):
            factors = face_factors(speed(a - 1, part), speed(a, part), half)
            fluxes = []
            for k, field in enumerate(fields):
                after = state(field, a + 1, part)
                step = after - here[k]
                slope = limited(step, steps[k])
                fluxes.append(face_flux(factors, before[k], here[k], slopes[k], slope))
                if lower is not None:
                    swept[field, a - 1 - first, pl.ds(part, 8)] = before[k] - (fluxes[k] - lower[k])
                before[k], here[k], steps[k], slopes[k] = here[k], after, step, slope
            lower = fluxes


def sweep_y(zero, swept, work, numbers, fields, factors, wide):
    cases = [(number, field) for number in numbers for field in fields]

    def rows(number, field, start):
        return swept[field, number, pl.ds(zero + start, wide)]

    for number, field in cases:
        start = [rows(number, field, first) for first in range(4)]
        steps = [after - before for before, after in zip(start, start[1:])]
        slopes = [limited(after, before) for before, after in zip(steps, steps[1:])]
        work[field, number, 0:wide] = face_flux(factors[number], start[1], start[2], *slopes)
    moved = {}
    for number, field in cases:
        flux, above = [work[field, number, pl.ds(zero + start, wide)] for start in (0, 1)]
        moved[number, field] = rows(number, field, 2) - (above - flux)
    return [[moved[number, field] for field in fields] for number in numbers]


def sweep_z(moved, factors):
    final = []
    for value in moved:
        below, above = down(value), up(value)
        step = value - below
        slopes = limited(step, below - pltpu.roll(value, 2, 1)), limited(above - value, step)
        flux = face_flux(factors, below, value, *slopes)
        final.append(value - (up(flux) - flux))
    return final


def spread_columns(zero, columns, tall, half, cells, stress, heat, growth):
    for a in columns:
        z = read(zero, cells, a, TOP - 4, tall, ZV)
        spread = (
            read(zero, cells, a + 1, TOP - 4, tall, XV)
            - read(zero, cells, a - 1, TOP - 4, tall, XV)
            + (read(zero, cells, a, TOP - 3, tall, YV) - read(zero, cells, a, TOP - 5, tall, YV))
            + (up(z) - down(z))
        )
        warmth = per_mass(read(zero, cells, a, TOP - 4, tall, ENERGY), spread)
        write(heat, a, warmth)
        write(stress, a, read(zero, cells, a, TOP - 4, tall, DENSITY) * warmth)
        write(growth, a, half * spread)


def advance_columns(zero, columns, wide, half, cells, stress, heat, growth, passive, state, energies, nx):
    for a in columns:
        density, energy, x, y, z = [read(zero, cells, a, TOP - 2, wide, field) for field in range(5)]
        grown = read(zero, growth, a, 2, wide)
        centre = read(zero, stress, a, 2, wide)
        scale = half / density
        density_one = density / (1.0 + grown)
        energy = energy - read(zero, heat, a, 2, wide) * grown
        write(passive, a, density_one, 0)
        write(passive, a, density_one * energy, 1)
        write(state, a, x - scale * (read(zero, stress, a + 1, 2, wide) - read(zero, stress, a - 1, 2, wide)), 0)
        write(state, a, y - scale * (read(zero, stress, a, 3, wide) - read(zero, stress, a, 1, wide)), 1)
        write(state, a, z - scale * (up(centre) - down(centre)), 2)
        if 0 <= a < nx:
            write(energies, a, energy)


def flow_columns(zero, first, last, ny, half, state, energies, swept, work, speed_y, speed_z, flows):
    wide = ny + 4
    sweep_x(
        lambda field, a, part: read(zero, state, a, part, 8, field),
        lambda a, part: read(zero, state, a, part, 8, 0),
        swept, (0, 1, 2), first, last, wide, half,
    )
    numbers = range(last - first)
    factors = []
    for number in numbers:
        below, here = [swept[1, number, pl.ds(zero + start, wide)] for start in (1, 2)]
        factors.append(face_factors(below, here, half))
        write(speed_y, first + number, swept[1, number, 0:wide])
    peak = None
    for a, moved in zip(range(first, last), sweep_y(zero, swept, work, numbers, (0, 1, 2), factors, wide)):
        write(speed_z, a, moved[2])
        final = sweep_z(moved, face_factors(down(moved[2]), moved[2], half))
        for field in range(3):
            write(flows, a, final[field][:ny], field)
        signal = (
            jnp.sqrt(0.56 * read(zero, energies, a, 2, wide))
            + jnp.abs(final[0])
            + jnp.abs(final[1])
            + jnp.abs(final[2])
        )
        peak = signal if peak is None else jnp.maximum(peak, signal)
    return peak


def inner_kernel(nx, ny, dt_ref, *refs):
    own, y_edges = refs[0], refs[1:3]
    cells, stress, state, passive, energies, speed_y, speed_z, flows, peak_ref = refs[3:12]
    heat, growth, swept, work = refs[12:]
    zero = hidden_zero()
    half = 0.5 * dt_ref[0]
    for field in range(5):
        for a in range(nx):
            cells[field, a, pl.ds(TOP, ny), :] = own[field, a, pl.ds(0, ny), :]
    for link, edge in zip(LINKS, y_edges):
        low = is_low(link)
        for field, a, rows, offset in y_layers(nx)[0]:
            cells[field, a, pl.ds(TOP + pick(low, -rows, ny), rows), :] = edge[pl.ds(zero + offset, rows), :]
    cells = [(cells, 0, nx, 0)]
    stress, heat, growth = [[(ref, 1, nx - 1, 0)] for ref in (stress, heat, growth)]
    state, passive, energies = [[(ref, 2, nx - 2, 0)] for ref in (state, passive, energies)]
    speed_y, speed_z, flows = [[(ref, 4, nx - 4, 0)] for ref in (speed_y, speed_z, flows)]
    spread_columns(zero, range(1, nx - 1), ny + 12, half, cells, stress, heat, growth)
    advance_columns(
        zero, range(2, nx - 2), ny + 4, half, cells, stress, heat, growth, passive, state, energies, nx
    )
    peak_ref[...] = flow_columns(
        zero, 4, nx - 4, ny, half, state, energies, swept, work, speed_y, speed_z, flows
    )


def outer_pieces(ref, nx, reach, inside):
    return [(ref, -reach, inside, 0), (ref, nx - inside, nx + reach, reach + inside)]


def outer_kernel(nx, ny, dt_ref, *refs):
    x_edges, corners = refs[0:2], refs[2:4]
    cells_in, stress_in, state_in, energies_in, peak_in = refs[4:9]
    state_out, passive_out, speed_y, speed_z, flows, increment_ref = refs[9:15]
    beyond, third, stress_out, heat, growth, energies_out = refs[15:21]
    swept, work = refs[21:23], refs[23:25]
    nz = increment_ref.shape[-1]
    zero = hidden_zero()
    half = 0.5 * dt_ref[0]
    wide, tall = ny + 4, ny + 12

    columns, singles, rows_of_corner = corner_layers()
    for k, (side, edge) in enumerate(zip(SIDES, x_edges)):
        for number, (field, past) in enumerate(x_layers()):
            column = LEFT - past if side < 0 else LEFT - 1 + past
            beyond[field, column, pl.ds(TOP, ny), :] = edge[pl.ds(zero + number * ny, ny), :]
        offset = len(x_layers()) * ny
        third[k, EDGE_KINDS, pl.ds(TOP, ny), :] = edge[pl.ds(zero + offset, ny), :]
        offset += ny
        for row in (0, ny - 1):
            for kind in range(EDGE_KINDS):
                third[k, kind, pl.ds(TOP + row, 1), :] = edge[pl.ds(offset, 1), :]
                offset += 1
    for link, corner in zip(LINKS, corners):
        low = is_low(link)
        for k, side in enumerate(SIDES):
            base, total = k * rows_of_corner, corner.shape[0]
            for _, field, past, rows, offset in columns:
                column = LEFT - past if side < 0 else LEFT - 1 + past
                to = pl.ds(TOP + pick(low, -rows, ny), rows)
                beyond[field, column, to, :] = corner[span(zero, base + offset, rows, total), :]
            to = pl.ds(TOP + pick(low, -2, ny + 1), 1)
            third[k, EDGE_KINDS, to, :] = corner[span(zero, base + singles, 1, total), :]
            for kind in range(EDGE_KINDS):
                to = pl.ds(TOP + pick(low, -1, ny), 1)
                third[k, kind, to, :] = corner[span(zero, base + singles + 1 + kind, 1, total), :]

    cells = [(cells_in, 0, nx, 0)] + outer_pieces(beyond, nx, LEFT, 0)
    stress = outer_pieces(stress_out, nx, 3, 2) + [(stress_in, 2, nx - 2, 1)]
    heat, growth = outer_pieces(heat, nx, 2, 2), outer_pieces(growth, nx, 2, 2)
    state = outer_pieces(state_out, nx, 2, 2) + [(state_in, 2, nx - 2, 0)]
    passive = outer_pieces(passive_out, nx, 2, 2)
    energies = outer_pieces(energies_out, nx, 0, 2) + [(energies_in, 2, nx - 2, 0)]
    speed_y, speed_z, flows = [outer_pieces(ref, nx, 0, 4) for ref in (speed_y, speed_z, flows)]

    row = lax.broadcasted_iota(jnp.int32, (tall, nz), 0) - 4
    for k, a in enumerate((-3, nx + 2)):
        above, below = [third[k, 3, pl.ds(zero + start, tall)] for start in (TOP - 3, TOP - 5)]
        density, energy, spread, _, whole = [third[k, kind, pl.ds(zero + TOP - 4, tall)] for kind in range(5)]
        spread += jnp.where((row == -1) | (row == ny - 1), above, -below)
        split = (row == -1) | (row == 0) | (row == ny - 1) | (row == ny)
        write(stress, a, jnp.where(split, density * per_mass(energy, spread), whole))

    ends = (*range(-2, 2), *range(nx - 2, nx + 2))
    spread_columns(zero, ends, tall, half, cells, stress, heat, growth)
    advance_columns(zero, ends, wide, half, cells, stress, heat, growth, passive, state, energies, nx)
    peak = peak_in[...]
    for k, first in enumerate((0, nx - 4)):
        peak = jnp.maximum(
            peak,
            flow_columns(
                zero, first, first + 4, ny, half, state, energies, swept[k], work[k], speed_y, speed_z, flows
            ),
        )
    peak = jnp.max(jnp.where(row[4 : 4 + wide] < ny, peak, 0.0), axis=0, keepdims=True)
    increment_ref[...] = jnp.broadcast_to(0.3 / peak, increment_ref.shape)


def carry_kernel(nx, ny, dt_ref, *refs):
    state_in, passive_in, speed_y_in, speed_z_in, flows_in = refs[0:5]
    state_out, passive_out, speed_y_out, speed_z_out, flows_out = refs[5:10]
    density_out, energy_out, flow_outs, swept, work, written = refs[10], refs[11], refs[12:15], refs[15], refs[16], refs[17]
    zero = hidden_zero()
    half = 0.5 * dt_ref[0]
    wide = ny + 4
    copies = []
    for k in range(3):
        for piece, (ref, first, last, number) in enumerate([(flows_in, 4, nx - 4, 0)] + outer_pieces(flows_out, nx, 0, 4)):
            source = ref.at[k, pl.ds(number, last - first)]
            copies.append(
                pltpu.make_async_copy(source, flow_outs[k].at[pl.ds(first, last - first)], written.at[k, piece])
            )
    for copy in copies:
        copy.start()
    state = outer_pieces(state_out, nx, 2, 2) + [(state_in, 2, nx - 2, 0)]
    passive = outer_pieces(passive_out, nx, 2, 2) + [(passive_in, 2, nx - 2, 0)]
    speed_y = outer_pieces(speed_y_out, nx, 0, 4) + [(speed_y_in, 4, nx - 4, 0)]
    speed_z = outer_pieces(speed_z_out, nx, 0, 4) + [(speed_z_in, 4, nx - 4, 0)]
    sweep_x(
        lambda field, a, part: read(zero, passive, a, part, 8, field),
        lambda a, part: read(zero, state, a, part, 8, 0),
        swept, (0, 1), 0, nx, wide, half,
    )
    factors = [face_factors(*[read(zero, speed_y, a, start, wide) for start in (1, 2)], half) for a in range(nx)]
    for a, moved in enumerate(sweep_y(zero, swept, work, range(nx), (0, 1), factors, wide)):
        along = read(zero, speed_z, a, 0, wide)
        final = sweep_z(moved, face_factors(down(along), along, half))
        density_out[a] = final[0][:ny]
        energy_out[a] = final[1][:ny]
    for copy in copies:
        copy.wait()


def body(density0, energy0, x_velocity, y_velocity, z_velocity, time_increment):
    nx, ny, nz = density0.shape
    fields = (density0, energy0, x_velocity, y_velocity, z_velocity)
    wide, tall = ny + 4, ny + 12

    def array(*shape):
        return jax.ShapeDtypeStruct((*shape, nz), jnp.float32)

    def scratch(*shape):
        return pltpu.VMEM((*shape, nz), jnp.float32)

    def limit(mebibytes):
        return pltpu.CompilerParams(vmem_limit_bytes=mebibytes * 1024 * 1024)

    x_edge, y_edge, corner = array(x_edge_rows(ny)), array(y_layers(nx)[1]), array(2 * corner_layers()[2])
    placed = [pltpu.with_memory_space_constraint(field, pltpu.HBM) for field in fields]
    x_edges = pl.pallas_call(
        functools.partial(x_pack_kernel, nx, ny),
        out_shape=[x_edge] * 2,
        in_specs=[HBM] * 5,
        out_specs=[VMEM] * 2,
        scratch_shapes=[scratch(5, 8, ny), scratch(6, ny + 20), pltpu.SemaphoreType.DMA((5, 2))],
        compiler_params=limit(4),
        name="x_pack",
    )(*placed)
    x_edges = [along_x(edge, side) for edge, side in zip(x_edges, SIDES)]
    own, *y_edges = pl.pallas_call(
        functools.partial(y_pack_kernel, nx, ny),
        out_shape=[array(5, nx, ny + 12), y_edge, y_edge],
        in_specs=[HBM] * 5,
        out_specs=[VMEM] * 3,
        scratch_shapes=[pltpu.SemaphoreType.DMA((5,))],
        compiler_params=limit(4),
        name="y_pack",
    )(*placed)
    y_edges = [along_y(edge, link) for edge, link in zip(y_edges, LINKS)]
    corners = pl.pallas_call(
        functools.partial(corner_kernel, ny),
        out_shape=[corner] * 2,
        in_specs=[VMEM] * 2,
        out_specs=[VMEM] * 2,
        compiler_params=limit(4),
        name="corners",
    )(*x_edges)
    corners = [along_y(corner, link) for corner, link in zip(corners, LINKS)]
    increment = time_increment.reshape(1)
    passed_in = [array(3, nx - 4, wide), array(2, nx - 4, wide), array(nx - 8, wide + 8), array(nx - 8, wide), array(3, nx - 8, ny)]
    passed_out = [array(3, 8, wide), array(2, 8, wide), array(8, wide + 8), array(8, wide), array(3, 8, ny)]
    cells, stress, state_in, passive_in, energies, *rest_in, peak = pl.pallas_call(
        functools.partial(inner_kernel, nx, ny),
        out_shape=[
            array(5, nx, ny + 20),
            array(nx - 2, tall),
            *passed_in[:2],
            array(nx - 4, wide + 8),
            *passed_in[2:],
            array(wide),
        ],
        in_specs=[SMEM] + [VMEM] * 3,
        out_specs=[VMEM] * 9,
        scratch_shapes=[
            scratch(nx - 2, tall),
            scratch(nx - 2, tall),
            scratch(3, nx - 8, wide + 8),
            scratch(3, nx - 8, wide + 8),
        ],
        compiler_params=limit(8),
        cost_estimate=pl.CostEstimate(flops=5 * 10**6, bytes_accessed=2 * 10**6, transcendentals=0),
        name="inner",
    )(increment, own, *y_edges)
    *outer, smallest = pl.pallas_call(
        functools.partial(outer_kernel, nx, ny),
        out_shape=passed_out + [array(lax.axis_size(("gx", "gy")))],
        in_specs=[SMEM] + [VMEM] * 9,
        out_specs=[VMEM] * 6,
        scratch_shapes=[
            scratch(5, 2 * LEFT, ny + 20),
            scratch(2, EDGE_KINDS + 1, ny + 20),
            scratch(10, tall),
            scratch(8, tall),
            scratch(8, tall),
            scratch(4, wide + 8),
            scratch(3, 4, wide + 8),
            scratch(3, 4, wide + 8),
            scratch(3, 4, wide + 8),
            scratch(3, 4, wide + 8),
        ],
        compiler_params=limit(8),
        name="outer",
    )(increment, *x_edges, *corners, cells, stress, state_in, energies, peak)
    outs = pl.pallas_call(
        functools.partial(carry_kernel, nx, ny),
        out_shape=[array(nx, ny)] * 5,
        in_specs=[SMEM] + [VMEM] * 10,
        out_specs=[VMEM] * 2 + [HBM] * 3,
        scratch_shapes=[
            scratch(2, nx, wide + 8),
            scratch(2, nx, wide + 8),
            pltpu.SemaphoreType.DMA((3, 3)),
        ],
        compiler_params=limit(8),
        cost_estimate=pl.CostEstimate(flops=10**7, bytes_accessed=4 * 10**6, transcendentals=0),
        name="carry",
    )(increment, state_in, passive_in, *rest_in, *outer)
    return (*outs, jnp.min(lax.all_to_all(smallest, ("gx", "gy"), 0, 0, tiled=True)))


def solution(mesh):
    cells = P("gx", "gy", None)
    return jax.shard_map(
        body,
        mesh=mesh,
        in_specs=(cells,) * 5 + (P(),),
        out_specs=(cells,) * 5 + (P(),),
        check_vma=False,
    )
```

```python
import functools

import jax
import jax.numpy as jnp
from jax import lax
from jax.experimental import pallas as pl
from jax.experimental.pallas import tpu as pltpu
from jax.sharding import PartitionSpec as P

DENSITY, ENERGY, XV, YV, ZV = range(5)
TOP = 8
LEFT = 3
SIDES = (-1, 1)
NEAR, FAR = "near", "far"
LINKS = (FAR, NEAR)
EDGE_KINDS = 4
VMEM = pl.BlockSpec(memory_space=pltpu.VMEM)
HBM = pl.BlockSpec(memory_space=pltpu.HBM)
SMEM = pl.BlockSpec(memory_space=pltpu.SMEM)


def ghost_rows(field):
    return 4 if field == YV else 3


def x_layers():
    return [(field, past) for field in range(5) for past in (1, 2)] + [(XV, 3)]


def x_edge_rows(ny):
    return (len(x_layers()) + 1) * ny + 2 * EDGE_KINDS


def y_layers(nx):
    found, offset = [], 0
    for a in range(nx):
        for field in range(5):
            found.append((field, a, ghost_rows(field), offset))
            offset += ghost_rows(field)
    return found, (offset // 8 + 2) * 8


def corner_layers():
    found, offset = [], 0
    for number, (field, past) in enumerate(x_layers()):
        found.append((number, field, past, ghost_rows(field), offset))
        offset += ghost_rows(field)
    return found, offset, -(-(offset + 1 + EDGE_KINDS) // 8) * 8


def is_low(link):
    odd = lax.rem(lax.axis_index("gy"), 2)
    return odd if link == NEAR else 1 - odd


def pick(flag, one, other):
    return flag * one + (1 - flag) * other


def along_x(value, side):
    count = lax.axis_size("gx")
    return lax.ppermute(value, "gx", [((i + side) % count, i) for i in range(count)])


def along_y(value, link):
    count = lax.axis_size("gy")
    partners = [i ^ 1 if link == NEAR else (((i - 1) ^ 1) + 1) % count for i in range(count)]
    return lax.ppermute(value, "gy", list(enumerate(partners)))


def hidden_zero():
    return lax.shift_right_logical(lax.axis_index("gx"), 20)


def span(zero, start, count, total):
    return pl.ds(start if start + -(-count // 8) * 8 > total else zero + start, count)


def per_mass(energy, spread):
    return 0.4 * energy + 0.5 * jnp.square(jnp.minimum(0.5 * spread, 0.0))


def x_pack_kernel(nx, ny, *refs):
    fields, x_edges, near, padded, arrived = refs[:5], refs[5:7], refs[7], refs[8], refs[9]
    zero = hidden_zero()
    order = (ZV, YV, XV, ENERGY, DENSITY)
    copies = {}
    for field in order:
        width = 4 if field == XV else 3
        for k, (first, place_at) in enumerate(((nx - width, 4 - width), (0, 4))):
            copies[field, k] = pltpu.make_async_copy(
                fields[field].at[pl.ds(first, width)], near.at[field, pl.ds(place_at, width)], arrived.at[field, k]
            )
    for copy in copies.values():
        copy.start()
    thirds = (1, 6)
    for current in order:
        for k, (side, edge) in enumerate(zip(SIDES, x_edges)):
            copies[current, k].wait()
            if current == ZV:
                padded[k] = jnp.zeros_like(padded[k])
                padded[2 + k, pl.ds(TOP, ny), :] = up(near[ZV, thirds[k]]) - down(near[ZV, thirds[k]])
            if current == YV:
                padded[k, pl.ds(TOP, ny), :] = near[YV, thirds[k]]
            for number, (field, past) in enumerate(x_layers()):
                if field == current:
                    edge[pl.ds(zero + number * ny, ny), :] = near[field, 4 - past if side < 0 else 3 + past]
    for k, edge in enumerate(x_edges):
        a = thirds[k]
        offset = len(x_layers()) * ny
        spread = near[XV, a + 1] - near[XV, a - 1]
        spread += padded[k, pl.ds(zero + (TOP + 1), ny), :] - padded[k, pl.ds(zero + (TOP - 1), ny), :]
        spread += padded[2 + k, pl.ds(TOP, ny), :]
        edge[pl.ds(zero + offset, ny), :] = near[DENSITY, a] * per_mass(near[ENERGY, a], spread)
        offset += ny
        padded[2 + k, pl.ds(TOP, ny), :] = spread
        for row in (0, ny - 1):
            for value in (near[DENSITY, a, pl.ds(row, 1), :], near[ENERGY, a, pl.ds(row, 1), :],
                          padded[2 + k, pl.ds(TOP + row, 1), :], near[YV, a, pl.ds(row, 1), :]):
                edge[pl.ds(offset, 1), :] = value
                offset += 1


def y_pack_kernel(nx, ny, *refs):
    fields, own, y_edges, arrived = refs[:5], refs[5], refs[6:8], refs[8]
    zero = hidden_zero()
    copies = [
        pltpu.make_async_copy(fields[field], own.at[field, pl.ds(0, nx), pl.ds(0, ny), :], arrived.at[field])
        for field in range(5)
    ]
    for copy in copies:
        copy.start()
    for current, copy in enumerate(copies):
        copy.wait()
        for link, edge in zip(LINKS, y_edges):
            for field, a, rows, offset in y_layers(nx)[0]:
                if field == current:
                    start = pick(is_low(link), 0, ny - rows)
                    edge[pl.ds(zero + offset, rows), :] = own[field, a, pl.ds(start, rows), :]


def corner_kernel(ny, *refs):
    x_edges, outs = refs[:2], refs[2:]
    zero = hidden_zero()
    columns, singles, rows_of_corner = corner_layers()
    for link, out in zip(LINKS, outs):
        low = is_low(link)
        for k, edge in enumerate(x_edges):
            base, total = k * rows_of_corner, out.shape[0]
            for number, _, _, rows, offset in columns:
                out[span(zero, base + offset, rows, total), :] = edge[pl.ds(number * ny + pick(low, 0, ny - rows), rows), :]
            number = len(x_layers())
            out[span(zero, base + singles, 1, total), :] = edge[pl.ds(number * ny + pick(low, 1, ny - 2), 1), :]
            first, last = [
                edge[pl.ds((number + 1) * ny + k * EDGE_KINDS, EDGE_KINDS), :] for k in range(2)
            ]
            out[span(zero, base + singles + 1, EDGE_KINDS, total), :] = jnp.where(low == 1, first, last)


def limited(above, below):
    return jnp.minimum(jnp.maximum(above, jnp.minimum(below, 0.0)), jnp.maximum(below, 0.0))


def face_factors(v_minus, v, half_increment):
    courant = half_increment * (v_minus + v)
    size = jnp.abs(courant)
    return courant, 0.5 * size * (1.0 - size), courant > 0.0


def face_flux(factors, f_minus, f, s_minus, s):
    courant, slope_factor, upward = factors
    return courant * jnp.where(upward, f_minus, f) + slope_factor * jnp.where(upward, s_minus, s)


def up(value):
    return pltpu.roll(value, value.shape[-1] - 1, value.ndim - 1)


def down(value):
    return pltpu.roll(value, 1, value.ndim - 1)


def place(pieces, a):
    for ref, first, last, number in pieces:
        if first <= a < last:
            return ref, a - first + number
    raise ValueError(a)


def read(zero, pieces, a, start, count, *field):
    ref, number = place(pieces, a)
    return ref[(*field, number, pl.ds(zero + start, count), slice(None))]


def write(pieces, a, value, *field):
    ref, number = place(pieces, a)
    ref[(*field, number, pl.ds(0, value.shape[0]), slice(None))] = value


def sweep_x(state, speed, swept, fields, first, last, wide, half):
    for part in range(0, wide, 8):
        before = [state(field, first - 1, part) for field in fields]
        here = [state(field, first, part) for field in fields]
        steps = [h - b for h, b in zip(here, before)]
        slopes = [limited(st, b - state(field, first - 2, part)) for field, st, b in zip(fields, steps, before)]
        lower = None
        for a in range(first, last + 1):
            factors = face_factors(speed(a - 1, part), speed(a, part), half)
            fluxes = []
            for k, field in enumerate(fields):
                after = state(field, a + 1, part)
                step = after - here[k]
                slope = limited(step, steps[k])
                fluxes.append(face_flux(factors, before[k], here[k], slopes[k], slope))
                if lower is not None:
                    swept[field, a - 1 - first, pl.ds(part, 8)] = before[k] - (fluxes[k] - lower[k])
                before[k], here[k], steps[k], slopes[k] = here[k], after, step, slope
            lower = fluxes


def sweep_y(zero, swept, work, numbers, fields, factors, wide):
    cases = [(number, field) for number in numbers for field in fields]

    def rows(number, field, start):
        return swept[field, number, pl.ds(zero + start, wide)]

    for number, field in cases:
        start = [rows(number, field, first) for first in range(4)]
        steps = [after - before for before, after in zip(start, start[1:])]
        slopes = [limited(after, before) for before, after in zip(steps, steps[1:])]
        work[field, number, 0:wide] = face_flux(factors[number], start[1], start[2], *slopes)
    moved = {}
    for number, field in cases:
        flux, above = [work[field, number, pl.ds(zero + start, wide)] for start in (0, 1)]
        moved[number, field] = rows(number, field, 2) - (above - flux)
    return [[moved[number, field] for field in fields] for number in numbers]


def sweep_z(moved, factors):
    final = []
    for value in moved:
        below, above = down(value), up(value)
        step = value - below
        slopes = limited(step, below - pltpu.roll(value, 2, 1)), limited(above - value, step)
        flux = face_flux(factors, below, value, *slopes)
        final.append(value - (up(flux) - flux))
    return final


def spread_columns(zero, columns, tall, half, cells, stress, heat, growth):
    for a in columns:
        z = read(zero, cells, a, TOP - 4, tall, ZV)
        spread = (
            read(zero, cells, a + 1, TOP - 4, tall, XV)
            - read(zero, cells, a - 1, TOP - 4, tall, XV)
            + (read(zero, cells, a, TOP - 3, tall, YV) - read(zero, cells, a, TOP - 5, tall, YV))
            + (up(z) - down(z))
        )
        warmth = per_mass(read(zero, cells, a, TOP - 4, tall, ENERGY), spread)
        write(heat, a, warmth)
        write(stress, a, read(zero, cells, a, TOP - 4, tall, DENSITY) * warmth)
        write(growth, a, half * spread)


def advance_columns(zero, columns, wide, half, cells, stress, heat, growth, passive, state, roots, nx):
    for a in columns:
        density, energy, x, y, z = [read(zero, cells, a, TOP - 2, wide, field) for field in range(5)]
        grown = read(zero, growth, a, 2, wide)
        centre = read(zero, stress, a, 2, wide)
        scale = half / density
        density_one = density / (1.0 + grown)
        energy = energy - read(zero, heat, a, 2, wide) * grown
        write(passive, a, density_one, 0)
        write(passive, a, density_one * energy, 1)
        write(state, a, x - scale * (read(zero, stress, a + 1, 2, wide) - read(zero, stress, a - 1, 2, wide)), 0)
        write(state, a, y - scale * (read(zero, stress, a, 3, wide) - read(zero, stress, a, 1, wide)), 1)
        write(state, a, z - scale * (up(centre) - down(centre)), 2)
        if 0 <= a < nx:
            write(roots, a, jnp.sqrt(0.56 * energy))


def flow_columns(zero, first, last, ny, half, state, roots, swept, work, speed_y, speed_z, flows):
    wide = ny + 4
    sweep_x(
        lambda field, a, part: read(zero, state, a, part, 8, field),
        lambda a, part: read(zero, state, a, part, 8, 0),
        swept, (0, 1, 2), first, last, wide, half,
    )
    numbers = range(last - first)
    factors = []
    for number in numbers:
        below, here = [swept[1, number, pl.ds(zero + start, wide)] for start in (1, 2)]
        factors.append(face_factors(below, here, half))
        write(speed_y, first + number, swept[1, number, 0:wide])
    peak = None
    for a, moved in zip(range(first, last), sweep_y(zero, swept, work, numbers, (0, 1, 2), factors, wide)):
        write(speed_z, a, moved[2])
        final = sweep_z(moved, face_factors(down(moved[2]), moved[2], half))
        for field in range(3):
            write(flows, a, final[field][:ny], field)
        signal = (
            read(zero, roots, a, 2, wide)
            + jnp.abs(final[0])
            + jnp.abs(final[1])
            + jnp.abs(final[2])
        )
        peak = signal if peak is None else jnp.maximum(peak, signal)
    return peak


def inner_kernel(nx, ny, dt_ref, *refs):
    own, y_edges = refs[0], refs[1:3]
    cells, stress, state, passive, roots, speed_y, speed_z, flows, peak_ref = refs[3:12]
    heat, growth, swept, work = refs[12:]
    zero = hidden_zero()
    half = 0.5 * dt_ref[0]
    for field in range(5):
        for a in range(nx):
            cells[field, a, pl.ds(TOP, ny), :] = own[field, a, pl.ds(0, ny), :]
    for link, edge in zip(LINKS, y_edges):
        low = is_low(link)
        for field, a, rows, offset in y_layers(nx)[0]:
            cells[field, a, pl.ds(TOP + pick(low, -rows, ny), rows), :] = edge[pl.ds(zero + offset, rows), :]
    cells = [(cells, 0, nx, 0)]
    stress, heat, growth = [[(ref, 1, nx - 1, 0)] for ref in (stress, heat, growth)]
    state, passive, roots = [[(ref, 2, nx - 2, 0)] for ref in (state, passive, roots)]
    speed_y, speed_z, flows = [[(ref, 4, nx - 4, 0)] for ref in (speed_y, speed_z, flows)]
    spread_columns(zero, range(1, nx - 1), ny + 12, half, cells, stress, heat, growth)
    advance_columns(
        zero, range(2, nx - 2), ny + 4, half, cells, stress, heat, growth, passive, state, roots, nx
    )
    peak_ref[...] = flow_columns(
        zero, 4, nx - 4, ny, half, state, roots, swept, work, speed_y, speed_z, flows
    )


def outer_pieces(ref, nx, reach, inside):
    return [(ref, -reach, inside, 0), (ref, nx - inside, nx + reach, reach + inside)]


def outer_kernel(nx, ny, dt_ref, *refs):
    x_edges, corners = refs[0:2], refs[2:4]
    cells_in, stress_in, state_in, roots_in, peak_in = refs[4:9]
    state_out, passive_out, speed_y, speed_z, flows, increment_ref = refs[9:15]
    beyond, third, stress_out, heat, growth, roots_out = refs[15:21]
    swept, work = refs[21:23], refs[23:25]
    nz = increment_ref.shape[-1]
    zero = hidden_zero()
    half = 0.5 * dt_ref[0]
    wide, tall = ny + 4, ny + 12

    columns, singles, rows_of_corner = corner_layers()
    for k, (side, edge) in enumerate(zip(SIDES, x_edges)):
        for number, (field, past) in enumerate(x_layers()):
            column = LEFT - past if side < 0 else LEFT - 1 + past
            beyond[field, column, pl.ds(TOP, ny), :] = edge[pl.ds(zero + number * ny, ny), :]
        offset = len(x_layers()) * ny
        third[k, EDGE_KINDS, pl.ds(TOP, ny), :] = edge[pl.ds(zero + offset, ny), :]
        offset += ny
        for row in (0, ny - 1):
            for kind in range(EDGE_KINDS):
                third[k, kind, pl.ds(TOP + row, 1), :] = edge[pl.ds(offset, 1), :]
                offset += 1
    for link, corner in zip(LINKS, corners):
        low = is_low(link)
        for k, side in enumerate(SIDES):
            base, total = k * rows_of_corner, corner.shape[0]
            for _, field, past, rows, offset in columns:
                column = LEFT - past if side < 0 else LEFT - 1 + past
                to = pl.ds(TOP + pick(low, -rows, ny), rows)
                beyond[field, column, to, :] = corner[span(zero, base + offset, rows, total), :]
            to = pl.ds(TOP + pick(low, -2, ny + 1), 1)
            third[k, EDGE_KINDS, to, :] = corner[span(zero, base + singles, 1, total), :]
            for kind in range(EDGE_KINDS):
                to = pl.ds(TOP + pick(low, -1, ny), 1)
                third[k, kind, to, :] = corner[span(zero, base + singles + 1 + kind, 1, total), :]

    cells = [(cells_in, 0, nx, 0)] + outer_pieces(beyond, nx, LEFT, 0)
    stress = outer_pieces(stress_out, nx, 3, 2) + [(stress_in, 2, nx - 2, 1)]
    heat, growth = outer_pieces(heat, nx, 2, 2), outer_pieces(growth, nx, 2, 2)
    state = outer_pieces(state_out, nx, 2, 2) + [(state_in, 2, nx - 2, 0)]
    passive = outer_pieces(passive_out, nx, 2, 2)
    roots = outer_pieces(roots_out, nx, 0, 2) + [(roots_in, 2, nx - 2, 0)]
    speed_y, speed_z, flows = [outer_pieces(ref, nx, 0, 4) for ref in (speed_y, speed_z, flows)]

    row = lax.broadcasted_iota(jnp.int32, (tall, nz), 0) - 4
    for k, a in enumerate((-3, nx + 2)):
        above, below = [third[k, 3, pl.ds(zero + start, tall)] for start in (TOP - 3, TOP - 5)]
        density, energy, spread, _, whole = [third[k, kind, pl.ds(zero + TOP - 4, tall)] for kind in range(5)]
        spread += jnp.where((row == -1) | (row == ny - 1), above, -below)
        split = (row == -1) | (row == 0) | (row == ny - 1) | (row == ny)
        write(stress, a, jnp.where(split, density * per_mass(energy, spread), whole))

    ends = (*range(-2, 2), *range(nx - 2, nx + 2))
    spread_columns(zero, ends, tall, half, cells, stress, heat, growth)
    advance_columns(zero, ends, wide, half, cells, stress, heat, growth, passive, state, roots, nx)
    peak = peak_in[...]
    for k, first in enumerate((0, nx - 4)):
        peak = jnp.maximum(
            peak,
            flow_columns(
                zero, first, first + 4, ny, half, state, roots, swept[k], work[k], speed_y, speed_z, flows
            ),
        )
    peak = jnp.max(jnp.where(row[4 : 4 + wide] < ny, peak, 0.0), axis=0, keepdims=True)
    increment_ref[...] = jnp.broadcast_to(0.3 / peak, increment_ref.shape)


def carry_kernel(nx, ny, dt_ref, *refs):
    state_in, passive_in, speed_y_in, speed_z_in, flows_in = refs[0:5]
    state_out, passive_out, speed_y_out, speed_z_out, flows_out = refs[5:10]
    density_out, energy_out, flow_outs, swept, work, written = refs[10], refs[11], refs[12:15], refs[15], refs[16], refs[17]
    zero = hidden_zero()
    half = 0.5 * dt_ref[0]
    wide = ny + 4
    copies = []
    for k in range(3):
        for piece, (ref, first, last, number) in enumerate([(flows_in, 4, nx - 4, 0)] + outer_pieces(flows_out, nx, 0, 4)):
            source = ref.at[k, pl.ds(number, last - first)]
            copies.append(
                pltpu.make_async_copy(source, flow_outs[k].at[pl.ds(first, last - first)], written.at[k, piece])
            )
    for copy in copies:
        copy.start()
    state = outer_pieces(state_out, nx, 2, 2) + [(state_in, 2, nx - 2, 0)]
    passive = outer_pieces(passive_out, nx, 2, 2) + [(passive_in, 2, nx - 2, 0)]
    speed_y = outer_pieces(speed_y_out, nx, 0, 4) + [(speed_y_in, 4, nx - 4, 0)]
    speed_z = outer_pieces(speed_z_out, nx, 0, 4) + [(speed_z_in, 4, nx - 4, 0)]
    sweep_x(
        lambda field, a, part: read(zero, passive, a, part, 8, field),
        lambda a, part: read(zero, state, a, part, 8, 0),
        swept, (0, 1), 0, nx, wide, half,
    )
    factors = [face_factors(*[read(zero, speed_y, a, start, wide) for start in (1, 2)], half) for a in range(nx)]
    for a, moved in enumerate(sweep_y(zero, swept, work, range(nx), (0, 1), factors, wide)):
        along = read(zero, speed_z, a, 0, wide)
        final = sweep_z(moved, face_factors(down(along), along, half))
        density_out[a] = final[0][:ny]
        energy_out[a] = final[1][:ny]
    for copy in copies:
        copy.wait()


def body(density0, energy0, x_velocity, y_velocity, z_velocity, time_increment):
    nx, ny, nz = density0.shape
    fields = (density0, energy0, x_velocity, y_velocity, z_velocity)
    wide, tall = ny + 4, ny + 12

    def array(*shape):
        return jax.ShapeDtypeStruct((*shape, nz), jnp.float32)

    def scratch(*shape):
        return pltpu.VMEM((*shape, nz), jnp.float32)

    def limit(mebibytes):
        return pltpu.CompilerParams(vmem_limit_bytes=mebibytes * 1024 * 1024)

    x_edge, y_edge, corner = array(x_edge_rows(ny)), array(y_layers(nx)[1]), array(2 * corner_layers()[2])
    placed = [pltpu.with_memory_space_constraint(field, pltpu.HBM) for field in fields]
    x_edges = pl.pallas_call(
        functools.partial(x_pack_kernel, nx, ny),
        out_shape=[x_edge] * 2,
        in_specs=[HBM] * 5,
        out_specs=[VMEM] * 2,
        scratch_shapes=[scratch(5, 8, ny), scratch(4, ny + 20), pltpu.SemaphoreType.DMA((5, 2))],
        compiler_params=limit(4),
        name="x_pack",
    )(*placed)
    x_edges = [along_x(edge, side) for edge, side in zip(x_edges, SIDES)]
    own, *y_edges = pl.pallas_call(
        functools.partial(y_pack_kernel, nx, ny),
        out_shape=[array(5, nx, ny + 12), y_edge, y_edge],
        in_specs=[HBM] * 5,
        out_specs=[VMEM] * 3,
        scratch_shapes=[pltpu.SemaphoreType.DMA((5,))],
        compiler_params=limit(4),
        name="y_pack",
    )(*placed)
    y_edges = [along_y(edge, link) for edge, link in zip(y_edges, LINKS)]
    corners = pl.pallas_call(
        functools.partial(corner_kernel, ny),
        out_shape=[corner] * 2,
        in_specs=[VMEM] * 2,
        out_specs=[VMEM] * 2,
        compiler_params=limit(4),
        name="corners",
    )(*x_edges)
    corners = [along_y(corner, link) for corner, link in zip(corners, LINKS)]
    increment = time_increment.reshape(1)
    passed_in = [array(3, nx - 4, wide), array(2, nx - 4, wide), array(nx - 8, wide + 8), array(nx - 8, wide), array(3, nx - 8, ny)]
    passed_out = [array(3, 8, wide), array(2, 8, wide), array(8, wide + 8), array(8, wide), array(3, 8, ny)]
    cells, stress, state_in, passive_in, roots, *rest_in, peak = pl.pallas_call(
        functools.partial(inner_kernel, nx, ny),
        out_shape=[
            array(5, nx, ny + 20),
            array(nx - 2, tall),
            *passed_in[:2],
            array(nx - 4, wide + 8),
            *passed_in[2:],
            array(wide),
        ],
        in_specs=[SMEM] + [VMEM] * 3,
        out_specs=[VMEM] * 9,
        scratch_shapes=[
            scratch(nx - 2, tall),
            scratch(nx - 2, tall),
            scratch(3, nx - 8, wide + 8),
            scratch(3, nx - 8, wide + 8),
        ],
        compiler_params=limit(8),
        cost_estimate=pl.CostEstimate(flops=5 * 10**6, bytes_accessed=2 * 10**6, transcendentals=0),
        name="inner",
    )(increment, own, *y_edges)
    *outer, smallest = pl.pallas_call(
        functools.partial(outer_kernel, nx, ny),
        out_shape=passed_out + [array(lax.axis_size(("gx", "gy")))],
        in_specs=[SMEM] + [VMEM] * 9,
        out_specs=[VMEM] * 6,
        scratch_shapes=[
            scratch(5, 2 * LEFT, ny + 20),
            scratch(2, EDGE_KINDS + 1, ny + 20),
            scratch(10, tall),
            scratch(8, tall),
            scratch(8, tall),
            scratch(4, wide + 8),
            scratch(3, 4, wide + 8),
            scratch(3, 4, wide + 8),
            scratch(3, 4, wide + 8),
            scratch(3, 4, wide + 8),
        ],
        compiler_params=limit(8),
        name="outer",
    )(increment, *x_edges, *corners, cells, stress, state_in, roots, peak)
    outs = pl.pallas_call(
        functools.partial(carry_kernel, nx, ny),
        out_shape=[array(nx, ny)] * 5,
        in_specs=[SMEM] + [VMEM] * 10,
        out_specs=[VMEM] * 2 + [HBM] * 3,
        scratch_shapes=[
            scratch(2, nx, wide + 8),
            scratch(2, nx, wide + 8),
            pltpu.SemaphoreType.DMA((3, 3)),
        ],
        compiler_params=limit(8),
        cost_estimate=pl.CostEstimate(flops=10**7, bytes_accessed=4 * 10**6, transcendentals=0),
        name="carry",
    )(increment, state_in, passive_in, *rest_in, *outer)
    return (*outs, jnp.min(lax.all_to_all(smallest, ("gx", "gy"), 0, 0, tiled=True)))


def solution(mesh):
    cells = P("gx", "gy", None)
    return jax.shard_map(
        body,
        mesh=mesh,
        in_specs=(cells,) * 5 + (P(),),
        out_specs=(cells,) * 5 + (P(),),
        check_vma=False,
    )
```
